32 devices in a mesh: dp: 16 (over z, y, x), tensor: 2 (over core).
Axes of the slice: x: 2, y: 2, z: 4, core: 2. Of those that a mesh axis runs over, the one named last changes fastest.
Arguments:
- layer_input: bfloat16 [20480, 1536], P('dp'), may hold values from -6 to 6
- branch_point: int32 [16, 2], P('dp'), may hold values from 512 to 1024, as said below
- attn_gain: float32 [1536], replicated, may hold values from 0.5 to 1.5
- w_query: bfloat16 [1536, 1536], P(None, 'tensor'), may hold values from -0.15625 to 0.15625
- w_key: bfloat16 [1536, 768], P(None, 'tensor'), may hold values from -0.15625 to 0.15625
- w_value: bfloat16 [1536, 768], P(None, 'tensor'), may hold values from -0.15625 to 0.15625
- w_out: bfloat16 [1536, 1536], P('tensor'), may hold values from -0.875 to 0.875
- ffn_gain: float32 [1536], replicated, may hold values from 0.5 to 1.5
- w_gate: bfloat16 [1536, 4096], P(None, 'tensor'), may hold values from -0.15625 to 0.15625
- w_up: bfloat16 [1536, 4096], P(None, 'tensor'), may hold values from -0.15625 to 0.15625
- w_down: bfloat16 [4096, 1536], P('tensor'), may hold values from -0.09375 to 0.09375
- cotangent: bfloat16 [20480, 1536], P('dp'), may hold values from -6 to 6
Outputs:
- output: bfloat16 [20480, 1536], P('dp')
- grad_input: bfloat16 [20480, 1536], P('dp')
- grad_attn_gain: float32 [1536], P('dp')
- grad_query: float32 [1536, 1536], P('dp', 'tensor')
- grad_key: float32 [1536, 768], P('dp', 'tensor')
- grad_value: float32 [1536, 768], P('dp', 'tensor')
- grad_out_proj: float32 [1536, 1536], P('tensor', 'dp')
- grad_ffn_gain: float32 [1536], P('dp')
- grad_gate: float32 [1536, 4096], P('dp', 'tensor')
- grad_up: float32 [1536, 4096], P('dp', 'tensor')
- grad_down: float32 [4096, 1536], P('tensor', 'dp')
The draws below stay inside these ranges and needn't reach their ends.
Inputs may be any that keep to these rules, and one draw needn't show every extreme that they name: `branch_point`: in every group one continuation follows the whole prompt; every continuation follows 1024 // 2 prompt tokens or more.
All inputs are finite; a program needn't handle non-finite values.
Results may differ from the reference program's by a relative error of at most 0.017.
Values may be sent and summed in bfloat16 or wider, within the bound.
No kernel may reach another device: no remote copies, remote signals or barrier semaphores. Data moves between devices by JAX's collectives and lax.ppermute only.
A program may use at most 320 MiB of HBM per device.

```python
import jax
import jax.numpy as jnp
from jax import lax

D = 1536
HEADS = 16
KV_HEADS = 8
HEAD_DIM = 96
FF = 4096
PROMPT = 1024
CONT_LEN = 128
CONT = 2
GROUP_TOK = 1280
GROUPS = 16
TOKENS = 20480


def draw_branch_point(key, part):
    key = jax.random.fold_in(key, 7)
    first_key, second_key = jax.random.split(key)
    spread = jax.random.randint(first_key, (GROUPS, CONT), PROMPT // 2, PROMPT + 1)
    chosen = jax.random.randint(second_key, (GROUPS, 1), 0, CONT)
    columns = jnp.arange(CONT, dtype=jnp.int32)[None, :]
    return jnp.where(columns == chosen, PROMPT, spread).astype(jnp.int32)


def with_spikes(drawn, own_key, source, target, parts, factor):
    def block_of(position):
        return (jnp.arange(drawn.shape[position]) // (drawn.shape[position] // parts)).reshape((-1,) + (1,) * (drawn.ndim - 1 - position))

    near = jax.random.permutation(own_key, parts)[block_of(target)]
    second = (block_of(target) + parts // 2) % parts
    return jnp.where((block_of(source) == near) | (block_of(source) == second), factor * drawn, drawn)


def shard_levels(own_key, shape, shards, low, largest):
    gain = 1.0
    for axis_at, blocks in shards:
        draws = jax.random.uniform(jax.random.fold_in(jax.random.fold_in(own_key, 6), axis_at), (blocks,), jnp.float32, low / len(shards), largest / len(shards))
        gain = gain * jnp.repeat(jnp.exp(draws), shape[axis_at] // blocks).reshape((-1,) + (1,) * (len(shape) - 1 - axis_at))
    return gain


def gaussian(rng, shape, width, reach, cuts=(), kind=jnp.bfloat16):
    entries = jax.random.normal(rng, shape, jnp.float32) * width
    if len(cuts) > 0:
        entries = shard_levels(rng, shape, cuts, -0.22, 0.18) * entries
    return jnp.clip(entries, min=-reach, max=reach).astype(kind)


def bell_draw_with(key, shape, width, limit, cuts, heavy, held_as=jnp.bfloat16):
    array = width * jax.random.normal(key, shape, jnp.float32)
    if cuts:
        array = array * shard_levels(key, shape, cuts, -0.22, 0.18)
    return jnp.clip(with_spikes(array, jax.random.fold_in(key, 3), *heavy), -limit, limit).astype(held_as)


def setup_inputs(seed: int = 0) -> dict:
    splits = jax.random.split(jax.random.key(seed), 13)
    return {
        "layer_input": bell_draw_with(splits[0], (TOKENS, D), 1.0, 6.0, ((0, 16),), (0, 1, 16, 2.0)),
        "branch_point": draw_branch_point(jax.random.fold_in(splits[12], 71), 0),
        "attn_gain": jnp.clip(1.0 + 0.1 * jax.random.normal(splits[2], (D,), jnp.float32), 0.5, 1.5),
        "w_query": gaussian(splits[3], (D, HEADS * HEAD_DIM), D ** -0.5, 0.15625, ((1, 2),)),
        "w_key": gaussian(splits[4], (D, KV_HEADS * HEAD_DIM), D ** -0.5, 0.15625, ((1, 2),)),
        "w_value": gaussian(splits[5], (D, KV_HEADS * HEAD_DIM), D ** -0.5, 0.15625, ((1, 2),)),
        "w_out": gaussian(splits[6], (HEADS * HEAD_DIM, D), (HEADS * HEAD_DIM // 32) ** -0.5, 0.875, ((0, 2),)),
        "ffn_gain": jnp.clip(1.0 + 0.1 * jax.random.normal(splits[7], (D,), jnp.float32), 0.5, 1.5),
        "w_gate": gaussian(splits[8], (D, FF), D ** -0.5, 0.15625, ((1, 2),)),
        "w_up": gaussian(splits[9], (D, FF), D ** -0.5, 0.15625, ((1, 2),)),
        "w_down": gaussian(splits[10], (FF, D), FF ** -0.5, 0.09375, ((0, 2),)),
        "cotangent": bell_draw_with(splits[11], (TOKENS, D), 1.0, 6.0, ((0, 16),), (0, 1, 16, 2.0)),
    }


@jax.custom_vjp
def low(v):
    return lax.optimization_barrier(v.astype(jnp.bfloat16)).astype(jnp.float32)

@jax.custom_vjp
def low_back(v):
    return v

def low_keep(v):
    return (low(v), None)

def low_pass(kept, grad):
    return (grad,)

def back_keep(v):
    return (v, None)

def back_low(kept, grad):
    return (low(grad),)
low.defvjp(low_keep, low_pass)
low_back.defvjp(back_keep, back_low)
epsilon = 1e-05
rope_base = 100000.0
highest = lax.Precision.HIGHEST

def rms_norm(values, scale_gain):
    return values * lax.rsqrt(lax.optimization_barrier(jnp.mean(values * values, axis=-1, keepdims=True)) + epsilon) * scale_gain

def group_layout(branch):
    row_ids = jnp.arange(GROUP_TOK, dtype=jnp.int32)
    cont_ids = jnp.arange(CONT, dtype=jnp.int32)
    owners = jnp.concatenate([jnp.full((PROMPT,), -1, jnp.int32), jnp.repeat(cont_ids, CONT_LEN)])
    reaches = lax.optimization_barrier(jnp.sum(jnp.where(owners[:, None] == cont_ids[None, :], branch[None, :], 0), axis=1)).astype(jnp.int32)
    offset = jnp.maximum(row_ids - PROMPT, 0) % CONT_LEN
    positions = jnp.where(owners < 0, row_ids, reaches + offset).astype(jnp.int32)
    own_block = (owners[:, None] == owners[None, :]) & (row_ids[None, :] <= row_ids[:, None])
    into_prompt = (owners[None, :] < 0) & (owners[:, None] >= 0) & (row_ids[None, :] < reaches[:, None])
    return (positions, own_block | into_prompt)

def rotary(tensor, positions):
    half_dim = tensor.shape[-1] // 2
    frequency = rope_base ** (-jnp.arange(half_dim, dtype=jnp.float32) * 2.0 / tensor.shape[-1])
    angles = positions.astype(jnp.float32)[:, None] * frequency[None, :]
    cosine = jnp.cos(angles)[:, None, :]
    sine_part = jnp.sin(angles)[:, None, :]
    leading = tensor[..., :half_dim]
    trailing = tensor[..., half_dim:]
    return jnp.concatenate([leading * cosine - trailing * sine_part, trailing * cosine + leading * sine_part], axis=-1)

def group_forward(inputs, branch, attn_gain, w_query, w_key, w_value, w_out, ffn_gain, w_gate, w_up, w_down):
    positions, allowed = group_layout(branch)
    act_one = low(rms_norm(inputs, attn_gain))
    query_lin = low_back(jnp.dot(act_one, w_query, precision=highest)).reshape(GROUP_TOK, HEADS, HEAD_DIM)
    key_lin = low_back(jnp.dot(act_one, w_key, precision=highest)).reshape(GROUP_TOK, KV_HEADS, HEAD_DIM)
    value_lin = low_back(jnp.dot(act_one, w_value, precision=highest)).reshape(GROUP_TOK, KV_HEADS, HEAD_DIM)
    queries = low(rotary(query_lin, positions)).reshape(GROUP_TOK, KV_HEADS, HEADS // KV_HEADS, HEAD_DIM)
    keys = low(rotary(key_lin, positions))
    values = low(value_lin)
    scores = low_back(jnp.einsum('qkgd,pkd->kgqp', queries, keys, precision=highest) * HEAD_DIM ** (-0.5))
    scores = jnp.where(allowed[None, None], scores, -1e+30)
    probs = low(jax.nn.softmax(scores, axis=-1))
    mixed = jnp.einsum('kgqp,pkd->qkgd', probs, values, precision=highest).reshape(GROUP_TOK, HEADS * HEAD_DIM)
    mixed = low(low_back(mixed))
    hidden_state = inputs + low_back(jnp.dot(mixed, w_out, precision=highest))
    act_two = low(rms_norm(hidden_state, ffn_gain))
    gate = low_back(jnp.dot(act_two, w_gate, precision=highest))
    up_proj = low_back(jnp.dot(act_two, w_up, precision=highest))
    hidden_units = low(jax.nn.silu(gate) * up_proj)
    return hidden_state + low_back(jnp.dot(hidden_units, w_down, precision=highest))

def reference(layer_input, branch_point, attn_gain, w_query, w_key, w_value, w_out, ffn_gain, w_gate, w_up, w_down, cotangent):
    params = tuple((tensor.astype(jnp.float32) for tensor in (attn_gain, w_query, w_key, w_value, w_out, ffn_gain, w_gate, w_up, w_down)))
    inputs = layer_input.astype(jnp.float32).reshape(GROUPS, GROUP_TOK, D)
    cotangents = cotangent.astype(jnp.float32).reshape(GROUPS, GROUP_TOK, D)

    def one_group(totals, item):
        group_in, branch, group_cot = item

        def forward(group_values, *weights):
            return group_forward(group_values, branch, *weights)
        result, pull = jax.vjp(jax.checkpoint(forward), group_in, *params)
        grads = pull(group_cot)
        summed = tuple((total + grad for total, grad in zip(totals, grads[1:])))
        return (summed, (result, grads[0]))
    zeros = tuple((jnp.zeros_like(tensor) for tensor in params))
    totals, (results, input_grads) = lax.scan(one_group, zeros, (inputs, branch_point, cotangents))
    output = results.reshape(TOKENS, D).astype(jnp.bfloat16)
    grad_input = input_grads.reshape(TOKENS, D).astype(jnp.bfloat16)
    return (output, grad_input, totals[0], totals[1], totals[2], totals[3], totals[4], totals[5], totals[6], totals[7], totals[8])
```

```python
import jax
import jax.numpy as jnp
from jax import lax
from jax.sharding import PartitionSpec as P

HEAD_DIM = 96
PROMPT = 1024
CONT_LEN = 128
CONT = 2
GROUP_TOK = 1280


epsilon = 1e-05
rope_base = 100000.0


def rms_norm(values, scale_gain):
    return (
        values * lax.rsqrt(jnp.mean(values * values, axis=-1, keepdims=True) + epsilon) * scale_gain
    )


def group_layout(branch):
    row_ids = jnp.arange(GROUP_TOK, dtype=jnp.int32)
    cont_ids = jnp.arange(CONT, dtype=jnp.int32)
    owners = jnp.concatenate([jnp.full((PROMPT,), -1, jnp.int32), jnp.repeat(cont_ids, CONT_LEN)])
    reaches = jnp.sum(jnp.where(owners[:, None] == cont_ids[None, :], branch[None, :], 0), axis=1)
    offset = jnp.maximum(row_ids - PROMPT, 0) % CONT_LEN
    positions = jnp.where(owners < 0, row_ids, reaches + offset)
    own_block = (owners[:, None] == owners[None, :]) & (row_ids[None, :] <= row_ids[:, None])
    into_prompt = (
        (owners[None, :] < 0) & (owners[:, None] >= 0) & (row_ids[None, :] < reaches[:, None])
    )
    return (positions, own_block | into_prompt)


def rotary(tensor, positions):
    half_dim = tensor.shape[-1] // 2
    frequency = rope_base ** (-jnp.arange(half_dim, dtype=jnp.float32) * 2.0 / tensor.shape[-1])
    angles = positions.astype(jnp.float32)[:, None] * frequency[None, :]
    cosine = jnp.cos(angles)[:, None, :]
    sine_part = jnp.sin(angles)[:, None, :]
    leading = tensor[..., :half_dim]
    trailing = tensor[..., half_dim:]
    return jnp.concatenate(
        [leading * cosine - trailing * sine_part, trailing * cosine + leading * sine_part], axis=-1
    )


def block_scores(query_block, allowed_block, keys):
    scores = jnp.einsum(
        "qkgd,pkd->kgqp", query_block, keys, preferred_element_type=jnp.float32
    ) * HEAD_DIM ** (-0.5)
    return jnp.where(allowed_block[None, None], scores, -1e30)


def swiglu(gate, up_proj):
    return jax.nn.silu(gate) * up_proj


def exchange_sum(partial):
    sent = partial.astype(jnp.bfloat16)
    received = lax.ppermute(sent, "tensor", [(0, 1), (1, 0)])
    return sent.astype(jnp.float32) + received.astype(jnp.float32)


def scatter_sum(grads, order):
    size = lax.axis_size("dp")
    bits = size.bit_length() - 1
    me = lax.axis_index("dp")
    work = grads.astype(jnp.bfloat16)
    rows, width = work.shape
    work = work.reshape((2,) * bits + (rows // size, width))
    left = list(range(bits))[::-1]
    for bit in [b for b in order if b < bits] + list(range(len(order), bits)):
        axis = left.index(bit)
        mine = (me >> bit) & 1
        sent = lax.dynamic_index_in_dim(work, 1 - mine, axis, keepdims=False)
        kept = lax.dynamic_index_in_dim(work, mine, axis, keepdims=False)
        pairs = [(i, i ^ (1 << bit)) for i in range(size)]
        received = lax.ppermute(sent, "dp", pairs)
        total = kept.astype(jnp.float32) + received.astype(jnp.float32)
        left.pop(axis)
        work = total.astype(jnp.bfloat16) if left else total
    return work


X_FIRST = (0, 1, 2, 3)
Y_FIRST = (1, 0, 2, 3)


def per_device(
    layer_input,
    branch_point,
    attn_gain,
    w_query,
    w_key,
    w_value,
    w_out,
    ffn_gain,
    w_gate,
    w_up,
    w_down,
    cotangent,
):
    positions, allowed = group_layout(branch_point[0])
    local_heads = w_query.shape[1] // HEAD_DIM
    local_kv = w_key.shape[1] // HEAD_DIM
    grouping = local_heads // local_kv
    block_rows = GROUP_TOK // 2
    scale = HEAD_DIM ** (-0.5)
    inputs = layer_input.astype(jnp.float32)
    grad_out = cotangent.astype(jnp.float32)
    normed_one, pull_one = jax.vjp(rms_norm, inputs, attn_gain)
    act_one = normed_one.astype(jnp.bfloat16)
    query_lin = jnp.dot(act_one, w_query, preferred_element_type=jnp.float32).reshape(
        GROUP_TOK, local_heads, HEAD_DIM
    )
    key_lin = jnp.dot(act_one, w_key, preferred_element_type=jnp.float32).reshape(
        GROUP_TOK, local_kv, HEAD_DIM
    )
    value_lin = jnp.dot(act_one, w_value, preferred_element_type=jnp.float32).reshape(
        GROUP_TOK, local_kv, HEAD_DIM
    )
    queries = (
        rotary(query_lin, positions)
        .astype(jnp.bfloat16)
        .reshape(2, block_rows, local_kv, grouping, HEAD_DIM)
    )
    keys = rotary(key_lin, positions).astype(jnp.bfloat16)
    values = value_lin.astype(jnp.bfloat16)
    allowed_blocks = allowed.reshape(2, block_rows, GROUP_TOK)

    def forward_block(item):
        scores = block_scores(item[0], item[1], keys)
        largest = jnp.max(scores, axis=-1, keepdims=True)
        shifted = jnp.exp(scores - largest)
        totals = jnp.sum(shifted, axis=-1, keepdims=True)
        probs = (shifted / totals).astype(jnp.bfloat16)
        result = jnp.einsum("kgqp,pkd->qkgd", probs, values, preferred_element_type=jnp.float32)
        return (result, (largest + jnp.log(totals))[..., 0])

    mixed, log_totals = lax.map(forward_block, (queries, allowed_blocks))
    mixed = mixed.reshape(GROUP_TOK, local_heads * HEAD_DIM).astype(jnp.bfloat16)
    partial_attn = jnp.dot(mixed, w_out, preferred_element_type=jnp.float32)
    hidden_state = inputs + exchange_sum(partial_attn)
    normed_two, pull_two = jax.vjp(rms_norm, hidden_state, ffn_gain)
    act_two = normed_two.astype(jnp.bfloat16)
    gate = jnp.dot(act_two, w_gate, preferred_element_type=jnp.float32)
    up_proj = jnp.dot(act_two, w_up, preferred_element_type=jnp.float32)
    units_full, pull_units = jax.vjp(swiglu, gate, up_proj)
    hidden_units = units_full.astype(jnp.bfloat16)
    partial_ffn = jnp.dot(hidden_units, w_down, preferred_element_type=jnp.float32)
    output = (hidden_state + exchange_sum(partial_ffn)).astype(jnp.bfloat16)
    half = hidden_units.shape[1] // 2
    grad_down_a, grad_down_b = [
        scatter_sum(
            jnp.einsum("td,tf->df", cotangent, part, preferred_element_type=jnp.float32), order
        )
        for part, order in (
            (hidden_units[:, :half], X_FIRST),
            (hidden_units[:, half:], Y_FIRST),
        )
    ]
    grad_units = jnp.einsum("td,fd->tf", cotangent, w_down, preferred_element_type=jnp.float32)
    grad_gate_full, grad_up_full = pull_units(grad_units)
    grad_gate_lin = grad_gate_full.astype(jnp.bfloat16)
    grad_up_lin = grad_up_full.astype(jnp.bfloat16)
    grad_gate_w = jnp.einsum(
        "td,tf->df", act_two, grad_gate_lin, preferred_element_type=jnp.float32
    )
    grad_up_w = jnp.einsum("td,tf->df", act_two, grad_up_lin, preferred_element_type=jnp.float32)
    partial_two = jnp.einsum("tf,df->td", grad_gate_lin, w_gate, preferred_element_type=jnp.float32)
    partial_two = partial_two + jnp.einsum(
        "tf,df->td", grad_up_lin, w_up, preferred_element_type=jnp.float32
    )
    grad_act_two = exchange_sum(partial_two)
    grad_from_two, grad_ffn_gain = pull_two(grad_act_two)
    grad_hidden = grad_out + grad_from_two
    grad_attention = grad_hidden.astype(jnp.bfloat16)
    grad_out_w = jnp.einsum("td,tc->dc", grad_attention, mixed, preferred_element_type=jnp.float32)
    grad_mixed = jnp.einsum(
        "td,cd->tc", grad_attention, w_out, preferred_element_type=jnp.float32
    ).astype(jnp.bfloat16)
    grad_mixed = grad_mixed.reshape(2, block_rows, local_kv, grouping, HEAD_DIM)

    def backward_block(carry, item):
        key_grads, value_grads = carry
        query_block, allowed_block, grad_block, block_totals = item
        scores = block_scores(query_block, allowed_block, keys)
        probs_full = jnp.exp(scores - block_totals[..., None])
        grad_probs = jnp.einsum(
            "qkgd,pkd->kgqp", grad_block, values, preferred_element_type=jnp.float32
        )
        weighted = jnp.sum(probs_full * grad_probs, axis=-1, keepdims=True)
        grad_scores = (probs_full * (grad_probs - weighted)).astype(jnp.bfloat16)
        query_grad = (
            jnp.einsum("kgqp,pkd->qkgd", grad_scores, keys, preferred_element_type=jnp.float32)
            * scale
        )
        key_grads = (
            key_grads
            + jnp.einsum(
                "kgqp,qkgd->pkd", grad_scores, query_block, preferred_element_type=jnp.float32
            )
            * scale
        )
        value_grads = value_grads + jnp.einsum(
            "kgqp,qkgd->pkd",
            probs_full.astype(jnp.bfloat16),
            grad_block,
            preferred_element_type=jnp.float32,
        )
        return ((key_grads, value_grads), query_grad)

    empty = jnp.zeros((GROUP_TOK, local_kv, HEAD_DIM), jnp.float32)
    (key_grads, value_grads), query_grads = lax.scan(
        backward_block, (empty, empty), (queries, allowed_blocks, grad_mixed, log_totals)
    )
    back_positions = -positions
    grad_query_lin = rotary(query_grads.reshape(GROUP_TOK, local_heads, HEAD_DIM), back_positions)
    grad_query_lin = grad_query_lin.reshape(GROUP_TOK, local_heads * HEAD_DIM).astype(jnp.bfloat16)
    grad_key_lin = (
        rotary(key_grads, back_positions)
        .reshape(GROUP_TOK, local_kv * HEAD_DIM)
        .astype(jnp.bfloat16)
    )
    grad_value_lin = value_grads.reshape(GROUP_TOK, local_kv * HEAD_DIM).astype(jnp.bfloat16)
    grad_query_w = jnp.einsum(
        "td,tc->dc", act_one, grad_query_lin, preferred_element_type=jnp.float32
    )
    grad_key_w = jnp.einsum("td,tc->dc", act_one, grad_key_lin, preferred_element_type=jnp.float32)
    grad_value_w = jnp.einsum(
        "td,tc->dc", act_one, grad_value_lin, preferred_element_type=jnp.float32
    )
    partial_one = jnp.einsum(
        "tc,dc->td", grad_query_lin, w_query, preferred_element_type=jnp.float32
    )
    partial_one = partial_one + jnp.einsum(
        "tc,dc->td", grad_key_lin, w_key, preferred_element_type=jnp.float32
    )
    partial_one = partial_one + jnp.einsum(
        "tc,dc->td", grad_value_lin, w_value, preferred_element_type=jnp.float32
    )
    grad_act_one = exchange_sum(partial_one)
    grad_from_one, grad_attn_gain = pull_one(grad_act_one)
    grad_input = (grad_hidden + grad_from_one).astype(jnp.bfloat16)
    gains = jnp.stack([grad_attn_gain, grad_ffn_gain], axis=1)
    gains = lax.psum_scatter(gains, "dp", scatter_dimension=0, tiled=True)
    return (
        output,
        grad_input,
        gains[:, 0],
        scatter_sum(grad_query_w, Y_FIRST),
        scatter_sum(grad_key_w, X_FIRST),
        scatter_sum(grad_value_w, X_FIRST),
        scatter_sum(grad_out_w, X_FIRST).T,
        gains[:, 1],
        scatter_sum(grad_gate_w, X_FIRST),
        scatter_sum(grad_up_w, Y_FIRST),
        jnp.concatenate([grad_down_a.T, grad_down_b.T], axis=0),
    )


def solution(mesh):
    placed = (
        P("dp", None),
        P("dp", None),
        P(),
        P(None, "tensor"),
        P(None, "tensor"),
        P(None, "tensor"),
        P("tensor", None),
        P(),
        P(None, "tensor"),
        P(None, "tensor"),
        P("tensor", None),
        P("dp", None),
    )
    return jax.shard_map(
        per_device,
        mesh=mesh,
        in_specs=placed,
        out_specs=(
            P("dp", None),
            P("dp", None),
            P("dp"),
            P("dp", "tensor"),
            P("dp", "tensor"),
            P("dp", "tensor"),
            P("tensor", "dp"),
            P("dp"),
            P("dp", "tensor"),
            P("dp", "tensor"),
            P("tensor", "dp"),
        ),
        check_vma=False,
    )
```

```python
import jax
import jax.numpy as jnp
import numpy as np
from jax import lax
from jax.experimental import pallas as pl
from jax.experimental.pallas import tpu as pltpu
from jax.sharding import PartitionSpec as P

HEAD_DIM = 96
PROMPT = 1024
CONT_LEN = 128
CONT = 2
GROUP_TOK = 1280
BLOCK = 256
BLOCKS = GROUP_TOK // BLOCK
LANES = 128
MIB = 1 << 20
epsilon = 1e-05
rope_base = 100000.0
LOG2E = 1.4426950408889634
SCORE_SCALE = HEAD_DIM ** (-0.5)
NT = (((1,), (1,)), ((), ()))
TN = (((0,), (0,)), ((), ()))


def matmul(left, right, dims=(((1,), (0,)), ((), ()))):
    return lax.dot_general(left, right, dims, preferred_element_type=jnp.float32)


def rope_tables(branch):
    half = HEAD_DIM // 2
    frequency = rope_base ** (-np.arange(half, dtype=np.float64) * 2.0 / HEAD_DIM)
    angles = np.arange(PROMPT + CONT_LEN, dtype=np.float64)[:, None] * frequency[None, :]
    pad = np.zeros((angles.shape[0], LANES - HEAD_DIM))
    cosine = np.concatenate([np.cos(angles), np.cos(angles), pad], axis=1)
    sine = np.concatenate([-np.sin(angles), np.sin(angles), pad], axis=1)
    both = jnp.asarray(np.stack([cosine, sine]), jnp.float32)
    parts = [both[:, :PROMPT]]
    for c in range(CONT):
        parts.append(lax.dynamic_slice_in_dim(both, branch[c], CONT_LEN, axis=1))
    return jnp.concatenate(parts, axis=1)


def lane_ids(shape):
    return lax.broadcasted_iota(jnp.int32, shape, 1)


def swap_halves(head):
    half = HEAD_DIM // 2
    return jnp.where(
        lane_ids(head.shape) < half, pltpu.roll(head, LANES - half, 1), pltpu.roll(head, half, 1)
    )


def take_head(full, h):
    first = h * HEAD_DIM
    start, shift = first // LANES * LANES, first % LANES
    width = LANES if shift + HEAD_DIM <= LANES else 2 * LANES
    part = full[:, start : start + width]
    return part[:, :LANES] if shift == 0 else pltpu.roll(part, width - shift, 1)[:, :LANES]


def join_heads(heads):
    lanes = lane_ids(heads[0].shape)
    out = []
    for i in range(0, len(heads), 4):
        one, two, three = (pltpu.roll(heads[i + j], LANES - 32 * j, 1) for j in (1, 2, 3))
        out.append(jnp.where(lanes < 96, heads[i], one))
        out.append(jnp.where(lanes < 64, one, two))
        out.append(jnp.where(lanes < 32, two, three))
    return jnp.concatenate(out, axis=1)


def own_mask(shape, query_axis, block):
    query = lax.broadcasted_iota(jnp.int32, shape, query_axis) & (BLOCK - 1)
    key = lax.broadcasted_iota(jnp.int32, shape, 1 - query_axis)
    mask = key <= query
    if block * BLOCK >= PROMPT:
        mask = mask & ((key // CONT_LEN) == (query // CONT_LEN))
    return mask


def reach_mask(shape, query_axis, branch_ref):
    query = lax.broadcasted_iota(jnp.int32, shape, query_axis) & (BLOCK - 1)
    key = lax.broadcasted_iota(jnp.int32, shape, 1 - query_axis) + PROMPT // 2
    return key < jnp.where(query < CONT_LEN, branch_ref[0, 0], branch_ref[0, 1])


def attention_forward_kernel(
    branch_ref, x_ref, gain_ref, wq_ref, wk_ref, wv_ref, wo_ref, rope_ref,
    act_ref, q_ref, k_ref, v_ref, mixed_ref, lse_ref, part_ref, o_ref,
):
    kv_heads = k_ref.shape[0]
    group = 2 * BLOCK

    def project(i, carry):
        rows = pl.ds(pl.multiple_of(i * BLOCK, BLOCK), BLOCK)
        x = x_ref[rows, :].astype(jnp.float32)
        norm = lax.rsqrt(jnp.mean(x * x, axis=-1, keepdims=True) + epsilon)
        act = (x * norm * gain_ref[...]).astype(jnp.bfloat16)
        act_ref[rows, :] = act
        cosine, sine = rope_ref[0, rows, :], rope_ref[1, rows, :]
        full = matmul(act, wq_ref[...])
        for h in range(2 * kv_heads):
            head = take_head(full, h)
            rotated = head * cosine + swap_halves(head) * sine
            q_ref[h // 2, i, pl.ds(h % 2 * BLOCK, BLOCK), :] = rotated.astype(jnp.bfloat16)
        full = matmul(act, wk_ref[...])
        for h in range(kv_heads):
            head = take_head(full, h)
            rotated = head * cosine + swap_halves(head) * sine
            k_ref[h, rows, :] = rotated.astype(jnp.bfloat16)
        full = matmul(act, wv_ref[...])
        lanes = lane_ids((BLOCK, LANES))
        for h in range(kv_heads):
            head = jnp.where(lanes < HEAD_DIM, take_head(full, h), 0.0)
            v_ref[h, rows, :] = jnp.where(lanes == HEAD_DIM, 1.0, head).astype(jnp.bfloat16)
        return carry

    lax.fori_loop(0, BLOCKS, project, 0)

    factor = SCORE_SCALE * LOG2E

    def attend(h, carry):
        for i in range(BLOCKS):
            query = q_ref[h, i]
            before = i * BLOCK
            own = matmul(query, k_ref[h, before : before + BLOCK], NT)
            own = jnp.where(own_mask(own.shape, 0, i), own, -1e30)
            largest = jnp.max(own, axis=-1, keepdims=True)
            spans = []
            if i > 0:
                cuts = [0, before] if before < PROMPT else [0, PROMPT // 2, PROMPT]
                for low, high in zip(cuts[:-1], cuts[1:]):
                    scores = matmul(query, k_ref[h, low:high], NT)
                    if before >= PROMPT and low > 0:
                        scores = jnp.where(reach_mask(scores.shape, 0, branch_ref), scores, -1e30)
                    largest = jnp.maximum(largest, jnp.max(scores, axis=-1, keepdims=True))
                    spans.append((low, high, scores))
            shift = largest * factor
            probs = jnp.exp2(own * factor - shift).astype(jnp.bfloat16)
            total = matmul(probs, v_ref[h, before : before + BLOCK])
            for low, high, scores in spans:
                probs = jnp.exp2(scores * factor - shift).astype(jnp.bfloat16)
                total += matmul(probs, v_ref[h, low:high])
            sums = total[:, HEAD_DIM : HEAD_DIM + 1]
            mixed = total / sums
            for g in range(2):
                o_ref[2 * h + g, before : before + BLOCK, :] = mixed[g * BLOCK : (g + 1) * BLOCK]
            logs = shift + jnp.log2(sums)
            lse_ref[h, i] = jnp.broadcast_to(logs, (group, LANES)).T[0:1, :]
        return carry

    lax.fori_loop(0, kv_heads, attend, 0)

    def finish(i, carry):
        rows = pl.ds(pl.multiple_of(i * BLOCK, BLOCK), BLOCK)
        mixed = join_heads([o_ref[h, rows, :] for h in range(2 * kv_heads)]).astype(jnp.bfloat16)
        mixed_ref[rows, :] = mixed
        part_ref[rows, :] = matmul(mixed, wo_ref[...]).astype(jnp.bfloat16)
        return carry

    lax.fori_loop(0, BLOCKS, finish, 0)


def attention_forward(branch, x, gain, wq, wk, wv, wo, rope):
    kv_heads = wk.shape[1] // HEAD_DIM
    rows, width = x.shape
    bf = jnp.bfloat16
    vmem = pl.BlockSpec(memory_space=pltpu.VMEM)
    return pl.pallas_call(
        attention_forward_kernel,
        out_shape=(
            jax.ShapeDtypeStruct((rows, width), bf),
            jax.ShapeDtypeStruct((kv_heads, BLOCKS, 2 * BLOCK, LANES), bf),
            jax.ShapeDtypeStruct((kv_heads, rows, LANES), bf),
            jax.ShapeDtypeStruct((kv_heads, rows, LANES), bf),
            jax.ShapeDtypeStruct((rows, wq.shape[1]), bf),
            jax.ShapeDtypeStruct((kv_heads, BLOCKS, 1, 2 * BLOCK), jnp.float32),
            jax.ShapeDtypeStruct((rows, width), bf),
        ),
        in_specs=[pl.BlockSpec(memory_space=pltpu.SMEM)] + [vmem] * 7,
        out_specs=[vmem] * 7,
        scratch_shapes=[pltpu.VMEM((2 * kv_heads, rows, LANES), jnp.float32)],
        compiler_params=pltpu.CompilerParams(vmem_limit_bytes=60 * MIB),
        cost_estimate=pl.CostEstimate(flops=20 * 10**9, bytes_accessed=40 * 10**6, transcendentals=0),
        name="attention_forward",
    )(branch, x, gain.reshape(1, width), wq, wk, wv, wo, rope)


def attention_backward_kernel(
    branch_ref, gatt_ref, q_ref, k_ref, v_ref, lse_ref, wo_ref, wq_ref, wk_ref, wv_ref, rope_ref,
    gq_ref, gk_ref, gv_ref, part_ref, do_ref, dq_ref, dk_ref, dv_ref,
):
    kv_heads = k_ref.shape[0]
    group = 2 * BLOCK
    factor = SCORE_SCALE * LOG2E

    def project(i, carry):
        rows = pl.ds(pl.multiple_of(i * BLOCK, BLOCK), BLOCK)
        full = matmul(gatt_ref[rows, :], wo_ref[...], NT)
        lanes = lane_ids((BLOCK, LANES))
        for h in range(2 * kv_heads):
            head = jnp.where(lanes < HEAD_DIM, take_head(full, h), 0.0)
            do_ref[h // 2, i, pl.ds(h % 2 * BLOCK, BLOCK), :] = head.astype(jnp.bfloat16)
        return carry

    lax.fori_loop(0, BLOCKS, project, 0)

    def attend(h, carry):
        for i in reversed(range(BLOCKS)):
            query, grad, logs = q_ref[h, i], do_ref[h, i], lse_ref[h, i]
            before = i * BLOCK
            cuts = [(before, before + BLOCK)]
            if i > 0 and before < PROMPT:
                cuts += [(0, before)]
            elif i > 0:
                cuts += [(0, PROMPT // 2), (PROMPT // 2, PROMPT)]
            spans, weighted = [], 0.0
            for low, high in cuts:
                scores = matmul(k_ref[h, low:high], query, NT)
                probs = jnp.exp2(scores * factor - logs)
                if low == before:
                    probs = jnp.where(own_mask(probs.shape, 1, i), probs, 0.0)
                elif before >= PROMPT and low > 0:
                    probs = jnp.where(reach_mask(probs.shape, 1, branch_ref), probs, 0.0)
                grad_probs = matmul(v_ref[h, low:high], grad, NT)
                weighted += jnp.sum(probs * grad_probs, axis=0, keepdims=True)
                spans.append((low, high, probs, grad_probs))
            grad_query = jnp.zeros((group, LANES), jnp.float32)
            for low, high, probs, grad_probs in spans:
                grad_scores = (probs * (grad_probs - weighted)).astype(jnp.bfloat16)
                grad_query += matmul(grad_scores, k_ref[h, low:high], TN)
                grad_key = matmul(grad_scores, query)
                grad_value = matmul(probs.astype(jnp.bfloat16), grad)
                if before >= PROMPT:
                    dk_ref[h, low:high] = grad_key
                    dv_ref[h, low:high] = grad_value
                else:
                    dk_ref[h, low:high] += grad_key
                    dv_ref[h, low:high] += grad_value
            dq_ref[h, i] = grad_query
        return carry

    lax.fori_loop(0, kv_heads, attend, 0)

    def finish(i, carry):
        rows = pl.ds(pl.multiple_of(i * BLOCK, BLOCK), BLOCK)
        cosine, sine = rope_ref[0, rows, :] * SCORE_SCALE, rope_ref[1, rows, :] * SCORE_SCALE
        heads = []
        for h in range(2 * kv_heads):
            head = dq_ref[h // 2, i, pl.ds(h % 2 * BLOCK, BLOCK), :]
            heads.append(head * cosine - swap_halves(head) * sine)
        grad_q = join_heads(heads).astype(jnp.bfloat16)
        heads = []
        for h in range(kv_heads):
            head = dk_ref[h, rows, :]
            heads.append(head * cosine - swap_halves(head) * sine)
        grad_k = join_heads(heads).astype(jnp.bfloat16)
        grad_v = join_heads([dv_ref[h, rows, :] for h in range(kv_heads)]).astype(jnp.bfloat16)
        gq_ref[rows, :] = grad_q
        gk_ref[rows, :] = grad_k
        gv_ref[rows, :] = grad_v
        part = matmul(grad_q, wq_ref[...], NT)
        part += matmul(grad_k, wk_ref[...], NT)
        part += matmul(grad_v, wv_ref[...], NT)
        part_ref[rows, :] = part.astype(jnp.bfloat16)
        return carry

    lax.fori_loop(0, BLOCKS, finish, 0)


def attention_backward(branch, gatt, q, k, v, lse, wo, wq, wk, wv, rope):
    kv_heads = k.shape[0]
    rows, width = gatt.shape
    bf = jnp.bfloat16
    vmem = pl.BlockSpec(memory_space=pltpu.VMEM)
    return pl.pallas_call(
        attention_backward_kernel,
        out_shape=(
            jax.ShapeDtypeStruct((rows, wq.shape[1]), bf),
            jax.ShapeDtypeStruct((rows, wk.shape[1]), bf),
            jax.ShapeDtypeStruct((rows, wv.shape[1]), bf),
            jax.ShapeDtypeStruct((rows, width), bf),
        ),
        in_specs=[pl.BlockSpec(memory_space=pltpu.SMEM)] + [vmem] * 10,
        out_specs=[vmem] * 4,
        scratch_shapes=[
            pltpu.VMEM((kv_heads, BLOCKS, 2 * BLOCK, LANES), bf),
            pltpu.VMEM((kv_heads, BLOCKS, 2 * BLOCK, LANES), jnp.float32),
            pltpu.VMEM((kv_heads, rows, LANES), jnp.float32),
            pltpu.VMEM((kv_heads, rows, LANES), jnp.float32),
        ],
        compiler_params=pltpu.CompilerParams(vmem_limit_bytes=60 * MIB),
        cost_estimate=pl.CostEstimate(flops=35 * 10**9, bytes_accessed=40 * 10**6, transcendentals=0),
        name="attention_backward",
    )(branch, gatt, q, k, v, lse, wo, wq, wk, wv, rope)


def rms_norm(values, scale_gain):
    return (
        values * lax.rsqrt(jnp.mean(values * values, axis=-1, keepdims=True) + epsilon) * scale_gain
    )


def swiglu(gate, up_proj):
    return jax.nn.silu(gate) * up_proj


def exchange_sum(partial):
    sent = partial.astype(jnp.bfloat16)
    received = lax.ppermute(sent, "tensor", [(0, 1), (1, 0)])
    return sent.astype(jnp.float32) + received.astype(jnp.float32)


def scatter_sum(grads, order):
    size = lax.axis_size("dp")
    bits = size.bit_length() - 1
    me = lax.axis_index("dp")
    work = grads.astype(jnp.bfloat16)
    rows, width = work.shape
    work = work.reshape((2,) * bits + (rows // size, width))
    left = list(range(bits))[::-1]
    for bit in [b for b in order if b < bits] + list(range(len(order), bits)):
        axis = left.index(bit)
        mine = (me >> bit) & 1
        sent = lax.dynamic_index_in_dim(work, 1 - mine, axis, keepdims=False)
        kept = lax.dynamic_index_in_dim(work, mine, axis, keepdims=False)
        pairs = [(i, i ^ (1 << bit)) for i in range(size)]
        received = lax.ppermute(sent, "dp", pairs)
        total = kept.astype(jnp.float32) + received.astype(jnp.float32)
        left.pop(axis)
        work = total.astype(jnp.bfloat16) if left else total
    return work


X_FIRST = (0, 1, 2, 3)
Y_FIRST = (1, 0, 2, 3)


def per_device(
    layer_input,
    branch_point,
    attn_gain,
    w_query,
    w_key,
    w_value,
    w_out,
    ffn_gain,
    w_gate,
    w_up,
    w_down,
    cotangent,
):
    rope = rope_tables(branch_point[0])
    inputs = layer_input.astype(jnp.float32)
    grad_out = cotangent.astype(jnp.float32)
    _, pull_one = jax.vjp(rms_norm, inputs, attn_gain)
    act_one, queries, keys, values, mixed, log_sums, partial_attn = attention_forward(
        branch_point, layer_input, attn_gain, w_query, w_key, w_value, w_out, rope
    )
    hidden_state = inputs + exchange_sum(partial_attn)
    normed_two, pull_two = jax.vjp(rms_norm, hidden_state, ffn_gain)
    act_two = normed_two.astype(jnp.bfloat16)
    gate = jnp.dot(act_two, w_gate, preferred_element_type=jnp.float32)
    up_proj = jnp.dot(act_two, w_up, preferred_element_type=jnp.float32)
    units_full, pull_units = jax.vjp(swiglu, gate, up_proj)
    hidden_units = units_full.astype(jnp.bfloat16)
    partial_ffn = jnp.dot(hidden_units, w_down, preferred_element_type=jnp.float32)
    output = (hidden_state + exchange_sum(partial_ffn)).astype(jnp.bfloat16)
    half = hidden_units.shape[1] // 2
    grad_down_a, grad_down_b = [
        scatter_sum(
            jnp.einsum("td,tf->df", cotangent, part, preferred_element_type=jnp.float32), order
        )
        for part, order in (
            (hidden_units[:, :half], X_FIRST),
            (hidden_units[:, half:], Y_FIRST),
        )
    ]
    grad_units = jnp.einsum("td,fd->tf", cotangent, w_down, preferred_element_type=jnp.float32)
    grad_gate_full, grad_up_full = pull_units(grad_units)
    grad_gate_lin = grad_gate_full.astype(jnp.bfloat16)
    grad_up_lin = grad_up_full.astype(jnp.bfloat16)
    grad_gate_w = jnp.einsum(
        "td,tf->df", act_two, grad_gate_lin, preferred_element_type=jnp.float32
    )
    grad_up_w = jnp.einsum("td,tf->df", act_two, grad_up_lin, preferred_element_type=jnp.float32)
    partial_two = jnp.einsum("tf,df->td", grad_gate_lin, w_gate, preferred_element_type=jnp.float32)
    partial_two = partial_two + jnp.einsum(
        "tf,df->td", grad_up_lin, w_up, preferred_element_type=jnp.float32
    )
    grad_act_two = exchange_sum(partial_two)
    grad_from_two, grad_ffn_gain = pull_two(grad_act_two)
    grad_hidden = grad_out + grad_from_two
    grad_attention = grad_hidden.astype(jnp.bfloat16)
    grad_out_w = jnp.einsum("td,tc->dc", grad_attention, mixed, preferred_element_type=jnp.float32)
    grad_query_lin, grad_key_lin, grad_value_lin, partial_one = attention_backward(
        branch_point, grad_attention, queries, keys, values, log_sums,
        w_out, w_query, w_key, w_value, rope,
    )
    grad_query_w = jnp.einsum(
        "td,tc->dc", act_one, grad_query_lin, preferred_element_type=jnp.float32
    )
    grad_key_w = jnp.einsum("td,tc->dc", act_one, grad_key_lin, preferred_element_type=jnp.float32)
    grad_value_w = jnp.einsum(
        "td,tc->dc", act_one, grad_value_lin, preferred_element_type=jnp.float32
    )
    grad_act_one = exchange_sum(partial_one)
    grad_from_one, grad_attn_gain = pull_one(grad_act_one)
    grad_input = (grad_hidden + grad_from_one).astype(jnp.bfloat16)
    rows = grad_attn_gain.shape[0] // lax.axis_size("dp")
    gains = lax.psum(jnp.stack([grad_attn_gain, grad_ffn_gain]), "dp")
    gains = lax.dynamic_slice_in_dim(gains, lax.axis_index("dp") * rows, rows, axis=1)
    return (
        output,
        grad_input,
        gains[0],
        scatter_sum(grad_query_w, Y_FIRST),
        scatter_sum(grad_key_w, X_FIRST),
        scatter_sum(grad_value_w, X_FIRST),
        scatter_sum(grad_out_w, X_FIRST).T,
        gains[1],
        scatter_sum(grad_gate_w, X_FIRST),
        scatter_sum(grad_up_w, Y_FIRST),
        jnp.concatenate([grad_down_a.T, grad_down_b.T], axis=0),
    )


def solution(mesh):
    placed = (
        P("dp", None),
        P("dp", None),
        P(),
        P(None, "tensor"),
        P(None, "tensor"),
        P(None, "tensor"),
        P("tensor", None),
        P(),
        P(None, "tensor"),
        P(None, "tensor"),
        P("tensor", None),
        P("dp", None),
    )
    return jax.shard_map(
        per_device,
        mesh=mesh,
        in_specs=placed,
        out_specs=(
            P("dp", None),
            P("dp", None),
            P("dp"),
            P("dp", "tensor"),
            P("dp", "tensor"),
            P("dp", "tensor"),
            P("tensor", "dp"),
            P("dp"),
            P("dp", "tensor"),
            P("dp", "tensor"),
            P("tensor", "dp"),
        ),
        check_vma=False,
    )
```

```python
import functools

import jax
import jax.numpy as jnp
import numpy as np
from jax import lax
from jax.experimental import pallas as pl
from jax.experimental.pallas import tpu as pltpu
from jax.sharding import PartitionSpec as P

HEAD_DIM = 96
PROMPT = 1024
CONT_LEN = 128
CONT = 2
GROUP_TOK = 1280
BLOCK = 256
BLOCKS = GROUP_TOK // BLOCK
LANES = 128
MIB = 1 << 20
CHEAP = pl.CostEstimate(flops=10**6, bytes_accessed=10**5, transcendentals=0)
epsilon = 1e-05
rope_base = 100000.0
LOG2E = 1.4426950408889634
SCORE_SCALE = HEAD_DIM ** (-0.5)
NT = (((1,), (1,)), ((), ()))
TN = (((0,), (0,)), ((), ()))


def matmul(left, right, dims=(((1,), (0,)), ((), ()))):
    return lax.dot_general(left, right, dims, preferred_element_type=jnp.float32)


def rope_tables(branch):
    half = HEAD_DIM // 2
    frequency = rope_base ** (-np.arange(half, dtype=np.float64) * 2.0 / HEAD_DIM)
    angles = np.arange(PROMPT + CONT_LEN, dtype=np.float64)[:, None] * frequency[None, :]
    pad = np.zeros((angles.shape[0], LANES - HEAD_DIM))
    cosine = np.concatenate([np.cos(angles), np.cos(angles), pad], axis=1)
    sine = np.concatenate([-np.sin(angles), np.sin(angles), pad], axis=1)
    both = jnp.asarray(np.stack([cosine, sine]), jnp.float32)
    parts = [both[:, :PROMPT]]
    for c in range(CONT):
        parts.append(lax.dynamic_slice_in_dim(both, branch[c], CONT_LEN, axis=1))
    return jnp.concatenate(parts, axis=1)


def lane_ids(shape):
    return lax.broadcasted_iota(jnp.int32, shape, 1)


def swap_halves(head):
    half = HEAD_DIM // 2
    return jnp.where(
        lane_ids(head.shape) < half, pltpu.roll(head, LANES - half, 1), pltpu.roll(head, half, 1)
    )


def take_head(full, h):
    first = h * HEAD_DIM
    start, shift = first // LANES * LANES, first % LANES
    width = LANES if shift + HEAD_DIM <= LANES else 2 * LANES
    part = full[:, start : start + width]
    return part[:, :LANES] if shift == 0 else pltpu.roll(part, width - shift, 1)[:, :LANES]


def join_heads(heads):
    lanes = lane_ids(heads[0].shape)
    out = []
    for i in range(0, len(heads), 4):
        one, two, three = (pltpu.roll(heads[i + j], LANES - 32 * j, 1) for j in (1, 2, 3))
        out.append(jnp.where(lanes < 96, heads[i], one))
        out.append(jnp.where(lanes < 64, one, two))
        out.append(jnp.where(lanes < 32, two, three))
    return jnp.concatenate(out, axis=1)


def own_mask(shape, query_axis, block):
    query = lax.broadcasted_iota(jnp.int32, shape, query_axis) & (BLOCK - 1)
    key = lax.broadcasted_iota(jnp.int32, shape, 1 - query_axis)
    mask = key <= query
    if block * BLOCK >= PROMPT:
        mask = mask & ((key // CONT_LEN) == (query // CONT_LEN))
    return mask


def reach_mask(shape, query_axis, branch_ref):
    query = lax.broadcasted_iota(jnp.int32, shape, query_axis) & (BLOCK - 1)
    key = lax.broadcasted_iota(jnp.int32, shape, 1 - query_axis) + PROMPT // 2
    return key < jnp.where(query < CONT_LEN, branch_ref[0, 0], branch_ref[0, 1])


def attention_forward_kernel(
    branch_ref, x_ref, gain_ref, wq_ref, wk_ref, wv_ref, wo_ref, rope_ref,
    act_ref, act_t_ref, q_ref, k_ref, v_ref, mixed_ref, lse_ref, part_ref, o_ref,
):
    kv_heads = k_ref.shape[0]
    group = 2 * BLOCK

    def project(i, carry):
        rows = pl.ds(pl.multiple_of(i * BLOCK, BLOCK), BLOCK)
        x = x_ref[rows, :].astype(jnp.float32)
        norm = lax.rsqrt(jnp.mean(x * x, axis=-1, keepdims=True) + epsilon)
        act = x * norm * gain_ref[...]
        act_t_ref[:, rows] = act.T.astype(jnp.bfloat16)
        act = act.astype(jnp.bfloat16)
        act_ref[rows, :] = act
        cosine, sine = rope_ref[0, rows, :], rope_ref[1, rows, :]
        full = matmul(act, wq_ref[...])
        for h in range(2 * kv_heads):
            head = take_head(full, h)
            rotated = head * cosine + swap_halves(head) * sine
            q_ref[h // 2, i, pl.ds(h % 2 * BLOCK, BLOCK), :] = rotated.astype(jnp.bfloat16)
        full = matmul(act, wk_ref[...])
        for h in range(kv_heads):
            head = take_head(full, h)
            rotated = head * cosine + swap_halves(head) * sine
            k_ref[h, rows, :] = rotated.astype(jnp.bfloat16)
        full = matmul(act, wv_ref[...])
        lanes = lane_ids((BLOCK, LANES))
        for h in range(kv_heads):
            head = jnp.where(lanes < HEAD_DIM, take_head(full, h), 0.0)
            v_ref[h, rows, :] = jnp.where(lanes == HEAD_DIM, 1.0, head).astype(jnp.bfloat16)
        return carry

    lax.fori_loop(0, BLOCKS, project, 0)

    factor = SCORE_SCALE * LOG2E

    def attend(h, carry):
        for i in range(BLOCKS):
            query = q_ref[h, i]
            before = i * BLOCK
            own = matmul(query, k_ref[h, before : before + BLOCK], NT)
            own = jnp.where(own_mask(own.shape, 0, i), own, -1e30)
            largest = jnp.max(own, axis=-1, keepdims=True)
            spans = []
            if i > 0:
                cuts = [0, before] if before < PROMPT else [0, PROMPT // 2, PROMPT]
                for low, high in zip(cuts[:-1], cuts[1:]):
                    scores = matmul(query, k_ref[h, low:high], NT)
                    if before >= PROMPT and low > 0:
                        scores = jnp.where(reach_mask(scores.shape, 0, branch_ref), scores, -1e30)
                    largest = jnp.maximum(largest, jnp.max(scores, axis=-1, keepdims=True))
                    spans.append((low, high, scores))
            shift = largest * factor
            probs = jnp.exp2(own * factor - shift).astype(jnp.bfloat16)
            total = matmul(probs, v_ref[h, before : before + BLOCK])
            for low, high, scores in spans:
                probs = jnp.exp2(scores * factor - shift).astype(jnp.bfloat16)
                total += matmul(probs, v_ref[h, low:high])
            sums = total[:, HEAD_DIM : HEAD_DIM + 1]
            mixed = total / sums
            for g in range(2):
                o_ref[2 * h + g, before : before + BLOCK, :] = mixed[g * BLOCK : (g + 1) * BLOCK]
            logs = shift + jnp.log2(sums)
            lse_ref[h, i] = jnp.broadcast_to(logs, (group, LANES)).T[0:1, :]
        return carry

    lax.fori_loop(0, kv_heads, attend, 0)

    def finish(i, carry):
        rows = pl.ds(pl.multiple_of(i * BLOCK, BLOCK), BLOCK)
        mixed = join_heads([o_ref[h, rows, :] for h in range(2 * kv_heads)]).astype(jnp.bfloat16)
        mixed_ref[rows, :] = mixed
        part_ref[rows, :] = matmul(mixed, wo_ref[...]).astype(jnp.bfloat16)
        return carry

    lax.fori_loop(0, BLOCKS, finish, 0)


def attention_forward(branch, x, gain, wq, wk, wv, wo, rope):
    kv_heads = wk.shape[1] // HEAD_DIM
    rows, width = x.shape
    bf = jnp.bfloat16
    vmem = pl.BlockSpec(memory_space=pltpu.VMEM)
    return pl.pallas_call(
        attention_forward_kernel,
        out_shape=(
            jax.ShapeDtypeStruct((rows, width), bf),
            jax.ShapeDtypeStruct((width, rows), bf),
            jax.ShapeDtypeStruct((kv_heads, BLOCKS, 2 * BLOCK, LANES), bf),
            jax.ShapeDtypeStruct((kv_heads, rows, LANES), bf),
            jax.ShapeDtypeStruct((kv_heads, rows, LANES), bf),
            jax.ShapeDtypeStruct((rows, wq.shape[1]), bf),
            jax.ShapeDtypeStruct((kv_heads, BLOCKS, 1, 2 * BLOCK), jnp.float32),
            jax.ShapeDtypeStruct((rows, width), bf),
        ),
        in_specs=[pl.BlockSpec(memory_space=pltpu.SMEM)] + [vmem] * 7,
        out_specs=[vmem] * 8,
        scratch_shapes=[pltpu.VMEM((2 * kv_heads, rows, LANES), jnp.float32)],
        compiler_params=pltpu.CompilerParams(vmem_limit_bytes=60 * MIB),
        cost_estimate=CHEAP,
        name="attention_forward",
    )(branch, x, gain.reshape(1, width), wq, wk, wv, wo, rope)


def attention_backward_kernel(
    part, branch_ref, gatt_ref, q_ref, k_ref, v_ref, lse_ref, wo_ref, wq_ref, wkv_ref, rope_ref, *refs
):
    first_ref, refs = (refs[:2], refs[2:]) if part else ((), refs)
    gq_ref, gkv_ref = refs[:2]
    part_ref = refs[2] if part else None
    do_ref, dq_ref, dk_ref, dv_ref = refs[-4:]
    kv_heads = k_ref.shape[0]
    width = wo_ref.shape[0]
    group = 2 * BLOCK
    factor = SCORE_SCALE * LOG2E

    def project(i, carry):
        rows = pl.ds(pl.multiple_of(i * BLOCK, BLOCK), BLOCK)
        full = matmul(gatt_ref[rows, :], wo_ref[...], NT)
        lanes = lane_ids((BLOCK, LANES))
        for h in range(2 * kv_heads):
            head = jnp.where(lanes < HEAD_DIM, take_head(full, h), 0.0)
            do_ref[h // 2, i, pl.ds(h % 2 * BLOCK, BLOCK), :] = head.astype(jnp.bfloat16)
        return carry

    lax.fori_loop(0, BLOCKS, project, 0)

    def attend(h, carry):
        for i in reversed(range(BLOCKS)):
            query, grad, logs = q_ref[h, i], do_ref[h, i], lse_ref[h, i]
            before = i * BLOCK
            cuts = [(before, before + BLOCK)]
            if i > 0 and before < PROMPT:
                cuts += [(0, before)]
            elif i > 0:
                cuts += [(0, PROMPT // 2), (PROMPT // 2, PROMPT)]
            spans, weighted = [], 0.0
            for low, high in cuts:
                scores = matmul(k_ref[h, low:high], query, NT)
                probs = jnp.exp2(scores * factor - logs)
                if low == before:
                    probs = jnp.where(own_mask(probs.shape, 1, i), probs, 0.0)
                elif before >= PROMPT and low > 0:
                    probs = jnp.where(reach_mask(probs.shape, 1, branch_ref), probs, 0.0)
                grad_probs = matmul(v_ref[h, low:high], grad, NT)
                weighted += jnp.sum(probs * grad_probs, axis=0, keepdims=True)
                spans.append((low, high, probs, grad_probs))
            grad_query = jnp.zeros((group, LANES), jnp.float32)
            for low, high, probs, grad_probs in spans:
                grad_scores = (probs * (grad_probs - weighted)).astype(jnp.bfloat16)
                grad_query += matmul(grad_scores, k_ref[h, low:high], TN)
                grad_key = matmul(grad_scores, query)
                grad_value = matmul(probs.astype(jnp.bfloat16), grad)
                if before >= PROMPT:
                    dk_ref[h, low:high] = grad_key
                    dv_ref[h, low:high] = grad_value
                else:
                    dk_ref[h, low:high] += grad_key
                    dv_ref[h, low:high] += grad_value
            dq_ref[h, i] = grad_query
        return carry

    lax.fori_loop(0, kv_heads, attend, 0)

    def finish(i, carry):
        rows = pl.ds(pl.multiple_of(i * BLOCK, BLOCK), BLOCK)
        cosine, sine = rope_ref[0, rows, :] * SCORE_SCALE, rope_ref[1, rows, :] * SCORE_SCALE
        heads = []
        for h in range(2 * kv_heads):
            head = dq_ref[h // 2, i, pl.ds(h % 2 * BLOCK, BLOCK), :]
            heads.append(head * cosine - swap_halves(head) * sine)
        grad_q = join_heads(heads).astype(jnp.bfloat16)
        heads = []
        for h in range(kv_heads):
            head = dk_ref[h, rows, :]
            heads.append(head * cosine - swap_halves(head) * sine)
        heads += [dv_ref[h, rows, :] for h in range(kv_heads)]
        grad_kv = join_heads(heads).astype(jnp.bfloat16)
        gq_ref[rows, :] = grad_q
        gkv_ref[rows, :] = grad_kv
        if part:
            total = matmul(first_ref[0][rows, :], wq_ref[:, :width], NT)
            total += matmul(first_ref[1][rows, :], wkv_ref[:, :width], NT)
            total += matmul(grad_q, wq_ref[:, width:], NT)
            total += matmul(grad_kv, wkv_ref[:, width:], NT)
            part_ref[rows, :] = total.astype(jnp.bfloat16)
        return carry

    lax.fori_loop(0, BLOCKS, finish, 0)


def attention_backward(part, branch, gatt, q, k, v, lse, wo, wq, wkv, rope, first):
    kv_heads = k.shape[0] // 2
    rows, width = gatt.shape
    bf = jnp.bfloat16
    vmem = pl.BlockSpec(memory_space=pltpu.VMEM)

    def half(array):
        shape = (array.shape[0] // 2,) + array.shape[1:]
        return pl.BlockSpec(shape, lambda i: (part,) + (0,) * (len(shape) - 1))

    def whole(array):
        return pl.BlockSpec(array.shape, lambda i: (0,) * array.ndim)

    small = jax.ShapeDtypeStruct((rows, wq.shape[1] // 2), bf)
    outs = (small, small) + ((jax.ShapeDtypeStruct((rows, width), bf),) if part else ())
    weights = (wq, wkv, rope, *first)
    return pl.pallas_call(
        functools.partial(attention_backward_kernel, part),
        grid=(1,),
        out_shape=outs,
        in_specs=[pl.BlockSpec(memory_space=pltpu.SMEM), whole(gatt)]
        + [half(a) for a in (q, k, v, lse, wo)]
        + [whole(a) for a in weights],
        out_specs=[whole(o) for o in outs],
        scratch_shapes=[
            pltpu.VMEM((kv_heads, BLOCKS, 2 * BLOCK, LANES), bf),
            pltpu.VMEM((kv_heads, BLOCKS, 2 * BLOCK, LANES), jnp.float32),
            pltpu.VMEM((kv_heads, rows, LANES), jnp.float32),
            pltpu.VMEM((kv_heads, rows, LANES), jnp.float32),
        ],
        compiler_params=pltpu.CompilerParams(vmem_limit_bytes=60 * MIB),
        cost_estimate=CHEAP,
        name="attention_backward",
    )(branch, gatt, q, k, v, lse, wo, *weights)


HBM = pl.BlockSpec(memory_space=pl.ANY)
SMEM = pl.BlockSpec(memory_space=pltpu.SMEM)
VMEM = pl.BlockSpec(memory_space=pltpu.VMEM)
KERNEL_BLOCKS = 16
ROW_BLOCK = 128
CUTS = ((0, 512), (512, 1024), (1024, 1536), (1536, 2048))


NN = (((1,), (0,)), ((), ()))


def start(source, target, sem):
    copy = pltpu.make_async_copy(source, target, sem)
    copy.start()
    return copy


def split_copies(tile, low, high, at, sent, kept, axis, mine, sems, k):
    copies = []
    for half, target in ((1 - mine, sent), (mine, kept)):
        part = tile.at[:, :, half] if axis == 0 else tile.at[:, half]
        copies.append(
            start(
                part.at[:, :, :, pl.ds(low, high - low)],
                target.at[:, :, :, pl.ds(at, high - low)],
                sems.at[k + len(copies)],
            )
        )
    return copies


def gradient_tile(tile, left_ref, right):
    blocks, rows = tile.shape[0], 4 * tile.shape[3]

    def step(z, carry):
        first = pl.multiple_of(z * rows, rows)
        out = matmul(left_ref[pl.ds(first, rows), :], right)
        tile[z] = out.astype(jnp.bfloat16).reshape(tile.shape[1:])
        return carry

    lax.fori_loop(0, blocks, step, 0)


def ffn_kernel(first, count, aliased, *refs):
    (bits_ref, act_hbm, cot_hbm, act_t_hbm, cot_t_hbm, wg_hbm, wu_hbm, wd_hbm), refs = refs[:8], refs[8:]
    refs = refs[3:] if aliased else refs
    (hidden_hbm, ggate_hbm, gup_hbm, sent_a, kept_a, sent_b, kept_b), refs = refs[:7], refs[7:]
    act, cot, act_t, cot_t, wg, wu, wd, hidden, ggate, gup, tiles, in_sems, row_sems, out_sems = refs
    units = pl.ds(first, count)
    weights = [
        start(wg_hbm.at[:, units], wg, in_sems.at[0]),
        start(wu_hbm.at[:, units], wu, in_sems.at[1]),
    ]
    blocks = act.shape[0] // BLOCK
    rows = [pl.ds(i * BLOCK, BLOCK) for i in range(blocks)]
    act_in = [start(act_hbm.at[rows[0]], act.at[rows[0]], row_sems.at[0, 0])]
    weights.append(start(wd_hbm.at[units], wd, in_sems.at[2]))
    cot_in = [start(cot_hbm.at[rows[0]], cot.at[rows[0]], row_sems.at[1, 0])]
    for i in range(1, blocks):
        act_in.append(start(act_hbm.at[rows[i]], act.at[rows[i]], row_sems.at[0, i]))
        cot_in.append(start(cot_hbm.at[rows[i]], cot.at[rows[i]], row_sems.at[1, i]))
    turned = [
        start(cot_t_hbm, cot_t, in_sems.at[3]),
        start(act_t_hbm, act_t, in_sems.at[4]),
    ]
    for copy in weights:
        copy.wait()
    for i in range(blocks):
        act_in[i].wait()
        cot_in[i].wait()

        def units_step(j, carry):
            cols = pl.ds(pl.multiple_of(j * BLOCK, BLOCK), BLOCK)
            gate = matmul(act[rows[i], :], wg[:, cols])
            up = matmul(act[rows[i], :], wu[:, cols])
            grad = matmul(cot[rows[i], :], wd[cols, :], NT)
            sigmoid = 1.0 / (1.0 + jnp.exp(-gate))
            silu = gate * sigmoid
            hidden[rows[i], cols] = (silu * up).astype(jnp.bfloat16)
            ggate[rows[i], cols] = (grad * up * (sigmoid * (1.0 + gate * (1.0 - sigmoid)))).astype(jnp.bfloat16)
            gup[rows[i], cols] = (grad * silu).astype(jnp.bfloat16)
            return carry

        lax.fori_loop(0, count // BLOCK, units_step, 0)
    copies = [
        start(hidden, hidden_hbm.at[:, units], out_sems.at[0]),
        start(ggate, ggate_hbm.at[:, units], out_sems.at[1]),
        start(gup, gup_hbm.at[:, units], out_sems.at[2]),
    ]
    half = count // 2
    x, y = bits_ref[0], bits_ref[1]
    turned[0].wait()
    gradient_tile(tiles.at[0], cot_t, hidden[...])
    copies += split_copies(tiles.at[0], 0, half, count, sent_a, kept_a, 0, x, out_sems, 3)
    copies += split_copies(tiles.at[0], half, count, count, sent_b, kept_b, 1, y, out_sems, 5)
    turned[1].wait()
    gradient_tile(tiles.at[1], act_t, ggate[...])
    copies += split_copies(tiles.at[1], 0, count, 0, sent_a, kept_a, 0, x, out_sems, 7)
    gradient_tile(tiles.at[2], act_t, gup[...])
    copies += split_copies(tiles.at[2], 0, count, 0, sent_b, kept_b, 1, y, out_sems, 9)
    for copy in copies:
        copy.wait()


def ffn_chunk(bits, blocks, act, cot, act_t, cot_t, wg, wu, wd, before, first, count):
    rows, width = act.shape
    bf = jnp.bfloat16
    piece = jax.ShapeDtypeStruct((blocks // 4, 2, width // blocks, count + count // 2), bf)
    units = jax.ShapeDtypeStruct((rows, wg.shape[1]), bf)
    return pl.pallas_call(
        functools.partial(ffn_kernel, first, count, bool(before)),
        out_shape=(units,) * 3 + (piece,) * 4,
        in_specs=[SMEM] + [HBM] * (7 + len(before)),
        out_specs=[HBM] * 7,
        scratch_shapes=[
            pltpu.VMEM((rows, width), bf),
            pltpu.VMEM((rows, width), bf),
            pltpu.VMEM((width, rows), bf),
            pltpu.VMEM((width, rows), bf),
            pltpu.VMEM((width, count), bf),
            pltpu.VMEM((width, count), bf),
            pltpu.VMEM((count, width), bf),
            pltpu.VMEM((rows, count), bf),
            pltpu.VMEM((rows, count), bf),
            pltpu.VMEM((rows, count), bf),
            pltpu.VMEM((3, blocks // 4, 2, 2, width // blocks, count), bf),
            pltpu.SemaphoreType.DMA((5,)),
            pltpu.SemaphoreType.DMA((2, rows // BLOCK)),
            pltpu.SemaphoreType.DMA((11,)),
        ],
        input_output_aliases={8 + i: i for i in range(len(before))},
        compiler_params=pltpu.CompilerParams(vmem_limit_bytes=60 * MIB),
        cost_estimate=CHEAP,
        name="ffn_chunk",
    )(bits, act, cot, act_t, cot_t, wg, wu, wd, *before)


def gradient_kernel(lefts, parts, bits_ref, *refs):
    def cut(count):
        nonlocal refs
        head, refs = refs[:count], refs[count:]
        return head

    left_hbm, right_hbm, pieces = cut(lefts), cut(len(parts)), cut(4)
    left, right, tiles, (in_sems, out_sems) = cut(lefts), cut(len(parts)), cut(len(parts)), refs
    left_in = [start(a, b, in_sems.at[i]) for i, (a, b) in enumerate(zip(left_hbm, left))]
    right_in = [start(a, b, in_sems.at[lefts + i]) for i, (a, b) in enumerate(zip(right_hbm, right))]
    copies = []
    for i, (which, places) in enumerate(parts):
        if left_in[which] is not None:
            left_in[which].wait()
            left_in[which] = None
        right_in[i].wait()
        gradient_tile(tiles[i], left[which], right[i][...])
        for low, high, at, first in places:
            sent, kept = pieces[2 * first], pieces[2 * first + 1]
            copies += split_copies(tiles[i], low, high, at, sent, kept, first, bits_ref[first], out_sems, len(copies))
    for copy in copies:
        copy.wait()


def gradient_pieces(bits, blocks, lefts, rights, which, places):
    width, rows = lefts[0].shape
    bf = jnp.bfloat16
    flat = [place for part in places for place in part]
    widths = [sum(high - low for low, high, _, first in flat if first == axis) for axis in (0, 1)]
    pieces = [jax.ShapeDtypeStruct((blocks // 4, 2, width // blocks, w), bf) for w in widths for _ in range(2)]
    return pl.pallas_call(
        functools.partial(gradient_kernel, len(lefts), tuple(zip(which, places))),
        out_shape=tuple(pieces),
        in_specs=[SMEM] + [HBM] * (len(lefts) + len(rights)),
        out_specs=[HBM] * 4,
        scratch_shapes=[pltpu.VMEM(a.shape, bf) for a in (*lefts, *rights)]
        + [pltpu.VMEM((blocks // 4, 2, 2, width // blocks, r.shape[1]), bf) for r in rights]
        + [pltpu.SemaphoreType.DMA((len(lefts) + len(rights),)), pltpu.SemaphoreType.DMA((2 * len(flat),))],
        compiler_params=pltpu.CompilerParams(vmem_limit_bytes=60 * MIB),
        cost_estimate=CHEAP,
        name="gradient_pieces",
    )(bits, *lefts, *rights)


def projection_kernel(dims, count, *refs):
    left_hbm, right_hbm, out_hbm, refs = refs[:count], refs[count : 2 * count], refs[2 * count], refs[2 * count + 1 :]
    left, right, (out, left_sems, right_sems, out_sems) = refs[:count], refs[count : 2 * count], refs[2 * count :]
    turned = dims is NT
    rows, width = out.shape

    def columns(ref, n):
        cut = pl.ds(n * BLOCK, BLOCK)
        return ref.at[cut, :] if turned else ref.at[:, cut]

    def load_right(n):
        return [
            start(columns(right_hbm[p], n), columns(right[p], n), right_sems.at[p, n]) for p in range(count)
        ]

    def load_left(i):
        cut = pl.ds(i * BLOCK, BLOCK)
        return [start(left_hbm[p].at[cut], left[p].at[cut], left_sems.at[p, i]) for p in range(count)]

    rights, lefts = [load_right(0)], [load_left(i) for i in range(rows // BLOCK)]
    rights += [load_right(n) for n in range(1, width // BLOCK)]
    copies = []
    for n in range(width // BLOCK):
        for copy in rights[n]:
            copy.wait()

        def step(i, carry):
            cut = pl.ds(pl.multiple_of(i * BLOCK, BLOCK), BLOCK)
            total = sum(matmul(left[p][cut, :], columns(right[p], n)[...], dims) for p in range(count))
            out[cut, n * BLOCK : (n + 1) * BLOCK] = total.astype(jnp.bfloat16)
            return carry

        if n == 0:
            for i in range(rows // BLOCK):
                for copy in lefts[i]:
                    copy.wait()
                step(i, 0)
        else:
            lax.fori_loop(0, rows // BLOCK, step, 0)
        cut = pl.ds(n * BLOCK, BLOCK)
        copies.append(start(out.at[:, cut], out_hbm.at[:, cut], out_sems.at[n]))
    for copy in copies:
        copy.wait()


def projection(lefts, rights, dims):
    rows = lefts[0].shape[0]
    width = rights[0].shape[0 if dims is NT else 1]
    bf, count = jnp.bfloat16, len(lefts)
    return pl.pallas_call(
        functools.partial(projection_kernel, dims, count),
        out_shape=jax.ShapeDtypeStruct((rows, width), bf),
        in_specs=[HBM] * (2 * count),
        out_specs=HBM,
        scratch_shapes=[pltpu.VMEM(a.shape, bf) for a in (*lefts, *rights)]
        + [
            pltpu.VMEM((rows, width), bf),
            pltpu.SemaphoreType.DMA((count, rows // BLOCK)),
            pltpu.SemaphoreType.DMA((count, width // BLOCK)),
            pltpu.SemaphoreType.DMA((width // BLOCK,)),
        ],
        compiler_params=pltpu.CompilerParams(vmem_limit_bytes=60 * MIB),
        cost_estimate=CHEAP,
        name="projection",
    )(*lefts, *rights)


def add_two(one, two):
    return one.astype(jnp.float32) + two.astype(jnp.float32)


def second_kernel(bits_ref, *refs):
    ins, outs = refs[: len(refs) // 2], refs[len(refs) // 2 :]
    for i in range(0, len(ins), 2):
        kept, got, send, keep = ins[i], ins[i + 1], outs[i], outs[i + 1]
        mine = bits_ref[1 - i // 2 % 2]
        send[0] = add_two(kept[0, 1 - mine], got[0, 1 - mine]).astype(jnp.bfloat16)
        keep[0] = add_two(kept[0, mine], got[0, mine]).astype(jnp.bfloat16)


def second_sums(bits, *arrays):
    def spec(array):
        shape = (1,) + array.shape[1:]
        return pl.BlockSpec(shape, lambda z: (z,) + (0,) * (len(shape) - 1))

    outs = [jax.ShapeDtypeStruct((a.shape[0],) + a.shape[2:], a.dtype) for a in arrays]
    return pl.pallas_call(
        second_kernel,
        grid=(arrays[0].shape[0],),
        out_shape=tuple(outs),
        in_specs=[SMEM] + [spec(a) for a in arrays],
        out_specs=[spec(o) for o in outs],
        compiler_params=pltpu.CompilerParams(vmem_limit_bytes=60 * MIB),
        cost_estimate=CHEAP,
        name="second_sums",
    )(bits, *arrays)


def third_kernel(bits_ref, *refs):
    ins, (send, keep) = refs[:-2], refs[-2:]
    low = bits_ref[2] & 1
    for target, half in ((send, 1 - low), (keep, low)):
        for high in range(2):
            at = 0
            for kept, got in zip(ins[0::2], ins[1::2]):
                width = kept.shape[-1]
                block = add_two(kept[2 * high + half], got[2 * high + half])
                target[high, :, at : at + width] = block.astype(jnp.bfloat16)
                at += width


def third_sums(bits, *pieces):
    width = sum(p.shape[-1] for p in pieces[0::2])
    pair = jax.ShapeDtypeStruct((2, pieces[0].shape[1], width), jnp.bfloat16)
    return pl.pallas_call(
        third_kernel,
        out_shape=(pair, pair),
        in_specs=[SMEM] + [VMEM] * len(pieces),
        out_specs=[VMEM] * 2,
        compiler_params=pltpu.CompilerParams(vmem_limit_bytes=60 * MIB),
        cost_estimate=CHEAP,
        name="third_sums",
    )(bits, *pieces)


def fourth_kernel(bits_ref, kept, got, send, keep):
    high = bits_ref[2] >> 1
    send[...] = add_two(kept[1 - high], got[1 - high]).astype(jnp.bfloat16)
    keep[...] = add_two(kept[high], got[high]).astype(jnp.bfloat16)


def fourth_sums(bits, kept, got):
    block = jax.ShapeDtypeStruct(kept.shape[1:], kept.dtype)
    return pl.pallas_call(
        fourth_kernel,
        out_shape=(block, block),
        in_specs=[SMEM] + [VMEM] * 2,
        out_specs=[VMEM] * 2,
        compiler_params=pltpu.CompilerParams(vmem_limit_bytes=60 * MIB),
        cost_estimate=CHEAP,
        name="fourth_sums",
    )(bits, kept, got)


def over_dp(array, flip):
    size = lax.axis_size("dp")
    return lax.ppermute(array, "dp", [(i, i ^ flip) for i in range(size)])


def after(arrays, *needed):
    return lax.optimization_barrier((arrays, needed))[0]


def first_stage(pieces):
    if lax.axis_size("dp") != KERNEL_BLOCKS:
        return pieces
    sent_a, kept_a, sent_b, kept_b = pieces
    return (kept_a, over_dp(sent_a, 1), kept_b, over_dp(sent_b, 2))


def second_stage(bits, *pieces):
    if lax.axis_size("dp") != KERNEL_BLOCKS:
        return pieces
    sums = second_sums(bits, *[p for piece in pieces for p in piece])
    return [
        (sums[i + 1], over_dp(sums[i], 2), sums[i + 3], over_dp(sums[i + 2], 1)) for i in range(0, len(sums), 4)
    ]


def third_stage(bits, *pieces):
    if lax.axis_size("dp") != KERNEL_BLOCKS:
        return pieces
    send, keep = third_sums(bits, *[p for piece in pieces for p in piece])
    return (keep, over_dp(send, 4))


def fourth_stage(bits, pieces):
    if lax.axis_size("dp") != KERNEL_BLOCKS:
        return pieces
    send, keep = fourth_sums(bits, *pieces)
    return (keep, over_dp(send, 8))


def ffn_sums_kernel(*refs):
    ins, (gate_ref, up_ref, down_ref) = refs[:-3], refs[-3:]
    per = len(CUTS) // (len(ins) // 2)
    for i, (low, high) in enumerate(CUTS):
        kept, got = ins[2 * (i // per)], ins[2 * (i // per) + 1]
        count, half = high - low, (high - low) // 2
        cut = slice(3 * count * (i % per), 3 * count * (i % per + 1))
        total = add_two(kept[:, cut], got[:, cut])
        gate_ref[:, low:high] = total[:, :count]
        down_ref[low : low + half, :] = total[:, count : count + half].T
        up_ref[:, low:high] = total[:, count + half : 2 * count + half]
        down_ref[low + half : high, :] = total[:, 2 * count + half :].T


def ffn_sums(pieces):
    if lax.axis_size("dp") != KERNEL_BLOCKS:
        return pieces
    rows, units = pieces[0].shape[0], CUTS[-1][1]
    wide = jax.ShapeDtypeStruct((rows, units), jnp.float32)
    return pl.pallas_call(
        ffn_sums_kernel,
        out_shape=(wide, wide, jax.ShapeDtypeStruct((units, rows), jnp.float32)),
        in_specs=[VMEM] * len(pieces),
        out_specs=[VMEM] * 3,
        compiler_params=pltpu.CompilerParams(vmem_limit_bytes=60 * MIB),
        cost_estimate=CHEAP,
        name="ffn_sums",
    )(*pieces)


def joined(pieces):
    sent_a, kept_a, sent_b, kept_b = pieces
    first, second = lax.axis_index("dp") & 1, lax.axis_index("dp") >> 1 & 1
    out = []
    for sent, kept, axis, mine in ((sent_a, kept_a, 2, first), (sent_b, kept_b, 1, second)):
        low = jnp.where(mine == 0, kept, sent)
        high = jnp.where(mine == 0, sent, kept)
        out.append(jnp.stack([low, high], axis=axis).reshape(-1, sent.shape[-1]))
    return out


def scatter_sum(grads):
    size = lax.axis_size("dp")
    bits = size.bit_length() - 1
    me = lax.axis_index("dp")
    rows, width = grads.shape
    work = grads.reshape((2,) * bits + (rows // size, width))
    for bit in range(bits):
        axis = bits - 1 - bit
        mine = (me >> bit) & 1
        sent = lax.dynamic_index_in_dim(work, 1 - mine, axis, keepdims=False)
        kept = lax.dynamic_index_in_dim(work, mine, axis, keepdims=False)
        work = kept.astype(jnp.float32) + over_dp(sent, 1 << bit).astype(jnp.float32)
        work = work.astype(grads.dtype)
    return work.astype(jnp.float32)


def to_other_core(array):
    return lax.ppermute(array, "tensor", [(0, 1), (1, 0)])


def norm_kernel(x_ref, own_ref, got_ref, gain_ref, act_ref, act_t_ref):
    hidden = x_ref[...].astype(jnp.float32) + add_two(own_ref[...], got_ref[...])
    norm = lax.rsqrt(jnp.mean(hidden * hidden, axis=-1, keepdims=True) + epsilon)
    act = hidden * norm * gain_ref[...]
    act_ref[...] = act.astype(jnp.bfloat16)
    act_t_ref[...] = act.T.astype(jnp.bfloat16)


def row_call(kernel, name, rows, width, ins, outs):
    specs = {
        "rows": pl.BlockSpec((ROW_BLOCK, width), lambda i: (i, 0)),
        "turned": pl.BlockSpec((width, ROW_BLOCK), lambda i: (0, i)),
        "vector": pl.BlockSpec((1, width), lambda i: (0, 0)),
    }
    shapes = {
        "rows": jax.ShapeDtypeStruct((rows, width), jnp.bfloat16),
        "turned": jax.ShapeDtypeStruct((width, rows), jnp.bfloat16),
        "vector": jax.ShapeDtypeStruct((1, width), jnp.float32),
    }
    return pl.pallas_call(
        kernel,
        grid=(rows // ROW_BLOCK,),
        out_shape=tuple(shapes[o] for o in outs),
        in_specs=[specs[i] for i in ins],
        out_specs=[specs[o] for o in outs],
        compiler_params=pltpu.CompilerParams(vmem_limit_bytes=60 * MIB),
        cost_estimate=CHEAP,
        name=name,
    )


def norm_grad(value, grad, gain):
    scale = lax.rsqrt(jnp.mean(value * value, axis=-1, keepdims=True) + epsilon)
    scaled = grad * gain
    back = scale * scaled - value * scale**3 * jnp.mean(scaled * value, axis=-1, keepdims=True)
    return back, jnp.sum(grad * value * scale, axis=0, keepdims=True)


def add_to_vector(ref, value):
    @pl.when(pl.program_id(0) == 0)
    def _():
        ref[...] = jnp.zeros_like(ref)

    ref[...] += value


def middle_kernel(
    x_ref, own_ref, got_ref, two_own_ref, two_got_ref, cot_ref, gain_ref,
    gatt_ref, gatt_t_ref, gain_grad_ref,
):
    hidden = x_ref[...].astype(jnp.float32) + add_two(own_ref[...], got_ref[...])
    grad = add_two(two_own_ref[...], two_got_ref[...])
    back, gain_grad = norm_grad(hidden, grad, gain_ref[...])
    total = cot_ref[...].astype(jnp.float32) + back
    gatt_ref[...] = total.astype(jnp.bfloat16)
    gatt_t_ref[...] = total.T.astype(jnp.bfloat16)
    add_to_vector(gain_grad_ref, gain_grad)


def output_kernel(x_ref, own_ref, got_ref, ffn_own_ref, ffn_got_ref, out_ref):
    hidden = x_ref[...].astype(jnp.float32) + add_two(own_ref[...], got_ref[...])
    out_ref[...] = (hidden + add_two(ffn_own_ref[...], ffn_got_ref[...])).astype(jnp.bfloat16)


def input_kernel(x_ref, gatt_ref, own_ref, got_ref, gain_ref, out_ref, gain_grad_ref):
    grad = add_two(own_ref[...], got_ref[...])
    back, gain_grad = norm_grad(x_ref[...].astype(jnp.float32), grad, gain_ref[...])
    out_ref[...] = (gatt_ref[...].astype(jnp.float32) + back).astype(jnp.bfloat16)
    add_to_vector(gain_grad_ref, gain_grad)


def per_device(
    layer_input,
    branch_point,
    attn_gain,
    w_query,
    w_key,
    w_value,
    w_out,
    ffn_gain,
    w_gate,
    w_up,
    w_down,
    cotangent,
):
    rows, width = layer_input.shape
    size = lax.axis_size("dp")
    by_kernel = size == KERNEL_BLOCKS
    blocks = KERNEL_BLOCKS
    me = lax.axis_index("dp")
    bits = jnp.stack([me & 1, me >> 1 & 1, me >> 2 & 3]).astype(jnp.int32)
    rope = rope_tables(branch_point[0])
    act_one, act_one_t, queries, keys, values, mixed, log_sums, attn_own = attention_forward(
        branch_point, layer_input, attn_gain, w_query, w_key, w_value, w_out, rope
    )
    attn_got = to_other_core(attn_own)
    cot_t = cotangent.T
    gain_two = ffn_gain.reshape(1, width)
    act_two, act_two_t = row_call(
        norm_kernel, "norm_two", rows, width, ["rows"] * 3 + ["vector"], ["rows", "turned"]
    )(layer_input, attn_own, attn_got, gain_two)
    heads, kv = mixed.shape[1], w_key.shape[1]
    half, kv_half = heads // 2, kv // 2
    units = ()

    def chunk(i, *needed):
        nonlocal units
        low, high = CUTS[i]
        *units, sent_a, kept_a, sent_b, kept_b = ffn_chunk(
            bits, blocks, after(act_two, *needed), cotangent, act_two_t, cot_t,
            w_gate, w_up, w_down, units, low, high - low,
        )
        return sent_a, kept_a, sent_b, kept_b

    def backward(part, *needed):
        return attention_backward(
            part, branch_point, after(grad_attention, *needed), queries, keys, values, log_sums,
            w_out, w_query, w_key_value, rope, list(needed[:2]) if part else [],
        )

    w_key_value = jnp.concatenate(
        [w_key[:, :kv_half], w_value[:, :kv_half], w_key[:, kv_half:], w_value[:, kv_half:]], axis=1
    )
    pieces = [chunk(0)]
    one = [first_stage(pieces[0])]
    pieces.append(chunk(1))
    pieces[1] = after(pieces[1], one[0])
    one.append(first_stage(pieces[1]))
    pieces.append(chunk(2, pieces[1]))
    pieces[2] = after(pieces[2], one[1])
    one.append(first_stage(pieces[2]))
    pieces.append(chunk(3, pieces[2]))
    *units, pieces[3], one[2] = after((*units, pieces[3], one[2]))
    two = second_stage(bits, *after(one[:2], pieces[3]))
    hidden_units, grad_gate_lin, grad_up_lin = units
    two_own = projection(after([grad_gate_lin, grad_up_lin], two[0][0]), [w_gate, w_up], NT)
    two_own, two = after((two_own, two))
    two_got = to_other_core(two_own)
    one.append(first_stage(after(pieces[3], two_own)))
    three = [third_stage(bits, *two)]
    ffn_own = projection([after(hidden_units, two_own, three[0][0])], [w_down], NN)
    grad_attention, grad_attention_t, grad_ffn_gain = row_call(
        middle_kernel, "middle", rows, width, ["rows"] * 6 + ["vector"], ["rows", "turned", "vector"]
    )(layer_input, attn_own, attn_got, two_own, two_got, after(cotangent, ffn_own), gain_two)
    grad_attention, *last, three[0] = after((grad_attention, *one[2:], three[0]))
    two = second_stage(bits, *last)
    four = [fourth_stage(bits, three[0])]
    back_one = backward(0, two[0][0], four[0][0], grad_attention)
    back_one, two, four[0] = after((back_one, two, four[0]))
    three.append(third_stage(bits, *two))
    early = gradient_pieces(
        bits, blocks, [after(grad_attention_t, three[1][0]), act_one_t], [mixed, *back_one], [0, 1, 1],
        [((0, half, 0, 0), (half, heads, 0, 1)), ((0, half, half, 0),), ((0, half, half, 1),)],
    )
    early_one = first_stage(early)
    *back_two, one_own = backward(1, *back_one, early)
    back_two, one_own, early_one, three[1] = after((back_two, one_own, early_one, three[1]))
    one_got = to_other_core(one_own)
    (early_two,) = second_stage(bits, early_one)
    four.append(fourth_stage(bits, three[1]))
    late = gradient_pieces(
        bits, blocks, [after(act_one_t, early_two[0], four[1][0])], back_two, [0, 0],
        [((0, half, 0, 0),), ((0, half, 0, 1),)],
    )
    late_one = first_stage(late)
    grad_input, grad_attn_gain = row_call(
        input_kernel, "input", rows, width, ["rows"] * 4 + ["vector"], ["rows", "vector"]
    )(layer_input, after(grad_attention, late), one_own, one_got, attn_gain.reshape(1, width))
    grad_input, late_one, early_two, four[1] = after((grad_input, late_one, early_two, four[1]))
    ffn_got = to_other_core(after(ffn_own, grad_input))
    early_three = third_stage(bits, early_two)
    (late_two,) = second_stage(bits, late_one)
    (output,) = row_call(output_kernel, "output", rows, width, ["rows"] * 5, ["rows"])(
        layer_input, attn_own, attn_got, after(ffn_own, grad_input, late_two[0], early_three[0]), ffn_got
    )
    early_three, late_two = after((early_three, late_two), output)
    early_four = fourth_stage(bits, early_three)
    late_three = third_stage(bits, late_two)
    done = [after(piece, output, early_four[0], late_three[0]) for piece in four]
    grads_down = ffn_sums([p for piece in done for p in piece])
    late_three = after(late_three, grads_down)
    late_four = fourth_stage(bits, late_three)
    gains = jnp.concatenate([grad_attn_gain, grad_ffn_gain]).reshape(2, size, width // size)
    gains = scatter_sum(gains.transpose(1, 0, 2).reshape(size, 2 * width // size))[0]
    if by_kernel:
        grad_gate, grad_up, grad_down = grads_down
        sums = jnp.concatenate([add_two(*early_four), add_two(*late_four)], axis=1)
    else:
        whole = [p for piece in pieces + [early, late] for p in joined(piece)]
        sums = scatter_sum(jnp.concatenate(whole, axis=1))
        gates, ups, downs = [], [], []
        for low, high in CUTS:
            parts = jnp.split(sums[:, 3 * low : 3 * high], [high - low, (high - low) * 3 // 2, (high - low) * 5 // 2], axis=1)
            for total, part in zip((gates, downs, ups, downs), parts):
                total.append(part)
        grad_gate, grad_up, grad_down = (jnp.concatenate(t, axis=1) for t in (gates, ups, downs))
        grad_down = grad_down.T
        sums = sums[:, 3 * CUTS[-1][1] :]
    names = (("out", half), ("query", half), ("out", half), ("key", kv_half), ("value", kv_half))
    names += (("query", half), ("key", kv_half), ("value", kv_half))
    found, at = {}, 0
    for name, count in names:
        found.setdefault(name, []).append(sums[:, at : at + count])
        at += count
    found = {name: jnp.concatenate(parts, axis=1) for name, parts in found.items()}
    return (
        output,
        grad_input,
        gains[: width // size],
        found["query"],
        found["key"],
        found["value"],
        found["out"].T,
        gains[width // size :],
        grad_gate,
        grad_up,
        grad_down,
    )


def solution(mesh):
    placed = (
        P("dp", None),
        P("dp", None),
        P(),
        P(None, "tensor"),
        P(None, "tensor"),
        P(None, "tensor"),
        P("tensor", None),
        P(),
        P(None, "tensor"),
        P(None, "tensor"),
        P("tensor", None),
        P("dp", None),
    )
    return jax.shard_map(
        per_device,
        mesh=mesh,
        in_specs=placed,
        out_specs=(
            P("dp", None),
            P("dp", None),
            P("dp"),
            P("dp", "tensor"),
            P("dp", "tensor"),
            P("dp", "tensor"),
            P("tensor", "dp"),
            P("dp"),
            P("dp", "tensor"),
            P("dp", "tensor"),
            P("tensor", "dp"),
        ),
        check_vma=False,
    )
```

```python
import functools

import jax
import jax.numpy as jnp
import numpy as np
from jax import lax
from jax.experimental import pallas as pl
from jax.experimental.pallas import tpu as pltpu
from jax.sharding import PartitionSpec as P

HEAD_DIM = 96
PROMPT = 1024
CONT_LEN = 128
CONT = 2
GROUP_TOK = 1280
BLOCK = 256
BLOCKS = GROUP_TOK // BLOCK
LANES = 128
MIB = 1 << 20
CHEAP = pl.CostEstimate(flops=10**6, bytes_accessed=10**5, transcendentals=0)
epsilon = 1e-05
rope_base = 100000.0
LOG2E = 1.4426950408889634
SCORE_SCALE = HEAD_DIM ** (-0.5)
NT = (((1,), (1,)), ((), ()))
TN = (((0,), (0,)), ((), ()))

LONG = pl.CostEstimate(flops=10**11, bytes_accessed=10**5, transcendentals=0)


def matmul(left, right, dims=(((1,), (0,)), ((), ()))):
    return lax.dot_general(left, right, dims, preferred_element_type=jnp.float32)


def rope_tables():
    half = HEAD_DIM // 2
    frequency = rope_base ** (-np.arange(half, dtype=np.float64) * 2.0 / HEAD_DIM)
    angles = np.arange(PROMPT + CONT_LEN, dtype=np.float64)[:, None] * frequency[None, :]
    pad = np.zeros((angles.shape[0], LANES - HEAD_DIM))
    cosine = np.concatenate([np.cos(angles), np.cos(angles), pad], axis=1)
    sine = np.concatenate([-np.sin(angles), np.sin(angles), pad], axis=1)
    return jnp.asarray(np.stack([cosine, sine]), jnp.float32)


def place_rope(branch_ref, table_ref, rope_ref):
    rope_ref[:, :PROMPT, :] = table_ref[:, :PROMPT, :]
    for c in range(CONT):
        rows = pl.ds(PROMPT + c * CONT_LEN, CONT_LEN)
        for i in range(2):
            rope_ref[i, rows, :] = table_ref[i, pl.ds(branch_ref[0, c], CONT_LEN), :]


def lane_ids(shape):
    return lax.broadcasted_iota(jnp.int32, shape, 1)


def swap_halves(head):
    half = HEAD_DIM // 2
    return jnp.where(
        lane_ids(head.shape) < half, pltpu.roll(head, LANES - half, 1), pltpu.roll(head, half, 1)
    )


def take_head(full, h):
    first = h * HEAD_DIM
    start, shift = first // LANES * LANES, first % LANES
    width = LANES if shift + HEAD_DIM <= LANES else 2 * LANES
    part = full[:, start : start + width]
    return part[:, :LANES] if shift == 0 else pltpu.roll(part, width - shift, 1)[:, :LANES]


def join_heads(heads):
    lanes = lane_ids(heads[0].shape)
    out = []
    for i in range(0, len(heads), 4):
        one, two, three = (pltpu.roll(heads[i + j], LANES - 32 * j, 1) for j in (1, 2, 3))
        out.append(jnp.where(lanes < 96, heads[i], one))
        out.append(jnp.where(lanes < 64, one, two))
        out.append(jnp.where(lanes < 32, two, three))
    return jnp.concatenate(out, axis=1)


def own_mask(shape, query_axis, block):
    query = lax.broadcasted_iota(jnp.int32, shape, query_axis) & (BLOCK - 1)
    key = lax.broadcasted_iota(jnp.int32, shape, 1 - query_axis)
    mask = key <= query
    if block * BLOCK >= PROMPT:
        mask = mask & ((key // CONT_LEN) == (query // CONT_LEN))
    return mask


def reach_mask(shape, query_axis, branch_ref):
    query = lax.broadcasted_iota(jnp.int32, shape, query_axis) & (BLOCK - 1)
    key = lax.broadcasted_iota(jnp.int32, shape, 1 - query_axis) + PROMPT // 2
    return key < jnp.where(query < CONT_LEN, branch_ref[0, 0], branch_ref[0, 1])


def attention_forward_kernel(
    branch_ref, x_ref, gain_ref, wq_ref, wk_ref, wv_ref, wo_ref, table_ref,
    act_t_ref, q_ref, k_ref, v_ref, mixed_ref, lse_ref, part_ref, o_ref, rope_ref,
):
    kv_heads = k_ref.shape[0]
    group = 2 * BLOCK
    place_rope(branch_ref, table_ref, rope_ref)

    def project(i, carry):
        rows = pl.ds(pl.multiple_of(i * BLOCK, BLOCK), BLOCK)
        x = x_ref[rows, :].astype(jnp.float32)
        norm = lax.rsqrt(jnp.mean(x * x, axis=-1, keepdims=True) + epsilon)
        act = x * norm * gain_ref[...][None, :]
        act_t_ref[:, rows] = act.T.astype(jnp.bfloat16)
        act = act.astype(jnp.bfloat16)
        cosine, sine = rope_ref[0, rows, :], rope_ref[1, rows, :]
        full = matmul(act, wq_ref[...])
        for h in range(2 * kv_heads):
            head = take_head(full, h)
            rotated = head * cosine + swap_halves(head) * sine
            q_ref[h // 2, i, pl.ds(h % 2 * BLOCK, BLOCK), :] = rotated.astype(jnp.bfloat16)
        full = matmul(act, wk_ref[...])
        for h in range(kv_heads):
            head = take_head(full, h)
            rotated = head * cosine + swap_halves(head) * sine
            k_ref[h, rows, :] = rotated.astype(jnp.bfloat16)
        full = matmul(act, wv_ref[...])
        lanes = lane_ids((BLOCK, LANES))
        for h in range(kv_heads):
            head = jnp.where(lanes < HEAD_DIM, take_head(full, h), 0.0)
            v_ref[h, rows, :] = jnp.where(lanes == HEAD_DIM, 1.0, head).astype(jnp.bfloat16)
        return carry

    lax.fori_loop(0, BLOCKS, project, 0)

    factor = SCORE_SCALE * LOG2E

    def attend(h, carry):
        for i in range(BLOCKS):
            query = q_ref[h, i]
            before = i * BLOCK
            own = matmul(query, k_ref[h, before : before + BLOCK], NT)
            own = jnp.where(own_mask(own.shape, 0, i), own, -1e30)
            largest = jnp.max(own, axis=-1, keepdims=True)
            spans = []
            if i > 0:
                cuts = [0, before] if before < PROMPT else [0, PROMPT // 2, PROMPT]
                for low, high in zip(cuts[:-1], cuts[1:]):
                    scores = matmul(query, k_ref[h, low:high], NT)
                    if before >= PROMPT and low > 0:
                        scores = jnp.where(reach_mask(scores.shape, 0, branch_ref), scores, -1e30)
                    largest = jnp.maximum(largest, jnp.max(scores, axis=-1, keepdims=True))
                    spans.append((low, high, scores))
            shift = largest * factor
            probs = jnp.exp2(own * factor - shift).astype(jnp.bfloat16)
            total = matmul(probs, v_ref[h, before : before + BLOCK])
            for low, high, scores in spans:
                probs = jnp.exp2(scores * factor - shift).astype(jnp.bfloat16)
                total += matmul(probs, v_ref[h, low:high])
            sums = total[:, HEAD_DIM : HEAD_DIM + 1]
            mixed = total / sums
            for g in range(2):
                o_ref[2 * h + g, before : before + BLOCK, :] = mixed[g * BLOCK : (g + 1) * BLOCK]
            logs = shift + jnp.log2(sums)
            lse_ref[h, i] = jnp.broadcast_to(logs, (group, LANES)).T[0:1, :]
        return carry

    lax.fori_loop(0, kv_heads, attend, 0)

    def finish(i, carry):
        rows = pl.ds(pl.multiple_of(i * BLOCK, BLOCK), BLOCK)
        mixed = join_heads([o_ref[h, rows, :] for h in range(2 * kv_heads)]).astype(jnp.bfloat16)
        mixed_ref[rows, :] = mixed
        part_ref[rows, :] = matmul(mixed, wo_ref[...]).astype(jnp.bfloat16)
        return carry

    lax.fori_loop(0, BLOCKS, finish, 0)


def attention_forward(branch, x, gain, wq, wk, wv, wo, rope):
    kv_heads = wk.shape[1] // HEAD_DIM
    rows, width = x.shape
    bf = jnp.bfloat16
    vmem = pl.BlockSpec(memory_space=pltpu.VMEM)
    return pl.pallas_call(
        attention_forward_kernel,
        out_shape=(
            jax.ShapeDtypeStruct((width, rows), bf),
            jax.ShapeDtypeStruct((kv_heads, BLOCKS, 2 * BLOCK, LANES), bf),
            jax.ShapeDtypeStruct((kv_heads, rows, LANES), bf),
            jax.ShapeDtypeStruct((kv_heads, rows, LANES), bf),
            jax.ShapeDtypeStruct((rows, wq.shape[1]), bf),
            jax.ShapeDtypeStruct((kv_heads, BLOCKS, 1, 2 * BLOCK), jnp.float32),
            jax.ShapeDtypeStruct((rows, width), bf),
        ),
        in_specs=[pl.BlockSpec(memory_space=pltpu.SMEM)] + [vmem] * 7,
        out_specs=[vmem] * 7,
        scratch_shapes=[
            pltpu.VMEM((2 * kv_heads, rows, LANES), jnp.float32),
            pltpu.VMEM((2, rows, LANES), jnp.float32),
        ],
        compiler_params=pltpu.CompilerParams(vmem_limit_bytes=60 * MIB),
        cost_estimate=CHEAP,
        name="attention_forward",
    )(branch, x, gain, wq, wk, wv, wo, rope)


def attention_backward_kernel(
    part, branch_ref, gatt_ref, q_ref, k_ref, v_ref, lse_ref, wo_ref, wq_ref, wkv_ref, table_ref, *refs
):
    first_ref, refs = (refs[:2], refs[2:]) if part else ((), refs)
    gq_ref, gkv_ref = refs[:2]
    part_ref = refs[2] if part else None
    do_ref, dq_ref, dk_ref, dv_ref, rope_ref = refs[-5:]
    kv_heads = k_ref.shape[0]
    width = wo_ref.shape[0]
    group = 2 * BLOCK
    factor = SCORE_SCALE * LOG2E

    place_rope(branch_ref, table_ref, rope_ref)

    def project(i, carry):
        rows = pl.ds(pl.multiple_of(i * BLOCK, BLOCK), BLOCK)
        full = matmul(gatt_ref[rows, :], wo_ref[...], NT)
        lanes = lane_ids((BLOCK, LANES))
        for h in range(2 * kv_heads):
            head = jnp.where(lanes < HEAD_DIM, take_head(full, h), 0.0)
            do_ref[h // 2, i, pl.ds(h % 2 * BLOCK, BLOCK), :] = head.astype(jnp.bfloat16)
        return carry

    lax.fori_loop(0, BLOCKS, project, 0)

    def attend(h, carry):
        for i in reversed(range(BLOCKS)):
            query, grad, logs = q_ref[h, i], do_ref[h, i], lse_ref[h, i]
            before = i * BLOCK
            cuts = [(before, before + BLOCK)]
            if i > 0 and before < PROMPT:
                cuts += [(0, before)]
            elif i > 0:
                cuts += [(0, PROMPT // 2), (PROMPT // 2, PROMPT)]
            spans, weighted = [], 0.0
            for low, high in cuts:
                scores = matmul(k_ref[h, low:high], query, NT)
                probs = jnp.exp2(scores * factor - logs)
                if low == before:
                    probs = jnp.where(own_mask(probs.shape, 1, i), probs, 0.0)
                elif before >= PROMPT and low > 0:
                    probs = jnp.where(reach_mask(probs.shape, 1, branch_ref), probs, 0.0)
                grad_probs = matmul(v_ref[h, low:high], grad, NT)
                weighted += jnp.sum(probs * grad_probs, axis=0, keepdims=True)
                spans.append((low, high, probs, grad_probs))
            grad_query = jnp.zeros((group, LANES), jnp.float32)
            for low, high, probs, grad_probs in spans:
                grad_scores = (probs * (grad_probs - weighted)).astype(jnp.bfloat16)
                grad_query += matmul(grad_scores, k_ref[h, low:high], TN)
                grad_key = matmul(grad_scores, query)
                grad_value = matmul(probs.astype(jnp.bfloat16), grad)
                if before >= PROMPT:
                    dk_ref[h, low:high] = grad_key
                    dv_ref[h, low:high] = grad_value
                else:
                    dk_ref[h, low:high] += grad_key
                    dv_ref[h, low:high] += grad_value
            dq_ref[h, i] = grad_query
        return carry

    lax.fori_loop(0, kv_heads, attend, 0)

    def finish(i, carry):
        rows = pl.ds(pl.multiple_of(i * BLOCK, BLOCK), BLOCK)
        cosine, sine = rope_ref[0, rows, :] * SCORE_SCALE, rope_ref[1, rows, :] * SCORE_SCALE
        heads = []
        for h in range(2 * kv_heads):
            head = dq_ref[h // 2, i, pl.ds(h % 2 * BLOCK, BLOCK), :]
            heads.append(head * cosine - swap_halves(head) * sine)
        grad_q = join_heads(heads).astype(jnp.bfloat16)
        heads = []
        for h in range(kv_heads):
            head = dk_ref[h, rows, :]
            heads.append(head * cosine - swap_halves(head) * sine)
        heads += [dv_ref[h, rows, :] for h in range(kv_heads)]
        grad_kv = join_heads(heads).astype(jnp.bfloat16)
        gq_ref[rows, :] = grad_q
        gkv_ref[rows, :] = grad_kv
        if part:
            grad_q = jnp.concatenate([first_ref[0][rows, :], grad_q], axis=1)
            grad_kv = jnp.concatenate([first_ref[1][rows, :], grad_kv], axis=1)
            total = matmul(grad_q, wq_ref[...], NT) + matmul(grad_kv, wkv_ref[...], NT)
            part_ref[rows, :] = total.astype(jnp.bfloat16)
        return carry

    lax.fori_loop(0, BLOCKS, finish, 0)


def attention_backward(part, branch, gatt, q, k, v, lse, wo, wq, wkv, rope, first):
    kv_heads = k.shape[0] // 2
    rows, width = gatt.shape
    bf = jnp.bfloat16
    vmem = pl.BlockSpec(memory_space=pltpu.VMEM)

    def half(array):
        shape = (array.shape[0] // 2,) + array.shape[1:]
        return pl.BlockSpec(shape, lambda i: (part,) + (0,) * (len(shape) - 1))

    def whole(array):
        return pl.BlockSpec(array.shape, lambda i: (0,) * array.ndim)

    small = jax.ShapeDtypeStruct((rows, wq.shape[1] // 2), bf)
    outs = (small, small) + ((jax.ShapeDtypeStruct((rows, width), bf),) if part else ())
    weights = (wq, wkv, rope, *first)
    return pl.pallas_call(
        functools.partial(attention_backward_kernel, part),
        grid=(1,),
        out_shape=outs,
        in_specs=[pl.BlockSpec(memory_space=pltpu.SMEM), whole(gatt)]
        + [half(a) for a in (q, k, v, lse, wo)]
        + [whole(a) for a in weights],
        out_specs=[whole(o) for o in outs],
        scratch_shapes=[
            pltpu.VMEM((kv_heads, BLOCKS, 2 * BLOCK, LANES), bf),
            pltpu.VMEM((kv_heads, BLOCKS, 2 * BLOCK, LANES), jnp.float32),
            pltpu.VMEM((kv_heads, rows, LANES), jnp.float32),
            pltpu.VMEM((kv_heads, rows, LANES), jnp.float32),
            pltpu.VMEM((2, rows, LANES), jnp.float32),
        ],
        compiler_params=pltpu.CompilerParams(vmem_limit_bytes=60 * MIB),
        cost_estimate=CHEAP,
        name="attention_backward",
    )(branch, gatt, q, k, v, lse, wo, *weights)


HBM = pl.BlockSpec(memory_space=pl.ANY)
SMEM = pl.BlockSpec(memory_space=pltpu.SMEM)
VMEM = pl.BlockSpec(memory_space=pltpu.VMEM)
KERNEL_BLOCKS = 16
WIDE = 512
CUTS = ((0, 512), (512, 1024), (1024, 1536), (1536, 2048))


NN = (((1,), (0,)), ((), ()))


def start(source, target, sem):
    copy = pltpu.make_async_copy(source, target, sem)
    copy.start()
    return copy


def rows_of(blocks, width):
    return (blocks // 4, 2, 2, None, width)


def split_copies(tile, low, high, at, sent, kept, axis, mine, sems, k, begin=True):
    copies = []
    for half, target in ((1 - mine, sent), (mine, kept)):
        part = tile.at[:, :, half] if axis == 0 else tile.at[:, half]
        copy = pltpu.make_async_copy(
            part.at[:, :, :, pl.ds(low, high - low)],
            target.at[:, :, :, pl.ds(at, high - low)],
            sems.at[k + len(copies)],
        )
        if begin:
            copy.start()
        copies.append(copy)
    return copies


def gradient_tile(tile, left, right):
    zs = tile.shape[0] // 2
    tall = left.shape[0] // 2

    def step(i, carry):
        out = matmul(left[pl.ds(pl.multiple_of(i * tall, tall), tall), :], right[...])
        tile[pl.ds(i * zs, zs)] = out.astype(jnp.bfloat16).reshape((zs,) + tile.shape[1:])
        return carry

    lax.fori_loop(0, 2, step, 0)


def ffn_kernel(first, count, aliased, *refs):
    (bits_ref, act_hbm, cot_hbm, act_t_hbm, cot_t_hbm, wg_hbm, wu_hbm, wd_hbm), refs = refs[:8], refs[8:]
    refs = refs[3:] if aliased else refs
    (hidden_hbm, ggate_hbm, gup_hbm, sent_a, kept_a, sent_b, kept_b), refs = refs[:7], refs[7:]
    act, cot, lefts, wg, wu, wd, lines, tiles, in_sems, row_sems, out_sems = refs
    units = pl.ds(first, count)
    tall = act.shape[0] // 2

    def rows_in(i, which):
        rows = pl.ds(pl.multiple_of(i * tall, tall), tall)
        source, target = ((act_hbm, act), (cot_hbm, cot))[which]
        return pltpu.make_async_copy(source.at[rows], target.at[rows], row_sems.at[which, i])

    weights = [start(wg_hbm.at[:, units], wg, in_sems.at[0])]
    rows_in(0, 0).start()
    weights.append(start(wu_hbm.at[:, units], wu, in_sems.at[1]))
    weights.append(start(wd_hbm.at[units], wd, in_sems.at[2]))
    rows_in(0, 1).start()
    rows_in(1, 0).start()
    rows_in(1, 1).start()
    sources = [
        start(cot_t_hbm, lefts.at[0], in_sems.at[3]),
        start(act_t_hbm, lefts.at[1], in_sems.at[4]),
    ]
    for copy in weights:
        copy.wait()

    def units_step(i, carry):
        rows = pl.ds(pl.multiple_of(i * tall, tall), tall)
        rows_in(i, 0).wait()
        gate = matmul(act[rows, :], wg[...])
        up = matmul(act[rows, :], wu[...])
        rows_in(i, 1).wait()
        grad = matmul(cot[rows, :], wd[...], NT)
        sigmoid = 1.0 / (1.0 + jnp.exp(-gate))
        silu = gate * sigmoid
        lines[0, rows, :] = (silu * up).astype(jnp.bfloat16)
        lines[1, rows, :] = (grad * up * (sigmoid * (1.0 + gate * (1.0 - sigmoid)))).astype(jnp.bfloat16)
        lines[2, rows, :] = (grad * silu).astype(jnp.bfloat16)
        return carry

    lax.fori_loop(0, 2, units_step, 0)
    copies = [
        start(lines.at[0], hidden_hbm.at[:, units], out_sems.at[0]),
        start(lines.at[1], ggate_hbm.at[:, units], out_sems.at[1]),
        start(lines.at[2], gup_hbm.at[:, units], out_sems.at[2]),
    ]
    half = count // 2
    x, y = bits_ref[0], bits_ref[1]
    for copy in sources:
        copy.wait()

    def stores(t, begin):
        if t == 0:
            return split_copies(tiles.at[0], 0, half, count, sent_a, kept_a, 0, x, out_sems, 3, begin) + split_copies(
                tiles.at[0], half, count, count, sent_b, kept_b, 1, y, out_sems, 5, begin
            )
        if t == 1:
            return split_copies(tiles.at[1], 0, count, 0, sent_a, kept_a, 0, x, out_sems, 7, begin)
        return split_copies(tiles.at[2], 0, count, 0, sent_b, kept_b, 1, y, out_sems, 9, begin)

    def tile_step(t, carry):
        gradient_tile(tiles.at[t], lefts.at[jnp.minimum(t, 1)], lines.at[t])
        for one in range(3):

            @pl.when(t == one)
            def _(one=one):
                stores(one, True)

        return carry

    lax.fori_loop(0, 3, tile_step, 0)
    for t in range(3):
        copies += stores(t, False)
    for copy in copies:
        copy.wait()


def ffn_chunk(bits, blocks, act, cot, act_t, cot_t, wg, wu, wd, before, first, count):
    rows, width = act.shape
    bf = jnp.bfloat16
    piece = jax.ShapeDtypeStruct((blocks // 4, 2, width // blocks, count + count // 2), bf)
    units = jax.ShapeDtypeStruct((rows, wg.shape[1]), bf)
    return pl.pallas_call(
        functools.partial(ffn_kernel, first, count, bool(before)),
        out_shape=(units,) * 3 + (piece,) * 4,
        in_specs=[SMEM] + [HBM] * (7 + len(before)),
        out_specs=[HBM] * 7,
        scratch_shapes=[
            pltpu.VMEM((rows, width), bf),
            pltpu.VMEM((rows, width), bf),
            pltpu.VMEM((2, width, rows), bf),
            pltpu.VMEM((width, count), bf),
            pltpu.VMEM((width, count), bf),
            pltpu.VMEM((count, width), bf),
            pltpu.VMEM((3, rows, count), bf),
            pltpu.VMEM((3, blocks // 4, 2, 2, width // blocks, count), bf),
            pltpu.SemaphoreType.DMA((5,)),
            pltpu.SemaphoreType.DMA((2, 2)),
            pltpu.SemaphoreType.DMA((11,)),
        ],
        input_output_aliases={8 + i: i for i in range(len(before))},
        compiler_params=pltpu.CompilerParams(vmem_limit_bytes=60 * MIB),
        cost_estimate=CHEAP,
        name="ffn_chunk",
    )(bits, act, cot, act_t, cot_t, wg, wu, wd, *before)


def gradient_kernel(lefts, parts, bits_ref, *refs):
    def cut(count):
        nonlocal refs
        head, refs = refs[:count], refs[count:]
        return head

    left_hbm, right_hbm, pieces = cut(lefts), cut(len(parts)), cut(4)
    left, right, tiles, (in_sems, out_sems) = cut(lefts), cut(len(parts)), cut(len(parts)), refs
    left_in = [start(a, b, in_sems.at[i]) for i, (a, b) in enumerate(zip(left_hbm, left))]
    right_in = [start(a, b, in_sems.at[lefts + i]) for i, (a, b) in enumerate(zip(right_hbm, right))]
    copies = []
    for i, (which, places) in enumerate(parts):
        if left_in[which] is not None:
            left_in[which].wait()
            left_in[which] = None
        right_in[i].wait()
        gradient_tile(tiles[i], left[which], right[i])
        for low, high, at, first in places:
            sent, kept = pieces[2 * first], pieces[2 * first + 1]
            copies += split_copies(tiles[i], low, high, at, sent, kept, first, bits_ref[first], out_sems, len(copies))
    for copy in copies:
        copy.wait()


def gradient_pieces(bits, blocks, lefts, rights, which, places):
    width, rows = lefts[0].shape
    bf = jnp.bfloat16
    flat = [place for part in places for place in part]
    widths = [sum(high - low for low, high, _, first in flat if first == axis) for axis in (0, 1)]
    pieces = [jax.ShapeDtypeStruct((blocks // 4, 2, width // blocks, w), bf) for w in widths for _ in range(2)]
    return pl.pallas_call(
        functools.partial(gradient_kernel, len(lefts), tuple(zip(which, places))),
        out_shape=tuple(pieces),
        in_specs=[SMEM] + [HBM] * (len(lefts) + len(rights)),
        out_specs=[HBM] * 4,
        scratch_shapes=[pltpu.VMEM(a.shape, bf) for a in (*lefts, *rights)]
        + [pltpu.VMEM((blocks // 4, 2, 2, width // blocks, r.shape[1]), bf) for r in rights]
        + [pltpu.SemaphoreType.DMA((len(lefts) + len(rights),)), pltpu.SemaphoreType.DMA((2 * len(flat),))],
        compiler_params=pltpu.CompilerParams(vmem_limit_bytes=60 * MIB),
        cost_estimate=CHEAP,
        name="gradient_pieces",
    )(bits, *lefts, *rights)


def projection_kernel(dims, count, *refs):
    left_hbm, right_hbm, out_hbm, refs = refs[:count], refs[count : 2 * count], refs[2 * count], refs[2 * count + 1 :]
    left, right, (out, left_sems, right_sems, out_sems) = refs[:count], refs[count : 2 * count], refs[2 * count :]
    turned = dims is NT
    rows, width = out.shape
    tall = rows // 2

    def columns(ref, n):
        cut = pl.ds(pl.multiple_of(n * WIDE, WIDE), WIDE)
        return ref.at[cut, :] if turned else ref.at[:, cut]

    def right_in(p, n):
        return pltpu.make_async_copy(columns(right_hbm[p], n), columns(right[p], n), right_sems.at[p, n])

    def left_in(p, i):
        cut = pl.ds(pl.multiple_of(i * tall, tall), tall)
        return pltpu.make_async_copy(left_hbm[p].at[cut], left[p].at[cut], left_sems.at[p, i])

    def out_copy(n):
        wide = pl.ds(pl.multiple_of(n * WIDE, WIDE), WIDE)
        return pltpu.make_async_copy(out.at[:, wide], out_hbm.at[:, wide], out_sems.at[n])

    for p in range(count):
        right_in(p, 0).start()
        left_in(p, 0).start()
    for p in range(count):
        left_in(p, 1).start()
    for n in range(1, width // WIDE):
        for p in range(count):
            right_in(p, n).start()

    def step(j, carry):
        n, i = j // 2, j % 2

        @pl.when(i == 0)
        def _():
            for p in range(count):
                right_in(p, n).wait()

        @pl.when(n == 0)
        def _():
            for p in range(count):
                left_in(p, i).wait()

        cut = pl.ds(pl.multiple_of(i * tall, tall), tall)
        total = sum(matmul(left[p][cut, :], columns(right[p], n)[...], dims) for p in range(count))
        out[cut, pl.ds(pl.multiple_of(n * WIDE, WIDE), WIDE)] = total.astype(jnp.bfloat16)

        @pl.when(i == 1)
        def _():
            out_copy(n).start()

        return carry

    lax.fori_loop(0, 2 * width // WIDE, step, 0)
    for n in range(width // WIDE):
        out_copy(n).wait()


def projection(lefts, rights, dims):
    rows = lefts[0].shape[0]
    width = rights[0].shape[0 if dims is NT else 1]
    bf, count = jnp.bfloat16, len(lefts)
    return pl.pallas_call(
        functools.partial(projection_kernel, dims, count),
        out_shape=jax.ShapeDtypeStruct((rows, width), bf),
        in_specs=[HBM] * (2 * count),
        out_specs=HBM,
        scratch_shapes=[pltpu.VMEM(a.shape, bf) for a in (*lefts, *rights)]
        + [
            pltpu.VMEM((rows, width), bf),
            pltpu.SemaphoreType.DMA((count, 2)),
            pltpu.SemaphoreType.DMA((count, width // WIDE)),
            pltpu.SemaphoreType.DMA((width // WIDE,)),
        ],
        compiler_params=pltpu.CompilerParams(vmem_limit_bytes=60 * MIB),
        cost_estimate=CHEAP,
        name="projection",
    )(*lefts, *rights)


def add_two(one, two):
    return one.astype(jnp.float32) + two.astype(jnp.float32)


def second_steps(bits_ref, ins_hbm, ins, outs_hbm, outs):
    steps = []
    for z in range(outs[0].shape[0]):

        def compute(z=z):
            for i in range(2):
                kept, got, send, keep, mine = *ins[2 * i : 2 * i + 2], *outs[2 * i : 2 * i + 2], bits_ref[1 - i]
                send[z] = add_two(kept[z, 1 - mine], got[z, 1 - mine]).astype(jnp.bfloat16)
                keep[z] = add_two(kept[z, mine], got[z, mine]).astype(jnp.bfloat16)

        steps.append((
            [(a.at[z], b.at[z]) for a, b in zip(ins_hbm, ins)],
            compute,
            [(a.at[z], b.at[z]) for a, b in zip(outs, outs_hbm)],
        ))
    return steps


def third_steps(bits_ref, ins_hbm, ins, outs_hbm, outs):
    low = bits_ref[2] & 1
    steps = []
    for half, out, out_hbm in zip((1 - low, low), outs, outs_hbm):
        for high in range(2):
            block = 2 * high + half

            def compute(block=block, out=out, high=high):
                width = ins[0].shape[-1]
                out[high, :, :width] = add_two(ins[0][block], ins[1][block]).astype(jnp.bfloat16)
                out[high, :, width:] = add_two(ins[2][block], ins[3][block]).astype(jnp.bfloat16)

            steps.append((
                [(a.at[block], b.at[block]) for a, b in zip(ins_hbm, ins)], compute, [(out.at[high], out_hbm.at[high])]
            ))
    return steps


def fourth_steps(bits_ref, ins_hbm, ins, outs_hbm, outs):
    high = bits_ref[2] >> 1
    steps = []
    for block, out, out_hbm in zip((1 - high, high), outs, outs_hbm):

        def compute(block=block, out=out):
            for i in range(0, len(ins), 2):
                width = ins[i].shape[-1]
                total = add_two(ins[i][block], ins[i + 1][block])
                out[:, i // 2 * width : (i // 2 + 1) * width] = total.astype(jnp.bfloat16)

        steps.append((
            [(a.at[block], b.at[block]) for a, b in zip(ins_hbm, ins)], compute, [(out, out_hbm)]
        ))
    return steps


def sums_kernel(jobs, bits_ref, *refs):
    count, made = sum(j[1] for j in jobs), sum(j[2] for j in jobs)
    ins_hbm, outs_hbm, refs = refs[:count], refs[count : count + made], refs[count + made :]
    ins, outs, (in_sems, out_sems) = refs[:count], refs[count : count + made], refs[count + made :]
    steps = []
    for build, n, m in jobs:
        steps += build(bits_ref, ins_hbm[:n], ins[:n], outs_hbm[:m], outs[:m])
        ins_hbm, ins, outs_hbm, outs = ins_hbm[n:], ins[n:], outs_hbm[m:], outs[m:]
    stream(steps, in_sems, out_sems)


def sums(bits, second=None, third=None, fourth=None, cost=None):
    jobs, ins, outs = [], [], []
    if second is not None:
        made = [a.shape[:1] + a.shape[2:] for a in second]
        jobs.append((second_steps, 4, 4))
        ins, outs = ins + list(second), outs + made
    if third is not None:
        made = [(2, third[0].shape[1], third[0].shape[2] + third[2].shape[2])] * 2
        jobs.append((third_steps, 4, 2))
        ins, outs = ins + list(third), outs + made
    if fourth is not None:
        made = [(fourth[0].shape[1], sum(a.shape[2] for a in fourth[::2]))] * 2
        jobs.append((fourth_steps, len(fourth), 2))
        ins, outs = ins + list(fourth), outs + made
    bf = jnp.bfloat16
    results = pl.pallas_call(
        functools.partial(sums_kernel, tuple(jobs)),
        out_shape=tuple(jax.ShapeDtypeStruct(o, bf) for o in outs),
        in_specs=[SMEM] + [HBM] * len(ins),
        out_specs=[HBM] * len(outs),
        scratch_shapes=[pltpu.VMEM(a.shape, bf) for a in ins]
        + [pltpu.VMEM(o, bf) for o in outs]
        + [pltpu.SemaphoreType.DMA((4 * len(ins),)), pltpu.SemaphoreType.DMA((4 * len(outs),))],
        compiler_params=pltpu.CompilerParams(vmem_limit_bytes=60 * MIB),
        cost_estimate=cost or CHEAP,
        name="sums",
    )(bits, *ins)
    split = []
    for _, _, m in jobs:
        split.append(results[:m])
        results = results[m:]
    return split[0] if len(split) == 1 else split


def over_dp(array, flip):
    size = lax.axis_size("dp")
    return lax.ppermute(array, "dp", [(i, i ^ flip) for i in range(size)])


def after(arrays, *needed):
    return lax.optimization_barrier((arrays, needed))[0]


def first_stage(pieces):
    sent_a, kept_a, sent_b, kept_b = pieces
    return (kept_a, over_dp(sent_a, 1), kept_b, over_dp(sent_b, 2))


def second_stage(sent_a, kept_a, sent_b, kept_b):
    return (kept_a, over_dp(sent_a, 2), kept_b, over_dp(sent_b, 1))


def third_stage(send, keep):
    return (keep, over_dp(send, 4))


def fourth_stage(send, keep):
    return (keep, over_dp(send, 8))


def ffn_sums_kernel(*refs):
    ins, (gate_ref, up_ref, down_ref) = refs[:-3], refs[-3:]
    chunks = [
        (kept, got, at)
        for kept, got in zip(ins[0::2], ins[1::2])
        for at in range(0, kept.shape[-1], 3 * (CUTS[0][1] - CUTS[0][0]))
    ]
    for (low, high), (kept, got, at) in zip(CUTS, chunks):
        count, half = high - low, (high - low) // 2
        total = add_two(kept[:, at : at + 3 * count], got[:, at : at + 3 * count])
        gate_ref[:, low:high] = total[:, :count]
        down_ref[low : low + half, :] = total[:, count : count + half].T
        up_ref[:, low:high] = total[:, count + half : 2 * count + half]
        down_ref[low + half : high, :] = total[:, 2 * count + half :].T


def ffn_sums(pieces):
    rows, units = pieces[0].shape[0], CUTS[-1][1]
    wide = jax.ShapeDtypeStruct((rows, units), jnp.float32)
    return pl.pallas_call(
        ffn_sums_kernel,
        out_shape=(wide, wide, jax.ShapeDtypeStruct((units, rows), jnp.float32)),
        in_specs=[VMEM] * len(pieces),
        out_specs=[VMEM] * 3,
        compiler_params=pltpu.CompilerParams(vmem_limit_bytes=60 * MIB),
        cost_estimate=CHEAP,
        name="ffn_sums",
    )(*pieces)


def joined(pieces):
    sent_a, kept_a, sent_b, kept_b = pieces
    first, second = lax.axis_index("dp") & 1, lax.axis_index("dp") >> 1 & 1
    out = []
    for sent, kept, axis, mine in ((sent_a, kept_a, 2, first), (sent_b, kept_b, 1, second)):
        low = jnp.where(mine == 0, kept, sent)
        high = jnp.where(mine == 0, sent, kept)
        out.append(jnp.stack([low, high], axis=axis).reshape(-1, sent.shape[-1]))
    return out


def scatter_sum(grads):
    size = lax.axis_size("dp")
    bits = size.bit_length() - 1
    me = lax.axis_index("dp")
    rows, width = grads.shape
    work = grads.reshape((2,) * bits + (rows // size, width))
    for bit in range(bits):
        axis = bits - 1 - bit
        mine = (me >> bit) & 1
        sent = lax.dynamic_index_in_dim(work, 1 - mine, axis, keepdims=False)
        kept = lax.dynamic_index_in_dim(work, mine, axis, keepdims=False)
        work = kept.astype(jnp.float32) + over_dp(sent, 1 << bit).astype(jnp.float32)
        work = work.astype(grads.dtype)
    return work.astype(jnp.float32)


def gain_stage(work, bit):
    mine = (lax.axis_index("dp") >> bit) & 1
    axis = work.ndim - 2
    sent = lax.dynamic_index_in_dim(work, 1 - mine, axis, keepdims=False)
    return lax.dynamic_index_in_dim(work, mine, axis, keepdims=False), over_dp(sent, 1 << bit)


def to_other_core(array):
    return lax.ppermute(array, "tensor", [(0, 1), (1, 0)])


def norm_grad(value, grad, gain):
    scale = lax.rsqrt(jnp.mean(value * value, axis=-1, keepdims=True) + epsilon)
    scaled = grad * gain
    back = scale * scaled - value * scale**3 * jnp.mean(scaled * value, axis=-1, keepdims=True)
    return back, jnp.sum(grad * value * scale, axis=0, keepdims=True)


def stream(steps, in_sems, out_sems):
    waits, count = [], 0
    for loads, _, _ in steps:
        waits.append([start(*pair, in_sems.at[count + i]) for i, pair in enumerate(loads)])
        count += len(loads)
    copies = []
    for wait, (_, compute, stores) in zip(waits, steps):
        for copy in wait:
            copy.wait()
        compute()
        for pair in stores:
            copies.append(start(*pair, out_sems.at[len(copies)]))
    for copy in copies:
        copy.wait()


def row_kernel(function, turned, vectors, count, outs, *refs):
    def cut(n):
        nonlocal refs
        head, refs = refs[:n], refs[n:]
        return head

    ins_hbm, vector, outs_hbm = cut(count), cut(1), cut(outs)
    sums = cut(vectors)
    ins, held, (in_sems, out_sems) = cut(count), cut(outs), refs
    steps = []
    for i in range(ins[0].shape[0] // BLOCK):
        rows = pl.ds(i * BLOCK, BLOCK)
        places = [(slice(None), rows) if t else (rows, slice(None)) for t in turned]

        def compute(i=i, rows=rows, places=places):
            results = function(*(ref[rows, :].astype(jnp.float32) for ref in ins), vector[0][...])
            for ref, place, result, t in zip(held, places, results, turned):
                ref[place] = (result.T if t else result).astype(jnp.bfloat16)
            for ref, result in zip(sums, results[len(held) :]):
                if i == 0:
                    ref[...] = result
                else:
                    ref[...] += result

        steps.append((
            [(a.at[rows], b.at[rows]) for a, b in zip(ins_hbm, ins)],
            compute,
            [(a.at[place], b.at[place]) for a, b, place in zip(held, outs_hbm, places)],
        ))
    stream(steps, in_sems, out_sems)


def row_call(function, name, ins, vector, turned, vectors=0):
    rows, width = ins[0].shape
    bf, blocks = jnp.bfloat16, rows // BLOCK
    outs = [jax.ShapeDtypeStruct((width, rows) if t else (rows, width), bf) for t in turned]
    return pl.pallas_call(
        functools.partial(row_kernel, function, turned, vectors, len(ins), len(outs)),
        out_shape=tuple(outs + [jax.ShapeDtypeStruct((1, width), jnp.float32)] * vectors),
        in_specs=[HBM] * len(ins) + [VMEM],
        out_specs=[HBM] * len(outs) + [VMEM] * vectors,
        scratch_shapes=[pltpu.VMEM(a.shape, bf) for a in (*ins, *outs)]
        + [pltpu.SemaphoreType.DMA((len(ins) * blocks,)), pltpu.SemaphoreType.DMA((len(outs) * blocks,))],
        compiler_params=pltpu.CompilerParams(vmem_limit_bytes=60 * MIB),
        cost_estimate=CHEAP,
        name=name,
    )(*ins, vector)


def norm_rows(x, own, got, gain):
    hidden = x + (own + got)
    norm = lax.rsqrt(jnp.mean(hidden * hidden, axis=-1, keepdims=True) + epsilon)
    act = hidden * norm * gain
    return hidden, act, act


def middle_rows(hidden, own, got, cot, gain):
    back, gain_grad = norm_grad(hidden, own + got, gain)
    total = cot + back
    return total, total, gain_grad


def output_rows(hidden, own, got, gain):
    return (hidden + (own + got),)


def input_rows(x, gatt, own, got, gain):
    back, gain_grad = norm_grad(x, own + got, gain)
    return gatt + back, gain_grad


def attention_grads(total, half, kv_half):
    names = (("out", half), ("query", half), ("out", half), ("key", kv_half), ("value", kv_half))
    names += (("query", half), ("key", kv_half), ("value", kv_half))
    found, at = {}, 0
    for name, count in names:
        found.setdefault(name, []).append(total[:, at : at + count])
        at += count
    found = {name: jnp.concatenate(parts, axis=1) for name, parts in found.items()}
    return found["query"], found["key"], found["value"], found["out"].T


def plain(names, chunk, backward):
    v = dict(names)
    layer_input, hidden, bits, blocks, size = (v[n] for n in ("layer_input", "hidden", "bits", "blocks", "size"))
    rows, width = layer_input.shape
    half, kv_half, heads = v["half"], v["kv_half"], v["heads"]
    pieces = []
    for i in range(len(CUTS)):
        units, piece = chunk(i, whole=True)
        pieces.append(piece)
    hidden_units, grad_gate_lin, grad_up_lin = units
    two_own = projection([grad_gate_lin, grad_up_lin], [v["w_gate"], v["w_up"]], NT)
    ffn_own = projection([hidden_units], [v["w_down"]], NN)
    grad_attention, grad_attention_t, grad_ffn_gain = row_call(
        middle_rows, "middle", [hidden, two_own, to_other_core(two_own), v["cotangent"]], v["gain_two"], [0, 1], 1
    )
    (output,) = row_call(output_rows, "output", [hidden, ffn_own, to_other_core(ffn_own)], v["gain_two"], [0])
    back_one = backward(0, gatt=grad_attention)
    pieces.append(gradient_pieces(
        bits, blocks, [grad_attention_t, v["act_one_t"]], [v["mixed"], *back_one], [0, 1, 1],
        [((0, half, 0, 0), (half, heads, 0, 1)), ((0, half, half, 0),), ((0, half, half, 1),)],
    ))
    *back_two, one_own = backward(1, *back_one, gatt=grad_attention)
    pieces.append(gradient_pieces(
        bits, blocks, [v["act_one_t"]], back_two, [0, 0], [((0, half, 0, 0),), ((0, half, 0, 1),)]
    ))
    grad_input, grad_attn_gain = row_call(
        input_rows, "input", [layer_input, grad_attention, one_own, to_other_core(one_own)],
        v["attn_gain"].reshape(1, width), [0], 1,
    )
    gains = jnp.concatenate([grad_attn_gain, grad_ffn_gain]).reshape(2, size, width // size)
    gains = scatter_sum(gains.transpose(1, 0, 2).reshape(size, 2 * width // size))[0]
    total = scatter_sum(jnp.concatenate([p for piece in pieces for p in joined(piece)], axis=1))
    gates, ups, downs = [], [], []
    for low, high in CUTS:
        count = high - low
        parts = jnp.split(total[:, 3 * low : 3 * high], [count, count * 3 // 2, count * 5 // 2], axis=1)
        for found, part in zip((gates, downs, ups, downs), parts):
            found.append(part)
    return (
        output,
        grad_input,
        gains[: width // size],
        *attention_grads(total[:, 3 * CUTS[-1][1] :], half, kv_half),
        gains[width // size :],
        jnp.concatenate(gates, axis=1),
        jnp.concatenate(ups, axis=1),
        jnp.concatenate(downs, axis=1).T,
    )


def per_device(
    layer_input,
    branch_point,
    attn_gain,
    w_query,
    w_key,
    w_value,
    w_out,
    ffn_gain,
    w_gate,
    w_up,
    w_down,
    cotangent,
):
    rows, width = layer_input.shape
    size = lax.axis_size("dp")
    by_kernel = size == KERNEL_BLOCKS
    blocks = KERNEL_BLOCKS
    me = lax.axis_index("dp")
    bits = jnp.stack([me & 1, me >> 1 & 1, me >> 2 & 3]).astype(jnp.int32)
    rope = rope_tables()
    act_one_t, queries, keys, values, mixed, log_sums, attn_own = attention_forward(
        branch_point, layer_input, attn_gain, w_query, w_key, w_value, w_out, rope
    )
    attn_got = to_other_core(attn_own)
    kv_half = w_key.shape[1] // 2
    w_key_value = jnp.concatenate(
        [w_key[:, :kv_half], w_value[:, :kv_half], w_key[:, kv_half:], w_value[:, kv_half:]], axis=1
    )
    cot_t = cotangent.T
    gain_two = ffn_gain.reshape(1, width)
    hidden, act_two, act_two_t = row_call(
        norm_rows, "norm_two", [layer_input, attn_own, attn_got], after(gain_two, cot_t, w_key_value), [0, 0, 1]
    )
    heads, kv = mixed.shape[1], w_key.shape[1]
    half = heads // 2
    units = ()

    def chunk(i, *needed, whole=False):
        nonlocal units
        low, high = CUTS[i]
        *units, sent_a, kept_a, sent_b, kept_b = ffn_chunk(
            bits, blocks, after(act_two, *needed), cotangent, act_two_t, cot_t,
            w_gate, w_up, w_down, units, low, high - low,
        )
        piece = (sent_a, kept_a, sent_b, kept_b)
        return (units, piece) if whole else piece

    def backward(part, *needed, gatt=None):
        return attention_backward(
            part, branch_point, after(grad_attention if gatt is None else gatt, *needed), queries, keys, values, log_sums,
            w_out, w_query, w_key_value, rope, list(needed[:2]) if part else [],
        )

    if not by_kernel:
        return plain(locals(), chunk, backward)
    pieces = [chunk(0)]
    one = [first_stage(pieces[0])]
    pieces.append(chunk(1))
    one.append(first_stage(pieces[1]))
    pieces.append(chunk(2, pieces[1]))
    pieces[2], one[0] = after((pieces[2], one[0]))
    joint = sums(bits, second=one[0])
    two = [second_stage(*joint)]
    pieces.append(chunk(3, joint))
    *units, pieces[3], one[1], two[0] = after((*units, pieces[3], one[1], two[0]))
    joint = sums(bits, second=one[1], third=two[0])
    two.append(second_stage(*joint[0]))
    three = [third_stage(*joint[1])]
    one.append(first_stage(after(pieces[2], units)))
    hidden_units, grad_gate_lin, grad_up_lin = units
    two_own = projection(after([grad_gate_lin, grad_up_lin], joint), [w_gate, w_up], NT)
    two_own, three[0] = after((two_own, three[0]))
    two_got = to_other_core(two_own)
    ffn_own = projection([after(hidden_units, two_own)], [w_down], NN)
    ffn_own, one[2], two[1] = after((ffn_own, one[2], two[1]))
    joint = sums(bits, second=one[2], third=two[1], cost=LONG)
    two.append(second_stage(*joint[0]))
    three.append(third_stage(*joint[1]))
    one.append(first_stage(after(pieces[3], ffn_own)))
    grad_attention, grad_attention_t, grad_ffn_gain = row_call(
        middle_rows, "middle", [hidden, two_own, two_got, after(cotangent, joint)], gain_two, [0, 1], 1
    )
    grad_attention, three[0], three[1] = after((grad_attention, three[0], three[1]))
    joint = sums(bits, fourth=(*three[0], *three[1]))
    four = [fourth_stage(*joint)]
    back_one = backward(0, grad_attention, joint)
    back_one, two[2], one[3], four[0] = after((back_one, two[2], one[3], four[0]))
    joint = sums(bits, second=one[3], third=two[2])
    two.append(second_stage(*joint[0]))
    three.append(third_stage(*joint[1]))
    early = gradient_pieces(
        bits, blocks, [after(grad_attention_t, joint), act_one_t], [mixed, *back_one], [0, 1, 1],
        [((0, half, 0, 0), (half, heads, 0, 1)), ((0, half, half, 0),), ((0, half, half, 1),)],
    )
    early, two[3], three[2] = after((early, two[3], three[2]))
    joint = sums(bits, third=two[3], fourth=three[2])
    three.append(third_stage(*joint[0]))
    four.append(fourth_stage(*joint[1]))
    early_one = first_stage(early)
    ffn_got = to_other_core(after(ffn_own, early))
    *back_two, one_own = backward(1, *back_one, early, joint)
    back_two, one_own, early_one, three[3], four[1], ffn_got = after(
        (back_two, one_own, early_one, three[3], four[1], ffn_got)
    )
    one_got = to_other_core(one_own)
    joint = sums(bits, second=early_one, fourth=three[3])
    early_two = second_stage(*joint[0])
    four.append(fourth_stage(*joint[1]))
    late = gradient_pieces(
        bits, blocks, [after(act_one_t, joint)], back_two, [0, 0], [((0, half, 0, 0),), ((0, half, 0, 1),)]
    )
    late, one_got = after((late, one_got))
    late_one = first_stage(late)
    grad_input, grad_attn_gain = row_call(
        input_rows, "input", [layer_input, after(grad_attention, late), one_own, one_got],
        attn_gain.reshape(1, width), [0], 1,
    )
    grad_input, late_one, early_two = after((grad_input, late_one, early_two))
    joint = sums(bits, second=late_one, third=early_two)
    late_two = second_stage(*joint[0])
    early_three = third_stage(*joint[1])
    gains = jnp.concatenate([grad_attn_gain, grad_ffn_gain]).reshape(2, size, width // size)
    gains = gains.transpose(1, 0, 2).reshape(2, 2, 2, 2, 2 * width // size)
    gains = gain_stage(after(gains, joint), 0)
    (output,) = row_call(output_rows, "output", [hidden, after(ffn_own, joint), ffn_got], gain_two, [0])
    output, late_two, early_three, gains = after((output, late_two, early_three, gains))
    joint = sums(bits, third=late_two, fourth=early_three)
    late_three = third_stage(*joint[0])
    early_four = fourth_stage(*joint[1])
    gains = gain_stage(gains[0] + gains[1], 1)
    grad_gate, grad_up, grad_down = ffn_sums(after([p for piece in four for p in piece], joint))
    late_three, gains, grad_down = after((late_three, gains, grad_down))
    joint = sums(bits, fourth=late_three)
    late_four = fourth_stage(*joint)
    gains = gain_stage(after(gains[0] + gains[1], joint), 2)
    gains = gain_stage(gains[0] + gains[1], 3)
    gains = gains[0] + gains[1]
    total = jnp.concatenate([add_two(*early_four), add_two(*late_four)], axis=1)
    return (
        output,
        grad_input,
        gains[: width // size],
        *attention_grads(total, half, kv_half),
        gains[width // size :],
        grad_gate,
        grad_up,
        grad_down,
    )


def solution(mesh):
    placed = (
        P("dp", None),
        P("dp", None),
        P(),
        P(None, "tensor"),
        P(None, "tensor"),
        P(None, "tensor"),
        P("tensor", None),
        P(),
        P(None, "tensor"),
        P(None, "tensor"),
        P("tensor", None),
        P("dp", None),
    )
    return jax.shard_map(
        per_device,
        mesh=mesh,
        in_specs=placed,
        out_specs=(
            P("dp", None),
            P("dp", None),
            P("dp"),
            P("dp", "tensor"),
            P("dp", "tensor"),
            P("dp", "tensor"),
            P("tensor", "dp"),
            P("dp"),
            P("dp", "tensor"),
            P("dp", "tensor"),
            P("tensor", "dp"),
        ),
        check_vma=False,
    )
```

```python
import functools

import jax
import jax.numpy as jnp
import numpy as np
from jax import lax
from jax.experimental import pallas as pl
from jax.experimental.pallas import tpu as pltpu
from jax.sharding import PartitionSpec as P

HEAD_DIM = 96
PROMPT = 1024
CONT_LEN = 128
CONT = 2
GROUP_TOK = 1280
BLOCK = 256
BLOCKS = GROUP_TOK // BLOCK
LANES = 128
MIB = 1 << 20
CHEAP = pl.CostEstimate(flops=10**6, bytes_accessed=10**5, transcendentals=0)
epsilon = 1e-05
rope_base = 100000.0
LOG2E = 1.4426950408889634
SCORE_SCALE = HEAD_DIM ** (-0.5)
NT = (((1,), (1,)), ((), ()))
TN = (((0,), (0,)), ((), ()))

LONG = pl.CostEstimate(flops=10**11, bytes_accessed=10**5, transcendentals=0)


def matmul(left, right, dims=(((1,), (0,)), ((), ()))):
    return lax.dot_general(left, right, dims, preferred_element_type=jnp.float32)


HBM = pl.BlockSpec(memory_space=pl.ANY)
SMEM = pl.BlockSpec(memory_space=pltpu.SMEM)
VMEM = pl.BlockSpec(memory_space=pltpu.VMEM)


def start(source, target, sem):
    copy = pltpu.make_async_copy(source, target, sem)
    copy.start()
    return copy


def rows_of(blocks, width):
    return (blocks // 4, 2, 2, None, width)


def rope_tables():
    half = HEAD_DIM // 2
    frequency = rope_base ** (-np.arange(half, dtype=np.float64) * 2.0 / HEAD_DIM)
    angles = np.arange(PROMPT + CONT_LEN, dtype=np.float64)[:, None] * frequency[None, :]
    pad = np.zeros((angles.shape[0], LANES - HEAD_DIM))
    cosine = np.concatenate([np.cos(angles), np.cos(angles), pad], axis=1)
    sine = np.concatenate([-np.sin(angles), np.sin(angles), pad], axis=1)
    return jnp.asarray(np.stack([cosine, sine]), jnp.float32)


def place_rope(branch_ref, table_ref, rope_ref):
    rope_ref[:, :PROMPT, :] = table_ref[:, :PROMPT, :]
    for c in range(CONT):
        rows = pl.ds(PROMPT + c * CONT_LEN, CONT_LEN)
        for i in range(2):
            rope_ref[i, rows, :] = table_ref[i, pl.ds(branch_ref[0, c], CONT_LEN), :]


def lane_ids(shape):
    return lax.broadcasted_iota(jnp.int32, shape, 1)


def swap_halves(head):
    half = HEAD_DIM // 2
    return jnp.where(
        lane_ids(head.shape) < half, pltpu.roll(head, LANES - half, 1), pltpu.roll(head, half, 1)
    )


def take_head(full, h):
    first = h * HEAD_DIM
    start, shift = first // LANES * LANES, first % LANES
    width = LANES if shift + HEAD_DIM <= LANES else 2 * LANES
    part = full[:, start : start + width]
    return part[:, :LANES] if shift == 0 else pltpu.roll(part, width - shift, 1)[:, :LANES]


def join_heads(heads):
    lanes = lane_ids(heads[0].shape)
    out = []
    for i in range(0, len(heads), 4):
        one, two, three = (pltpu.roll(heads[i + j], LANES - 32 * j, 1) for j in (1, 2, 3))
        out.append(jnp.where(lanes < 96, heads[i], one))
        out.append(jnp.where(lanes < 64, one, two))
        out.append(jnp.where(lanes < 32, two, three))
    return jnp.concatenate(out, axis=1)


def own_mask(shape, query_axis, block):
    query = lax.broadcasted_iota(jnp.int32, shape, query_axis) & (BLOCK - 1)
    key = lax.broadcasted_iota(jnp.int32, shape, 1 - query_axis)
    mask = key <= query
    if block * BLOCK >= PROMPT:
        mask = mask & ((key // CONT_LEN) == (query // CONT_LEN))
    return mask


def reach_mask(shape, query_axis, branch_ref):
    query = lax.broadcasted_iota(jnp.int32, shape, query_axis) & (BLOCK - 1)
    key = lax.broadcasted_iota(jnp.int32, shape, 1 - query_axis) + PROMPT // 2
    return key < jnp.where(query < CONT_LEN, branch_ref[0, 0], branch_ref[0, 1])


def attention_forward_kernel(
    branch_ref, gain_ref, *refs,
):
    ins_hbm, outs_hbm, ins, outs, (o_ref, rope_ref, in_sems, x_sems, out_sems, row_sems) = (
        refs[:6], refs[6:13], refs[13:19], refs[19:26], refs[26:],
    )
    x_ref, wq_ref, wk_ref, wv_ref, wo_ref, table_ref = ins
    act_t_ref, q_ref, k_ref, v_ref, mixed_ref, lse_ref, part_ref = outs
    kv_heads = k_ref.shape[0]
    group = 2 * BLOCK

    def x_in(i):
        rows = pl.ds(pl.multiple_of(i * BLOCK, BLOCK), BLOCK)
        return pltpu.make_async_copy(ins_hbm[0].at[rows], x_ref.at[rows], x_sems.at[i])

    def rows_out(n, which, i):
        rows = pl.ds(pl.multiple_of(i * BLOCK, BLOCK), BLOCK)
        return pltpu.make_async_copy(outs[n].at[rows], outs_hbm[n].at[rows], row_sems.at[which, i])

    x_in(0).start()
    loads = {n: start(ins_hbm[n], ins[n], in_sems.at[n]) for n in (1, 5, 2, 3)}
    for i in range(1, BLOCKS):
        x_in(i).start()
    loads[4] = start(ins_hbm[4], wo_ref, in_sems.at[4])
    for n in (5, 1, 2, 3):
        loads[n].wait()
    place_rope(branch_ref, table_ref, rope_ref)

    def project(i, carry):
        rows = pl.ds(pl.multiple_of(i * BLOCK, BLOCK), BLOCK)
        x_in(i).wait()
        x = x_ref[rows, :].astype(jnp.float32)
        norm = lax.rsqrt(jnp.mean(x * x, axis=-1, keepdims=True) + epsilon)
        act = x * norm * gain_ref[...][None, :]
        act_t_ref[:, rows] = act.T.astype(jnp.bfloat16)
        act = act.astype(jnp.bfloat16)
        cosine, sine = rope_ref[0, rows, :], rope_ref[1, rows, :]
        full = matmul(act, wq_ref[...])
        for h in range(2 * kv_heads):
            head = take_head(full, h)
            rotated = head * cosine + swap_halves(head) * sine
            q_ref[h // 2, i, pl.ds(h % 2 * BLOCK, BLOCK), :] = rotated.astype(jnp.bfloat16)
        full = matmul(act, wk_ref[...])
        for h in range(kv_heads):
            head = take_head(full, h)
            rotated = head * cosine + swap_halves(head) * sine
            k_ref[h, rows, :] = rotated.astype(jnp.bfloat16)
        full = matmul(act, wv_ref[...])
        lanes = lane_ids((BLOCK, LANES))
        for h in range(kv_heads):
            head = jnp.where(lanes < HEAD_DIM, take_head(full, h), 0.0)
            v_ref[h, rows, :] = jnp.where(lanes == HEAD_DIM, 1.0, head).astype(jnp.bfloat16)
        return carry

    lax.fori_loop(0, BLOCKS, project, 0)
    stores = [start(outs[n], outs_hbm[n], out_sems.at[n]) for n in range(4)]
    factor = SCORE_SCALE * LOG2E

    def attend(h, carry):
        for i in range(BLOCKS):
            query = q_ref[h, i]
            before = i * BLOCK
            own = matmul(query, k_ref[h, before : before + BLOCK], NT)
            own = jnp.where(own_mask(own.shape, 0, i), own, -1e30)
            largest = jnp.max(own, axis=-1, keepdims=True)
            spans = []
            if i > 0:
                cuts = [0, before] if before < PROMPT else [0, PROMPT // 2, PROMPT]
                for low, high in zip(cuts[:-1], cuts[1:]):
                    scores = matmul(query, k_ref[h, low:high], NT)
                    if before >= PROMPT and low > 0:
                        scores = jnp.where(reach_mask(scores.shape, 0, branch_ref), scores, -1e30)
                    largest = jnp.maximum(largest, jnp.max(scores, axis=-1, keepdims=True))
                    spans.append((low, high, scores))
            shift = largest * factor
            probs = jnp.exp2(own * factor - shift).astype(jnp.bfloat16)
            total = matmul(probs, v_ref[h, before : before + BLOCK])
            for low, high, scores in spans:
                probs = jnp.exp2(scores * factor - shift).astype(jnp.bfloat16)
                total += matmul(probs, v_ref[h, low:high])
            sums = total[:, HEAD_DIM : HEAD_DIM + 1]
            mixed = total / sums
            for g in range(2):
                o_ref[2 * h + g, before : before + BLOCK, :] = mixed[g * BLOCK : (g + 1) * BLOCK]
            logs = shift + jnp.log2(sums)
            lse_ref[h, i] = jnp.broadcast_to(logs, (group, LANES)).T[0:1, :]
        return carry

    lax.fori_loop(0, kv_heads, attend, 0)
    stores.append(start(lse_ref, outs_hbm[5], out_sems.at[5]))
    loads[4].wait()

    def finish(i, carry):
        rows = pl.ds(pl.multiple_of(i * BLOCK, BLOCK), BLOCK)
        mixed = join_heads([o_ref[h, rows, :] for h in range(2 * kv_heads)]).astype(jnp.bfloat16)
        mixed_ref[rows, :] = mixed
        part_ref[rows, :] = matmul(mixed, wo_ref[...]).astype(jnp.bfloat16)
        rows_out(4, 0, i).start()
        rows_out(6, 1, i).start()
        return carry

    lax.fori_loop(0, BLOCKS, finish, 0)
    for copy in stores:
        copy.wait()
    for i in range(BLOCKS):
        rows_out(4, 0, i).wait()
        rows_out(6, 1, i).wait()


def attention_forward(branch, x, gain, wq, wk, wv, wo, rope):
    kv_heads = wk.shape[1] // HEAD_DIM
    rows, width = x.shape
    bf = jnp.bfloat16
    ins = (x, wq, wk, wv, wo, rope)
    outs = (
        jax.ShapeDtypeStruct((width, rows), bf),
        jax.ShapeDtypeStruct((kv_heads, BLOCKS, 2 * BLOCK, LANES), bf),
        jax.ShapeDtypeStruct((kv_heads, rows, LANES), bf),
        jax.ShapeDtypeStruct((kv_heads, rows, LANES), bf),
        jax.ShapeDtypeStruct((rows, wq.shape[1]), bf),
        jax.ShapeDtypeStruct((kv_heads, BLOCKS, 1, 2 * BLOCK), jnp.float32),
        jax.ShapeDtypeStruct((rows, width), bf),
    )
    return pl.pallas_call(
        attention_forward_kernel,
        out_shape=outs,
        in_specs=[SMEM, VMEM] + [HBM] * 6,
        out_specs=[HBM] * 7,
        scratch_shapes=[pltpu.VMEM(a.shape, a.dtype) for a in ins + outs]
        + [
            pltpu.VMEM((2 * kv_heads, rows, LANES), jnp.float32),
            pltpu.VMEM((2, rows, LANES), jnp.float32),
            pltpu.SemaphoreType.DMA((6,)),
            pltpu.SemaphoreType.DMA((BLOCKS,)),
            pltpu.SemaphoreType.DMA((6,)),
            pltpu.SemaphoreType.DMA((2, BLOCKS)),
        ],
        compiler_params=pltpu.CompilerParams(vmem_limit_bytes=60 * MIB),
        cost_estimate=CHEAP,
        name="attention_forward",
    )(branch, gain, *ins)


def attention_backward_kernel(
    part, branch_ref, *refs
):
    def cut(count):
        nonlocal refs
        head, refs = refs[:count], refs[count:]
        return head

    count, made = (11, 3) if part else (7, 2)
    ins_hbm, outs_hbm, ins, outs = cut(count), cut(made), cut(count), cut(made)
    do_ref, dq_ref, dk_ref, dv_ref, rope_ref, in_sems, gatt_sems, row_sems = refs
    gatt_ref, wo_ref, q_ref, k_ref, v_ref, lse_ref, table_ref = ins[:7]
    wq_ref, wkv_ref, *first_ref = ins[7:] if part else (None, None)
    gq_ref, gkv_ref = outs[:2]
    part_ref = outs[2] if part else None
    kv_heads = k_ref.shape[0]
    group = 2 * BLOCK
    factor = SCORE_SCALE * LOG2E

    def gatt_in(i):
        rows = pl.ds(pl.multiple_of(i * BLOCK, BLOCK), BLOCK)
        return pltpu.make_async_copy(ins_hbm[0].at[rows], gatt_ref.at[rows], gatt_sems.at[i])

    def rows_out(n, i):
        rows = pl.ds(pl.multiple_of(i * BLOCK, BLOCK), BLOCK)
        return pltpu.make_async_copy(outs[n].at[rows], outs_hbm[n].at[rows], row_sems.at[n, i])

    loads = []
    for n in range(1, count):
        size = ins[n].shape[0]
        source = ins_hbm[n].at[pl.ds(part * size, size)] if n < 6 else ins_hbm[n]
        loads.append(start(source, ins[n], in_sems.at[n]))
        if n == 1:
            for i in range(BLOCKS):
                gatt_in(i).start()
    loads[0].wait()

    def project(i, carry):
        rows = pl.ds(pl.multiple_of(i * BLOCK, BLOCK), BLOCK)
        gatt_in(i).wait()
        full = matmul(gatt_ref[rows, :], wo_ref[...], NT)
        lanes = lane_ids((BLOCK, LANES))
        for h in range(2 * kv_heads):
            head = jnp.where(lanes < HEAD_DIM, take_head(full, h), 0.0)
            do_ref[h // 2, i, pl.ds(h % 2 * BLOCK, BLOCK), :] = head.astype(jnp.bfloat16)
        return carry

    lax.fori_loop(0, BLOCKS, project, 0)
    for copy in loads[1:6]:
        copy.wait()
    place_rope(branch_ref, table_ref, rope_ref)

    def attend(h, carry):
        for i in reversed(range(BLOCKS)):
            query, grad, logs = q_ref[h, i], do_ref[h, i], lse_ref[h, i]
            before = i * BLOCK
            cuts = [(before, before + BLOCK)]
            if i > 0 and before < PROMPT:
                cuts += [(0, before)]
            elif i > 0:
                cuts += [(0, PROMPT // 2), (PROMPT // 2, PROMPT)]
            spans, weighted = [], 0.0
            for low, high in cuts:
                scores = matmul(k_ref[h, low:high], query, NT)
                probs = jnp.exp2(scores * factor - logs)
                if low == before:
                    probs = jnp.where(own_mask(probs.shape, 1, i), probs, 0.0)
                elif before >= PROMPT and low > 0:
                    probs = jnp.where(reach_mask(probs.shape, 1, branch_ref), probs, 0.0)
                grad_probs = matmul(v_ref[h, low:high], grad, NT)
                weighted += jnp.sum(probs * grad_probs, axis=0, keepdims=True)
                spans.append((low, high, probs, grad_probs))
            grad_query = jnp.zeros((group, LANES), jnp.float32)
            for low, high, probs, grad_probs in spans:
                grad_scores = (probs * (grad_probs - weighted)).astype(jnp.bfloat16)
                grad_query += matmul(grad_scores, k_ref[h, low:high], TN)
                grad_key = matmul(grad_scores, query)
                grad_value = matmul(probs.astype(jnp.bfloat16), grad)
                if before >= PROMPT:
                    dk_ref[h, low:high] = grad_key
                    dv_ref[h, low:high] = grad_value
                else:
                    dk_ref[h, low:high] += grad_key
                    dv_ref[h, low:high] += grad_value
            dq_ref[h, i] = grad_query
        return carry

    lax.fori_loop(0, kv_heads, attend, 0)
    for copy in loads[6:]:
        copy.wait()

    def finish(i, carry):
        rows = pl.ds(pl.multiple_of(i * BLOCK, BLOCK), BLOCK)
        cosine, sine = rope_ref[0, rows, :] * SCORE_SCALE, rope_ref[1, rows, :] * SCORE_SCALE
        heads = []
        for h in range(2 * kv_heads):
            head = dq_ref[h // 2, i, pl.ds(h % 2 * BLOCK, BLOCK), :]
            heads.append(head * cosine - swap_halves(head) * sine)
        grad_q = join_heads(heads).astype(jnp.bfloat16)
        heads = []
        for h in range(kv_heads):
            head = dk_ref[h, rows, :]
            heads.append(head * cosine - swap_halves(head) * sine)
        heads += [dv_ref[h, rows, :] for h in range(kv_heads)]
        grad_kv = join_heads(heads).astype(jnp.bfloat16)
        gq_ref[rows, :] = grad_q
        gkv_ref[rows, :] = grad_kv
        if part:
            grad_q = jnp.concatenate([first_ref[0][rows, :], grad_q], axis=1)
            grad_kv = jnp.concatenate([first_ref[1][rows, :], grad_kv], axis=1)
            total = matmul(grad_q, wq_ref[...], NT) + matmul(grad_kv, wkv_ref[...], NT)
            part_ref[rows, :] = total.astype(jnp.bfloat16)
        for n in range(made):
            rows_out(n, i).start()
        return carry

    lax.fori_loop(0, BLOCKS, finish, 0)
    for n in range(made):
        for i in range(BLOCKS):
            rows_out(n, i).wait()


def attention_backward(part, branch, gatt, q, k, v, lse, wo, wq, wkv, rope, first):
    kv_heads = k.shape[0] // 2
    rows, width = gatt.shape
    bf = jnp.bfloat16
    small = jax.ShapeDtypeStruct((rows, wq.shape[1] // 2), bf)
    outs = (small, small) + ((jax.ShapeDtypeStruct((rows, width), bf),) if part else ())
    ins = (gatt, wo, q, k, v, lse, rope) + ((wq, wkv, *first) if part else ())

    def held(n, array):
        halves = (array.shape[0] // 2,) + array.shape[1:]
        return pltpu.VMEM(halves if 0 < n < 6 else array.shape, array.dtype)

    return pl.pallas_call(
        functools.partial(attention_backward_kernel, part),
        out_shape=outs,
        in_specs=[SMEM] + [HBM] * len(ins),
        out_specs=[HBM] * len(outs),
        scratch_shapes=[held(n, a) for n, a in enumerate(ins)]
        + [pltpu.VMEM(o.shape, bf) for o in outs]
        + [
            pltpu.VMEM((kv_heads, BLOCKS, 2 * BLOCK, LANES), bf),
            pltpu.VMEM((kv_heads, BLOCKS, 2 * BLOCK, LANES), jnp.float32),
            pltpu.VMEM((kv_heads, rows, LANES), jnp.float32),
            pltpu.VMEM((kv_heads, rows, LANES), jnp.float32),
            pltpu.VMEM((2, rows, LANES), jnp.float32),
            pltpu.SemaphoreType.DMA((len(ins),)),
            pltpu.SemaphoreType.DMA((BLOCKS,)),
            pltpu.SemaphoreType.DMA((len(outs), BLOCKS)),
        ],
        compiler_params=pltpu.CompilerParams(vmem_limit_bytes=60 * MIB),
        cost_estimate=CHEAP,
        name="attention_backward",
    )(branch, *ins)


KERNEL_BLOCKS = 16
WIDE = 512
FEW = 16
CUTS = ((0, 512), (512, 1024), (1024, 1536), (1536, 2048))


NN = (((1,), (0,)), ((), ()))


def split_copies(tile, low, high, at, sent, kept, axis, mine, sems, k, begin=True):
    copies = []
    for half, target in ((1 - mine, sent), (mine, kept)):
        part = tile.at[:, :, half] if axis == 0 else tile.at[:, half]
        copy = pltpu.make_async_copy(
            part.at[:, :, :, pl.ds(low, high - low)],
            target.at[:, :, :, pl.ds(at, high - low)],
            sems.at[k + len(copies)],
        )
        if begin:
            copy.start()
        copies.append(copy)
    return copies


def gradient_tile(tile, left, right):
    zs = tile.shape[0] // 2
    tall = left.shape[0] // 2

    def step(i, carry):
        out = matmul(left[pl.ds(pl.multiple_of(i * tall, tall), tall), :], right[...])
        tile[pl.ds(i * zs, zs)] = out.astype(jnp.bfloat16).reshape((zs,) + tile.shape[1:])
        return carry

    lax.fori_loop(0, 2, step, 0)


def ffn_kernel(first, count, aliased, *refs):
    (bits_ref, act_hbm, cot_hbm, act_t_hbm, cot_t_hbm, wg_hbm, wu_hbm, wd_hbm), refs = refs[:8], refs[8:]
    refs = refs[3:] if aliased else refs
    (hidden_hbm, ggate_hbm, gup_hbm, sent_a, kept_a, sent_b, kept_b), refs = refs[:7], refs[7:]
    act, cot, lefts, wg, wu, wd, lines, tiles, in_sems, row_sems, out_sems = refs
    units = pl.ds(first, count)
    tall = act.shape[0] // 2

    def rows_in(i, which):
        rows = pl.ds(pl.multiple_of(i * tall, tall), tall)
        source, target = ((act_hbm, act), (cot_hbm, cot))[which]
        return pltpu.make_async_copy(source.at[rows], target.at[rows], row_sems.at[which, i])

    weights = [start(wg_hbm.at[:, units], wg, in_sems.at[0])]
    rows_in(0, 0).start()
    weights.append(start(wu_hbm.at[:, units], wu, in_sems.at[1]))
    weights.append(start(wd_hbm.at[units], wd, in_sems.at[2]))
    rows_in(0, 1).start()
    rows_in(1, 0).start()
    rows_in(1, 1).start()
    sources = [
        start(cot_t_hbm, lefts.at[0], in_sems.at[3]),
        start(act_t_hbm, lefts.at[1], in_sems.at[4]),
    ]
    weights[0].wait()

    def units_step(i, carry):
        rows = pl.ds(pl.multiple_of(i * tall, tall), tall)
        rows_in(i, 0).wait()
        gate = matmul(act[rows, :], wg[...])

        @pl.when(i == 0)
        def _():
            weights[1].wait()
            weights[2].wait()

        up = matmul(act[rows, :], wu[...])
        rows_in(i, 1).wait()
        grad = matmul(cot[rows, :], wd[...], NT)
        sigmoid = 1.0 / (1.0 + jnp.exp(-gate))
        silu = gate * sigmoid
        lines[0, rows, :] = (silu * up).astype(jnp.bfloat16)
        lines[1, rows, :] = (grad * up * (sigmoid * (1.0 + gate * (1.0 - sigmoid)))).astype(jnp.bfloat16)
        lines[2, rows, :] = (grad * silu).astype(jnp.bfloat16)
        return carry

    lax.fori_loop(0, 2, units_step, 0)
    copies = [
        start(lines.at[0], hidden_hbm.at[:, units], out_sems.at[0]),
        start(lines.at[1], ggate_hbm.at[:, units], out_sems.at[1]),
        start(lines.at[2], gup_hbm.at[:, units], out_sems.at[2]),
    ]
    half = count // 2
    x, y = bits_ref[0], bits_ref[1]
    for copy in sources:
        copy.wait()

    def stores(t, begin):
        if t == 0:
            return split_copies(tiles.at[0], 0, half, count, sent_a, kept_a, 0, x, out_sems, 3, begin) + split_copies(
                tiles.at[0], half, count, count, sent_b, kept_b, 1, y, out_sems, 5, begin
            )
        if t == 1:
            return split_copies(tiles.at[1], 0, count, 0, sent_a, kept_a, 0, x, out_sems, 7, begin)
        return split_copies(tiles.at[2], 0, count, 0, sent_b, kept_b, 1, y, out_sems, 9, begin)

    def tile_step(t, carry):
        gradient_tile(tiles.at[t], lefts.at[jnp.minimum(t, 1)], lines.at[t])
        for one in range(3):

            @pl.when(t == one)
            def _(one=one):
                stores(one, True)

        return carry

    lax.fori_loop(0, 3, tile_step, 0)
    for t in range(3):
        copies += stores(t, False)
    for copy in copies:
        copy.wait()


def ffn_chunk(bits, blocks, act, cot, act_t, cot_t, wg, wu, wd, before, first, count):
    rows, width = act.shape
    bf = jnp.bfloat16
    piece = jax.ShapeDtypeStruct((blocks // 4, 2, width // blocks, count + count // 2), bf)
    units = jax.ShapeDtypeStruct((rows, wg.shape[1]), bf)
    return pl.pallas_call(
        functools.partial(ffn_kernel, first, count, bool(before)),
        out_shape=(units,) * 3 + (piece,) * 4,
        in_specs=[SMEM] + [HBM] * (7 + len(before)),
        out_specs=[HBM] * 7,
        scratch_shapes=[
            pltpu.VMEM((rows, width), bf),
            pltpu.VMEM((rows, width), bf),
            pltpu.VMEM((2, width, rows), bf),
            pltpu.VMEM((width, count), bf),
            pltpu.VMEM((width, count), bf),
            pltpu.VMEM((count, width), bf),
            pltpu.VMEM((3, rows, count), bf),
            pltpu.VMEM((3, blocks // 4, 2, 2, width // blocks, count), bf),
            pltpu.SemaphoreType.DMA((5,)),
            pltpu.SemaphoreType.DMA((2, 2)),
            pltpu.SemaphoreType.DMA((11,)),
        ],
        input_output_aliases={8 + i: i for i in range(len(before))},
        compiler_params=pltpu.CompilerParams(vmem_limit_bytes=60 * MIB),
        cost_estimate=CHEAP,
        name="ffn_chunk",
    )(bits, act, cot, act_t, cot_t, wg, wu, wd, *before)


def gradient_kernel(lefts, parts, bits_ref, *refs):
    def cut(count):
        nonlocal refs
        head, refs = refs[:count], refs[count:]
        return head

    left_hbm, right_hbm, pieces = cut(lefts), cut(len(parts)), cut(4)
    left, right, tiles, (in_sems, out_sems) = cut(lefts), cut(len(parts)), cut(len(parts)), refs
    left_in = [start(a, b, in_sems.at[i]) for i, (a, b) in enumerate(zip(left_hbm, left))]
    right_in = [start(a, b, in_sems.at[lefts + i]) for i, (a, b) in enumerate(zip(right_hbm, right))]
    copies = []
    for i, (which, places) in enumerate(parts):
        if left_in[which] is not None:
            left_in[which].wait()
            left_in[which] = None
        right_in[i].wait()
        gradient_tile(tiles[i], left[which], right[i])
        for low, high, at, first in places:
            sent, kept = pieces[2 * first], pieces[2 * first + 1]
            copies += split_copies(tiles[i], low, high, at, sent, kept, first, bits_ref[first], out_sems, len(copies))
    for copy in copies:
        copy.wait()


def gradient_pieces(bits, blocks, lefts, rights, which, places):
    width, rows = lefts[0].shape
    bf = jnp.bfloat16
    flat = [place for part in places for place in part]
    widths = [sum(high - low for low, high, _, first in flat if first == axis) for axis in (0, 1)]
    pieces = [jax.ShapeDtypeStruct((blocks // 4, 2, width // blocks, w), bf) for w in widths for _ in range(2)]
    return pl.pallas_call(
        functools.partial(gradient_kernel, len(lefts), tuple(zip(which, places))),
        out_shape=tuple(pieces),
        in_specs=[SMEM] + [HBM] * (len(lefts) + len(rights)),
        out_specs=[HBM] * 4,
        scratch_shapes=[pltpu.VMEM(a.shape, bf) for a in (*lefts, *rights)]
        + [pltpu.VMEM((blocks // 4, 2, 2, width // blocks, r.shape[1]), bf) for r in rights]
        + [pltpu.SemaphoreType.DMA((len(lefts) + len(rights),)), pltpu.SemaphoreType.DMA((2 * len(flat),))],
        compiler_params=pltpu.CompilerParams(vmem_limit_bytes=60 * MIB),
        cost_estimate=CHEAP,
        name="gradient_pieces",
    )(bits, *lefts, *rights)


def projection_kernel(dims, count, *refs):
    left_hbm, right_hbm, out_hbm, refs = refs[:count], refs[count : 2 * count], refs[2 * count], refs[2 * count + 1 :]
    left, right, (out, left_sems, right_sems, out_sems) = refs[:count], refs[count : 2 * count], refs[2 * count :]
    turned = dims is NT
    rows, width = out.shape
    tall = rows // 2

    def columns(ref, n):
        cut = pl.ds(pl.multiple_of(n * WIDE, WIDE), WIDE)
        return ref.at[cut, :] if turned else ref.at[:, cut]

    def right_in(p, n):
        return pltpu.make_async_copy(columns(right_hbm[p], n), columns(right[p], n), right_sems.at[p, n])

    def left_in(p, i):
        cut = pl.ds(pl.multiple_of(i * tall, tall), tall)
        return pltpu.make_async_copy(left_hbm[p].at[cut], left[p].at[cut], left_sems.at[p, i])

    def out_copy(n):
        wide = pl.ds(pl.multiple_of(n * WIDE, WIDE), WIDE)
        return pltpu.make_async_copy(out.at[:, wide], out_hbm.at[:, wide], out_sems.at[n])

    for p in range(count):
        right_in(p, 0).start()
        left_in(p, 0).start()
    for p in range(count):
        left_in(p, 1).start()
    for n in range(1, width // WIDE):
        for p in range(count):
            right_in(p, n).start()

    def step(j, carry):
        n, i = j // 2, j % 2

        @pl.when(i == 0)
        def _():
            for p in range(count):
                right_in(p, n).wait()

        @pl.when(n == 0)
        def _():
            for p in range(count):
                left_in(p, i).wait()

        cut = pl.ds(pl.multiple_of(i * tall, tall), tall)
        total = sum(matmul(left[p][cut, :], columns(right[p], n)[...], dims) for p in range(count))
        out[cut, pl.ds(pl.multiple_of(n * WIDE, WIDE), WIDE)] = total.astype(jnp.bfloat16)

        @pl.when(i == 1)
        def _():
            out_copy(n).start()

        return carry

    lax.fori_loop(0, 2 * width // WIDE, step, 0)
    for n in range(width // WIDE):
        out_copy(n).wait()


def projection(lefts, rights, dims):
    rows = lefts[0].shape[0]
    width = rights[0].shape[0 if dims is NT else 1]
    bf, count = jnp.bfloat16, len(lefts)
    return pl.pallas_call(
        functools.partial(projection_kernel, dims, count),
        out_shape=jax.ShapeDtypeStruct((rows, width), bf),
        in_specs=[HBM] * (2 * count),
        out_specs=HBM,
        scratch_shapes=[pltpu.VMEM(a.shape, bf) for a in (*lefts, *rights)]
        + [
            pltpu.VMEM((rows, width), bf),
            pltpu.SemaphoreType.DMA((count, 2)),
            pltpu.SemaphoreType.DMA((count, width // WIDE)),
            pltpu.SemaphoreType.DMA((width // WIDE,)),
        ],
        compiler_params=pltpu.CompilerParams(vmem_limit_bytes=60 * MIB),
        cost_estimate=CHEAP,
        name="projection",
    )(*lefts, *rights)


def add_two(one, two):
    return one.astype(jnp.float32) + two.astype(jnp.float32)


def second_steps(bits_ref, ins_hbm, ins, outs_hbm, outs):
    steps = []
    for z in range(outs[0].shape[0]):

        def compute(z=z):
            for i in range(2):
                kept, got, send, keep, mine = *ins[2 * i : 2 * i + 2], *outs[2 * i : 2 * i + 2], bits_ref[1 - i]
                send[z] = kept[z, 1 - mine] + got[z, 1 - mine]
                keep[z] = kept[z, mine] + got[z, mine]

        steps.append((
            [(a.at[z], b.at[z]) for a, b in zip(ins_hbm, ins)],
            compute,
            [(a.at[z], b.at[z]) for a, b in zip(outs, outs_hbm)],
        ))
    return steps


def third_steps(bits_ref, ins_hbm, ins, outs_hbm, outs):
    low = bits_ref[2] & 1
    steps = []
    for half, out, out_hbm in zip((1 - low, low), outs, outs_hbm):
        for high in range(2):
            block = 2 * high + half

            def compute(block=block, out=out, high=high):
                width = ins[0].shape[-1]
                out[high, :, :width] = ins[0][block] + ins[1][block]
                out[high, :, width:] = ins[2][block] + ins[3][block]

            steps.append((
                [(a.at[block], b.at[block]) for a, b in zip(ins_hbm, ins)], compute, [(out.at[high], out_hbm.at[high])]
            ))
    return steps


def fourth_steps(bits_ref, ins_hbm, ins, outs_hbm, outs):
    high = bits_ref[2] >> 1
    steps = []
    for block, out, out_hbm in zip((1 - high, high), outs, outs_hbm):

        def compute(block=block, out=out):
            for i in range(0, len(ins), 2):
                width = ins[i].shape[-1]
                out[:, i // 2 * width : (i // 2 + 1) * width] = ins[i][block] + ins[i + 1][block]

        steps.append((
            [(a.at[block], b.at[block]) for a, b in zip(ins_hbm, ins)], compute, [(out, out_hbm)]
        ))
    return steps


def sums_kernel(jobs, bits_ref, *refs):
    count, made = sum(j[1] for j in jobs), sum(j[2] for j in jobs)
    ins_hbm, outs_hbm, refs = refs[:count], refs[count : count + made], refs[count + made :]
    ins, outs, (in_sems, out_sems) = refs[:count], refs[count : count + made], refs[count + made :]
    steps = []
    for build, n, m in jobs:
        steps += build(bits_ref, ins_hbm[:n], ins[:n], outs_hbm[:m], outs[:m])
        ins_hbm, ins, outs_hbm, outs = ins_hbm[n:], ins[n:], outs_hbm[m:], outs[m:]
    stream(steps, in_sems, out_sems)


def sums(bits, second=None, third=None, fourth=None, cost=None):
    jobs, ins, outs = [], [], []
    if second is not None:
        made = [a.shape[:1] + a.shape[2:] for a in second]
        jobs.append((second_steps, 4, 4))
        ins, outs = ins + list(second), outs + made
    if third is not None:
        made = [(2, third[0].shape[1], third[0].shape[2] + third[2].shape[2])] * 2
        jobs.append((third_steps, 4, 2))
        ins, outs = ins + list(third), outs + made
    if fourth is not None:
        made = [(fourth[0].shape[1], sum(a.shape[2] for a in fourth[::2]))] * 2
        jobs.append((fourth_steps, len(fourth), 2))
        ins, outs = ins + list(fourth), outs + made
    bf = jnp.bfloat16
    results = pl.pallas_call(
        functools.partial(sums_kernel, tuple(jobs)),
        out_shape=tuple(jax.ShapeDtypeStruct(o, bf) for o in outs),
        in_specs=[SMEM] + [HBM] * len(ins),
        out_specs=[HBM] * len(outs),
        scratch_shapes=[pltpu.VMEM(a.shape, bf) for a in ins]
        + [pltpu.VMEM(o, bf) for o in outs]
        + [pltpu.SemaphoreType.DMA((4 * len(ins),)), pltpu.SemaphoreType.DMA((4 * len(outs),))],
        compiler_params=pltpu.CompilerParams(vmem_limit_bytes=60 * MIB),
        cost_estimate=cost or CHEAP,
        name="sums",
    )(bits, *ins)
    split = []
    for _, _, m in jobs:
        split.append(results[:m])
        results = results[m:]
    return split[0] if len(split) == 1 else split


def over_dp(array, flip):
    size = lax.axis_size("dp")
    return lax.ppermute(array, "dp", [(i, i ^ flip) for i in range(size)])


def after(arrays, *needed):
    return lax.optimization_barrier((arrays, needed))[0]


def first_stage(pieces):
    sent_a, kept_a, sent_b, kept_b = pieces
    return (kept_a, over_dp(sent_a, 1), kept_b, over_dp(sent_b, 2))


def second_stage(sent_a, kept_a, sent_b, kept_b):
    return (kept_a, over_dp(sent_a, 2), kept_b, over_dp(sent_b, 1))


def third_stage(send, keep):
    return (keep, over_dp(send, 4))


def fourth_stage(send, keep):
    return (keep, over_dp(send, 8))


def ffn_sums_kernel(*refs):
    ins, (gate_ref, up_ref, down_ref) = refs[:-3], refs[-3:]
    chunks = [
        (kept, got, at)
        for kept, got in zip(ins[0::2], ins[1::2])
        for at in range(0, kept.shape[-1], 3 * (CUTS[0][1] - CUTS[0][0]))
    ]
    for (low, high), (kept, got, at) in zip(CUTS, chunks):
        count, half = high - low, (high - low) // 2
        total = add_two(kept[:, at : at + 3 * count], got[:, at : at + 3 * count])
        gate_ref[:, low:high] = total[:, :count]
        down_ref[:, low : low + half] = total[:, count : count + half]
        up_ref[:, low:high] = total[:, count + half : 2 * count + half]
        down_ref[:, low + half : high] = total[:, 2 * count + half :]


def ffn_sums(pieces):
    rows, units = pieces[0].shape[0], CUTS[-1][1]
    wide = jax.ShapeDtypeStruct((rows, units), jnp.float32)
    return pl.pallas_call(
        ffn_sums_kernel,
        out_shape=(wide,) * 3,
        in_specs=[VMEM] * len(pieces),
        out_specs=[VMEM] * 3,
        compiler_params=pltpu.CompilerParams(vmem_limit_bytes=60 * MIB),
        cost_estimate=CHEAP,
        name="ffn_sums",
    )(*pieces)


def joined(pieces):
    sent_a, kept_a, sent_b, kept_b = pieces
    first, second = lax.axis_index("dp") & 1, lax.axis_index("dp") >> 1 & 1
    out = []
    for sent, kept, axis, mine in ((sent_a, kept_a, 2, first), (sent_b, kept_b, 1, second)):
        low = jnp.where(mine == 0, kept, sent)
        high = jnp.where(mine == 0, sent, kept)
        out.append(jnp.stack([low, high], axis=axis).reshape(-1, sent.shape[-1]))
    return out


def scatter_sum(grads):
    size = lax.axis_size("dp")
    bits = size.bit_length() - 1
    me = lax.axis_index("dp")
    rows, width = grads.shape
    work = grads.reshape((2,) * bits + (rows // size, width))
    for bit in range(bits):
        axis = bits - 1 - bit
        mine = (me >> bit) & 1
        sent = lax.dynamic_index_in_dim(work, 1 - mine, axis, keepdims=False)
        kept = lax.dynamic_index_in_dim(work, mine, axis, keepdims=False)
        work = kept.astype(jnp.float32) + over_dp(sent, 1 << bit).astype(jnp.float32)
        work = work.astype(grads.dtype)
    return work.astype(jnp.float32)


def attention_sums_kernel(kv_half, kept_a, got_a, kept_b, got_b, query_ref, key_ref, value_ref, out_ref):
    half = query_ref.shape[1] // 2
    first, second = add_two(kept_a[...], got_a[...]), add_two(kept_b[...], got_b[...])
    out_ref[:, :half] = first[:, :half]
    out_ref[:, half:] = first[:, 2 * half : 3 * half]
    query_ref[:, :half] = first[:, half : 2 * half]
    query_ref[:, half:] = second[:, :half]
    first, second = first[:, 3 * half :], second[:, half:]
    key_ref[...] = jnp.concatenate([first[:, :kv_half], second[:, :kv_half]], axis=1)
    value_ref[...] = jnp.concatenate([first[:, kv_half:], second[:, kv_half:]], axis=1)


def attention_sums(kept_a, got_a, kept_b, got_b, kv_half):
    rows, heads = kept_b.shape
    shapes = [(rows, heads), (rows, heads // 2), (rows, heads // 2), (rows, heads)]
    *others, out = pl.pallas_call(
        functools.partial(attention_sums_kernel, kv_half),
        out_shape=tuple(jax.ShapeDtypeStruct(shape, jnp.float32) for shape in shapes),
        in_specs=[VMEM] * 4,
        out_specs=[VMEM] * 4,
        compiler_params=pltpu.CompilerParams(vmem_limit_bytes=60 * MIB),
        cost_estimate=CHEAP,
        name="attention_sums",
    )(kept_a, got_a, kept_b, got_b)
    return *others, out.T


def gain_stage(work, bit):
    mine = (lax.axis_index("dp") >> bit) & 1
    axis = work.ndim - 2
    sent = lax.dynamic_index_in_dim(work, 1 - mine, axis, keepdims=False)
    return lax.dynamic_index_in_dim(work, mine, axis, keepdims=False), over_dp(sent, 1 << bit)


def to_other_core(array):
    return lax.ppermute(array, "tensor", [(0, 1), (1, 0)])


def norm_grad(value, grad, gain):
    scale = lax.rsqrt(jnp.mean(value * value, axis=-1, keepdims=True) + epsilon)
    scaled = grad * gain
    back = scale * scaled - value * scale**3 * jnp.mean(scaled * value, axis=-1, keepdims=True)
    return back, grad * value * scale


def stream(steps, in_sems, out_sems):
    waits, count = [], 0
    for loads, _, _ in steps:
        waits.append([start(*pair, in_sems.at[count + i]) for i, pair in enumerate(loads)])
        count += len(loads)
    copies = []
    for wait, (_, compute, stores) in zip(waits, steps):
        for copy in wait:
            copy.wait()
        compute()
        for pair in stores:
            copies.append(start(*pair, out_sems.at[len(copies)]))
    for copy in copies:
        copy.wait()


def row_kernel(function, turned, vectors, count, outs, *refs):
    def cut(n):
        nonlocal refs
        head, refs = refs[:n], refs[n:]
        return head

    ins_hbm, vector, outs_hbm = cut(count), cut(1), cut(outs)
    sums = cut(vectors)
    ins, held, partial, (in_sems, out_sems) = cut(count), cut(outs), cut(vectors), refs
    gain = vector[0][...]
    direct = [ref for ref, t in zip(held, turned) if not t]
    for ref in partial:
        ref[...] = jnp.zeros_like(ref)
    steps = []
    for i in range(ins[0].shape[0] // BLOCK):
        rows = pl.ds(i * BLOCK, BLOCK)
        places = [(slice(None), rows) if t else (rows, slice(None)) for t in turned]

        def compute(i=i, rows=rows, places=places):
            def step(j, carry):
                few = pl.ds(pl.multiple_of(i * BLOCK + j * FEW, FEW), FEW)
                results = function(*(ref[few, :].astype(jnp.float32) for ref in ins), gain)
                for ref, result in zip(direct, results):
                    ref[few, :] = result.astype(jnp.bfloat16)
                for ref, result in zip(partial, results[len(direct) :]):
                    ref[...] += jnp.sum(result.reshape(FEW // 8, 8, -1), axis=0)
                return carry

            lax.fori_loop(0, BLOCK // FEW, step, 0, unroll=2)
            for n, t in enumerate(turned):
                if t:
                    held[n][places[n]] = held[n - 1][rows, :].astype(jnp.float32).T.astype(jnp.bfloat16)

        steps.append((
            [(a.at[rows], b.at[rows]) for a, b in zip(ins_hbm, ins)],
            compute,
            [(a.at[place], b.at[place]) for a, b, place in zip(held, outs_hbm, places)],
        ))
    stream(steps, in_sems, out_sems)
    for ref, part in zip(sums, partial):
        ref[...] = jnp.sum(part[...], axis=0, keepdims=True)


def row_call(function, name, ins, vector, turned, vectors=0):
    rows, width = ins[0].shape
    bf, blocks = jnp.bfloat16, rows // BLOCK
    outs = [jax.ShapeDtypeStruct((width, rows) if t else (rows, width), bf) for t in turned]
    return pl.pallas_call(
        functools.partial(row_kernel, function, turned, vectors, len(ins), len(outs)),
        out_shape=tuple(outs + [jax.ShapeDtypeStruct((1, width), jnp.float32)] * vectors),
        in_specs=[HBM] * len(ins) + [VMEM],
        out_specs=[HBM] * len(outs) + [VMEM] * vectors,
        scratch_shapes=[pltpu.VMEM(a.shape, bf) for a in (*ins, *outs)]
        + [pltpu.VMEM((8, width), jnp.float32)] * vectors
        + [pltpu.SemaphoreType.DMA((len(ins) * blocks,)), pltpu.SemaphoreType.DMA((len(outs) * blocks,))],
        compiler_params=pltpu.CompilerParams(vmem_limit_bytes=60 * MIB),
        cost_estimate=CHEAP,
        name=name,
    )(*ins, vector)


def norm_rows(x, own, got, gain):
    hidden = x + (own + got)
    norm = lax.rsqrt(jnp.mean(hidden * hidden, axis=-1, keepdims=True) + epsilon)
    act = hidden * norm * gain
    return hidden, act


def middle_rows(hidden, own, got, cot, gain):
    back, gain_grad = norm_grad(hidden, own + got, gain)
    total = cot + back
    return total, gain_grad


def output_rows(hidden, own, got, gain):
    return (hidden + (own + got),)


def input_rows(x, gatt, own, got, gain):
    back, gain_grad = norm_grad(x, own + got, gain)
    return gatt + back, gain_grad


def attention_grads(total, half, kv_half):
    names = (("out", half), ("query", half), ("out", half), ("key", kv_half), ("value", kv_half))
    names += (("query", half), ("key", kv_half), ("value", kv_half))
    found, at = {}, 0
    for name, count in names:
        found.setdefault(name, []).append(total[:, at : at + count])
        at += count
    found = {name: jnp.concatenate(parts, axis=1) for name, parts in found.items()}
    return found["query"], found["key"], found["value"], found["out"].T


def plain(names, chunk, backward):
    v = dict(names)
    layer_input, hidden, bits, blocks, size = (v[n] for n in ("layer_input", "hidden", "bits", "blocks", "size"))
    rows, width = layer_input.shape
    half, kv_half, heads = v["half"], v["kv_half"], v["heads"]
    pieces = []
    for i in range(len(CUTS)):
        units, piece = chunk(i, whole=True)
        pieces.append(piece)
    hidden_units, grad_gate_lin, grad_up_lin = units
    two_own = projection([grad_gate_lin, grad_up_lin], [v["w_gate"], v["w_up"]], NT)
    ffn_own = projection([hidden_units], [v["w_down"]], NN)
    grad_attention, grad_attention_t, grad_ffn_gain = row_call(
        middle_rows, "middle", [hidden, two_own, to_other_core(two_own), v["cotangent"]], v["gain_two"], [0, 1], 1
    )
    (output,) = row_call(output_rows, "output", [hidden, ffn_own, to_other_core(ffn_own)], v["gain_two"], [0])
    back_one = backward(0, gatt=grad_attention)
    pieces.append(gradient_pieces(
        bits, blocks, [grad_attention_t, v["act_one_t"]], [v["mixed"], *back_one], [0, 1, 1],
        [((0, half, 0, 0), (half, heads, 0, 1)), ((0, half, half, 0),), ((0, half, half, 1),)],
    ))
    *back_two, one_own = backward(1, *back_one, gatt=grad_attention)
    pieces.append(gradient_pieces(
        bits, blocks, [v["act_one_t"]], back_two, [0, 0], [((0, half, 0, 0),), ((0, half, 0, 1),)]
    ))
    grad_input, grad_attn_gain = row_call(
        input_rows, "input", [layer_input, grad_attention, one_own, to_other_core(one_own)],
        v["attn_gain"].reshape(1, width), [0], 1,
    )
    gains = jnp.concatenate([grad_attn_gain, grad_ffn_gain]).reshape(2, size, width // size)
    gains = scatter_sum(gains.transpose(1, 0, 2).reshape(size, 2 * width // size))[0]
    total = scatter_sum(jnp.concatenate([p for piece in pieces for p in joined(piece)], axis=1))
    gates, ups, downs = [], [], []
    for low, high in CUTS:
        count = high - low
        parts = jnp.split(total[:, 3 * low : 3 * high], [count, count * 3 // 2, count * 5 // 2], axis=1)
        for found, part in zip((gates, downs, ups, downs), parts):
            found.append(part)
    return (
        output,
        grad_input,
        gains[: width // size],
        *attention_grads(total[:, 3 * CUTS[-1][1] :], half, kv_half),
        gains[width // size :],
        jnp.concatenate(gates, axis=1),
        jnp.concatenate(ups, axis=1),
        jnp.concatenate(downs, axis=1).T,
    )


def per_device(
    layer_input,
    branch_point,
    attn_gain,
    w_query,
    w_key,
    w_value,
    w_out,
    ffn_gain,
    w_gate,
    w_up,
    w_down,
    cotangent,
):
    rows, width = layer_input.shape
    size = lax.axis_size("dp")
    by_kernel = size == KERNEL_BLOCKS
    blocks = KERNEL_BLOCKS
    me = lax.axis_index("dp")
    bits = jnp.stack([me & 1, me >> 1 & 1, me >> 2 & 3]).astype(jnp.int32)
    rope = rope_tables()
    act_one_t, queries, keys, values, mixed, log_sums, attn_own = attention_forward(
        branch_point, layer_input, attn_gain, w_query, w_key, w_value, w_out, rope
    )
    attn_got = to_other_core(attn_own)
    kv_half = w_key.shape[1] // 2
    w_key_value = jnp.concatenate(
        [w_key[:, :kv_half], w_value[:, :kv_half], w_key[:, kv_half:], w_value[:, kv_half:]], axis=1
    )
    cot_t = cotangent.T
    gain_two = ffn_gain.reshape(1, width)
    hidden, act_two, act_two_t = row_call(
        norm_rows, "norm_two", [layer_input, attn_own, attn_got], after(gain_two, cot_t, w_key_value), [0, 0, 1]
    )
    heads, kv = mixed.shape[1], w_key.shape[1]
    half = heads // 2
    units = ()

    def chunk(i, *needed, whole=False):
        nonlocal units
        low, high = CUTS[i]
        *units, sent_a, kept_a, sent_b, kept_b = ffn_chunk(
            bits, blocks, after(act_two, *needed), cotangent, act_two_t, cot_t,
            w_gate, w_up, w_down, units, low, high - low,
        )
        piece = (sent_a, kept_a, sent_b, kept_b)
        return (units, piece) if whole else piece

    def backward(part, *needed, gatt=None):
        return attention_backward(
            part, branch_point, after(grad_attention if gatt is None else gatt, *needed), queries, keys, values, log_sums,
            w_out, w_query, w_key_value, rope, list(needed[:2]) if part else [],
        )

    if not by_kernel:
        return plain(locals(), chunk, backward)
    pieces = [chunk(0)]
    one = [first_stage(pieces[0])]
    pieces.append(chunk(1))
    one.append(first_stage(pieces[1]))
    pieces.append(chunk(2, pieces[1]))
    pieces[2], one[0] = after((pieces[2], one[0]))
    joint = sums(bits, second=one[0])
    two = [second_stage(*joint)]
    pieces.append(chunk(3, joint))
    *units, pieces[3], one[1], two[0] = after((*units, pieces[3], one[1], two[0]))
    joint = sums(bits, second=one[1], third=two[0])
    two.append(second_stage(*joint[0]))
    three = [third_stage(*joint[1])]
    one.append(first_stage(after(pieces[2], units)))
    hidden_units, grad_gate_lin, grad_up_lin = units
    two_own = projection(after([grad_gate_lin, grad_up_lin], joint), [w_gate, w_up], NT)
    two_own, three[0] = after((two_own, three[0]))
    two_got = to_other_core(two_own)
    ffn_own = projection([after(hidden_units, two_own)], [w_down], NN)
    ffn_own, one[2], two[1] = after((ffn_own, one[2], two[1]))
    joint = sums(bits, second=one[2], third=two[1], cost=LONG)
    two.append(second_stage(*joint[0]))
    three.append(third_stage(*joint[1]))
    one.append(first_stage(after(pieces[3], ffn_own)))
    grad_attention, grad_attention_t, grad_ffn_gain = row_call(
        middle_rows, "middle", [hidden, two_own, two_got, after(cotangent, joint)], gain_two, [0, 1], 1
    )
    grad_attention, three[0], three[1] = after((grad_attention, three[0], three[1]))
    joint = sums(bits, fourth=(*three[0], *three[1]))
    four = [fourth_stage(*joint)]
    back_one = backward(0, grad_attention, joint)
    back_one, two[2], one[3], four[0] = after((back_one, two[2], one[3], four[0]))
    joint = sums(bits, second=one[3], third=two[2])
    two.append(second_stage(*joint[0]))
    three.append(third_stage(*joint[1]))
    early = gradient_pieces(
        bits, blocks, [after(grad_attention_t, joint), act_one_t], [mixed, *back_one], [0, 1, 1],
        [((0, half, 0, 0), (half, heads, 0, 1)), ((0, half, half, 0),), ((0, half, half, 1),)],
    )
    early, two[3], three[2] = after((early, two[3], three[2]))
    joint = sums(bits, third=two[3], fourth=three[2])
    three.append(third_stage(*joint[0]))
    four.append(fourth_stage(*joint[1]))
    early_one = first_stage(early)
    ffn_got = to_other_core(after(ffn_own, early))
    *back_two, one_own = backward(1, *back_one, early, joint)
    back_two, one_own, early_one, three[3], four[1], ffn_got = after(
        (back_two, one_own, early_one, three[3], four[1], ffn_got)
    )
    one_got = to_other_core(one_own)
    joint = sums(bits, second=early_one, fourth=three[3])
    early_two = second_stage(*joint[0])
    four.append(fourth_stage(*joint[1]))
    late = gradient_pieces(
        bits, blocks, [after(act_one_t, joint)], back_two, [0, 0], [((0, half, 0, 0),), ((0, half, 0, 1),)]
    )
    late, one_got = after((late, one_got))
    late_one = first_stage(late)
    (output,) = row_call(output_rows, "output", [hidden, after(ffn_own, late), ffn_got], gain_two, [0])
    output, early_two, four[2] = after((output, early_two, four[2]))
    joint = sums(bits, third=early_two)
    early_three = third_stage(*joint)
    grad_input, grad_attn_gain = row_call(
        input_rows, "input", [layer_input, after(grad_attention, joint), one_own, one_got],
        attn_gain.reshape(1, width), [0], 1,
    )
    grad_input, late_one, early_three = after((grad_input, late_one, early_three))
    joint = sums(bits, second=late_one, fourth=early_three)
    late_two = second_stage(*joint[0])
    early_four = fourth_stage(*joint[1])
    gains = jnp.concatenate([grad_attn_gain, grad_ffn_gain]).reshape(2, size, width // size)
    gains = gains.transpose(1, 0, 2).reshape(2, 2, 2, 2, 2 * width // size)
    gains = gain_stage(after(gains, joint), 0)
    grad_gate, grad_up, grad_down = ffn_sums(after([p for piece in four for p in piece], joint))
    grad_down, late_two, gains = after((grad_down, late_two, gains))
    joint = sums(bits, third=late_two)
    late_three = third_stage(*joint)
    gains = gain_stage(after(gains[0] + gains[1], joint), 1)
    late_three, gains, early_four = after((late_three, gains, early_four))
    joint = sums(bits, fourth=late_three)
    late_four = fourth_stage(*joint)
    gains = gains[0] + gains[1]
    gains = after(gains, joint).reshape(4, gains.shape[-1])
    z = me >> 2
    others = [over_dp(lax.dynamic_index_in_dim(gains, z ^ d, 0, keepdims=False), 4 * d) for d in (1, 2, 3)]
    gains = lax.dynamic_index_in_dim(gains, z, 0, keepdims=False) + sum(others)
    return (
        output,
        grad_input,
        gains[: width // size],
        *attention_sums(*early_four, *late_four, kv_half),
        gains[width // size :],
        grad_gate,
        grad_up,
        grad_down.T,
    )


def solution(mesh):
    placed = (
        P("dp", None),
        P("dp", None),
        P(),
        P(None, "tensor"),
        P(None, "tensor"),
        P(None, "tensor"),
        P("tensor", None),
        P(),
        P(None, "tensor"),
        P(None, "tensor"),
        P("tensor", None),
        P("dp", None),
    )
    return jax.shard_map(
        per_device,
        mesh=mesh,
        in_specs=placed,
        out_specs=(
            P("dp", None),
            P("dp", None),
            P("dp"),
            P("dp", "tensor"),
            P("dp", "tensor"),
            P("dp", "tensor"),
            P("tensor", "dp"),
            P("dp"),
            P("dp", "tensor"),
            P("dp", "tensor"),
            P("tensor", "dp"),
        ),
        check_vma=False,
    )
```

```python
import functools

import jax
import jax.numpy as jnp
import numpy as np
from jax import lax
from jax.experimental import pallas as pl
from jax.experimental.pallas import tpu as pltpu
from jax.sharding import PartitionSpec as P

HEAD_DIM = 96
PROMPT = 1024
CONT_LEN = 128
CONT = 2
GROUP_TOK = 1280
BLOCK = 256
BLOCKS = GROUP_TOK // BLOCK
LANES = 128
MIB = 1 << 20
VMEM_LIMIT = 64 * MIB
CHEAP = pl.CostEstimate(flops=10**6, bytes_accessed=10**5, transcendentals=0)
epsilon = 1e-05
rope_base = 100000.0
LOG2E = 1.4426950408889634
SCORE_SCALE = HEAD_DIM ** (-0.5)
NT = (((1,), (1,)), ((), ()))
TN = (((0,), (0,)), ((), ()))

LONG = pl.CostEstimate(flops=10**11, bytes_accessed=10**5, transcendentals=0)


def matmul(left, right, dims=(((1,), (0,)), ((), ()))):
    return lax.dot_general(left, right, dims, preferred_element_type=jnp.float32)


HBM = pl.BlockSpec(memory_space=pl.ANY)
SMEM = pl.BlockSpec(memory_space=pltpu.SMEM)
VMEM = pl.BlockSpec(memory_space=pltpu.VMEM)


def start(source, target, sem):
    copy = pltpu.make_async_copy(source, target, sem)
    copy.start()
    return copy


def rows_of(blocks, width):
    return (blocks // 4, 2, 2, None, width)


def rope_tables():
    half = HEAD_DIM // 2
    frequency = rope_base ** (-np.arange(half, dtype=np.float64) * 2.0 / HEAD_DIM)
    angles = np.arange(PROMPT + CONT_LEN, dtype=np.float64)[:, None] * frequency[None, :]
    pad = np.zeros((angles.shape[0], LANES - HEAD_DIM))
    cosine = np.concatenate([np.cos(angles), np.cos(angles), pad], axis=1)
    sine = np.concatenate([-np.sin(angles), np.sin(angles), pad], axis=1)
    return jnp.asarray(np.stack([cosine, sine]), jnp.float32)


def place_rope(branch_ref, table_ref, rope_ref):
    rope_ref[:, :PROMPT, :] = table_ref[:, :PROMPT, :]
    for c in range(CONT):
        rows = pl.ds(PROMPT + c * CONT_LEN, CONT_LEN)
        for i in range(2):
            rope_ref[i, rows, :] = table_ref[i, pl.ds(branch_ref[0, c], CONT_LEN), :]


def lane_ids(shape):
    return lax.broadcasted_iota(jnp.int32, shape, 1)


def swap_halves(head):
    half = HEAD_DIM // 2
    return jnp.where(
        lane_ids(head.shape) < half, pltpu.roll(head, LANES - half, 1), pltpu.roll(head, half, 1)
    )


def take_head(full, h):
    first = h * HEAD_DIM
    start, shift = first // LANES * LANES, first % LANES
    width = LANES if shift + HEAD_DIM <= LANES else 2 * LANES
    part = full[:, start : start + width]
    return part[:, :LANES] if shift == 0 else pltpu.roll(part, width - shift, 1)[:, :LANES]


def join_heads(heads):
    lanes = lane_ids(heads[0].shape)
    out = []
    for i in range(0, len(heads), 4):
        one, two, three = (pltpu.roll(heads[i + j], LANES - 32 * j, 1) for j in (1, 2, 3))
        out.append(jnp.where(lanes < 96, heads[i], one))
        out.append(jnp.where(lanes < 64, one, two))
        out.append(jnp.where(lanes < 32, two, three))
    return jnp.concatenate(out, axis=1)


def own_mask(shape, query_axis, block):
    query = lax.broadcasted_iota(jnp.int32, shape, query_axis) & (BLOCK - 1)
    key = lax.broadcasted_iota(jnp.int32, shape, 1 - query_axis)
    mask = key <= query
    if block * BLOCK >= PROMPT:
        mask = mask & ((key // CONT_LEN) == (query // CONT_LEN))
    return mask


def reach_mask(shape, query_axis, branch_ref):
    query = lax.broadcasted_iota(jnp.int32, shape, query_axis) & (BLOCK - 1)
    key = lax.broadcasted_iota(jnp.int32, shape, 1 - query_axis) + PROMPT // 2
    return key < jnp.where(query < CONT_LEN, branch_ref[0, 0], branch_ref[0, 1])


def attention_forward_kernel(
    branch_ref, gain_ref, *refs,
):
    ins_hbm, outs_hbm, ins, outs, (o_ref, rope_ref, in_sems, x_sems, out_sems, row_sems) = (
        refs[:6], refs[6:13], refs[13:19], refs[19:26], refs[26:],
    )
    x_ref, wq_ref, wk_ref, wv_ref, wo_ref, table_ref = ins
    act_t_ref, q_ref, k_ref, v_ref, mixed_ref, lse_ref, part_ref = outs
    kv_heads = k_ref.shape[0]
    group = 2 * BLOCK

    def x_in(i):
        rows = pl.ds(pl.multiple_of(i * BLOCK, BLOCK), BLOCK)
        return pltpu.make_async_copy(ins_hbm[0].at[rows], x_ref.at[rows], x_sems.at[i])

    def rows_out(n, which, i):
        rows = pl.ds(pl.multiple_of(i * BLOCK, BLOCK), BLOCK)
        return pltpu.make_async_copy(outs[n].at[rows], outs_hbm[n].at[rows], row_sems.at[which, i])

    x_in(0).start()
    loads = {n: start(ins_hbm[n], ins[n], in_sems.at[n]) for n in (1, 5, 2, 3)}
    for i in range(1, BLOCKS):
        x_in(i).start()
    loads[4] = start(ins_hbm[4], wo_ref, in_sems.at[4])
    for n in (5, 1, 2, 3):
        loads[n].wait()
    place_rope(branch_ref, table_ref, rope_ref)

    def project(i, carry):
        rows = pl.ds(pl.multiple_of(i * BLOCK, BLOCK), BLOCK)
        x_in(i).wait()
        x = x_ref[rows, :].astype(jnp.float32)
        norm = lax.rsqrt(jnp.mean(x * x, axis=-1, keepdims=True) + epsilon)
        act = x * norm * gain_ref[...][None, :]
        act_t_ref[:, rows] = act.T.astype(jnp.bfloat16)
        act = act.astype(jnp.bfloat16)
        cosine, sine = rope_ref[0, rows, :], rope_ref[1, rows, :]
        full = matmul(act, wq_ref[...])
        for h in range(2 * kv_heads):
            head = take_head(full, h)
            rotated = head * cosine + swap_halves(head) * sine
            q_ref[h // 2, i, pl.ds(h % 2 * BLOCK, BLOCK), :] = rotated.astype(jnp.bfloat16)
        full = matmul(act, wk_ref[...])
        for h in range(kv_heads):
            head = take_head(full, h)
            rotated = head * cosine + swap_halves(head) * sine
            k_ref[h, rows, :] = rotated.astype(jnp.bfloat16)
        full = matmul(act, wv_ref[...])
        lanes = lane_ids((BLOCK, LANES))
        for h in range(kv_heads):
            head = jnp.where(lanes < HEAD_DIM, take_head(full, h), 0.0)
            v_ref[h, rows, :] = jnp.where(lanes == HEAD_DIM, 1.0, head).astype(jnp.bfloat16)
        return carry

    lax.fori_loop(0, BLOCKS, project, 0)
    stores = [start(outs[n], outs_hbm[n], out_sems.at[n]) for n in range(4)]
    factor = SCORE_SCALE * LOG2E

    def attend(h, carry):
        for i in range(BLOCKS):
            query = q_ref[h, i]
            before = i * BLOCK
            own = matmul(query, k_ref[h, before : before + BLOCK], NT)
            own = jnp.where(own_mask(own.shape, 0, i), own, -1e30)
            largest = jnp.max(own, axis=-1, keepdims=True)
            spans = []
            if i > 0:
                cuts = [0, before] if before < PROMPT else [0, PROMPT // 2, PROMPT]
                for low, high in zip(cuts[:-1], cuts[1:]):
                    scores = matmul(query, k_ref[h, low:high], NT)
                    if before >= PROMPT and low > 0:
                        scores = jnp.where(reach_mask(scores.shape, 0, branch_ref), scores, -1e30)
                    largest = jnp.maximum(largest, jnp.max(scores, axis=-1, keepdims=True))
                    spans.append((low, high, scores))
            shift = largest * factor
            probs = jnp.exp2(own * factor - shift).astype(jnp.bfloat16)
            total = matmul(probs, v_ref[h, before : before + BLOCK])
            for low, high, scores in spans:
                probs = jnp.exp2(scores * factor - shift).astype(jnp.bfloat16)
                total += matmul(probs, v_ref[h, low:high])
            sums = total[:, HEAD_DIM : HEAD_DIM + 1]
            mixed = total / sums
            for g in range(2):
                o_ref[2 * h + g, before : before + BLOCK, :] = mixed[g * BLOCK : (g + 1) * BLOCK]
            logs = shift + jnp.log2(sums)
            lse_ref[h, i] = jnp.broadcast_to(logs, (group, LANES)).T[0:1, :]
        return carry

    lax.fori_loop(0, kv_heads, attend, 0)
    stores.append(start(lse_ref, outs_hbm[5], out_sems.at[5]))
    loads[4].wait()

    def finish(i, carry):
        rows = pl.ds(pl.multiple_of(i * BLOCK, BLOCK), BLOCK)
        mixed = join_heads([o_ref[h, rows, :] for h in range(2 * kv_heads)]).astype(jnp.bfloat16)
        mixed_ref[rows, :] = mixed
        part_ref[rows, :] = matmul(mixed, wo_ref[...]).astype(jnp.bfloat16)
        rows_out(4, 0, i).start()
        rows_out(6, 1, i).start()
        return carry

    lax.fori_loop(0, BLOCKS, finish, 0)
    for copy in stores:
        copy.wait()
    for i in range(BLOCKS):
        rows_out(4, 0, i).wait()
        rows_out(6, 1, i).wait()


def attention_forward(branch, x, gain, wq, wk, wv, wo, rope):
    kv_heads = wk.shape[1] // HEAD_DIM
    rows, width = x.shape
    bf = jnp.bfloat16
    ins = (x, wq, wk, wv, wo, rope)
    outs = (
        jax.ShapeDtypeStruct((width, rows), bf),
        jax.ShapeDtypeStruct((kv_heads, BLOCKS, 2 * BLOCK, LANES), bf),
        jax.ShapeDtypeStruct((kv_heads, rows, LANES), bf),
        jax.ShapeDtypeStruct((kv_heads, rows, LANES), bf),
        jax.ShapeDtypeStruct((rows, wq.shape[1]), bf),
        jax.ShapeDtypeStruct((kv_heads, BLOCKS, 1, 2 * BLOCK), jnp.float32),
        jax.ShapeDtypeStruct((rows, width), bf),
    )
    return pl.pallas_call(
        attention_forward_kernel,
        out_shape=outs,
        in_specs=[SMEM, VMEM] + [HBM] * 6,
        out_specs=[HBM] * 7,
        scratch_shapes=[pltpu.VMEM(a.shape, a.dtype) for a in ins + outs]
        + [
            pltpu.VMEM((2 * kv_heads, rows, LANES), jnp.float32),
            pltpu.VMEM((2, rows, LANES), jnp.float32),
            pltpu.SemaphoreType.DMA((6,)),
            pltpu.SemaphoreType.DMA((BLOCKS,)),
            pltpu.SemaphoreType.DMA((6,)),
            pltpu.SemaphoreType.DMA((2, BLOCKS)),
        ],
        compiler_params=pltpu.CompilerParams(vmem_limit_bytes=VMEM_LIMIT),
        cost_estimate=CHEAP,
        name="attention_forward",
    )(branch, gain, *ins)


def attention_backward_kernel(
    part, branch_ref, *refs
):
    def cut(count):
        nonlocal refs
        head, refs = refs[:count], refs[count:]
        return head

    count, made = (11, 3) if part else (7, 2)
    ins_hbm, outs_hbm, ins, outs = cut(count), cut(made), cut(count), cut(made)
    do_ref, dq_ref, dk_ref, dv_ref, rope_ref, in_sems, gatt_sems, row_sems = refs
    gatt_ref, wo_ref, q_ref, k_ref, v_ref, lse_ref, table_ref = ins[:7]
    wq_ref, wkv_ref, *first_ref = ins[7:] if part else (None, None)
    gq_ref, gkv_ref = outs[:2]
    part_ref = outs[2] if part else None
    kv_heads = k_ref.shape[0]
    group = 2 * BLOCK
    factor = SCORE_SCALE * LOG2E

    def gatt_in(i):
        rows = pl.ds(pl.multiple_of(i * BLOCK, BLOCK), BLOCK)
        return pltpu.make_async_copy(ins_hbm[0].at[rows], gatt_ref.at[rows], gatt_sems.at[i])

    def rows_out(n, i):
        rows = pl.ds(pl.multiple_of(i * BLOCK, BLOCK), BLOCK)
        return pltpu.make_async_copy(outs[n].at[rows], outs_hbm[n].at[rows], row_sems.at[n, i])

    loads = []
    for n in range(1, count):
        size = ins[n].shape[0]
        source = ins_hbm[n].at[pl.ds(part * size, size)] if n < 6 else ins_hbm[n]
        loads.append(start(source, ins[n], in_sems.at[n]))
        if n == 1:
            for i in range(BLOCKS):
                gatt_in(i).start()
    loads[0].wait()

    def project(i, carry):
        rows = pl.ds(pl.multiple_of(i * BLOCK, BLOCK), BLOCK)
        gatt_in(i).wait()
        full = matmul(gatt_ref[rows, :], wo_ref[...], NT)
        lanes = lane_ids((BLOCK, LANES))
        for h in range(2 * kv_heads):
            head = jnp.where(lanes < HEAD_DIM, take_head(full, h), 0.0)
            do_ref[h // 2, i, pl.ds(h % 2 * BLOCK, BLOCK), :] = head.astype(jnp.bfloat16)
        return carry

    lax.fori_loop(0, BLOCKS, project, 0)
    for copy in loads[1:6]:
        copy.wait()
    place_rope(branch_ref, table_ref, rope_ref)

    def attend(h, carry):
        for i in reversed(range(BLOCKS)):
            query, grad, logs = q_ref[h, i], do_ref[h, i], lse_ref[h, i]
            before = i * BLOCK
            cuts = [(before, before + BLOCK)]
            if i > 0 and before < PROMPT:
                cuts += [(0, before)]
            elif i > 0:
                cuts += [(0, PROMPT // 2), (PROMPT // 2, PROMPT)]
            spans, weighted = [], 0.0
            for low, high in cuts:
                scores = matmul(k_ref[h, low:high], query, NT)
                probs = jnp.exp2(scores * factor - logs)
                if low == before:
                    probs = jnp.where(own_mask(probs.shape, 1, i), probs, 0.0)
                elif before >= PROMPT and low > 0:
                    probs = jnp.where(reach_mask(probs.shape, 1, branch_ref), probs, 0.0)
                grad_probs = matmul(v_ref[h, low:high], grad, NT)
                weighted += jnp.sum(probs * grad_probs, axis=0, keepdims=True)
                spans.append((low, high, probs, grad_probs))
            grad_query = jnp.zeros((group, LANES), jnp.float32)
            for low, high, probs, grad_probs in spans:
                grad_scores = (probs * (grad_probs - weighted)).astype(jnp.bfloat16)
                grad_query += matmul(grad_scores, k_ref[h, low:high], TN)
                grad_key = matmul(grad_scores, query)
                grad_value = matmul(probs.astype(jnp.bfloat16), grad)
                if before >= PROMPT:
                    dk_ref[h, low:high] = grad_key
                    dv_ref[h, low:high] = grad_value
                else:
                    dk_ref[h, low:high] += grad_key
                    dv_ref[h, low:high] += grad_value
            dq_ref[h, i] = grad_query
        return carry

    lax.fori_loop(0, kv_heads, attend, 0)
    for copy in loads[6:]:
        copy.wait()

    def finish(i, carry):
        rows = pl.ds(pl.multiple_of(i * BLOCK, BLOCK), BLOCK)
        cosine, sine = rope_ref[0, rows, :] * SCORE_SCALE, rope_ref[1, rows, :] * SCORE_SCALE
        heads = []
        for h in range(2 * kv_heads):
            head = dq_ref[h // 2, i, pl.ds(h % 2 * BLOCK, BLOCK), :]
            heads.append(head * cosine - swap_halves(head) * sine)
        grad_q = join_heads(heads).astype(jnp.bfloat16)
        heads = []
        for h in range(kv_heads):
            head = dk_ref[h, rows, :]
            heads.append(head * cosine - swap_halves(head) * sine)
        heads += [dv_ref[h, rows, :] for h in range(kv_heads)]
        grad_kv = join_heads(heads).astype(jnp.bfloat16)
        gq_ref[rows, :] = grad_q
        gkv_ref[rows, :] = grad_kv
        if part:
            grad_q = jnp.concatenate([first_ref[0][rows, :], grad_q], axis=1)
            grad_kv = jnp.concatenate([first_ref[1][rows, :], grad_kv], axis=1)
            total = matmul(grad_q, wq_ref[...], NT) + matmul(grad_kv, wkv_ref[...], NT)
            part_ref[rows, :] = total.astype(jnp.bfloat16)
        for n in range(made):
            rows_out(n, i).start()
        return carry

    lax.fori_loop(0, BLOCKS, finish, 0)
    for n in range(made):
        for i in range(BLOCKS):
            rows_out(n, i).wait()


def attention_backward(part, branch, gatt, q, k, v, lse, wo, wq, wkv, rope, first):
    kv_heads = k.shape[0] // 2
    rows, width = gatt.shape
    bf = jnp.bfloat16
    small = jax.ShapeDtypeStruct((rows, wq.shape[1] // 2), bf)
    outs = (small, small) + ((jax.ShapeDtypeStruct((rows, width), bf),) if part else ())
    ins = (gatt, wo, q, k, v, lse, rope) + ((wq, wkv, *first) if part else ())

    def held(n, array):
        halves = (array.shape[0] // 2,) + array.shape[1:]
        return pltpu.VMEM(halves if 0 < n < 6 else array.shape, array.dtype)

    return pl.pallas_call(
        functools.partial(attention_backward_kernel, part),
        out_shape=outs,
        in_specs=[SMEM] + [HBM] * len(ins),
        out_specs=[HBM] * len(outs),
        scratch_shapes=[held(n, a) for n, a in enumerate(ins)]
        + [pltpu.VMEM(o.shape, bf) for o in outs]
        + [
            pltpu.VMEM((kv_heads, BLOCKS, 2 * BLOCK, LANES), bf),
            pltpu.VMEM((kv_heads, BLOCKS, 2 * BLOCK, LANES), jnp.float32),
            pltpu.VMEM((kv_heads, rows, LANES), jnp.float32),
            pltpu.VMEM((kv_heads, rows, LANES), jnp.float32),
            pltpu.VMEM((2, rows, LANES), jnp.float32),
            pltpu.SemaphoreType.DMA((len(ins),)),
            pltpu.SemaphoreType.DMA((BLOCKS,)),
            pltpu.SemaphoreType.DMA((len(outs), BLOCKS)),
        ],
        compiler_params=pltpu.CompilerParams(vmem_limit_bytes=VMEM_LIMIT),
        cost_estimate=CHEAP,
        name="attention_backward",
    )(branch, *ins)


KERNEL_BLOCKS = 16
WIDE = 512
FEW = 16
CUTS = ((0, 512), (512, 1024), (1024, 1536), (1536, 2048))


NN = (((1,), (0,)), ((), ()))


def split_copies(tile, low, high, at, sent, kept, axis, mine, sems, k, begin=True):
    copies = []
    for half, target in ((1 - mine, sent), (mine, kept)):
        part = tile.at[:, :, half] if axis == 0 else tile.at[:, half]
        copy = pltpu.make_async_copy(
            part.at[:, :, :, pl.ds(low, high - low)],
            target.at[:, :, :, pl.ds(at, high - low)],
            sems.at[k + len(copies)],
        )
        if begin:
            copy.start()
        copies.append(copy)
    return copies


def gradient_tile(tile, left, right, arrive=None):
    zs = tile.shape[0] // 2
    tall = left.shape[0] // 2

    def step(i, carry):
        if arrive is not None:
            arrive(i)
        out = matmul(left[pl.ds(pl.multiple_of(i * tall, tall), tall), :], right[...])
        tile[pl.ds(i * zs, zs)] = out.astype(jnp.bfloat16).reshape((zs,) + tile.shape[1:])
        return carry

    lax.fori_loop(0, 2, step, 0)


def ffn_kernel(first, count, norm, *refs):
    if norm:
        (bits_ref, gain_ref, *sums_hbm, cot_hbm, cot_t_hbm, wg_hbm, wu_hbm, wd_hbm), refs = refs[:10], refs[10:]
    else:
        (bits_ref, act_hbm, cot_hbm, act_t_hbm, cot_t_hbm, wg_hbm, wu_hbm, wd_hbm), refs = refs[:8], refs[11:]
    (hidden_hbm, ggate_hbm, gup_hbm, sent_a, kept_a, sent_b, kept_b), refs = refs[:7], refs[7:]
    if norm:
        (state_hbm, act_hbm, act_t_hbm, state, *held, sum_sems, made_sems), refs = refs[:9], refs[9:]
    act, cot, lefts, wg, wu, wd, lines, tiles, in_sems, row_sems, out_sems = refs
    units = pl.ds(first, count)
    tall = act.shape[0] // 2

    def rows_in(i, which):
        rows = pl.ds(pl.multiple_of(i * tall, tall), tall)
        source, target = ((act_hbm, act), (cot_hbm, cot))[which]
        return pltpu.make_async_copy(source.at[rows], target.at[rows], row_sems.at[which, i])

    def sums_in(which, i):
        rows = pl.ds(pl.multiple_of(i * BLOCK, BLOCK), BLOCK)
        return pltpu.make_async_copy(sums_hbm[which].at[rows], held[which].at[rows], sum_sems.at[which, i])

    if norm:
        for i in range(act.shape[0] // BLOCK):
            for which in range(3):
                sums_in(which, i).start()
    weights = [start(wg_hbm.at[:, units], wg, in_sems.at[0])]
    if not norm:
        rows_in(0, 0).start()
    weights.append(start(wu_hbm.at[:, units], wu, in_sems.at[1]))
    weights.append(start(wd_hbm.at[units], wd, in_sems.at[2]))
    rows_in(0, 1).start()
    if not norm:
        rows_in(1, 0).start()
    rows_in(1, 1).start()
    sources = [start(cot_t_hbm, lefts.at[0], in_sems.at[3])]
    if not norm:
        sources.append(start(act_t_hbm, lefts.at[1], in_sems.at[4]))

    def norm_step(i, carry):
        for which in range(3):
            sums_in(which, i).wait()

        def few_step(j, carry):
            few = pl.ds(pl.multiple_of(i * BLOCK + j * FEW, FEW), FEW)
            total, rows = norm_rows(*(ref[few, :].astype(jnp.float32) for ref in held), gain_ref[...][None, :])
            state[few, :] = total.astype(jnp.bfloat16)
            act[few, :] = rows.astype(jnp.bfloat16)
            return carry

        lax.fori_loop(0, BLOCK // FEW, few_step, 0, unroll=2)
        rows = pl.ds(pl.multiple_of(i * BLOCK, BLOCK), BLOCK)
        lefts[1, :, rows] = act[rows, :].astype(jnp.float32).T.astype(jnp.bfloat16)
        return carry

    made = []
    if norm:
        lax.fori_loop(0, act.shape[0] // BLOCK, norm_step, 0)
        pairs = ((state, state_hbm), (act, act_hbm), (lefts.at[1], act_t_hbm))
        made = [start(*pair, made_sems.at[i]) for i, pair in enumerate(pairs)]
    weights[0].wait()

    def units_step(i, carry):
        rows = pl.ds(pl.multiple_of(i * tall, tall), tall)
        if not norm:
            rows_in(i, 0).wait()
        gate = matmul(act[rows, :], wg[...])

        @pl.when(i == 0)
        def _():
            weights[1].wait()
            weights[2].wait()

        up = matmul(act[rows, :], wu[...])
        rows_in(i, 1).wait()
        grad = matmul(cot[rows, :], wd[...], NT)
        sigmoid = 1.0 / (1.0 + jnp.exp(-gate))
        silu = gate * sigmoid
        lines[0, rows, :] = (silu * up).astype(jnp.bfloat16)
        lines[1, rows, :] = (grad * up * (sigmoid * (1.0 + gate * (1.0 - sigmoid)))).astype(jnp.bfloat16)
        lines[2, rows, :] = (grad * silu).astype(jnp.bfloat16)
        return carry

    lax.fori_loop(0, 2, units_step, 0)
    copies = [
        start(lines.at[0], hidden_hbm.at[:, units], out_sems.at[0]),
        start(lines.at[1], ggate_hbm.at[:, units], out_sems.at[1]),
        start(lines.at[2], gup_hbm.at[:, units], out_sems.at[2]),
    ]
    half = count // 2
    x, y = bits_ref[0], bits_ref[1]
    for copy in sources:
        copy.wait()

    def stores(t, begin):
        if t == 0:
            return split_copies(tiles.at[0], 0, half, count, sent_a, kept_a, 0, x, out_sems, 3, begin) + split_copies(
                tiles.at[0], half, count, count, sent_b, kept_b, 1, y, out_sems, 5, begin
            )
        if t == 1:
            return split_copies(tiles.at[1], 0, count, 0, sent_a, kept_a, 0, x, out_sems, 7, begin)
        return split_copies(tiles.at[2], 0, count, 0, sent_b, kept_b, 1, y, out_sems, 9, begin)

    def tile_step(t, carry):
        gradient_tile(tiles.at[t], lefts.at[jnp.minimum(t, 1)], lines.at[t])
        for one in range(3):

            @pl.when(t == one)
            def _(one=one):
                stores(one, True)

        return carry

    lax.fori_loop(0, 3, tile_step, 0)
    copies += made
    for t in range(3):
        copies += stores(t, False)
    for copy in copies:
        copy.wait()


def ffn_chunk(bits, blocks, act, cot, cot_t, wg, wu, wd, before, first, count):
    norm = not before
    rows, width = cot.shape
    bf = jnp.bfloat16
    piece = jax.ShapeDtypeStruct((blocks // 4, 2, width // blocks, count + count // 2), bf)
    units = jax.ShapeDtypeStruct((rows, wg.shape[1]), bf)
    by_rows = jax.ShapeDtypeStruct((rows, width), bf)
    outs = (units,) * 3 + (piece,) * 4
    ins = (cot, cot_t, wg, wu, wd)
    if norm:
        outs += (by_rows, by_rows, jax.ShapeDtypeStruct((width, rows), bf))
        ins = (*act, *ins)
    else:
        ins = (act[0], cot, act[1], cot_t, wg, wu, wd, *before)
    return pl.pallas_call(
        functools.partial(ffn_kernel, first, count, norm),
        out_shape=outs,
        in_specs=[SMEM] + [VMEM] * norm + [HBM] * (len(ins) - norm),
        out_specs=[HBM] * len(outs),
        scratch_shapes=(
            [pltpu.VMEM((rows, width), bf)] * 4
            + [pltpu.SemaphoreType.DMA((3, rows // BLOCK)), pltpu.SemaphoreType.DMA((3,))]
        ) * norm
        + [
            pltpu.VMEM((rows, width), bf),
            pltpu.VMEM((rows, width), bf),
            pltpu.VMEM((2, width, rows), bf),
            pltpu.VMEM((width, count), bf),
            pltpu.VMEM((width, count), bf),
            pltpu.VMEM((count, width), bf),
            pltpu.VMEM((3, rows, count), bf),
            pltpu.VMEM((3, blocks // 4, 2, 2, width // blocks, count), bf),
            pltpu.SemaphoreType.DMA((5,)),
            pltpu.SemaphoreType.DMA((2, 2)),
            pltpu.SemaphoreType.DMA((11,)),
        ],
        input_output_aliases={8 + i: i for i in range(len(before))},
        compiler_params=pltpu.CompilerParams(vmem_limit_bytes=VMEM_LIMIT),
        cost_estimate=CHEAP,
        name="ffn_chunk",
    )(bits, *ins)


def gradient_kernel(lefts, parts, bits_ref, *refs):
    def cut(count):
        nonlocal refs
        head, refs = refs[:count], refs[count:]
        return head

    left_hbm, right_hbm, pieces = cut(lefts), cut(len(parts)), cut(4)
    left, right, tiles, (in_sems, out_sems) = cut(lefts), cut(len(parts)), cut(len(parts)), refs
    tall = left[0].shape[0] // 2

    def left_in(which, i):
        rows = pl.ds(pl.multiple_of(i * tall, tall), tall)
        return pltpu.make_async_copy(left_hbm[which].at[rows], left[which].at[rows], in_sems.at[2 * which + i])

    right_in, copies, seen = [], [], set()
    for i, (which, _) in enumerate(parts):
        if which not in seen:
            left_in(which, 0).start()
        right_in.append(start(right_hbm[i], right[i], in_sems.at[2 * lefts + i]))
        if which not in seen:
            left_in(which, 1).start()
        seen.add(which)
    for i, (which, places) in enumerate(parts):
        right_in[i].wait()
        arrive = functools.partial(lambda which, i: left_in(which, i).wait(), which) if which in seen else None
        seen.discard(which)
        gradient_tile(tiles[i], left[which], right[i], arrive)
        for low, high, at, first in places:
            sent, kept = pieces[2 * first], pieces[2 * first + 1]
            copies += split_copies(tiles[i], low, high, at, sent, kept, first, bits_ref[first], out_sems, len(copies))
    for copy in copies:
        copy.wait()


def gradient_pieces(bits, blocks, lefts, rights, which, places):
    width, rows = lefts[0].shape
    bf = jnp.bfloat16
    flat = [place for part in places for place in part]
    widths = [sum(high - low for low, high, _, first in flat if first == axis) for axis in (0, 1)]
    pieces = [jax.ShapeDtypeStruct((blocks // 4, 2, width // blocks, w), bf) for w in widths for _ in range(2)]
    return pl.pallas_call(
        functools.partial(gradient_kernel, len(lefts), tuple(zip(which, places))),
        out_shape=tuple(pieces),
        in_specs=[SMEM] + [HBM] * (len(lefts) + len(rights)),
        out_specs=[HBM] * 4,
        scratch_shapes=[pltpu.VMEM(a.shape, bf) for a in (*lefts, *rights)]
        + [pltpu.VMEM((blocks // 4, 2, 2, width // blocks, r.shape[1]), bf) for r in rights]
        + [pltpu.SemaphoreType.DMA((2 * len(lefts) + len(rights),)), pltpu.SemaphoreType.DMA((2 * len(flat),))],
        compiler_params=pltpu.CompilerParams(vmem_limit_bytes=VMEM_LIMIT),
        cost_estimate=CHEAP,
        name="gradient_pieces",
    )(bits, *lefts, *rights)


def projection_kernel(dims, count, *refs):
    left_hbm, right_hbm, out_hbm, refs = refs[:count], refs[count : 2 * count], refs[2 * count], refs[2 * count + 1 :]
    left, right, (out, left_sems, right_sems, out_sems) = refs[:count], refs[count : 2 * count], refs[2 * count :]
    turned = dims is NT
    rows, width = out.shape
    tall = rows // 2

    def columns(ref, n):
        cut = pl.ds(pl.multiple_of(n * WIDE, WIDE), WIDE)
        return ref.at[cut, :] if turned else ref.at[:, cut]

    def right_in(p, n):
        return pltpu.make_async_copy(columns(right_hbm[p], n), columns(right[p], n), right_sems.at[p, n])

    def left_in(p, i):
        cut = pl.ds(pl.multiple_of(i * tall, tall), tall)
        return pltpu.make_async_copy(left_hbm[p].at[cut], left[p].at[cut], left_sems.at[p, i])

    def out_copy(n):
        wide = pl.ds(pl.multiple_of(n * WIDE, WIDE), WIDE)
        return pltpu.make_async_copy(out.at[:, wide], out_hbm.at[:, wide], out_sems.at[n])

    for p in range(count):
        right_in(p, 0).start()
        left_in(p, 0).start()
    for p in range(count):
        left_in(p, 1).start()
    for n in range(1, width // WIDE):
        for p in range(count):
            right_in(p, n).start()

    def step(j, carry):
        n, i = j // 2, j % 2

        @pl.when(i == 0)
        def _():
            for p in range(count):
                right_in(p, n).wait()

        @pl.when(n == 0)
        def _():
            for p in range(count):
                left_in(p, i).wait()

        cut = pl.ds(pl.multiple_of(i * tall, tall), tall)
        total = sum(matmul(left[p][cut, :], columns(right[p], n)[...], dims) for p in range(count))
        out[cut, pl.ds(pl.multiple_of(n * WIDE, WIDE), WIDE)] = total.astype(jnp.bfloat16)

        @pl.when(i == 1)
        def _():
            out_copy(n).start()

        return carry

    lax.fori_loop(0, 2 * width // WIDE, step, 0)
    for n in range(width // WIDE):
        out_copy(n).wait()


def projection(lefts, rights, dims):
    rows = lefts[0].shape[0]
    width = rights[0].shape[0 if dims is NT else 1]
    bf, count = jnp.bfloat16, len(lefts)
    return pl.pallas_call(
        functools.partial(projection_kernel, dims, count),
        out_shape=jax.ShapeDtypeStruct((rows, width), bf),
        in_specs=[HBM] * (2 * count),
        out_specs=HBM,
        scratch_shapes=[pltpu.VMEM(a.shape, bf) for a in (*lefts, *rights)]
        + [
            pltpu.VMEM((rows, width), bf),
            pltpu.SemaphoreType.DMA((count, 2)),
            pltpu.SemaphoreType.DMA((count, width // WIDE)),
            pltpu.SemaphoreType.DMA((width // WIDE,)),
        ],
        compiler_params=pltpu.CompilerParams(vmem_limit_bytes=VMEM_LIMIT),
        cost_estimate=CHEAP,
        name="projection",
    )(*lefts, *rights)


def add_two(one, two):
    return one.astype(jnp.float32) + two.astype(jnp.float32)


def second_steps(bits_ref, ins_hbm, ins, outs_hbm, outs):
    steps = []
    for z in range(outs[0].shape[0]):

        def compute(z=z):
            for i in range(2):
                kept, got, send, keep, mine = *ins[2 * i : 2 * i + 2], *outs[2 * i : 2 * i + 2], bits_ref[1 - i]
                send[z] = kept[z, 1 - mine] + got[z, 1 - mine]
                keep[z] = kept[z, mine] + got[z, mine]

        steps.append((
            [(a.at[z], b.at[z]) for a, b in zip(ins_hbm, ins)],
            compute,
            [(a.at[z], b.at[z]) for a, b in zip(outs, outs_hbm)],
        ))
    return steps


def third_steps(bits_ref, ins_hbm, ins, outs_hbm, outs):
    low = bits_ref[2] & 1
    steps = []
    for half, out, out_hbm in zip((1 - low, low), outs, outs_hbm):
        for high in range(2):
            block = 2 * high + half

            def compute(block=block, out=out, high=high):
                width = ins[0].shape[-1]
                out[high, :, :width] = ins[0][block] + ins[1][block]
                out[high, :, width:] = ins[2][block] + ins[3][block]

            steps.append((
                [(a.at[block], b.at[block]) for a, b in zip(ins_hbm, ins)], compute, [(out.at[high], out_hbm.at[high])]
            ))
    return steps


def fourth_steps(bits_ref, ins_hbm, ins, outs_hbm, outs):
    high = bits_ref[2] >> 1
    steps = []
    for block, out, out_hbm in zip((1 - high, high), outs, outs_hbm):

        def compute(block=block, out=out):
            for i in range(0, len(ins), 2):
                width = ins[i].shape[-1]
                out[:, i // 2 * width : (i // 2 + 1) * width] = ins[i][block] + ins[i + 1][block]

        steps.append((
            [(a.at[block], b.at[block]) for a, b in zip(ins_hbm, ins)], compute, [(out, out_hbm)]
        ))
    return steps


def sums_kernel(jobs, bits_ref, *refs):
    count, made = sum(j[1] for j in jobs), sum(j[2] for j in jobs)
    ins_hbm, outs_hbm, refs = refs[:count], refs[count : count + made], refs[count + made :]
    ins, outs, (in_sems, out_sems) = refs[:count], refs[count : count + made], refs[count + made :]
    steps = []
    for build, n, m in jobs:
        steps += build(bits_ref, ins_hbm[:n], ins[:n], outs_hbm[:m], outs[:m])
        ins_hbm, ins, outs_hbm, outs = ins_hbm[n:], ins[n:], outs_hbm[m:], outs[m:]
    stream(steps, in_sems, out_sems)


def sums(bits, second=None, third=None, fourth=None, cost=None):
    jobs, ins, outs = [], [], []
    if second is not None:
        made = [a.shape[:1] + a.shape[2:] for a in second]
        jobs.append((second_steps, 4, 4))
        ins, outs = ins + list(second), outs + made
    if third is not None:
        made = [(2, third[0].shape[1], third[0].shape[2] + third[2].shape[2])] * 2
        jobs.append((third_steps, 4, 2))
        ins, outs = ins + list(third), outs + made
    if fourth is not None:
        made = [(fourth[0].shape[1], sum(a.shape[2] for a in fourth[::2]))] * 2
        jobs.append((fourth_steps, len(fourth), 2))
        ins, outs = ins + list(fourth), outs + made
    bf = jnp.bfloat16
    results = pl.pallas_call(
        functools.partial(sums_kernel, tuple(jobs)),
        out_shape=tuple(jax.ShapeDtypeStruct(o, bf) for o in outs),
        in_specs=[SMEM] + [HBM] * len(ins),
        out_specs=[HBM] * len(outs),
        scratch_shapes=[pltpu.VMEM(a.shape, bf) for a in ins]
        + [pltpu.VMEM(o, bf) for o in outs]
        + [pltpu.SemaphoreType.DMA((4 * len(ins),)), pltpu.SemaphoreType.DMA((4 * len(outs),))],
        compiler_params=pltpu.CompilerParams(vmem_limit_bytes=VMEM_LIMIT),
        cost_estimate=cost or CHEAP,
        name="sums",
    )(bits, *ins)
    split = []
    for _, _, m in jobs:
        split.append(results[:m])
        results = results[m:]
    return split[0] if len(split) == 1 else split


def over_dp(array, flip):
    size = lax.axis_size("dp")
    return lax.ppermute(array, "dp", [(i, i ^ flip) for i in range(size)])


def after(arrays, *needed):
    return lax.optimization_barrier((arrays, needed))[0]


def first_stage(pieces):
    sent_a, kept_a, sent_b, kept_b = pieces
    return (kept_a, over_dp(sent_a, 1), kept_b, over_dp(sent_b, 2))


def second_stage(sent_a, kept_a, sent_b, kept_b):
    return (kept_a, over_dp(sent_a, 2), kept_b, over_dp(sent_b, 1))


def third_stage(send, keep):
    return (keep, over_dp(send, 4))


def fourth_stage(send, keep):
    return (keep, over_dp(send, 8))


def attention_sums_kernel(kv_half, index_ref, *refs):
    weights, refs = refs[:3], refs[3:]
    kept_a, got_a, kept_b, got_b, query_ref, key_ref, value_ref, out_ref, gain_ref, *helds, sems = refs
    copies = weight_rows(index_ref, weights, helds, sems)
    half = query_ref.shape[1] // 2
    first, second = add_two(kept_a[...], got_a[...]), add_two(kept_b[...], got_b[...])
    out_ref[:, :half] = first[:, :half]
    out_ref[:, half:] = first[:, 2 * half : 3 * half]
    query_ref[:, :half] = first[:, half : 2 * half]
    query_ref[:, half:] = second[:, :half]
    first, second = first[:, 3 * half :], second[:, half:]
    key_ref[...] = jnp.concatenate([first[:, :kv_half], second[:, :kv_half]], axis=1)
    value_ref[...] = jnp.concatenate([first[:, kv_half:], second[:, kv_half:]], axis=1)
    for copy in copies:
        copy.wait()
    gain_ref[...] = as_row(
        sum(products(ref[...], held[...]) for ref, held in zip((query_ref, key_ref, value_ref), helds))
    )


def attention_sums(index, weights, kept_a, got_a, kept_b, got_b, kv_half):
    rows, heads = kept_b.shape
    shapes = [(rows, heads), (rows, heads // 2), (rows, heads // 2), (rows, heads), (1, LANES)]
    *others, out, gain = pl.pallas_call(
        functools.partial(attention_sums_kernel, kv_half),
        out_shape=tuple(jax.ShapeDtypeStruct(shape, jnp.float32) for shape in shapes),
        in_specs=[SMEM] + [HBM] * 3 + [VMEM] * 4,
        out_specs=[VMEM] * 5,
        scratch_shapes=[pltpu.VMEM((rows, w.shape[1]), w.dtype) for w in weights] + [pltpu.SemaphoreType.DMA((3,))],
        compiler_params=pltpu.CompilerParams(vmem_limit_bytes=VMEM_LIMIT),
        cost_estimate=CHEAP,
        name="attention_sums",
    )(index, *weights, kept_a, got_a, kept_b, got_b)
    return gain, (*others, out.T)


def joined(pieces):
    sent_a, kept_a, sent_b, kept_b = pieces
    first, second = lax.axis_index("dp") & 1, lax.axis_index("dp") >> 1 & 1
    out = []
    for sent, kept, axis, mine in ((sent_a, kept_a, 2, first), (sent_b, kept_b, 1, second)):
        low = jnp.where(mine == 0, kept, sent)
        high = jnp.where(mine == 0, sent, kept)
        out.append(jnp.stack([low, high], axis=axis).reshape(-1, sent.shape[-1]))
    return out


def scatter_sum(grads):
    size = lax.axis_size("dp")
    bits = size.bit_length() - 1
    me = lax.axis_index("dp")
    rows, width = grads.shape
    work = grads.reshape((2,) * bits + (rows // size, width))
    for bit in range(bits):
        axis = bits - 1 - bit
        mine = (me >> bit) & 1
        sent = lax.dynamic_index_in_dim(work, 1 - mine, axis, keepdims=False)
        kept = lax.dynamic_index_in_dim(work, mine, axis, keepdims=False)
        work = kept.astype(jnp.float32) + over_dp(sent, 1 << bit).astype(jnp.float32)
        work = work.astype(grads.dtype)
    return work.astype(jnp.float32)


def weight_rows(index_ref, weights, helds, sems):
    rows = helds[0].shape[0]
    block = pl.ds(pl.multiple_of(index_ref[0] * rows, rows), rows)
    return [start(w.at[block], h, sems.at[i]) for i, (w, h) in enumerate(zip(weights, helds))]


def products(gradient, weight):
    return jnp.sum(gradient * weight.astype(jnp.float32), axis=1, keepdims=True)


def as_row(column):
    column = jnp.concatenate([column, jnp.zeros((LANES - column.shape[0], 1), jnp.float32)], axis=0)
    return jnp.broadcast_to(column, (LANES, LANES)).T[:1]


def ffn_sums_kernel(index_ref, *refs):
    weights, refs = refs[:2], refs[2:]
    ins, (gate_ref, up_ref, down_ref, gain_ref, *helds, sems) = refs[:-7], refs[-7:]
    copies = weight_rows(index_ref, weights, helds, sems)
    chunks = [
        (kept, got, at)
        for kept, got in zip(ins[0::2], ins[1::2])
        for at in range(0, kept.shape[-1], 3 * (CUTS[0][1] - CUTS[0][0]))
    ]
    for copy in copies:
        copy.wait()
    gain = 0.0
    for (low, high), (kept, got, at) in zip(CUTS, chunks):
        count, half = high - low, (high - low) // 2
        total = add_two(kept[:, at : at + 3 * count], got[:, at : at + 3 * count])
        gate, up = total[:, :count], total[:, count + half : 2 * count + half]
        gate_ref[:, low:high] = gate
        down_ref[:, low : low + half] = total[:, count : count + half]
        up_ref[:, low:high] = up
        down_ref[:, low + half : high] = total[:, 2 * count + half :]
        gain += products(gate, helds[0][:, low:high]) + products(up, helds[1][:, low:high])
    gain_ref[...] = as_row(gain)


def ffn_sums(index, weights, pieces):
    rows, units = pieces[0].shape[0], CUTS[-1][1]
    wide = jax.ShapeDtypeStruct((rows, units), jnp.float32)
    return pl.pallas_call(
        ffn_sums_kernel,
        out_shape=(wide,) * 3 + (jax.ShapeDtypeStruct((1, LANES), jnp.float32),),
        in_specs=[SMEM] + [HBM] * 2 + [VMEM] * len(pieces),
        out_specs=[VMEM] * 4,
        scratch_shapes=[pltpu.VMEM((rows, w.shape[1]), w.dtype) for w in weights] + [pltpu.SemaphoreType.DMA((2,))],
        compiler_params=pltpu.CompilerParams(vmem_limit_bytes=VMEM_LIMIT),
        cost_estimate=CHEAP,
        name="ffn_sums",
    )(index, *weights, *pieces)


def gain_gradient(products_sum, gain, index):
    total = products_sum + to_other_core(products_sum)
    rows = gain.shape[0] // lax.axis_size("dp")
    return total[0, :rows] / lax.dynamic_slice_in_dim(gain, index[0] * rows, rows)


def to_other_core(array):
    return lax.ppermute(array, "tensor", [(0, 1), (1, 0)])


def norm_grad(value, grad, gain):
    scale = lax.rsqrt(jnp.mean(value * value, axis=-1, keepdims=True) + epsilon)
    scaled = grad * gain
    back = scale * scaled - value * scale**3 * jnp.mean(scaled * value, axis=-1, keepdims=True)
    return back


def stream(steps, in_sems, out_sems):
    waits, count = [], 0
    for loads, _, _ in steps:
        waits.append([start(*pair, in_sems.at[count + i]) for i, pair in enumerate(loads)])
        count += len(loads)
    copies = []
    for wait, (_, compute, stores) in zip(waits, steps):
        for copy in wait:
            copy.wait()
        compute()
        for pair in stores:
            copies.append(start(*pair, out_sems.at[len(copies)]))
    for copy in copies:
        copy.wait()


def row_kernel(function, turned, count, outs, *refs):
    def cut(n):
        nonlocal refs
        head, refs = refs[:n], refs[n:]
        return head

    ins_hbm, vector, outs_hbm = cut(count), cut(1), cut(outs)
    ins, held, (in_sems, out_sems) = cut(count), cut(outs), refs
    gain = vector[0][...][None, :]
    direct = [ref for ref, t in zip(held, turned) if not t]
    steps = []
    for i in range(ins[0].shape[0] // BLOCK):
        rows = pl.ds(i * BLOCK, BLOCK)
        places = [(slice(None), rows) if t else (rows, slice(None)) for t in turned]

        def compute(i=i, rows=rows, places=places):
            def step(j, carry):
                few = pl.ds(pl.multiple_of(i * BLOCK + j * FEW, FEW), FEW)
                results = function(*(ref[few, :].astype(jnp.float32) for ref in ins), gain)
                for ref, result in zip(direct, results):
                    ref[few, :] = result.astype(jnp.bfloat16)
                return carry

            lax.fori_loop(0, BLOCK // FEW, step, 0, unroll=2)
            for n, t in enumerate(turned):
                if t:
                    held[n][places[n]] = held[n - 1][rows, :].astype(jnp.float32).T.astype(jnp.bfloat16)

        steps.append((
            [(a.at[rows], b.at[rows]) for a, b in zip(ins_hbm, ins)],
            compute,
            [(a.at[place], b.at[place]) for a, b, place in zip(held, outs_hbm, places)],
        ))
    stream(steps, in_sems, out_sems)


def row_call(function, name, ins, vector, turned):
    rows, width = ins[0].shape
    bf, blocks = jnp.bfloat16, rows // BLOCK
    outs = [jax.ShapeDtypeStruct((width, rows) if t else (rows, width), bf) for t in turned]
    return pl.pallas_call(
        functools.partial(row_kernel, function, turned, len(ins), len(outs)),
        out_shape=tuple(outs),
        in_specs=[HBM] * len(ins) + [VMEM],
        out_specs=[HBM] * len(outs),
        scratch_shapes=[pltpu.VMEM(a.shape, bf) for a in (*ins, *outs)]
        + [pltpu.SemaphoreType.DMA((len(ins) * blocks,)), pltpu.SemaphoreType.DMA((len(outs) * blocks,))],
        compiler_params=pltpu.CompilerParams(vmem_limit_bytes=VMEM_LIMIT),
        cost_estimate=CHEAP,
        name=name,
    )(*ins, vector)


def norm_rows(x, own, got, gain):
    hidden = x + (own + got)
    norm = lax.rsqrt(jnp.mean(hidden * hidden, axis=-1, keepdims=True) + epsilon)
    act = hidden * norm * gain
    return hidden, act


def middle_rows(hidden, own, got, cot, gain):
    return (cot + norm_grad(hidden, own + got, gain),)


def output_rows(hidden, own, got, gain):
    return (hidden + (own + got),)


def input_rows(x, gatt, own, got, gain):
    return (gatt + norm_grad(x, own + got, gain),)


def attention_grads(total, half, kv_half):
    names = (("out", half), ("query", half), ("out", half), ("key", kv_half), ("value", kv_half))
    names += (("query", half), ("key", kv_half), ("value", kv_half))
    found, at = {}, 0
    for name, count in names:
        found.setdefault(name, []).append(total[:, at : at + count])
        at += count
    found = {name: jnp.concatenate(parts, axis=1) for name, parts in found.items()}
    return found["query"], found["key"], found["value"], found["out"].T


def plain(names, chunk, backward):
    v = dict(names)
    layer_input, hidden, bits, blocks, size = (v[n] for n in ("layer_input", "hidden", "bits", "blocks", "size"))
    rows, width = layer_input.shape
    half, kv_half, heads = v["half"], v["kv_half"], v["heads"]
    pieces = []
    for i in range(len(CUTS)):
        units, piece = chunk(i, whole=True)
        pieces.append(piece)
    hidden_units, grad_gate_lin, grad_up_lin = units
    two_own = projection([grad_gate_lin, grad_up_lin], [v["w_gate"], v["w_up"]], NT)
    ffn_own = projection([hidden_units], [v["w_down"]], NN)
    grad_attention, grad_attention_t = row_call(
        middle_rows, "middle", [hidden, two_own, to_other_core(two_own), v["cotangent"]], v["gain_two"], [0, 1]
    )
    (output,) = row_call(output_rows, "output", [hidden, ffn_own, to_other_core(ffn_own)], v["gain_two"], [0])
    back_one = backward(0, gatt=grad_attention)
    pieces.append(gradient_pieces(
        bits, blocks, [grad_attention_t, v["act_one_t"]], [v["mixed"], *back_one], [0, 1, 1],
        [((0, half, 0, 0), (half, heads, 0, 1)), ((0, half, half, 0),), ((0, half, half, 1),)],
    ))
    *back_two, one_own = backward(1, *back_one, gatt=grad_attention)
    pieces.append(gradient_pieces(
        bits, blocks, [v["act_one_t"]], back_two, [0, 0], [((0, half, 0, 0),), ((0, half, 0, 1),)]
    ))
    (grad_input,) = row_call(
        input_rows, "input", [layer_input, grad_attention, one_own, to_other_core(one_own)],
        v["attn_gain"], [0],
    )
    total = scatter_sum(jnp.concatenate([p for piece in pieces for p in joined(piece)], axis=1))
    gates, ups, downs = [], [], []
    for low, high in CUTS:
        count = high - low
        parts = jnp.split(total[:, 3 * low : 3 * high], [count, count * 3 // 2, count * 5 // 2], axis=1)
        for found, part in zip((gates, downs, ups, downs), parts):
            found.append(part)
    grad_gate, grad_up = jnp.concatenate(gates, axis=1), jnp.concatenate(ups, axis=1)
    attention = attention_grads(total[:, 3 * CUTS[-1][1] :], half, kv_half)

    def gain_of(gradients, weights, gain):
        count = width // size
        cut = [lax.dynamic_slice_in_dim(v[w], v["me"] * count, count).astype(jnp.float32) for w in weights]
        return gain_gradient(sum(jnp.sum(g * w, axis=1) for g, w in zip(gradients, cut))[None, :], gain, v["index"])

    return (
        output,
        grad_input,
        gain_of(attention[:3], ("w_query", "w_key", "w_value"), v["attn_gain"]),
        *attention,
        gain_of((grad_gate, grad_up), ("w_gate", "w_up"), v["ffn_gain"]),
        grad_gate,
        grad_up,
        jnp.concatenate(downs, axis=1).T,
    )


def per_device(
    layer_input,
    branch_point,
    attn_gain,
    w_query,
    w_key,
    w_value,
    w_out,
    ffn_gain,
    w_gate,
    w_up,
    w_down,
    cotangent,
):
    rows, width = layer_input.shape
    size = lax.axis_size("dp")
    by_kernel = size == KERNEL_BLOCKS
    blocks = KERNEL_BLOCKS
    me = lax.axis_index("dp")
    index = me.reshape(1).astype(jnp.int32)
    bits = jnp.stack([me & 1, me >> 1 & 1, me >> 2 & 3]).astype(jnp.int32)
    rope = rope_tables()
    act_one_t, queries, keys, values, mixed, log_sums, attn_own = attention_forward(
        branch_point, layer_input, attn_gain, w_query, w_key, w_value, w_out, rope
    )
    attn_got = to_other_core(attn_own)
    kv_half = w_key.shape[1] // 2
    w_key_value = jnp.concatenate(
        [w_key[:, :kv_half], w_value[:, :kv_half], w_key[:, kv_half:], w_value[:, kv_half:]], axis=1
    )
    cot_t = cotangent.T
    gain_two = ffn_gain
    *units, sent_a, kept_a, sent_b, kept_b, hidden, act_two, act_two_t = ffn_chunk(
        bits, blocks, (after(gain_two, cot_t, w_key_value), layer_input, attn_own, attn_got), cotangent, cot_t,
        w_gate, w_up, w_down, [], 0, CUTS[0][1],
    )
    first_piece = (sent_a, kept_a, sent_b, kept_b)
    heads, kv = mixed.shape[1], w_key.shape[1]
    half = heads // 2
    def chunk(i, *needed, whole=False):
        nonlocal units
        piece = first_piece
        if i > 0:
            low, high = CUTS[i]
            made = ffn_chunk(
                bits, blocks, (after(act_two, *needed), act_two_t), cotangent, cot_t,
                w_gate, w_up, w_down, units, low, high - low,
            )
            units, piece = made[:3], made[3:]
        return (units, piece) if whole else piece

    def backward(part, *needed, gatt=None):
        return attention_backward(
            part, branch_point, after(grad_attention if gatt is None else gatt, *needed), queries, keys, values, log_sums,
            w_out, w_query, w_key_value, rope, list(needed[:2]) if part else [],
        )

    if not by_kernel:
        return plain(locals(), chunk, backward)
    pieces = [chunk(0)]
    one = [first_stage(pieces[0])]
    pieces.append(chunk(1))
    one.append(first_stage(pieces[1]))
    pieces.append(chunk(2, pieces[1]))
    pieces[2], one[0] = after((pieces[2], one[0]))
    joint = sums(bits, second=one[0])
    two = [second_stage(*joint)]
    pieces.append(chunk(3, joint))
    *units, pieces[3], one[1], two[0] = after((*units, pieces[3], one[1], two[0]))
    joint = sums(bits, second=one[1], third=two[0])
    two.append(second_stage(*joint[0]))
    three = [third_stage(*joint[1])]
    one.append(first_stage(after(pieces[2], units)))
    hidden_units, grad_gate_lin, grad_up_lin = units
    two_own = projection(after([grad_gate_lin, grad_up_lin], joint), [w_gate, w_up], NT)
    two_own, three[0] = after((two_own, three[0]))
    two_got = to_other_core(two_own)
    ffn_own = projection([after(hidden_units, two_own)], [w_down], NN)
    ffn_own, one[2], two[1] = after((ffn_own, one[2], two[1]))
    joint = sums(bits, second=one[2], third=two[1], cost=LONG)
    two.append(second_stage(*joint[0]))
    three.append(third_stage(*joint[1]))
    one.append(first_stage(after(pieces[3], ffn_own)))
    grad_attention, grad_attention_t = row_call(
        middle_rows, "middle", [hidden, two_own, two_got, after(cotangent, joint)], gain_two, [0, 1]
    )
    grad_attention, three[0], three[1] = after((grad_attention, three[0], three[1]))
    joint = sums(bits, fourth=(*three[0], *three[1]))
    four = [fourth_stage(*joint)]
    back_one = backward(0, grad_attention, joint)
    back_one, two[2], one[3], four[0] = after((back_one, two[2], one[3], four[0]))
    joint = sums(bits, second=one[3], third=two[2])
    two.append(second_stage(*joint[0]))
    three.append(third_stage(*joint[1]))
    early = gradient_pieces(
        bits, blocks, [after(grad_attention_t, joint), act_one_t], [mixed, *back_one], [0, 1, 1],
        [((0, half, 0, 0), (half, heads, 0, 1)), ((0, half, half, 0),), ((0, half, half, 1),)],
    )
    early, two[3], three[2] = after((early, two[3], three[2]))
    joint = sums(bits, third=two[3], fourth=three[2])
    three.append(third_stage(*joint[0]))
    four.append(fourth_stage(*joint[1]))
    early_one = first_stage(early)
    ffn_got = to_other_core(after(ffn_own, early))
    *back_two, one_own = backward(1, *back_one, early, joint)
    back_two, one_own, early_one, three[3], four[1], ffn_got = after(
        (back_two, one_own, early_one, three[3], four[1], ffn_got)
    )
    one_got = to_other_core(one_own)
    joint = sums(bits, second=early_one, fourth=three[3])
    early_two = second_stage(*joint[0])
    four.append(fourth_stage(*joint[1]))
    late = gradient_pieces(
        bits, blocks, [after(act_one_t, joint)], back_two, [0, 0], [((0, half, 0, 0),), ((0, half, 0, 1),)]
    )
    late, one_got = after((late, one_got))
    late_one = first_stage(late)
    (output,) = row_call(output_rows, "output", [hidden, after(ffn_own, late), ffn_got], gain_two, [0])
    output, early_two, four[2] = after((output, early_two, four[2]))
    joint = sums(bits, third=early_two)
    early_three = third_stage(*joint)
    (grad_input,) = row_call(
        input_rows, "input", [layer_input, after(grad_attention, joint), one_own, one_got],
        attn_gain, [0],
    )
    grad_input, late_one, early_three = after((grad_input, late_one, early_three))
    joint = sums(bits, second=late_one, fourth=early_three)
    late_two = second_stage(*joint[0])
    early_four = fourth_stage(*joint[1])
    *ffn_grads, ffn_products = ffn_sums(index, [w_gate, w_up], after([p for piece in four for p in piece], joint))
    ffn_grads, late_two = after((ffn_grads, late_two))
    grad_gate, grad_up, grad_down = ffn_grads
    joint = sums(bits, third=late_two)
    late_three = third_stage(*joint)
    grad_ffn_gain = gain_gradient(after(ffn_products, joint), ffn_gain, index)
    late_three, early_four, grad_ffn_gain = after((late_three, early_four, grad_ffn_gain))
    joint = sums(bits, fourth=late_three)
    late_four = fourth_stage(*joint)
    products_sum, attention = attention_sums(index, [w_query, w_key, w_value], *early_four, *late_four, kv_half)
    grad_attn_gain = gain_gradient(products_sum, attn_gain, index)
    return (
        output,
        grad_input,
        grad_attn_gain,
        *attention,
        grad_ffn_gain,
        grad_gate,
        grad_up,
        grad_down.T,
    )


def solution(mesh):
    placed = (
        P("dp", None),
        P("dp", None),
        P(),
        P(None, "tensor"),
        P(None, "tensor"),
        P(None, "tensor"),
        P("tensor", None),
        P(),
        P(None, "tensor"),
        P(None, "tensor"),
        P("tensor", None),
        P("dp", None),
    )
    return jax.shard_map(
        per_device,
        mesh=mesh,
        in_specs=placed,
        out_specs=(
            P("dp", None),
            P("dp", None),
            P("dp"),
            P("dp", "tensor"),
            P("dp", "tensor"),
            P("dp", "tensor"),
            P("tensor", "dp"),
            P("dp"),
            P("dp", "tensor"),
            P("dp", "tensor"),
            P("tensor", "dp"),
        ),
        check_vma=False,
    )
```

```python
import functools

import jax
import jax.numpy as jnp
import numpy as np
from jax import lax
from jax.experimental import pallas as pl
from jax.experimental.pallas import tpu as pltpu
from jax.sharding import PartitionSpec as P

HEAD_DIM = 96
PROMPT = 1024
CONT_LEN = 128
CONT = 2
GROUP_TOK = 1280
BLOCK = 256
BLOCKS = GROUP_TOK // BLOCK
LANES = 128
MIB = 1 << 20
VMEM_LIMIT = 64 * MIB
CHEAP = pl.CostEstimate(flops=10**6, bytes_accessed=10**5, transcendentals=0)
epsilon = 1e-05
rope_base = 100000.0
LOG2E = 1.4426950408889634
SCORE_SCALE = HEAD_DIM ** (-0.5)
NT = (((1,), (1,)), ((), ()))
TN = (((0,), (0,)), ((), ()))

LONG = pl.CostEstimate(flops=10**11, bytes_accessed=10**5, transcendentals=0)


def matmul(left, right, dims=(((1,), (0,)), ((), ()))):
    return lax.dot_general(left, right, dims, preferred_element_type=jnp.float32)


HBM = pl.BlockSpec(memory_space=pl.ANY)
SMEM = pl.BlockSpec(memory_space=pltpu.SMEM)
VMEM = pl.BlockSpec(memory_space=pltpu.VMEM)


def start(source, target, sem):
    copy = pltpu.make_async_copy(source, target, sem)
    copy.start()
    return copy


def rows_of(blocks, width):
    return (blocks // 4, 2, 2, None, width)


def rope_tables():
    half = HEAD_DIM // 2
    frequency = rope_base ** (-np.arange(half, dtype=np.float64) * 2.0 / HEAD_DIM)
    angles = np.arange(PROMPT + CONT_LEN, dtype=np.float64)[:, None] * frequency[None, :]
    pad = np.zeros((angles.shape[0], LANES - HEAD_DIM))
    cosine = np.concatenate([np.cos(angles), np.cos(angles), pad], axis=1)
    sine = np.concatenate([-np.sin(angles), np.sin(angles), pad], axis=1)
    return jnp.asarray(np.stack([cosine, sine]), jnp.float32)


def place_rope(branch_ref, table_ref, rope_ref):
    rope_ref[:, :PROMPT, :] = table_ref[:, :PROMPT, :]
    for c in range(CONT):
        rows = pl.ds(PROMPT + c * CONT_LEN, CONT_LEN)
        for i in range(2):
            rope_ref[i, rows, :] = table_ref[i, pl.ds(branch_ref[0, c], CONT_LEN), :]


def lane_ids(shape):
    return lax.broadcasted_iota(jnp.int32, shape, 1)


def swap_halves(head):
    half = HEAD_DIM // 2
    return jnp.where(
        lane_ids(head.shape) < half, pltpu.roll(head, LANES - half, 1), pltpu.roll(head, half, 1)
    )


def take_head(full, h):
    first = h * HEAD_DIM
    start, shift = first // LANES * LANES, first % LANES
    width = LANES if shift + HEAD_DIM <= LANES else 2 * LANES
    part = full[:, start : start + width]
    return part[:, :LANES] if shift == 0 else pltpu.roll(part, width - shift, 1)[:, :LANES]


def join_heads(heads):
    lanes = lane_ids(heads[0].shape)
    out = []
    for i in range(0, len(heads), 4):
        one, two, three = (pltpu.roll(heads[i + j], LANES - 32 * j, 1) for j in (1, 2, 3))
        out.append(jnp.where(lanes < 96, heads[i], one))
        out.append(jnp.where(lanes < 64, one, two))
        out.append(jnp.where(lanes < 32, two, three))
    return jnp.concatenate(out, axis=1)


def own_mask(shape, query_axis, block):
    query = lax.broadcasted_iota(jnp.int32, shape, query_axis) & (BLOCK - 1)
    key = lax.broadcasted_iota(jnp.int32, shape, 1 - query_axis)
    mask = key <= query
    if block * BLOCK >= PROMPT:
        mask = mask & ((key // CONT_LEN) == (query // CONT_LEN))
    return mask


def reach_mask(shape, query_axis, branch_ref):
    query = lax.broadcasted_iota(jnp.int32, shape, query_axis) & (BLOCK - 1)
    key = lax.broadcasted_iota(jnp.int32, shape, 1 - query_axis) + PROMPT // 2
    return key < jnp.where(query < CONT_LEN, branch_ref[0, 0], branch_ref[0, 1])


def attention_forward_kernel(
    branch_ref, gain_ref, *refs,
):
    ins_hbm, outs_hbm, ins, outs, (o_ref, rope_ref, in_sems, x_sems, out_sems, row_sems) = (
        refs[:6], refs[6:13], refs[13:19], refs[19:26], refs[26:],
    )
    x_ref, wq_ref, wk_ref, wv_ref, wo_ref, table_ref = ins
    act_t_ref, q_ref, k_ref, v_ref, mixed_ref, lse_ref, part_ref = outs
    kv_heads = k_ref.shape[0]
    group = 2 * BLOCK

    def x_in(i):
        rows = pl.ds(pl.multiple_of(i * BLOCK, BLOCK), BLOCK)
        return pltpu.make_async_copy(ins_hbm[0].at[rows], x_ref.at[rows], x_sems.at[i])

    def rows_out(n, which, i):
        rows = pl.ds(pl.multiple_of(i * BLOCK, BLOCK), BLOCK)
        return pltpu.make_async_copy(outs[n].at[rows], outs_hbm[n].at[rows], row_sems.at[which, i])

    x_in(0).start()
    loads = {n: start(ins_hbm[n], ins[n], in_sems.at[n]) for n in (1, 5, 2, 3)}
    for i in range(1, BLOCKS):
        x_in(i).start()
    loads[4] = start(ins_hbm[4], wo_ref, in_sems.at[4])
    for n in (5, 1, 2, 3):
        loads[n].wait()
    place_rope(branch_ref, table_ref, rope_ref)

    def project(i, carry):
        rows = pl.ds(pl.multiple_of(i * BLOCK, BLOCK), BLOCK)
        x_in(i).wait()
        x = x_ref[rows, :].astype(jnp.float32)
        norm = lax.rsqrt(jnp.mean(x * x, axis=-1, keepdims=True) + epsilon)
        act = x * norm * gain_ref[...][None, :]
        act_t_ref[:, rows] = act.T.astype(jnp.bfloat16)
        act = act.astype(jnp.bfloat16)
        cosine, sine = rope_ref[0, rows, :], rope_ref[1, rows, :]
        full = matmul(act, wq_ref[...])
        for h in range(2 * kv_heads):
            head = take_head(full, h)
            rotated = head * cosine + swap_halves(head) * sine
            q_ref[h // 2, i, pl.ds(h % 2 * BLOCK, BLOCK), :] = rotated.astype(jnp.bfloat16)
        full = matmul(act, wk_ref[...])
        for h in range(kv_heads):
            head = take_head(full, h)
            rotated = head * cosine + swap_halves(head) * sine
            k_ref[h, rows, :] = rotated.astype(jnp.bfloat16)
        full = matmul(act, wv_ref[...])
        lanes = lane_ids((BLOCK, LANES))
        for h in range(kv_heads):
            head = jnp.where(lanes < HEAD_DIM, take_head(full, h), 0.0)
            v_ref[h, rows, :] = jnp.where(lanes == HEAD_DIM, 1.0, head).astype(jnp.bfloat16)
        return carry

    lax.fori_loop(0, BLOCKS, project, 0)
    stores = [start(outs[n], outs_hbm[n], out_sems.at[n]) for n in range(4)]
    factor = SCORE_SCALE * LOG2E

    def attend(h, carry):
        for i in range(BLOCKS):
            query = q_ref[h, i]
            before = i * BLOCK
            own = matmul(query, k_ref[h, before : before + BLOCK], NT)
            own = jnp.where(own_mask(own.shape, 0, i), own, -1e30)
            largest = jnp.max(own, axis=-1, keepdims=True)
            spans = []
            if i > 0:
                cuts = [0, before] if before < PROMPT else [0, PROMPT // 2, PROMPT]
                for low, high in zip(cuts[:-1], cuts[1:]):
                    scores = matmul(query, k_ref[h, low:high], NT)
                    if before >= PROMPT and low > 0:
                        scores = jnp.where(reach_mask(scores.shape, 0, branch_ref), scores, -1e30)
                    largest = jnp.maximum(largest, jnp.max(scores, axis=-1, keepdims=True))
                    spans.append((low, high, scores))
            shift = largest * factor
            probs = jnp.exp2(own * factor - shift).astype(jnp.bfloat16)
            total = matmul(probs, v_ref[h, before : before + BLOCK])
            for low, high, scores in spans:
                probs = jnp.exp2(scores * factor - shift).astype(jnp.bfloat16)
                total += matmul(probs, v_ref[h, low:high])
            sums = total[:, HEAD_DIM : HEAD_DIM + 1]
            mixed = total / sums
            for g in range(2):
                o_ref[2 * h + g, before : before + BLOCK, :] = mixed[g * BLOCK : (g + 1) * BLOCK]
            logs = shift + jnp.log2(sums)
            lse_ref[h, i] = jnp.broadcast_to(logs, (group, LANES)).T[0:1, :]
        return carry

    lax.fori_loop(0, kv_heads, attend, 0)
    stores.append(start(lse_ref, outs_hbm[5], out_sems.at[5]))
    loads[4].wait()

    def finish(i, carry):
        rows = pl.ds(pl.multiple_of(i * BLOCK, BLOCK), BLOCK)
        mixed = join_heads([o_ref[h, rows, :] for h in range(2 * kv_heads)]).astype(jnp.bfloat16)
        mixed_ref[rows, :] = mixed
        part_ref[rows, :] = matmul(mixed, wo_ref[...]).astype(jnp.bfloat16)
        rows_out(4, 0, i).start()
        rows_out(6, 1, i).start()
        return carry

    lax.fori_loop(0, BLOCKS, finish, 0)
    for copy in stores:
        copy.wait()
    for i in range(BLOCKS):
        rows_out(4, 0, i).wait()
        rows_out(6, 1, i).wait()


def attention_forward(branch, x, gain, wq, wk, wv, wo, rope):
    kv_heads = wk.shape[1] // HEAD_DIM
    rows, width = x.shape
    bf = jnp.bfloat16
    ins = (x, wq, wk, wv, wo, rope)
    outs = (
        jax.ShapeDtypeStruct((width, rows), bf),
        jax.ShapeDtypeStruct((kv_heads, BLOCKS, 2 * BLOCK, LANES), bf),
        jax.ShapeDtypeStruct((kv_heads, rows, LANES), bf),
        jax.ShapeDtypeStruct((kv_heads, rows, LANES), bf),
        jax.ShapeDtypeStruct((rows, wq.shape[1]), bf),
        jax.ShapeDtypeStruct((kv_heads, BLOCKS, 1, 2 * BLOCK), jnp.float32),
        jax.ShapeDtypeStruct((rows, width), bf),
    )
    return pl.pallas_call(
        attention_forward_kernel,
        out_shape=outs,
        in_specs=[SMEM, VMEM] + [HBM] * 6,
        out_specs=[HBM] * 7,
        scratch_shapes=[pltpu.VMEM(a.shape, a.dtype) for a in ins + outs]
        + [
            pltpu.VMEM((2 * kv_heads, rows, LANES), jnp.float32),
            pltpu.VMEM((2, rows, LANES), jnp.float32),
            pltpu.SemaphoreType.DMA((6,)),
            pltpu.SemaphoreType.DMA((BLOCKS,)),
            pltpu.SemaphoreType.DMA((6,)),
            pltpu.SemaphoreType.DMA((2, BLOCKS)),
        ],
        compiler_params=pltpu.CompilerParams(vmem_limit_bytes=VMEM_LIMIT),
        cost_estimate=CHEAP,
        name="attention_forward",
    )(branch, gain, *ins)


def attention_backward_kernel(
    part, branch_ref, *refs
):
    def cut(count):
        nonlocal refs
        head, refs = refs[:count], refs[count:]
        return head

    count, made = (11, 3) if part else (7, 2)
    ins_hbm, outs_hbm, ins, outs = cut(count), cut(made), cut(count), cut(made)
    do_ref, dq_ref, dk_ref, dv_ref, rope_ref, in_sems, gatt_sems, row_sems = refs
    gatt_ref, wo_ref, q_ref, k_ref, v_ref, lse_ref, table_ref = ins[:7]
    wq_ref, wkv_ref, *first_ref = ins[7:] if part else (None, None)
    gq_ref, gkv_ref = outs[:2]
    part_ref = outs[2] if part else None
    kv_heads = k_ref.shape[0]
    group = 2 * BLOCK
    factor = SCORE_SCALE * LOG2E

    def gatt_in(i):
        rows = pl.ds(pl.multiple_of(i * BLOCK, BLOCK), BLOCK)
        return pltpu.make_async_copy(ins_hbm[0].at[rows], gatt_ref.at[rows], gatt_sems.at[i])

    def rows_out(n, i):
        rows = pl.ds(pl.multiple_of(i * BLOCK, BLOCK), BLOCK)
        return pltpu.make_async_copy(outs[n].at[rows], outs_hbm[n].at[rows], row_sems.at[n, i])

    loads = []
    for n in range(1, count):
        size = ins[n].shape[0]
        source = ins_hbm[n].at[pl.ds(part * size, size)] if n < 6 else ins_hbm[n]
        loads.append(start(source, ins[n], in_sems.at[n]))
        if n == 1:
            for i in range(BLOCKS):
                gatt_in(i).start()
    loads[0].wait()

    def project(i, carry):
        rows = pl.ds(pl.multiple_of(i * BLOCK, BLOCK), BLOCK)
        gatt_in(i).wait()
        full = matmul(gatt_ref[rows, :], wo_ref[...], NT)
        lanes = lane_ids((BLOCK, LANES))
        for h in range(2 * kv_heads):
            head = jnp.where(lanes < HEAD_DIM, take_head(full, h), 0.0)
            do_ref[h // 2, i, pl.ds(h % 2 * BLOCK, BLOCK), :] = head.astype(jnp.bfloat16)
        return carry

    lax.fori_loop(0, BLOCKS, project, 0)
    for copy in loads[1:6]:
        copy.wait()
    place_rope(branch_ref, table_ref, rope_ref)

    def attend(h, carry):
        for i in reversed(range(BLOCKS)):
            query, grad, logs = q_ref[h, i], do_ref[h, i], lse_ref[h, i]
            before = i * BLOCK
            cuts = [(before, before + BLOCK)]
            if i > 0 and before < PROMPT:
                cuts += [(0, before)]
            elif i > 0:
                cuts += [(0, PROMPT // 2), (PROMPT // 2, PROMPT)]
            spans, weighted = [], 0.0
            for low, high in cuts:
                scores = matmul(k_ref[h, low:high], query, NT)
                probs = jnp.exp2(scores * factor - logs)
                if low == before:
                    probs = jnp.where(own_mask(probs.shape, 1, i), probs, 0.0)
                elif before >= PROMPT and low > 0:
                    probs = jnp.where(reach_mask(probs.shape, 1, branch_ref), probs, 0.0)
                grad_probs = matmul(v_ref[h, low:high], grad, NT)
                weighted += jnp.sum(probs * grad_probs, axis=0, keepdims=True)
                spans.append((low, high, probs, grad_probs))
            grad_query = jnp.zeros((group, LANES), jnp.float32)
            for low, high, probs, grad_probs in spans:
                grad_scores = (probs * (grad_probs - weighted)).astype(jnp.bfloat16)
                grad_query += matmul(grad_scores, k_ref[h, low:high], TN)
                grad_key = matmul(grad_scores, query)
                grad_value = matmul(probs.astype(jnp.bfloat16), grad)
                if before >= PROMPT:
                    dk_ref[h, low:high] = grad_key
                    dv_ref[h, low:high] = grad_value
                else:
                    dk_ref[h, low:high] += grad_key
                    dv_ref[h, low:high] += grad_value
            dq_ref[h, i] = grad_query
        return carry

    lax.fori_loop(0, kv_heads, attend, 0)
    for copy in loads[6:]:
        copy.wait()

    def finish(i, carry):
        rows = pl.ds(pl.multiple_of(i * BLOCK, BLOCK), BLOCK)
        cosine, sine = rope_ref[0, rows, :] * SCORE_SCALE, rope_ref[1, rows, :] * SCORE_SCALE
        heads = []
        for h in range(2 * kv_heads):
            head = dq_ref[h // 2, i, pl.ds(h % 2 * BLOCK, BLOCK), :]
            heads.append(head * cosine - swap_halves(head) * sine)
        grad_q = join_heads(heads).astype(jnp.bfloat16)
        heads = []
        for h in range(kv_heads):
            head = dk_ref[h, rows, :]
            heads.append(head * cosine - swap_halves(head) * sine)
        heads += [dv_ref[h, rows, :] for h in range(kv_heads)]
        grad_kv = join_heads(heads).astype(jnp.bfloat16)
        gq_ref[rows, :] = grad_q
        gkv_ref[rows, :] = grad_kv
        if part:
            grad_q = jnp.concatenate([first_ref[0][rows, :], grad_q], axis=1)
            grad_kv = jnp.concatenate([first_ref[1][rows, :], grad_kv], axis=1)
            total = matmul(grad_q, wq_ref[...], NT) + matmul(grad_kv, wkv_ref[...], NT)
            part_ref[rows, :] = total.astype(jnp.bfloat16)
        for n in range(made):
            rows_out(n, i).start()
        return carry

    lax.fori_loop(0, BLOCKS, finish, 0)
    for n in range(made):
        for i in range(BLOCKS):
            rows_out(n, i).wait()


def attention_backward(part, branch, gatt, q, k, v, lse, wo, wq, wkv, rope, first):
    kv_heads = k.shape[0] // 2
    rows, width = gatt.shape
    bf = jnp.bfloat16
    small = jax.ShapeDtypeStruct((rows, wq.shape[1] // 2), bf)
    outs = (small, small) + ((jax.ShapeDtypeStruct((rows, width), bf),) if part else ())
    ins = (gatt, wo, q, k, v, lse, rope) + ((wq, wkv, *first) if part else ())

    def held(n, array):
        halves = (array.shape[0] // 2,) + array.shape[1:]
        return pltpu.VMEM(halves if 0 < n < 6 else array.shape, array.dtype)

    return pl.pallas_call(
        functools.partial(attention_backward_kernel, part),
        out_shape=outs,
        in_specs=[SMEM] + [HBM] * len(ins),
        out_specs=[HBM] * len(outs),
        scratch_shapes=[held(n, a) for n, a in enumerate(ins)]
        + [pltpu.VMEM(o.shape, bf) for o in outs]
        + [
            pltpu.VMEM((kv_heads, BLOCKS, 2 * BLOCK, LANES), bf),
            pltpu.VMEM((kv_heads, BLOCKS, 2 * BLOCK, LANES), jnp.float32),
            pltpu.VMEM((kv_heads, rows, LANES), jnp.float32),
            pltpu.VMEM((kv_heads, rows, LANES), jnp.float32),
            pltpu.VMEM((2, rows, LANES), jnp.float32),
            pltpu.SemaphoreType.DMA((len(ins),)),
            pltpu.SemaphoreType.DMA((BLOCKS,)),
            pltpu.SemaphoreType.DMA((len(outs), BLOCKS)),
        ],
        compiler_params=pltpu.CompilerParams(vmem_limit_bytes=VMEM_LIMIT),
        cost_estimate=CHEAP,
        name="attention_backward",
    )(branch, *ins)


KERNEL_BLOCKS = 16
WIDE = 512
FEW = 16
CUTS = ((0, 512), (512, 1024), (1024, 1536), (1536, 2048))


NN = (((1,), (0,)), ((), ()))


def split_copies(tile, low, high, at, sent, kept, axis, mine, sems, k, begin=True):
    copies = []
    for half, target in ((1 - mine, sent), (mine, kept)):
        part = tile.at[:, :, half] if axis == 0 else tile.at[:, half]
        copy = pltpu.make_async_copy(
            part.at[:, :, :, pl.ds(low, high - low)],
            target.at[:, :, :, pl.ds(at, high - low)],
            sems.at[k + len(copies)],
        )
        if begin:
            copy.start()
        copies.append(copy)
    return copies


def gradient_tile(tile, left, right, arrive=None):
    parts = 1 if arrive is None else 2
    zs, tall = tile.shape[0] // parts, left.shape[0] // parts

    def step(i, carry):
        if arrive is not None:
            arrive(i)
        out = matmul(left[pl.ds(pl.multiple_of(i * tall, tall), tall), :], right[...])
        tile[pl.ds(i * zs, zs)] = out.astype(jnp.bfloat16).reshape((zs,) + tile.shape[1:])
        return carry

    lax.fori_loop(0, parts, step, 0)


def ffn_kernel(first, count, norm, *refs):
    if norm:
        (bits_ref, gain_ref, *sums_hbm, cot_hbm, cot_t_hbm, wg_hbm, wu_hbm, wd_hbm), refs = refs[:10], refs[10:]
    else:
        (bits_ref, act_hbm, cot_hbm, act_t_hbm, cot_t_hbm, wg_hbm, wu_hbm, wd_hbm), refs = refs[:8], refs[11:]
    (hidden_hbm, ggate_hbm, gup_hbm, sent_a, kept_a, sent_b, kept_b), refs = refs[:7], refs[7:]
    if norm:
        (state_hbm, act_hbm, act_t_hbm, state, *held, sum_sems, made_sems), refs = refs[:9], refs[9:]
    act, cot, lefts, wg, wu, wd, lines, tiles, in_sems, row_sems, out_sems = refs
    units = pl.ds(first, count)
    tall = act.shape[0] // 2

    def rows_in(i, which):
        rows = pl.ds(pl.multiple_of(i * tall, tall), tall)
        source, target = ((act_hbm, act), (cot_hbm, cot))[which]
        return pltpu.make_async_copy(source.at[rows], target.at[rows], row_sems.at[which, i])

    def sums_in(which, i):
        rows = pl.ds(pl.multiple_of(i * BLOCK, BLOCK), BLOCK)
        return pltpu.make_async_copy(sums_hbm[which].at[rows], held[which].at[rows], sum_sems.at[which, i])

    if norm:
        for i in range(act.shape[0] // BLOCK):
            for which in range(3):
                sums_in(which, i).start()
    weights = [start(wg_hbm.at[:, units], wg, in_sems.at[0])]
    if not norm:
        rows_in(0, 0).start()
    weights.append(start(wu_hbm.at[:, units], wu, in_sems.at[1]))
    weights.append(start(wd_hbm.at[units], wd, in_sems.at[2]))
    rows_in(0, 1).start()
    if not norm:
        rows_in(1, 0).start()
    rows_in(1, 1).start()
    sources = [start(cot_t_hbm, lefts.at[0], in_sems.at[3])]
    if not norm:
        sources.append(start(act_t_hbm, lefts.at[1], in_sems.at[4]))

    def norm_step(i, carry):
        for which in range(3):
            sums_in(which, i).wait()

        def few_step(j, carry):
            few = pl.ds(pl.multiple_of(i * BLOCK + j * FEW, FEW), FEW)
            total, rows = norm_rows(*(ref[few, :].astype(jnp.float32) for ref in held), gain_ref[...][None, :])
            state[few, :] = total.astype(jnp.bfloat16)
            act[few, :] = rows.astype(jnp.bfloat16)
            return carry

        lax.fori_loop(0, BLOCK // FEW, few_step, 0, unroll=4)
        rows = pl.ds(pl.multiple_of(i * BLOCK, BLOCK), BLOCK)
        lefts[1, :, rows] = act[rows, :].astype(jnp.float32).T.astype(jnp.bfloat16)
        return carry

    made = []
    if norm:
        lax.fori_loop(0, act.shape[0] // BLOCK, norm_step, 0)
        pairs = ((state, state_hbm), (act, act_hbm), (lefts.at[1], act_t_hbm))
        made = [start(*pair, made_sems.at[i]) for i, pair in enumerate(pairs)]
    weights[0].wait()

    def units_step(i, carry):
        rows = pl.ds(pl.multiple_of(i * tall, tall), tall)
        if not norm:
            rows_in(i, 0).wait()
        gate = matmul(act[rows, :], wg[...])

        @pl.when(i == 0)
        def _():
            weights[1].wait()
            weights[2].wait()

        up = matmul(act[rows, :], wu[...])
        rows_in(i, 1).wait()
        grad = matmul(cot[rows, :], wd[...], NT)
        sigmoid = 1.0 / (1.0 + jnp.exp(-gate))
        silu = gate * sigmoid
        lines[0, rows, :] = (silu * up).astype(jnp.bfloat16)
        lines[1, rows, :] = (grad * up * (sigmoid * (1.0 + gate * (1.0 - sigmoid)))).astype(jnp.bfloat16)
        lines[2, rows, :] = (grad * silu).astype(jnp.bfloat16)
        return carry

    lax.fori_loop(0, 2, units_step, 0)
    copies = [
        start(lines.at[0], hidden_hbm.at[:, units], out_sems.at[0]),
        start(lines.at[1], ggate_hbm.at[:, units], out_sems.at[1]),
        start(lines.at[2], gup_hbm.at[:, units], out_sems.at[2]),
    ]
    half = count // 2
    x, y = bits_ref[0], bits_ref[1]
    for copy in sources:
        copy.wait()

    def stores(t, begin):
        if t == 0:
            return split_copies(tiles.at[0], 0, half, count, sent_a, kept_a, 0, x, out_sems, 3, begin) + split_copies(
                tiles.at[0], half, count, count, sent_b, kept_b, 1, y, out_sems, 5, begin
            )
        if t == 1:
            return split_copies(tiles.at[1], 0, count, 0, sent_a, kept_a, 0, x, out_sems, 7, begin)
        return split_copies(tiles.at[2], 0, count, 0, sent_b, kept_b, 1, y, out_sems, 9, begin)

    def tile_step(t, carry):
        gradient_tile(tiles.at[t], lefts.at[jnp.minimum(t, 1)], lines.at[t])
        for one in range(3):

            @pl.when(t == one)
            def _(one=one):
                stores(one, True)

        return carry

    lax.fori_loop(0, 3, tile_step, 0)
    copies += made
    for t in range(3):
        copies += stores(t, False)
    for copy in copies:
        copy.wait()


def ffn_chunk(bits, blocks, act, cot, cot_t, wg, wu, wd, before, first, count):
    norm = not before
    rows, width = cot.shape
    bf = jnp.bfloat16
    piece = jax.ShapeDtypeStruct((blocks // 4, 2, width // blocks, count + count // 2), bf)
    units = jax.ShapeDtypeStruct((rows, wg.shape[1]), bf)
    by_rows = jax.ShapeDtypeStruct((rows, width), bf)
    outs = (units,) * 3 + (piece,) * 4
    ins = (cot, cot_t, wg, wu, wd)
    if norm:
        outs += (by_rows, by_rows, jax.ShapeDtypeStruct((width, rows), bf))
        ins = (*act, *ins)
    else:
        ins = (act[0], cot, act[1], cot_t, wg, wu, wd, *before)
    return pl.pallas_call(
        functools.partial(ffn_kernel, first, count, norm),
        out_shape=outs,
        in_specs=[SMEM] + [VMEM] * norm + [HBM] * (len(ins) - norm),
        out_specs=[HBM] * len(outs),
        scratch_shapes=(
            [pltpu.VMEM((rows, width), bf)] * 4
            + [pltpu.SemaphoreType.DMA((3, rows // BLOCK)), pltpu.SemaphoreType.DMA((3,))]
        ) * norm
        + [
            pltpu.VMEM((rows, width), bf),
            pltpu.VMEM((rows, width), bf),
            pltpu.VMEM((2, width, rows), bf),
            pltpu.VMEM((width, count), bf),
            pltpu.VMEM((width, count), bf),
            pltpu.VMEM((count, width), bf),
            pltpu.VMEM((3, rows, count), bf),
            pltpu.VMEM((3, blocks // 4, 2, 2, width // blocks, count), bf),
            pltpu.SemaphoreType.DMA((5,)),
            pltpu.SemaphoreType.DMA((2, 2)),
            pltpu.SemaphoreType.DMA((11,)),
        ],
        input_output_aliases={8 + i: i for i in range(len(before))},
        compiler_params=pltpu.CompilerParams(vmem_limit_bytes=VMEM_LIMIT),
        cost_estimate=CHEAP,
        name="ffn_chunk",
    )(bits, *ins)


def gradient_kernel(lefts, parts, bits_ref, *refs):
    def cut(count):
        nonlocal refs
        head, refs = refs[:count], refs[count:]
        return head

    left_hbm, right_hbm, pieces = cut(lefts), cut(len(parts)), cut(4)
    left, right, tiles, (in_sems, out_sems) = cut(lefts), cut(len(parts)), cut(len(parts)), refs
    tall = left[0].shape[0] // 2

    def left_in(which, i):
        rows = pl.ds(pl.multiple_of(i * tall, tall), tall)
        return pltpu.make_async_copy(left_hbm[which].at[rows], left[which].at[rows], in_sems.at[2 * which + i])

    right_in, copies, seen = [], [], set()
    for i, (which, _) in enumerate(parts):
        if which not in seen:
            left_in(which, 0).start()
        right_in.append(start(right_hbm[i], right[i], in_sems.at[2 * lefts + i]))
        if which not in seen:
            left_in(which, 1).start()
        seen.add(which)
    for i, (which, places) in enumerate(parts):
        right_in[i].wait()
        arrive = functools.partial(lambda which, i: left_in(which, i).wait(), which) if which in seen else None
        seen.discard(which)
        gradient_tile(tiles[i], left[which], right[i], arrive)
        for low, high, at, first in places:
            sent, kept = pieces[2 * first], pieces[2 * first + 1]
            copies += split_copies(tiles[i], low, high, at, sent, kept, first, bits_ref[first], out_sems, len(copies))
    for copy in copies:
        copy.wait()


def gradient_pieces(bits, blocks, lefts, rights, which, places):
    width, rows = lefts[0].shape
    bf = jnp.bfloat16
    flat = [place for part in places for place in part]
    widths = [sum(high - low for low, high, _, first in flat if first == axis) for axis in (0, 1)]
    pieces = [jax.ShapeDtypeStruct((blocks // 4, 2, width // blocks, w), bf) for w in widths for _ in range(2)]
    return pl.pallas_call(
        functools.partial(gradient_kernel, len(lefts), tuple(zip(which, places))),
        out_shape=tuple(pieces),
        in_specs=[SMEM] + [HBM] * (len(lefts) + len(rights)),
        out_specs=[HBM] * 4,
        scratch_shapes=[pltpu.VMEM(a.shape, bf) for a in (*lefts, *rights)]
        + [pltpu.VMEM((blocks // 4, 2, 2, width // blocks, r.shape[1]), bf) for r in rights]
        + [pltpu.SemaphoreType.DMA((2 * len(lefts) + len(rights),)), pltpu.SemaphoreType.DMA((2 * len(flat),))],
        compiler_params=pltpu.CompilerParams(vmem_limit_bytes=VMEM_LIMIT),
        cost_estimate=CHEAP,
        name="gradient_pieces",
    )(bits, *lefts, *rights)


def projection_kernel(dims, count, *refs):
    left_hbm, right_hbm, out_hbm, refs = refs[:count], refs[count : 2 * count], refs[2 * count], refs[2 * count + 1 :]
    left, right, (out, left_sems, right_sems, out_sems) = refs[:count], refs[count : 2 * count], refs[2 * count :]
    turned = dims is NT
    rows, width = out.shape
    tall = rows // 2

    def columns(ref, n):
        cut = pl.ds(pl.multiple_of(n * WIDE, WIDE), WIDE)
        return ref.at[cut, :] if turned else ref.at[:, cut]

    def right_in(p, n):
        return pltpu.make_async_copy(columns(right_hbm[p], n), columns(right[p], n), right_sems.at[p, n])

    def left_in(p, i):
        cut = pl.ds(pl.multiple_of(i * tall, tall), tall)
        return pltpu.make_async_copy(left_hbm[p].at[cut], left[p].at[cut], left_sems.at[p, i])

    def out_copy(n):
        wide = pl.ds(pl.multiple_of(n * WIDE, WIDE), WIDE)
        return pltpu.make_async_copy(out.at[:, wide], out_hbm.at[:, wide], out_sems.at[n])

    for p in range(count):
        right_in(p, 0).start()
        left_in(p, 0).start()
    for p in range(count):
        left_in(p, 1).start()
    for n in range(1, width // WIDE):
        for p in range(count):
            right_in(p, n).start()

    def step(j, carry):
        n, i = j // 2, j % 2

        @pl.when(i == 0)
        def _():
            for p in range(count):
                right_in(p, n).wait()

        @pl.when(n == 0)
        def _():
            for p in range(count):
                left_in(p, i).wait()

        cut = pl.ds(pl.multiple_of(i * tall, tall), tall)
        total = sum(matmul(left[p][cut, :], columns(right[p], n)[...], dims) for p in range(count))
        out[cut, pl.ds(pl.multiple_of(n * WIDE, WIDE), WIDE)] = total.astype(jnp.bfloat16)

        @pl.when(i == 1)
        def _():
            out_copy(n).start()

        return carry

    lax.fori_loop(0, 2 * width // WIDE, step, 0)
    for n in range(width // WIDE):
        out_copy(n).wait()


def projection(lefts, rights, dims):
    rows = lefts[0].shape[0]
    width = rights[0].shape[0 if dims is NT else 1]
    bf, count = jnp.bfloat16, len(lefts)
    return pl.pallas_call(
        functools.partial(projection_kernel, dims, count),
        out_shape=jax.ShapeDtypeStruct((rows, width), bf),
        in_specs=[HBM] * (2 * count),
        out_specs=HBM,
        scratch_shapes=[pltpu.VMEM(a.shape, bf) for a in (*lefts, *rights)]
        + [
            pltpu.VMEM((rows, width), bf),
            pltpu.SemaphoreType.DMA((count, 2)),
            pltpu.SemaphoreType.DMA((count, width // WIDE)),
            pltpu.SemaphoreType.DMA((width // WIDE,)),
        ],
        compiler_params=pltpu.CompilerParams(vmem_limit_bytes=VMEM_LIMIT),
        cost_estimate=CHEAP,
        name="projection",
    )(*lefts, *rights)


def add_two(one, two):
    return one.astype(jnp.float32) + two.astype(jnp.float32)


def second_steps(bits_ref, ins_hbm, ins, outs_hbm, outs):
    steps = []
    for z in range(outs[0].shape[0]):

        def compute(z=z):
            for i in range(2):
                kept, got, send, keep, mine = *ins[2 * i : 2 * i + 2], *outs[2 * i : 2 * i + 2], bits_ref[1 - i]
                send[z] = kept[z, 1 - mine] + got[z, 1 - mine]
                keep[z] = kept[z, mine] + got[z, mine]

        steps.append((
            [(a.at[z], b.at[z]) for a, b in zip(ins_hbm, ins)],
            compute,
            [(a.at[z], b.at[z]) for a, b in zip(outs, outs_hbm)],
        ))
    return steps


def third_steps(bits_ref, ins_hbm, ins, outs_hbm, outs):
    low = bits_ref[2] & 1
    steps = []
    for half, out, out_hbm in zip((1 - low, low), outs, outs_hbm):
        for high in range(2):
            block = 2 * high + half

            def compute(block=block, out=out, high=high):
                width = ins[0].shape[-1]
                out[high, :, :width] = ins[0][block] + ins[1][block]
                out[high, :, width:] = ins[2][block] + ins[3][block]

            steps.append((
                [(a.at[block], b.at[block]) for a, b in zip(ins_hbm, ins)], compute, [(out.at[high], out_hbm.at[high])]
            ))
    return steps


def fourth_steps(bits_ref, ins_hbm, ins, outs_hbm, outs):
    high = bits_ref[2] >> 1
    steps = []
    for block, out, out_hbm in zip((1 - high, high), outs, outs_hbm):

        def compute(block=block, out=out):
            for i in range(0, len(ins), 2):
                width = ins[i].shape[-1]
                out[:, i // 2 * width : (i // 2 + 1) * width] = ins[i][block] + ins[i + 1][block]

        steps.append((
            [(a.at[block], b.at[block]) for a, b in zip(ins_hbm, ins)], compute, [(out, out_hbm)]
        ))
    return steps


def sums_kernel(jobs, bits_ref, *refs):
    count, made = sum(j[1] for j in jobs), sum(j[2] for j in jobs)
    ins_hbm, outs_hbm, refs = refs[:count], refs[count : count + made], refs[count + made :]
    ins, outs, (in_sems, out_sems) = refs[:count], refs[count : count + made], refs[count + made :]
    steps = []
    for build, n, m in jobs:
        steps += build(bits_ref, ins_hbm[:n], ins[:n], outs_hbm[:m], outs[:m])
        ins_hbm, ins, outs_hbm, outs = ins_hbm[n:], ins[n:], outs_hbm[m:], outs[m:]
    stream(steps, in_sems, out_sems)


def sums(bits, second=None, third=None, fourth=None, cost=None):
    jobs, ins, outs = [], [], []
    if second is not None:
        made = [a.shape[:1] + a.shape[2:] for a in second]
        jobs.append((second_steps, 4, 4))
        ins, outs = ins + list(second), outs + made
    if third is not None:
        made = [(2, third[0].shape[1], third[0].shape[2] + third[2].shape[2])] * 2
        jobs.append((third_steps, 4, 2))
        ins, outs = ins + list(third), outs + made
    if fourth is not None:
        made = [(fourth[0].shape[1], sum(a.shape[2] for a in fourth[::2]))] * 2
        jobs.append((fourth_steps, len(fourth), 2))
        ins, outs = ins + list(fourth), outs + made
    bf = jnp.bfloat16
    results = pl.pallas_call(
        functools.partial(sums_kernel, tuple(jobs)),
        out_shape=tuple(jax.ShapeDtypeStruct(o, bf) for o in outs),
        in_specs=[SMEM] + [HBM] * len(ins),
        out_specs=[HBM] * len(outs),
        scratch_shapes=[pltpu.VMEM(a.shape, bf) for a in ins]
        + [pltpu.VMEM(o, bf) for o in outs]
        + [pltpu.SemaphoreType.DMA((4 * len(ins),)), pltpu.SemaphoreType.DMA((4 * len(outs),))],
        compiler_params=pltpu.CompilerParams(vmem_limit_bytes=VMEM_LIMIT),
        cost_estimate=cost or CHEAP,
        name="sums",
    )(bits, *ins)
    split = []
    for _, _, m in jobs:
        split.append(results[:m])
        results = results[m:]
    return split[0] if len(split) == 1 else split


def over_dp(array, flip):
    size = lax.axis_size("dp")
    return lax.ppermute(array, "dp", [(i, i ^ flip) for i in range(size)])


def after(arrays, *needed):
    return lax.optimization_barrier((arrays, needed))[0]


def first_stage(pieces):
    sent_a, kept_a, sent_b, kept_b = pieces
    return (kept_a, over_dp(sent_a, 1), kept_b, over_dp(sent_b, 2))


def second_stage(sent_a, kept_a, sent_b, kept_b):
    return (kept_a, over_dp(sent_a, 2), kept_b, over_dp(sent_b, 1))


def third_stage(send, keep):
    return (keep, over_dp(send, 4))


def fourth_stage(send, keep):
    return (keep, over_dp(send, 8))


def attention_sums_kernel(kv_half, index_ref, *refs):
    weights, refs = refs[:3], refs[3:]
    kept_a, got_a, kept_b, got_b, query_ref, key_ref, value_ref, out_ref, gain_ref, *helds, sems = refs
    copies = weight_rows(index_ref, weights, helds, sems)
    half = query_ref.shape[1] // 2
    first, second = add_two(kept_a[...], got_a[...]), add_two(kept_b[...], got_b[...])
    out_ref[:, :half] = first[:, :half]
    out_ref[:, half:] = first[:, 2 * half : 3 * half]
    query_ref[:, :half] = first[:, half : 2 * half]
    query_ref[:, half:] = second[:, :half]
    first, second = first[:, 3 * half :], second[:, half:]
    key_ref[...] = jnp.concatenate([first[:, :kv_half], second[:, :kv_half]], axis=1)
    value_ref[...] = jnp.concatenate([first[:, kv_half:], second[:, kv_half:]], axis=1)
    for copy in copies:
        copy.wait()
    gain_ref[...] = as_row(
        sum(products(ref[...], held[...]) for ref, held in zip((query_ref, key_ref, value_ref), helds))
    )


def attention_sums(index, weights, kept_a, got_a, kept_b, got_b, kv_half):
    rows, heads = kept_b.shape
    shapes = [(rows, heads), (rows, heads // 2), (rows, heads // 2), (rows, heads), (1, LANES)]
    *others, out, gain = pl.pallas_call(
        functools.partial(attention_sums_kernel, kv_half),
        out_shape=tuple(jax.ShapeDtypeStruct(shape, jnp.float32) for shape in shapes),
        in_specs=[SMEM] + [HBM] * 3 + [VMEM] * 4,
        out_specs=[VMEM] * 5,
        scratch_shapes=[pltpu.VMEM((rows, w.shape[1]), w.dtype) for w in weights] + [pltpu.SemaphoreType.DMA((3,))],
        compiler_params=pltpu.CompilerParams(vmem_limit_bytes=VMEM_LIMIT),
        cost_estimate=CHEAP,
        name="attention_sums",
    )(index, *weights, kept_a, got_a, kept_b, got_b)
    return gain, (*others, out.T)


def joined(pieces):
    sent_a, kept_a, sent_b, kept_b = pieces
    first, second = lax.axis_index("dp") & 1, lax.axis_index("dp") >> 1 & 1
    out = []
    for sent, kept, axis, mine in ((sent_a, kept_a, 2, first), (sent_b, kept_b, 1, second)):
        low = jnp.where(mine == 0, kept, sent)
        high = jnp.where(mine == 0, sent, kept)
        out.append(jnp.stack([low, high], axis=axis).reshape(-1, sent.shape[-1]))
    return out


def scatter_sum(grads):
    size = lax.axis_size("dp")
    bits = size.bit_length() - 1
    me = lax.axis_index("dp")
    rows, width = grads.shape
    work = grads.reshape((2,) * bits + (rows // size, width))
    for bit in range(bits):
        axis = bits - 1 - bit
        mine = (me >> bit) & 1
        sent = lax.dynamic_index_in_dim(work, 1 - mine, axis, keepdims=False)
        kept = lax.dynamic_index_in_dim(work, mine, axis, keepdims=False)
        work = kept.astype(jnp.float32) + over_dp(sent, 1 << bit).astype(jnp.float32)
        work = work.astype(grads.dtype)
    return work.astype(jnp.float32)


def weight_rows(index_ref, weights, helds, sems):
    rows = helds[0].shape[0]
    block = pl.ds(pl.multiple_of(index_ref[0] * rows, rows), rows)
    return [start(w.at[block], h, sems.at[i]) for i, (w, h) in enumerate(zip(weights, helds))]


def products(gradient, weight):
    return jnp.sum(gradient * weight.astype(jnp.float32), axis=1, keepdims=True)


def as_row(column):
    column = jnp.concatenate([column, jnp.zeros((LANES - column.shape[0], 1), jnp.float32)], axis=0)
    return jnp.broadcast_to(column, (LANES, LANES)).T[:1]


def ffn_sums_kernel(index_ref, *refs):
    weights, refs = refs[:2], refs[2:]
    ins, (gate_ref, up_ref, down_ref, gain_ref, *helds, sems) = refs[:-7], refs[-7:]
    copies = weight_rows(index_ref, weights, helds, sems)
    chunks = [
        (kept, got, at)
        for kept, got in zip(ins[0::2], ins[1::2])
        for at in range(0, kept.shape[-1], 3 * (CUTS[0][1] - CUTS[0][0]))
    ]
    for copy in copies:
        copy.wait()
    gain = 0.0
    for (low, high), (kept, got, at) in zip(CUTS, chunks):
        count, half = high - low, (high - low) // 2
        total = add_two(kept[:, at : at + 3 * count], got[:, at : at + 3 * count])
        gate, up = total[:, :count], total[:, count + half : 2 * count + half]
        gate_ref[:, low:high] = gate
        down_ref[:, low : low + half] = total[:, count : count + half]
        up_ref[:, low:high] = up
        down_ref[:, low + half : high] = total[:, 2 * count + half :]
        gain += products(gate, helds[0][:, low:high]) + products(up, helds[1][:, low:high])
    gain_ref[...] = as_row(gain)


def ffn_sums(index, weights, pieces):
    rows, units = pieces[0].shape[0], CUTS[-1][1]
    wide = jax.ShapeDtypeStruct((rows, units), jnp.float32)
    return pl.pallas_call(
        ffn_sums_kernel,
        out_shape=(wide,) * 3 + (jax.ShapeDtypeStruct((1, LANES), jnp.float32),),
        in_specs=[SMEM] + [HBM] * 2 + [VMEM] * len(pieces),
        out_specs=[VMEM] * 4,
        scratch_shapes=[pltpu.VMEM((rows, w.shape[1]), w.dtype) for w in weights] + [pltpu.SemaphoreType.DMA((2,))],
        compiler_params=pltpu.CompilerParams(vmem_limit_bytes=VMEM_LIMIT),
        cost_estimate=CHEAP,
        name="ffn_sums",
    )(index, *weights, *pieces)


def gain_gradient(products_sum, gain, index):
    total = products_sum + to_other_core(products_sum)
    rows = gain.shape[0] // lax.axis_size("dp")
    return total[0, :rows] / lax.dynamic_slice_in_dim(gain, index[0] * rows, rows)


def to_other_core(array):
    return lax.ppermute(array, "tensor", [(0, 1), (1, 0)])


def norm_grad(value, grad, gain):
    scale = lax.rsqrt(jnp.mean(value * value, axis=-1, keepdims=True) + epsilon)
    scaled = grad * gain
    back = scale * scaled - value * scale**3 * jnp.mean(scaled * value, axis=-1, keepdims=True)
    return back


def stream(steps, in_sems, out_sems):
    waits, count = [], 0
    for loads, _, _ in steps:
        waits.append([start(*pair, in_sems.at[count + i]) for i, pair in enumerate(loads)])
        count += len(loads)
    copies = []
    for wait, (_, compute, stores) in zip(waits, steps):
        for copy in wait:
            copy.wait()
        compute()
        for pair in stores:
            copies.append(start(*pair, out_sems.at[len(copies)]))
    for copy in copies:
        copy.wait()


def row_kernel(function, turned, count, outs, *refs):
    def cut(n):
        nonlocal refs
        head, refs = refs[:n], refs[n:]
        return head

    ins_hbm, vector, outs_hbm = cut(count), cut(1), cut(outs)
    ins, held, (in_sems, out_sems) = cut(count), cut(outs), refs
    gain = vector[0][...][None, :]
    direct = [ref for ref, t in zip(held, turned) if not t]
    steps = []
    for i in range(ins[0].shape[0] // BLOCK):
        rows = pl.ds(i * BLOCK, BLOCK)
        places = [(slice(None), rows) if t else (rows, slice(None)) for t in turned]

        def compute(i=i, rows=rows, places=places):
            def step(j, carry):
                few = pl.ds(pl.multiple_of(i * BLOCK + j * FEW, FEW), FEW)
                results = function(*(ref[few, :].astype(jnp.float32) for ref in ins), gain)
                for ref, result in zip(direct, results):
                    ref[few, :] = result.astype(jnp.bfloat16)
                return carry

            if direct:
                lax.fori_loop(0, BLOCK // FEW, step, 0, unroll=4)
            for n, t in enumerate(turned):
                if t:
                    source = ins[0] if t == 2 else held[n - 1]
                    held[n][places[n]] = source[rows, :].astype(jnp.float32).T.astype(jnp.bfloat16)

        steps.append((
            [(a.at[rows], b.at[rows]) for a, b in zip(ins_hbm, ins)],
            compute,
            [(a.at[place], b.at[place]) for a, b, place in zip(held, outs_hbm, places)],
        ))
    stream(steps, in_sems, out_sems)


def row_call(function, name, ins, vector, turned):
    rows, width = ins[0].shape
    bf, blocks = jnp.bfloat16, rows // BLOCK
    outs = [jax.ShapeDtypeStruct((width, rows) if t else (rows, width), bf) for t in turned]
    return pl.pallas_call(
        functools.partial(row_kernel, function, turned, len(ins), len(outs)),
        out_shape=tuple(outs),
        in_specs=[HBM] * len(ins) + [VMEM],
        out_specs=[HBM] * len(outs),
        scratch_shapes=[pltpu.VMEM(a.shape, bf) for a in (*ins, *outs)]
        + [pltpu.SemaphoreType.DMA((len(ins) * blocks,)), pltpu.SemaphoreType.DMA((len(outs) * blocks,))],
        compiler_params=pltpu.CompilerParams(vmem_limit_bytes=VMEM_LIMIT),
        cost_estimate=CHEAP,
        name=name,
    )(*ins, vector)


def norm_rows(x, own, got, gain):
    hidden = x + (own + got)
    norm = lax.rsqrt(jnp.mean(hidden * hidden, axis=-1, keepdims=True) + epsilon)
    act = hidden * norm * gain
    return hidden, act


def middle_rows(hidden, own, got, cot, gain):
    return (cot + norm_grad(hidden, own + got, gain),)


def output_rows(hidden, own, got, gain):
    return (hidden + (own + got),)


def input_rows(x, gatt, own, got, gain):
    return (gatt + norm_grad(x, own + got, gain),)


def attention_grads(total, half, kv_half):
    names = (("out", half), ("query", half), ("out", half), ("key", kv_half), ("value", kv_half))
    names += (("query", half), ("key", kv_half), ("value", kv_half))
    found, at = {}, 0
    for name, count in names:
        found.setdefault(name, []).append(total[:, at : at + count])
        at += count
    found = {name: jnp.concatenate(parts, axis=1) for name, parts in found.items()}
    return found["query"], found["key"], found["value"], found["out"].T


def plain(names, chunk, backward):
    v = dict(names)
    layer_input, hidden, bits, blocks, size = (v[n] for n in ("layer_input", "hidden", "bits", "blocks", "size"))
    rows, width = layer_input.shape
    half, kv_half, heads = v["half"], v["kv_half"], v["heads"]
    pieces = []
    for i in range(len(CUTS)):
        units, piece = chunk(i, whole=True)
        pieces.append(piece)
    hidden_units, grad_gate_lin, grad_up_lin = units
    two_own = projection([grad_gate_lin, grad_up_lin], [v["w_gate"], v["w_up"]], NT)
    ffn_own = projection([hidden_units], [v["w_down"]], NN)
    grad_attention, grad_attention_t = row_call(
        middle_rows, "middle", [hidden, two_own, to_other_core(two_own), v["cotangent"]], v["gain_two"], [0, 1]
    )
    (output,) = row_call(output_rows, "output", [hidden, ffn_own, to_other_core(ffn_own)], v["gain_two"], [0])
    back_one = backward(0, gatt=grad_attention)
    pieces.append(gradient_pieces(
        bits, blocks, [grad_attention_t, v["act_one_t"]], [v["mixed"], *back_one], [0, 1, 1],
        [((0, half, 0, 0), (half, heads, 0, 1)), ((0, half, half, 0),), ((0, half, half, 1),)],
    ))
    *back_two, one_own = backward(1, *back_one, gatt=grad_attention)
    pieces.append(gradient_pieces(
        bits, blocks, [v["act_one_t"]], back_two, [0, 0], [((0, half, 0, 0),), ((0, half, 0, 1),)]
    ))
    (grad_input,) = row_call(
        input_rows, "input", [layer_input, grad_attention, one_own, to_other_core(one_own)],
        v["attn_gain"], [0],
    )
    total = scatter_sum(jnp.concatenate([p for piece in pieces for p in joined(piece)], axis=1))
    gates, ups, downs = [], [], []
    for low, high in CUTS:
        count = high - low
        parts = jnp.split(total[:, 3 * low : 3 * high], [count, count * 3 // 2, count * 5 // 2], axis=1)
        for found, part in zip((gates, downs, ups, downs), parts):
            found.append(part)
    grad_gate, grad_up = jnp.concatenate(gates, axis=1), jnp.concatenate(ups, axis=1)
    attention = attention_grads(total[:, 3 * CUTS[-1][1] :], half, kv_half)

    def gain_of(gradients, weights, gain):
        count = width // size
        cut = [lax.dynamic_slice_in_dim(v[w], v["me"] * count, count).astype(jnp.float32) for w in weights]
        return gain_gradient(sum(jnp.sum(g * w, axis=1) for g, w in zip(gradients, cut))[None, :], gain, v["index"])

    return (
        output,
        grad_input,
        gain_of(attention[:3], ("w_query", "w_key", "w_value"), v["attn_gain"]),
        *attention,
        gain_of((grad_gate, grad_up), ("w_gate", "w_up"), v["ffn_gain"]),
        grad_gate,
        grad_up,
        jnp.concatenate(downs, axis=1).T,
    )


def per_device(
    layer_input,
    branch_point,
    attn_gain,
    w_query,
    w_key,
    w_value,
    w_out,
    ffn_gain,
    w_gate,
    w_up,
    w_down,
    cotangent,
):
    rows, width = layer_input.shape
    size = lax.axis_size("dp")
    by_kernel = size == KERNEL_BLOCKS
    blocks = KERNEL_BLOCKS
    me = lax.axis_index("dp")
    index = me.reshape(1).astype(jnp.int32)
    bits = jnp.stack([me & 1, me >> 1 & 1, me >> 2 & 3]).astype(jnp.int32)
    rope = rope_tables()
    act_one_t, queries, keys, values, mixed, log_sums, attn_own = attention_forward(
        branch_point, layer_input, attn_gain, w_query, w_key, w_value, w_out, rope
    )
    attn_got = to_other_core(attn_own)
    kv_half = w_key.shape[1] // 2
    w_key_value = jnp.concatenate(
        [w_key[:, :kv_half], w_value[:, :kv_half], w_key[:, kv_half:], w_value[:, kv_half:]], axis=1
    )
    (cot_t,) = row_call(lambda *_: (), "turn", [cotangent], ffn_gain, [2])
    gain_two = ffn_gain
    *units, sent_a, kept_a, sent_b, kept_b, hidden, act_two, act_two_t = ffn_chunk(
        bits, blocks, (after(gain_two, cot_t, w_key_value), layer_input, attn_own, attn_got), cotangent, cot_t,
        w_gate, w_up, w_down, [], 0, CUTS[0][1],
    )
    first_piece = (sent_a, kept_a, sent_b, kept_b)
    heads, kv = mixed.shape[1], w_key.shape[1]
    half = heads // 2
    def chunk(i, *needed, whole=False):
        nonlocal units
        piece = first_piece
        if i > 0:
            low, high = CUTS[i]
            made = ffn_chunk(
                bits, blocks, (after(act_two, *needed), act_two_t), cotangent, cot_t,
                w_gate, w_up, w_down, units, low, high - low,
            )
            units, piece = made[:3], made[3:]
        return (units, piece) if whole else piece

    def backward(part, *needed, gatt=None):
        return attention_backward(
            part, branch_point, after(grad_attention if gatt is None else gatt, *needed), queries, keys, values, log_sums,
            w_out, w_query, w_key_value, rope, list(needed[:2]) if part else [],
        )

    if not by_kernel:
        return plain(locals(), chunk, backward)
    pieces = [chunk(0)]
    one = [first_stage(pieces[0])]
    pieces.append(chunk(1))
    one.append(first_stage(pieces[1]))
    pieces.append(chunk(2, pieces[1]))
    pieces[2], one[0] = after((pieces[2], one[0]))
    joint = sums(bits, second=one[0])
    two = [second_stage(*joint)]
    pieces.append(chunk(3, joint))
    *units, pieces[3], one[1], two[0] = after((*units, pieces[3], one[1], two[0]))
    joint = sums(bits, second=one[1], third=two[0])
    two.append(second_stage(*joint[0]))
    three = [third_stage(*joint[1])]
    one.append(first_stage(after(pieces[2], units)))
    hidden_units, grad_gate_lin, grad_up_lin = units
    two_own = projection(after([grad_gate_lin, grad_up_lin], joint), [w_gate, w_up], NT)
    two_own, three[0] = after((two_own, three[0]))
    two_got = to_other_core(two_own)
    ffn_own = projection([after(hidden_units, two_own)], [w_down], NN)
    ffn_own, one[2], two[1] = after((ffn_own, one[2], two[1]))
    joint = sums(bits, second=one[2], third=two[1], cost=LONG)
    two.append(second_stage(*joint[0]))
    three.append(third_stage(*joint[1]))
    one.append(first_stage(after(pieces[3], ffn_own)))
    grad_attention, grad_attention_t = row_call(
        middle_rows, "middle", [hidden, two_own, two_got, after(cotangent, joint)], gain_two, [0, 1]
    )
    grad_attention, three[0], three[1] = after((grad_attention, three[0], three[1]))
    joint = sums(bits, fourth=(*three[0], *three[1]))
    four = [fourth_stage(*joint)]
    back_one = backward(0, grad_attention, joint)
    back_one, two[2], one[3], four[0] = after((back_one, two[2], one[3], four[0]))
    joint = sums(bits, second=one[3], third=two[2])
    two.append(second_stage(*joint[0]))
    three.append(third_stage(*joint[1]))
    early = gradient_pieces(
        bits, blocks, [after(grad_attention_t, joint), act_one_t], [mixed, *back_one], [0, 1, 1],
        [((0, half, 0, 0), (half, heads, 0, 1)), ((0, half, half, 0),), ((0, half, half, 1),)],
    )
    early, two[3], three[2] = after((early, two[3], three[2]))
    joint = sums(bits, third=two[3], fourth=three[2])
    three.append(third_stage(*joint[0]))
    four.append(fourth_stage(*joint[1]))
    early_one = first_stage(early)
    ffn_got = to_other_core(after(ffn_own, early))
    *back_two, one_own = backward(1, *back_one, early, joint)
    back_two, one_own, early_one, three[3], four[1], ffn_got = after(
        (back_two, one_own, early_one, three[3], four[1], ffn_got)
    )
    one_got = to_other_core(one_own)
    joint = sums(bits, second=early_one, fourth=three[3])
    early_two = second_stage(*joint[0])
    four.append(fourth_stage(*joint[1]))
    late = gradient_pieces(
        bits, blocks, [after(act_one_t, joint)], back_two, [0, 0], [((0, half, 0, 0),), ((0, half, 0, 1),)]
    )
    late, one_got = after((late, one_got))
    late_one = first_stage(late)
    (output,) = row_call(output_rows, "output", [hidden, after(ffn_own, late), ffn_got], gain_two, [0])
    output, early_two, four[2] = after((output, early_two, four[2]))
    joint = sums(bits, third=early_two)
    early_three = third_stage(*joint)
    (grad_input,) = row_call(
        input_rows, "input", [layer_input, after(grad_attention, joint), one_own, one_got],
        attn_gain, [0],
    )
    grad_input, late_one, early_three = after((grad_input, late_one, early_three))
    joint = sums(bits, second=late_one, fourth=early_three)
    late_two = second_stage(*joint[0])
    early_four = fourth_stage(*joint[1])
    *ffn_grads, ffn_products = ffn_sums(index, [w_gate, w_up], after([p for piece in four for p in piece], joint))
    ffn_grads, late_two = after((ffn_grads, late_two))
    grad_gate, grad_up, grad_down = ffn_grads
    joint = sums(bits, third=late_two)
    late_three = third_stage(*joint)
    grad_ffn_gain = gain_gradient(after(ffn_products, joint), ffn_gain, index)
    late_three, early_four, grad_ffn_gain = after((late_three, early_four, grad_ffn_gain))
    joint = sums(bits, fourth=late_three)
    late_four = fourth_stage(*joint)
    products_sum, attention = attention_sums(index, [w_query, w_key, w_value], *early_four, *late_four, kv_half)
    grad_attn_gain = gain_gradient(products_sum, attn_gain, index)
    return (
        output,
        grad_input,
        grad_attn_gain,
        *attention,
        grad_ffn_gain,
        grad_gate,
        grad_up,
        grad_down.T,
    )


def solution(mesh):
    placed = (
        P("dp", None),
        P("dp", None),
        P(),
        P(None, "tensor"),
        P(None, "tensor"),
        P(None, "tensor"),
        P("tensor", None),
        P(),
        P(None, "tensor"),
        P(None, "tensor"),
        P("tensor", None),
        P("dp", None),
    )
    return jax.shard_map(
        per_device,
        mesh=mesh,
        in_specs=placed,
        out_specs=(
            P("dp", None),
            P("dp", None),
            P("dp"),
            P("dp", "tensor"),
            P("dp", "tensor"),
            P("dp", "tensor"),
            P("tensor", "dp"),
            P("dp"),
            P("dp", "tensor"),
            P("dp", "tensor"),
            P("tensor", "dp"),
        ),
        check_vma=False,
    )
```

```python
import functools

import jax
import jax.numpy as jnp
import numpy as np
from jax import lax
from jax.experimental import pallas as pl
from jax.experimental.pallas import tpu as pltpu
from jax.sharding import PartitionSpec as P

HEAD_DIM = 96
PROMPT = 1024
CONT_LEN = 128
CONT = 2
GROUP_TOK = 1280
BLOCK = 256
BLOCKS = GROUP_TOK // BLOCK
LANES = 128
MIB = 1 << 20
VMEM_LIMIT = 64 * MIB
CHEAP = pl.CostEstimate(flops=10**6, bytes_accessed=10**5, transcendentals=0)
epsilon = 1e-05
rope_base = 100000.0
LOG2E = 1.4426950408889634
SCORE_SCALE = HEAD_DIM ** (-0.5)
NT = (((1,), (1,)), ((), ()))
TN = (((0,), (0,)), ((), ()))

LONG = pl.CostEstimate(flops=10**11, bytes_accessed=10**5, transcendentals=0)


def matmul(left, right, dims=(((1,), (0,)), ((), ()))):
    return lax.dot_general(left, right, dims, preferred_element_type=jnp.float32)


HBM = pl.BlockSpec(memory_space=pl.ANY)
SMEM = pl.BlockSpec(memory_space=pltpu.SMEM)
VMEM = pl.BlockSpec(memory_space=pltpu.VMEM)


def start(source, target, sem):
    copy = pltpu.make_async_copy(source, target, sem)
    copy.start()
    return copy


def rows_of(blocks, width):
    return (blocks // 4, 2, 2, None, width)


def rope_tables():
    half = HEAD_DIM // 2
    frequency = rope_base ** (-np.arange(half, dtype=np.float64) * 2.0 / HEAD_DIM)
    angles = np.arange(PROMPT + CONT_LEN, dtype=np.float64)[:, None] * frequency[None, :]
    pad = np.zeros((angles.shape[0], LANES - HEAD_DIM))
    cosine = np.concatenate([np.cos(angles), np.cos(angles), pad], axis=1)
    sine = np.concatenate([-np.sin(angles), np.sin(angles), pad], axis=1)
    return jnp.asarray(np.stack([cosine, sine]), jnp.float32)


def place_rope(branch_ref, table_ref, rope_ref):
    rope_ref[:, :PROMPT, :] = table_ref[:, :PROMPT, :]
    for c in range(CONT):
        rows = pl.ds(PROMPT + c * CONT_LEN, CONT_LEN)
        for i in range(2):
            rope_ref[i, rows, :] = table_ref[i, pl.ds(branch_ref[0, c], CONT_LEN), :]


def lane_ids(shape):
    return lax.broadcasted_iota(jnp.int32, shape, 1)


def swap_halves(head):
    half = HEAD_DIM // 2
    return jnp.where(
        lane_ids(head.shape) < half, pltpu.roll(head, LANES - half, 1), pltpu.roll(head, half, 1)
    )


def take_head(full, h):
    first = h * HEAD_DIM
    start, shift = first // LANES * LANES, first % LANES
    width = LANES if shift + HEAD_DIM <= LANES else 2 * LANES
    part = full[:, start : start + width]
    return part[:, :LANES] if shift == 0 else pltpu.roll(part, width - shift, 1)[:, :LANES]


def join_heads(heads):
    lanes = lane_ids(heads[0].shape)
    out = []
    for i in range(0, len(heads), 4):
        one, two, three = (pltpu.roll(heads[i + j], LANES - 32 * j, 1) for j in (1, 2, 3))
        out.append(jnp.where(lanes < 96, heads[i], one))
        out.append(jnp.where(lanes < 64, one, two))
        out.append(jnp.where(lanes < 32, two, three))
    return jnp.concatenate(out, axis=1)


def own_mask(shape, query_axis, block):
    query = lax.broadcasted_iota(jnp.int32, shape, query_axis) & (BLOCK - 1)
    key = lax.broadcasted_iota(jnp.int32, shape, 1 - query_axis)
    mask = key <= query
    if block * BLOCK >= PROMPT:
        mask = mask & ((key // CONT_LEN) == (query // CONT_LEN))
    return mask


def reach_mask(shape, query_axis, branch_ref):
    query = lax.broadcasted_iota(jnp.int32, shape, query_axis) & (BLOCK - 1)
    key = lax.broadcasted_iota(jnp.int32, shape, 1 - query_axis) + PROMPT // 2
    return key < jnp.where(query < CONT_LEN, branch_ref[0, 0], branch_ref[0, 1])


def attention_forward_kernel(
    branch_ref, gain_ref, *refs,
):
    ins_hbm, outs_hbm, ins, outs, (o_ref, rope_ref, in_sems, x_sems, out_sems, row_sems) = (
        refs[:6], refs[6:13], refs[13:19], refs[19:26], refs[26:],
    )
    x_ref, wq_ref, wk_ref, wv_ref, wo_ref, table_ref = ins
    act_t_ref, q_ref, k_ref, v_ref, mixed_ref, lse_ref, part_ref = outs
    kv_heads = k_ref.shape[0]
    group = 2 * BLOCK

    def x_in(i):
        rows = pl.ds(pl.multiple_of(i * BLOCK, BLOCK), BLOCK)
        return pltpu.make_async_copy(ins_hbm[0].at[rows], x_ref.at[rows], x_sems.at[i])

    def rows_out(n, which, i):
        rows = pl.ds(pl.multiple_of(i * BLOCK, BLOCK), BLOCK)
        return pltpu.make_async_copy(outs[n].at[rows], outs_hbm[n].at[rows], row_sems.at[which, i])

    x_in(0).start()
    loads = {n: start(ins_hbm[n], ins[n], in_sems.at[n]) for n in (1, 5, 2, 3)}
    for i in range(1, BLOCKS):
        x_in(i).start()
    loads[4] = start(ins_hbm[4], wo_ref, in_sems.at[4])
    for n in (5, 1, 2, 3):
        loads[n].wait()
    place_rope(branch_ref, table_ref, rope_ref)

    def project(i, carry):
        rows = pl.ds(pl.multiple_of(i * BLOCK, BLOCK), BLOCK)
        x_in(i).wait()
        x = x_ref[rows, :].astype(jnp.float32)
        norm = lax.rsqrt(jnp.mean(x * x, axis=-1, keepdims=True) + epsilon)
        act = x * norm * gain_ref[...][None, :]
        act_t_ref[:, rows] = act.T.astype(jnp.bfloat16)
        act = act.astype(jnp.bfloat16)
        cosine, sine = rope_ref[0, rows, :], rope_ref[1, rows, :]
        full = matmul(act, wq_ref[...])
        for h in range(2 * kv_heads):
            head = take_head(full, h)
            rotated = head * cosine + swap_halves(head) * sine
            q_ref[h // 2, i, pl.ds(h % 2 * BLOCK, BLOCK), :] = rotated.astype(jnp.bfloat16)
        full = matmul(act, wk_ref[...])
        for h in range(kv_heads):
            head = take_head(full, h)
            rotated = head * cosine + swap_halves(head) * sine
            k_ref[h, rows, :] = rotated.astype(jnp.bfloat16)
        full = matmul(act, wv_ref[...])
        lanes = lane_ids((BLOCK, LANES))
        for h in range(kv_heads):
            head = jnp.where(lanes < HEAD_DIM, take_head(full, h), 0.0)
            v_ref[h, rows, :] = jnp.where(lanes == HEAD_DIM, 1.0, head).astype(jnp.bfloat16)
        return carry

    lax.fori_loop(0, BLOCKS, project, 0)
    stores = [start(outs[n], outs_hbm[n], out_sems.at[n]) for n in range(4)]
    factor = SCORE_SCALE * LOG2E

    def attend(h, carry):
        for i in range(BLOCKS):
            query = q_ref[h, i]
            before = i * BLOCK
            own = matmul(query, k_ref[h, before : before + BLOCK], NT)
            own = jnp.where(own_mask(own.shape, 0, i), own, -1e30)
            largest = jnp.max(own, axis=-1, keepdims=True)
            spans = []
            if i > 0:
                cuts = [0, before] if before < PROMPT else [0, PROMPT // 2, PROMPT]
                for low, high in zip(cuts[:-1], cuts[1:]):
                    scores = matmul(query, k_ref[h, low:high], NT)
                    if before >= PROMPT and low > 0:
                        scores = jnp.where(reach_mask(scores.shape, 0, branch_ref), scores, -1e30)
                    largest = jnp.maximum(largest, jnp.max(scores, axis=-1, keepdims=True))
                    spans.append((low, high, scores))
            shift = largest * factor
            probs = jnp.exp2(own * factor - shift).astype(jnp.bfloat16)
            total = matmul(probs, v_ref[h, before : before + BLOCK])
            for low, high, scores in spans:
                probs = jnp.exp2(scores * factor - shift).astype(jnp.bfloat16)
                total += matmul(probs, v_ref[h, low:high])
            sums = total[:, HEAD_DIM : HEAD_DIM + 1]
            mixed = total / sums
            for g in range(2):
                o_ref[2 * h + g, before : before + BLOCK, :] = mixed[g * BLOCK : (g + 1) * BLOCK]
            logs = shift + jnp.log2(sums)
            lse_ref[h, i] = jnp.broadcast_to(logs, (group, LANES)).T[0:1, :]
        return carry

    lax.fori_loop(0, kv_heads, attend, 0)
    stores.append(start(lse_ref, outs_hbm[5], out_sems.at[5]))
    loads[4].wait()

    def finish(i, carry):
        rows = pl.ds(pl.multiple_of(i * BLOCK, BLOCK), BLOCK)
        mixed = join_heads([o_ref[h, rows, :] for h in range(2 * kv_heads)]).astype(jnp.bfloat16)
        mixed_ref[rows, :] = mixed
        part_ref[rows, :] = matmul(mixed, wo_ref[...]).astype(jnp.bfloat16)
        rows_out(4, 0, i).start()
        rows_out(6, 1, i).start()
        return carry

    lax.fori_loop(0, BLOCKS, finish, 0)
    for copy in stores:
        copy.wait()
    for i in range(BLOCKS):
        rows_out(4, 0, i).wait()
        rows_out(6, 1, i).wait()


def attention_forward(branch, x, gain, wq, wk, wv, wo, rope):
    kv_heads = wk.shape[1] // HEAD_DIM
    rows, width = x.shape
    bf = jnp.bfloat16
    ins = (x, wq, wk, wv, wo, rope)
    outs = (
        jax.ShapeDtypeStruct((width, rows), bf),
        jax.ShapeDtypeStruct((kv_heads, BLOCKS, 2 * BLOCK, LANES), bf),
        jax.ShapeDtypeStruct((kv_heads, rows, LANES), bf),
        jax.ShapeDtypeStruct((kv_heads, rows, LANES), bf),
        jax.ShapeDtypeStruct((rows, wq.shape[1]), bf),
        jax.ShapeDtypeStruct((kv_heads, BLOCKS, 1, 2 * BLOCK), jnp.float32),
        jax.ShapeDtypeStruct((rows, width), bf),
    )
    return pl.pallas_call(
        attention_forward_kernel,
        out_shape=outs,
        in_specs=[SMEM, VMEM] + [HBM] * 6,
        out_specs=[HBM] * 7,
        scratch_shapes=[pltpu.VMEM(a.shape, a.dtype) for a in ins + outs]
        + [
            pltpu.VMEM((2 * kv_heads, rows, LANES), jnp.float32),
            pltpu.VMEM((2, rows, LANES), jnp.float32),
            pltpu.SemaphoreType.DMA((6,)),
            pltpu.SemaphoreType.DMA((BLOCKS,)),
            pltpu.SemaphoreType.DMA((6,)),
            pltpu.SemaphoreType.DMA((2, BLOCKS)),
        ],
        compiler_params=pltpu.CompilerParams(vmem_limit_bytes=VMEM_LIMIT),
        cost_estimate=CHEAP,
        name="attention_forward",
    )(branch, gain, *ins)


def attention_backward_kernel(
    part, branch_ref, *refs
):
    def cut(count):
        nonlocal refs
        head, refs = refs[:count], refs[count:]
        return head

    count, made = (11, 3) if part else (7, 2)
    ins_hbm, outs_hbm, ins, outs = cut(count), cut(made), cut(count), cut(made)
    do_ref, dq_ref, dk_ref, dv_ref, rope_ref, in_sems, gatt_sems, row_sems = refs
    gatt_ref, wo_ref, q_ref, k_ref, v_ref, lse_ref, table_ref = ins[:7]
    wq_ref, wkv_ref, *first_ref = ins[7:] if part else (None, None)
    gq_ref, gkv_ref = outs[:2]
    part_ref = outs[2] if part else None
    kv_heads = k_ref.shape[0]
    group = 2 * BLOCK
    factor = SCORE_SCALE * LOG2E

    def gatt_in(i):
        rows = pl.ds(pl.multiple_of(i * BLOCK, BLOCK), BLOCK)
        return pltpu.make_async_copy(ins_hbm[0].at[rows], gatt_ref.at[rows], gatt_sems.at[i])

    def rows_out(n, i):
        rows = pl.ds(pl.multiple_of(i * BLOCK, BLOCK), BLOCK)
        return pltpu.make_async_copy(outs[n].at[rows], outs_hbm[n].at[rows], row_sems.at[n, i])

    loads = []
    for n in range(1, count):
        size = ins[n].shape[0]
        source = ins_hbm[n].at[pl.ds(part * size, size)] if n < 6 else ins_hbm[n]
        loads.append(start(source, ins[n], in_sems.at[n]))
        if n == 1:
            for i in range(BLOCKS):
                gatt_in(i).start()
    loads[0].wait()

    def project(i, carry):
        rows = pl.ds(pl.multiple_of(i * BLOCK, BLOCK), BLOCK)
        gatt_in(i).wait()
        full = matmul(gatt_ref[rows, :], wo_ref[...], NT)
        lanes = lane_ids((BLOCK, LANES))
        for h in range(2 * kv_heads):
            head = jnp.where(lanes < HEAD_DIM, take_head(full, h), 0.0)
            do_ref[h // 2, i, pl.ds(h % 2 * BLOCK, BLOCK), :] = head.astype(jnp.bfloat16)
        return carry

    lax.fori_loop(0, BLOCKS, project, 0)
    for copy in loads[1:6]:
        copy.wait()
    place_rope(branch_ref, table_ref, rope_ref)

    def attend(h, carry):
        for i in reversed(range(BLOCKS)):
            query, grad, logs = q_ref[h, i], do_ref[h, i], lse_ref[h, i]
            before = i * BLOCK
            cuts = [(before, before + BLOCK)]
            if i > 0 and before < PROMPT:
                cuts += [(0, before)]
            elif i > 0:
                cuts += [(0, PROMPT // 2), (PROMPT // 2, PROMPT)]
            spans, weighted = [], 0.0
            for low, high in cuts:
                scores = matmul(k_ref[h, low:high], query, NT)
                probs = jnp.exp2(scores * factor - logs)
                if low == before:
                    probs = jnp.where(own_mask(probs.shape, 1, i), probs, 0.0)
                elif before >= PROMPT and low > 0:
                    probs = jnp.where(reach_mask(probs.shape, 1, branch_ref), probs, 0.0)
                grad_probs = matmul(v_ref[h, low:high], grad, NT)
                weighted += jnp.sum(probs * grad_probs, axis=0, keepdims=True)
                spans.append((low, high, probs, grad_probs))
            grad_query = jnp.zeros((LANES, group), jnp.float32)
            for low, high, probs, grad_probs in spans:
                grad_scores = (probs * (grad_probs - weighted)).astype(jnp.bfloat16)
                grad_query += matmul(k_ref[h, low:high], grad_scores, TN)
                grad_key = matmul(grad_scores, query)
                grad_value = matmul(probs.astype(jnp.bfloat16), grad)
                if before >= PROMPT:
                    dk_ref[h, low:high] = grad_key
                    dv_ref[h, low:high] = grad_value
                else:
                    dk_ref[h, low:high] += grad_key
                    dv_ref[h, low:high] += grad_value
            dq_ref[h, i] = grad_query.T
        return carry

    lax.fori_loop(0, kv_heads, attend, 0)
    for copy in loads[6:]:
        copy.wait()

    def finish(i, carry):
        rows = pl.ds(pl.multiple_of(i * BLOCK, BLOCK), BLOCK)
        cosine, sine = rope_ref[0, rows, :] * SCORE_SCALE, rope_ref[1, rows, :] * SCORE_SCALE
        heads = []
        for h in range(2 * kv_heads):
            head = dq_ref[h // 2, i, pl.ds(h % 2 * BLOCK, BLOCK), :]
            heads.append(head * cosine - swap_halves(head) * sine)
        grad_q = join_heads(heads).astype(jnp.bfloat16)
        heads = []
        for h in range(kv_heads):
            head = dk_ref[h, rows, :]
            heads.append(head * cosine - swap_halves(head) * sine)
        heads += [dv_ref[h, rows, :] for h in range(kv_heads)]
        grad_kv = join_heads(heads).astype(jnp.bfloat16)
        gq_ref[rows, :] = grad_q
        gkv_ref[rows, :] = grad_kv
        if part:
            grad_q = jnp.concatenate([first_ref[0][rows, :], grad_q], axis=1)
            grad_kv = jnp.concatenate([first_ref[1][rows, :], grad_kv], axis=1)
            total = matmul(grad_q, wq_ref[...], NT) + matmul(grad_kv, wkv_ref[...], NT)
            part_ref[rows, :] = total.astype(jnp.bfloat16)
        for n in range(made):
            rows_out(n, i).start()
        return carry

    lax.fori_loop(0, BLOCKS, finish, 0)
    for n in range(made):
        for i in range(BLOCKS):
            rows_out(n, i).wait()


def attention_backward(part, branch, gatt, q, k, v, lse, wo, wq, wkv, rope, first):
    kv_heads = k.shape[0] // 2
    rows, width = gatt.shape
    bf = jnp.bfloat16
    small = jax.ShapeDtypeStruct((rows, wq.shape[1] // 2), bf)
    outs = (small, small) + ((jax.ShapeDtypeStruct((rows, width), bf),) if part else ())
    ins = (gatt, wo, q, k, v, lse, rope) + ((wq, wkv, *first) if part else ())

    def held(n, array):
        halves = (array.shape[0] // 2,) + array.shape[1:]
        return pltpu.VMEM(halves if 0 < n < 6 else array.shape, array.dtype)

    return pl.pallas_call(
        functools.partial(attention_backward_kernel, part),
        out_shape=outs,
        in_specs=[SMEM] + [HBM] * len(ins),
        out_specs=[HBM] * len(outs),
        scratch_shapes=[held(n, a) for n, a in enumerate(ins)]
        + [pltpu.VMEM(o.shape, bf) for o in outs]
        + [
            pltpu.VMEM((kv_heads, BLOCKS, 2 * BLOCK, LANES), bf),
            pltpu.VMEM((kv_heads, BLOCKS, 2 * BLOCK, LANES), jnp.float32),
            pltpu.VMEM((kv_heads, rows, LANES), jnp.float32),
            pltpu.VMEM((kv_heads, rows, LANES), jnp.float32),
            pltpu.VMEM((2, rows, LANES), jnp.float32),
            pltpu.SemaphoreType.DMA((len(ins),)),
            pltpu.SemaphoreType.DMA((BLOCKS,)),
            pltpu.SemaphoreType.DMA((len(outs), BLOCKS)),
        ],
        compiler_params=pltpu.CompilerParams(vmem_limit_bytes=VMEM_LIMIT),
        cost_estimate=CHEAP,
        name="attention_backward",
    )(branch, *ins)


KERNEL_BLOCKS = 16
WIDE = 512
FEW = 16
CUTS = ((0, 512), (512, 1024), (1024, 1536), (1536, 2048))


NN = (((1,), (0,)), ((), ()))


def split_copies(tile, low, high, at, sent, kept, axis, mine, sems, k, begin=True):
    copies = []
    for half, target in ((1 - mine, sent), (mine, kept)):
        part = tile.at[:, :, half] if axis == 0 else tile.at[:, half]
        copy = pltpu.make_async_copy(
            part.at[:, :, :, pl.ds(low, high - low)],
            target.at[:, :, :, pl.ds(at, high - low)],
            sems.at[k + len(copies)],
        )
        if begin:
            copy.start()
        copies.append(copy)
    return copies


def gradient_tile(tile, left, right, arrive=None):
    parts = 1 if arrive is None else 2
    zs, tall = tile.shape[0] // parts, left.shape[0] // parts

    def step(i, carry):
        if arrive is not None:
            arrive(i)
        out = matmul(left[pl.ds(pl.multiple_of(i * tall, tall), tall), :], right[...])
        tile[pl.ds(i * zs, zs)] = out.astype(jnp.bfloat16).reshape((zs,) + tile.shape[1:])
        return carry

    lax.fori_loop(0, parts, step, 0)


def ffn_kernel(first, count, norm, *refs):
    if norm:
        (bits_ref, gain_ref, *sums_hbm, cot_hbm, cot_t_hbm, wg_hbm, wu_hbm, wd_hbm), refs = refs[:10], refs[10:]
    else:
        (bits_ref, act_hbm, cot_hbm, act_t_hbm, cot_t_hbm, wg_hbm, wu_hbm, wd_hbm), refs = refs[:8], refs[11:]
    (hidden_hbm, ggate_hbm, gup_hbm, sent_a, kept_a, sent_b, kept_b), refs = refs[:7], refs[7:]
    if norm:
        (state_hbm, act_hbm, act_t_hbm, state, *held, sum_sems, made_sems), refs = refs[:9], refs[9:]
    act, cot, lefts, wg, wu, wd, lines, tiles, in_sems, row_sems, out_sems = refs
    units = pl.ds(first, count)
    tall = act.shape[0] // 2

    def rows_in(i, which):
        rows = pl.ds(pl.multiple_of(i * tall, tall), tall)
        source, target = ((act_hbm, act), (cot_hbm, cot))[which]
        return pltpu.make_async_copy(source.at[rows], target.at[rows], row_sems.at[which, i])

    def sums_in(which, i):
        rows = pl.ds(pl.multiple_of(i * BLOCK, BLOCK), BLOCK)
        return pltpu.make_async_copy(sums_hbm[which].at[rows], held[which].at[rows], sum_sems.at[which, i])

    if norm:
        for i in range(act.shape[0] // BLOCK):
            for which in range(3):
                sums_in(which, i).start()
    weights = [start(wg_hbm.at[:, units], wg, in_sems.at[0])]
    if not norm:
        rows_in(0, 0).start()
    weights.append(start(wu_hbm.at[:, units], wu, in_sems.at[1]))
    weights.append(start(wd_hbm.at[units], wd, in_sems.at[2]))
    rows_in(0, 1).start()
    if not norm:
        rows_in(1, 0).start()
    rows_in(1, 1).start()
    sources = [start(cot_t_hbm, lefts.at[0], in_sems.at[3])]
    if not norm:
        sources.append(start(act_t_hbm, lefts.at[1], in_sems.at[4]))

    def norm_step(i, carry):
        for which in range(3):
            sums_in(which, i).wait()

        def few_step(j, carry):
            few = pl.ds(pl.multiple_of(i * BLOCK + j * FEW, FEW), FEW)
            total, rows = norm_rows(*(ref[few, :].astype(jnp.float32) for ref in held), gain_ref[...][None, :])
            state[few, :] = total.astype(jnp.bfloat16)
            act[few, :] = rows.astype(jnp.bfloat16)
            return carry

        lax.fori_loop(0, BLOCK // FEW, few_step, 0, unroll=4)
        rows = pl.ds(pl.multiple_of(i * BLOCK, BLOCK), BLOCK)
        lefts[1, :, rows] = act[rows, :].astype(jnp.float32).T.astype(jnp.bfloat16)
        return carry

    made = []
    if norm:
        lax.fori_loop(0, act.shape[0] // BLOCK, norm_step, 0)
        pairs = ((state, state_hbm), (act, act_hbm), (lefts.at[1], act_t_hbm))
        made = [start(*pair, made_sems.at[i]) for i, pair in enumerate(pairs)]
    weights[0].wait()

    def units_step(i, carry):
        rows = pl.ds(pl.multiple_of(i * tall, tall), tall)
        if not norm:
            rows_in(i, 0).wait()
        gate = matmul(act[rows, :], wg[...])

        @pl.when(i == 0)
        def _():
            weights[1].wait()
            weights[2].wait()

        up = matmul(act[rows, :], wu[...])
        rows_in(i, 1).wait()
        grad = matmul(cot[rows, :], wd[...], NT)
        sigmoid = 1.0 / (1.0 + jnp.exp(-gate))
        silu = gate * sigmoid
        lines[0, rows, :] = (silu * up).astype(jnp.bfloat16)
        lines[1, rows, :] = (grad * up * (sigmoid * (1.0 + gate * (1.0 - sigmoid)))).astype(jnp.bfloat16)
        lines[2, rows, :] = (grad * silu).astype(jnp.bfloat16)
        return carry

    lax.fori_loop(0, 2, units_step, 0)
    copies = [
        start(lines.at[0], hidden_hbm.at[:, units], out_sems.at[0]),
        start(lines.at[1], ggate_hbm.at[:, units], out_sems.at[1]),
        start(lines.at[2], gup_hbm.at[:, units], out_sems.at[2]),
    ]
    half = count // 2
    x, y = bits_ref[0], bits_ref[1]
    for copy in sources:
        copy.wait()

    def stores(t, begin):
        if t == 0:
            return split_copies(tiles.at[0], 0, half, count, sent_a, kept_a, 0, x, out_sems, 3, begin) + split_copies(
                tiles.at[0], half, count, count, sent_b, kept_b, 1, y, out_sems, 5, begin
            )
        if t == 1:
            return split_copies(tiles.at[1], 0, count, 0, sent_a, kept_a, 0, x, out_sems, 7, begin)
        return split_copies(tiles.at[2], 0, count, 0, sent_b, kept_b, 1, y, out_sems, 9, begin)

    def tile_step(t, carry):
        gradient_tile(tiles.at[t], lefts.at[jnp.minimum(t, 1)], lines.at[t])
        for one in range(3):

            @pl.when(t == one)
            def _(one=one):
                stores(one, True)

        return carry

    lax.fori_loop(0, 3, tile_step, 0)
    copies += made
    for t in range(3):
        copies += stores(t, False)
    for copy in copies:
        copy.wait()


def ffn_chunk(bits, blocks, act, cot, cot_t, wg, wu, wd, before, first, count):
    norm = not before
    rows, width = cot.shape
    bf = jnp.bfloat16
    piece = jax.ShapeDtypeStruct((blocks // 4, 2, width // blocks, count + count // 2), bf)
    units = jax.ShapeDtypeStruct((rows, wg.shape[1]), bf)
    by_rows = jax.ShapeDtypeStruct((rows, width), bf)
    outs = (units,) * 3 + (piece,) * 4
    ins = (cot, cot_t, wg, wu, wd)
    if norm:
        outs += (by_rows, by_rows, jax.ShapeDtypeStruct((width, rows), bf))
        ins = (*act, *ins)
    else:
        ins = (act[0], cot, act[1], cot_t, wg, wu, wd, *before)
    return pl.pallas_call(
        functools.partial(ffn_kernel, first, count, norm),
        out_shape=outs,
        in_specs=[SMEM] + [VMEM] * norm + [HBM] * (len(ins) - norm),
        out_specs=[HBM] * len(outs),
        scratch_shapes=(
            [pltpu.VMEM((rows, width), bf)] * 4
            + [pltpu.SemaphoreType.DMA((3, rows // BLOCK)), pltpu.SemaphoreType.DMA((3,))]
        ) * norm
        + [
            pltpu.VMEM((rows, width), bf),
            pltpu.VMEM((rows, width), bf),
            pltpu.VMEM((2, width, rows), bf),
            pltpu.VMEM((width, count), bf),
            pltpu.VMEM((width, count), bf),
            pltpu.VMEM((count, width), bf),
            pltpu.VMEM((3, rows, count), bf),
            pltpu.VMEM((3, blocks // 4, 2, 2, width // blocks, count), bf),
            pltpu.SemaphoreType.DMA((5,)),
            pltpu.SemaphoreType.DMA((2, 2)),
            pltpu.SemaphoreType.DMA((11,)),
        ],
        input_output_aliases={8 + i: i for i in range(len(before))},
        compiler_params=pltpu.CompilerParams(vmem_limit_bytes=VMEM_LIMIT),
        cost_estimate=CHEAP,
        name="ffn_chunk",
    )(bits, *ins)


def gradient_kernel(lefts, parts, bits_ref, *refs):
    def cut(count):
        nonlocal refs
        head, refs = refs[:count], refs[count:]
        return head

    left_hbm, right_hbm, pieces = cut(lefts), cut(len(parts)), cut(4)
    left, right, tiles, (in_sems, out_sems) = cut(lefts), cut(len(parts)), cut(len(parts)), refs
    tall = left[0].shape[0] // 2

    def left_in(which, i):
        rows = pl.ds(pl.multiple_of(i * tall, tall), tall)
        return pltpu.make_async_copy(left_hbm[which].at[rows], left[which].at[rows], in_sems.at[2 * which + i])

    right_in, copies, seen = [], [], set()
    for i, (which, _) in enumerate(parts):
        if which not in seen:
            left_in(which, 0).start()
        right_in.append(start(right_hbm[i], right[i], in_sems.at[2 * lefts + i]))
        if which not in seen:
            left_in(which, 1).start()
        seen.add(which)
    for i, (which, places) in enumerate(parts):
        right_in[i].wait()
        arrive = functools.partial(lambda which, i: left_in(which, i).wait(), which) if which in seen else None
        seen.discard(which)
        gradient_tile(tiles[i], left[which], right[i], arrive)
        for low, high, at, first in places:
            sent, kept = pieces[2 * first], pieces[2 * first + 1]
            copies += split_copies(tiles[i], low, high, at, sent, kept, first, bits_ref[first], out_sems, len(copies))
    for copy in copies:
        copy.wait()


def gradient_pieces(bits, blocks, lefts, rights, which, places):
    width, rows = lefts[0].shape
    bf = jnp.bfloat16
    flat = [place for part in places for place in part]
    widths = [sum(high - low for low, high, _, first in flat if first == axis) for axis in (0, 1)]
    pieces = [jax.ShapeDtypeStruct((blocks // 4, 2, width // blocks, w), bf) for w in widths for _ in range(2)]
    return pl.pallas_call(
        functools.partial(gradient_kernel, len(lefts), tuple(zip(which, places))),
        out_shape=tuple(pieces),
        in_specs=[SMEM] + [HBM] * (len(lefts) + len(rights)),
        out_specs=[HBM] * 4,
        scratch_shapes=[pltpu.VMEM(a.shape, bf) for a in (*lefts, *rights)]
        + [pltpu.VMEM((blocks // 4, 2, 2, width // blocks, r.shape[1]), bf) for r in rights]
        + [pltpu.SemaphoreType.DMA((2 * len(lefts) + len(rights),)), pltpu.SemaphoreType.DMA((2 * len(flat),))],
        compiler_params=pltpu.CompilerParams(vmem_limit_bytes=VMEM_LIMIT),
        cost_estimate=CHEAP,
        name="gradient_pieces",
    )(bits, *lefts, *rights)


def projection_kernel(dims, count, *refs):
    left_hbm, right_hbm, out_hbm, refs = refs[:count], refs[count : 2 * count], refs[2 * count], refs[2 * count + 1 :]
    left, right, (out, left_sems, right_sems, out_sems) = refs[:count], refs[count : 2 * count], refs[2 * count :]
    turned = dims is NT
    rows, width = out.shape
    tall = rows // 2

    def columns(ref, n):
        cut = pl.ds(pl.multiple_of(n * WIDE, WIDE), WIDE)
        return ref.at[cut, :] if turned else ref.at[:, cut]

    def right_in(p, n):
        return pltpu.make_async_copy(columns(right_hbm[p], n), columns(right[p], n), right_sems.at[p, n])

    def left_in(p, i):
        cut = pl.ds(pl.multiple_of(i * tall, tall), tall)
        return pltpu.make_async_copy(left_hbm[p].at[cut], left[p].at[cut], left_sems.at[p, i])

    def out_copy(n):
        wide = pl.ds(pl.multiple_of(n * WIDE, WIDE), WIDE)
        return pltpu.make_async_copy(out.at[:, wide], out_hbm.at[:, wide], out_sems.at[n])

    for p in range(count):
        right_in(p, 0).start()
        left_in(p, 0).start()
    for p in range(count):
        left_in(p, 1).start()
    for n in range(1, width // WIDE):
        for p in range(count):
            right_in(p, n).start()

    def step(j, carry):
        n, i = j // 2, j % 2

        @pl.when(i == 0)
        def _():
            for p in range(count):
                right_in(p, n).wait()

        @pl.when(n == 0)
        def _():
            for p in range(count):
                left_in(p, i).wait()

        cut = pl.ds(pl.multiple_of(i * tall, tall), tall)
        total = sum(matmul(left[p][cut, :], columns(right[p], n)[...], dims) for p in range(count))
        out[cut, pl.ds(pl.multiple_of(n * WIDE, WIDE), WIDE)] = total.astype(jnp.bfloat16)

        @pl.when(i == 1)
        def _():
            out_copy(n).start()

        return carry

    lax.fori_loop(0, 2 * width // WIDE, step, 0)
    for n in range(width // WIDE):
        out_copy(n).wait()


def projection(lefts, rights, dims):
    rows = lefts[0].shape[0]
    width = rights[0].shape[0 if dims is NT else 1]
    bf, count = jnp.bfloat16, len(lefts)
    return pl.pallas_call(
        functools.partial(projection_kernel, dims, count),
        out_shape=jax.ShapeDtypeStruct((rows, width), bf),
        in_specs=[HBM] * (2 * count),
        out_specs=HBM,
        scratch_shapes=[pltpu.VMEM(a.shape, bf) for a in (*lefts, *rights)]
        + [
            pltpu.VMEM((rows, width), bf),
            pltpu.SemaphoreType.DMA((count, 2)),
            pltpu.SemaphoreType.DMA((count, width // WIDE)),
            pltpu.SemaphoreType.DMA((width // WIDE,)),
        ],
        compiler_params=pltpu.CompilerParams(vmem_limit_bytes=VMEM_LIMIT),
        cost_estimate=CHEAP,
        name="projection",
    )(*lefts, *rights)


def add_two(one, two):
    return one.astype(jnp.float32) + two.astype(jnp.float32)


def second_steps(bits_ref, ins_hbm, ins, outs_hbm, outs):
    steps = []
    for z in range(outs[0].shape[0]):

        def compute(z=z):
            for i in range(2):
                kept, got, send, keep, mine = *ins[2 * i : 2 * i + 2], *outs[2 * i : 2 * i + 2], bits_ref[1 - i]
                send[z] = kept[z, 1 - mine] + got[z, 1 - mine]
                keep[z] = kept[z, mine] + got[z, mine]

        steps.append((
            [(a.at[z], b.at[z]) for a, b in zip(ins_hbm, ins)],
            compute,
            [(a.at[z], b.at[z]) for a, b in zip(outs, outs_hbm)],
        ))
    return steps


def third_steps(bits_ref, ins_hbm, ins, outs_hbm, outs):
    low = bits_ref[2] & 1
    steps = []
    for half, out, out_hbm in zip((1 - low, low), outs, outs_hbm):
        for high in range(2):
            block = 2 * high + half

            def compute(block=block, out=out, high=high):
                width = ins[0].shape[-1]
                out[high, :, :width] = ins[0][block] + ins[1][block]
                out[high, :, width:] = ins[2][block] + ins[3][block]

            steps.append((
                [(a.at[block], b.at[block]) for a, b in zip(ins_hbm, ins)], compute, [(out.at[high], out_hbm.at[high])]
            ))
    return steps


def fourth_steps(bits_ref, ins_hbm, ins, outs_hbm, outs):
    high = bits_ref[2] >> 1
    steps = []
    for block, out, out_hbm in zip((1 - high, high), outs, outs_hbm):

        def compute(block=block, out=out):
            for i in range(0, len(ins), 2):
                width = ins[i].shape[-1]
                out[:, i // 2 * width : (i // 2 + 1) * width] = ins[i][block] + ins[i + 1][block]

        steps.append((
            [(a.at[block], b.at[block]) for a, b in zip(ins_hbm, ins)], compute, [(out, out_hbm)]
        ))
    return steps


def sums_kernel(jobs, bits_ref, *refs):
    count, made = sum(j[1] for j in jobs), sum(j[2] for j in jobs)
    ins_hbm, outs_hbm, refs = refs[:count], refs[count : count + made], refs[count + made :]
    ins, outs, (in_sems, out_sems) = refs[:count], refs[count : count + made], refs[count + made :]
    steps = []
    for build, n, m in jobs:
        steps += build(bits_ref, ins_hbm[:n], ins[:n], outs_hbm[:m], outs[:m])
        ins_hbm, ins, outs_hbm, outs = ins_hbm[n:], ins[n:], outs_hbm[m:], outs[m:]
    stream(steps, in_sems, out_sems)


def sums(bits, second=None, third=None, fourth=None, cost=None):
    jobs, ins, outs = [], [], []
    if second is not None:
        made = [a.shape[:1] + a.shape[2:] for a in second]
        jobs.append((second_steps, 4, 4))
        ins, outs = ins + list(second), outs + made
    if third is not None:
        made = [(2, third[0].shape[1], third[0].shape[2] + third[2].shape[2])] * 2
        jobs.append((third_steps, 4, 2))
        ins, outs = ins + list(third), outs + made
    if fourth is not None:
        made = [(fourth[0].shape[1], sum(a.shape[2] for a in fourth[::2]))] * 2
        jobs.append((fourth_steps, len(fourth), 2))
        ins, outs = ins + list(fourth), outs + made
    bf = jnp.bfloat16
    results = pl.pallas_call(
        functools.partial(sums_kernel, tuple(jobs)),
        out_shape=tuple(jax.ShapeDtypeStruct(o, bf) for o in outs),
        in_specs=[SMEM] + [HBM] * len(ins),
        out_specs=[HBM] * len(outs),
        scratch_shapes=[pltpu.VMEM(a.shape, bf) for a in ins]
        + [pltpu.VMEM(o, bf) for o in outs]
        + [pltpu.SemaphoreType.DMA((4 * len(ins),)), pltpu.SemaphoreType.DMA((4 * len(outs),))],
        compiler_params=pltpu.CompilerParams(vmem_limit_bytes=VMEM_LIMIT),
        cost_estimate=cost or CHEAP,
        name="sums",
    )(bits, *ins)
    split = []
    for _, _, m in jobs:
        split.append(results[:m])
        results = results[m:]
    return split[0] if len(split) == 1 else split


def over_dp(array, flip):
    size = lax.axis_size("dp")
    return lax.ppermute(array, "dp", [(i, i ^ flip) for i in range(size)])


def after(arrays, *needed):
    return lax.optimization_barrier((arrays, needed))[0]


def first_stage(pieces):
    sent_a, kept_a, sent_b, kept_b = pieces
    return (kept_a, over_dp(sent_a, 1), kept_b, over_dp(sent_b, 2))


def second_stage(sent_a, kept_a, sent_b, kept_b):
    return (kept_a, over_dp(sent_a, 2), kept_b, over_dp(sent_b, 1))


def third_stage(send, keep):
    return (keep, over_dp(send, 4))


def fourth_stage(send, keep):
    return (keep, over_dp(send, 8))


def attention_sums_kernel(kv_half, index_ref, *refs):
    weights, refs = refs[:3], refs[3:]
    kept_a, got_a, kept_b, got_b, query_ref, key_ref, value_ref, out_ref, gain_ref, *helds, sems = refs
    copies = weight_rows(index_ref, weights, helds, sems)
    half = query_ref.shape[1] // 2
    first, second = add_two(kept_a[...], got_a[...]), add_two(kept_b[...], got_b[...])
    out_ref[:, :half] = first[:, :half]
    out_ref[:, half:] = first[:, 2 * half : 3 * half]
    query_ref[:, :half] = first[:, half : 2 * half]
    query_ref[:, half:] = second[:, :half]
    first, second = first[:, 3 * half :], second[:, half:]
    key_ref[...] = jnp.concatenate([first[:, :kv_half], second[:, :kv_half]], axis=1)
    value_ref[...] = jnp.concatenate([first[:, kv_half:], second[:, kv_half:]], axis=1)
    for copy in copies:
        copy.wait()
    gain_ref[...] = as_row(
        sum(products(ref[...], held[...]) for ref, held in zip((query_ref, key_ref, value_ref), helds))
    )


def attention_sums(index, weights, kept_a, got_a, kept_b, got_b, kv_half):
    rows, heads = kept_b.shape
    shapes = [(rows, heads), (rows, heads // 2), (rows, heads // 2), (rows, heads), (1, LANES)]
    *others, out, gain = pl.pallas_call(
        functools.partial(attention_sums_kernel, kv_half),
        out_shape=tuple(jax.ShapeDtypeStruct(shape, jnp.float32) for shape in shapes),
        in_specs=[SMEM] + [HBM] * 3 + [VMEM] * 4,
        out_specs=[VMEM] * 5,
        scratch_shapes=[pltpu.VMEM((rows, w.shape[1]), w.dtype) for w in weights] + [pltpu.SemaphoreType.DMA((3,))],
        compiler_params=pltpu.CompilerParams(vmem_limit_bytes=VMEM_LIMIT),
        cost_estimate=CHEAP,
        name="attention_sums",
    )(index, *weights, kept_a, got_a, kept_b, got_b)
    return gain, (*others, out.T)


def joined(pieces):
    sent_a, kept_a, sent_b, kept_b = pieces
    first, second = lax.axis_index("dp") & 1, lax.axis_index("dp") >> 1 & 1
    out = []
    for sent, kept, axis, mine in ((sent_a, kept_a, 2, first), (sent_b, kept_b, 1, second)):
        low = jnp.where(mine == 0, kept, sent)
        high = jnp.where(mine == 0, sent, kept)
        out.append(jnp.stack([low, high], axis=axis).reshape(-1, sent.shape[-1]))
    return out


def scatter_sum(grads):
    size = lax.axis_size("dp")
    bits = size.bit_length() - 1
    me = lax.axis_index("dp")
    rows, width = grads.shape
    work = grads.reshape((2,) * bits + (rows // size, width))
    for bit in range(bits):
        axis = bits - 1 - bit
        mine = (me >> bit) & 1
        sent = lax.dynamic_index_in_dim(work, 1 - mine, axis, keepdims=False)
        kept = lax.dynamic_index_in_dim(work, mine, axis, keepdims=False)
        work = kept.astype(jnp.float32) + over_dp(sent, 1 << bit).astype(jnp.float32)
        work = work.astype(grads.dtype)
    return work.astype(jnp.float32)


def weight_rows(index_ref, weights, helds, sems):
    rows = helds[0].shape[0]
    block = pl.ds(pl.multiple_of(index_ref[0] * rows, rows), rows)
    return [start(w.at[block], h, sems.at[i]) for i, (w, h) in enumerate(zip(weights, helds))]


def products(gradient, weight):
    return jnp.sum(gradient * weight.astype(jnp.float32), axis=1, keepdims=True)


def as_row(column):
    column = jnp.concatenate([column, jnp.zeros((LANES - column.shape[0], 1), jnp.float32)], axis=0)
    return jnp.broadcast_to(column, (LANES, LANES)).T[:1]


def ffn_sums_kernel(index_ref, *refs):
    weights, refs = refs[:2], refs[2:]
    ins, (gate_ref, up_ref, down_ref, gain_ref, *helds, sems) = refs[:-7], refs[-7:]
    copies = weight_rows(index_ref, weights, helds, sems)
    chunks = [
        (kept, got, at)
        for kept, got in zip(ins[0::2], ins[1::2])
        for at in range(0, kept.shape[-1], 3 * (CUTS[0][1] - CUTS[0][0]))
    ]
    for copy in copies:
        copy.wait()
    gain = 0.0
    for (low, high), (kept, got, at) in zip(CUTS, chunks):
        count, half = high - low, (high - low) // 2
        total = add_two(kept[:, at : at + 3 * count], got[:, at : at + 3 * count])
        gate, up = total[:, :count], total[:, count + half : 2 * count + half]
        gate_ref[:, low:high] = gate
        down_ref[:, low : low + half] = total[:, count : count + half]
        up_ref[:, low:high] = up
        down_ref[:, low + half : high] = total[:, 2 * count + half :]
        gain += products(gate, helds[0][:, low:high]) + products(up, helds[1][:, low:high])
    gain_ref[...] = as_row(gain)


def ffn_sums(index, weights, pieces):
    rows, units = pieces[0].shape[0], CUTS[-1][1]
    wide = jax.ShapeDtypeStruct((rows, units), jnp.float32)
    return pl.pallas_call(
        ffn_sums_kernel,
        out_shape=(wide,) * 3 + (jax.ShapeDtypeStruct((1, LANES), jnp.float32),),
        in_specs=[SMEM] + [HBM] * 2 + [VMEM] * len(pieces),
        out_specs=[VMEM] * 4,
        scratch_shapes=[pltpu.VMEM((rows, w.shape[1]), w.dtype) for w in weights] + [pltpu.SemaphoreType.DMA((2,))],
        compiler_params=pltpu.CompilerParams(vmem_limit_bytes=VMEM_LIMIT),
        cost_estimate=CHEAP,
        name="ffn_sums",
    )(index, *weights, *pieces)


def gain_gradient(products_sum, gain, index):
    total = products_sum + to_other_core(products_sum)
    rows = gain.shape[0] // lax.axis_size("dp")
    return total[0, :rows] / lax.dynamic_slice_in_dim(gain, index[0] * rows, rows)


def to_other_core(array):
    return lax.ppermute(array, "tensor", [(0, 1), (1, 0)])


def norm_grad(value, grad, gain):
    scale = lax.rsqrt(jnp.mean(value * value, axis=-1, keepdims=True) + epsilon)
    scaled = grad * gain
    back = scale * scaled - value * scale**3 * jnp.mean(scaled * value, axis=-1, keepdims=True)
    return back


def stream(steps, in_sems, out_sems):
    waits, count = [], 0
    for loads, _, _ in steps:
        waits.append([start(*pair, in_sems.at[count + i]) for i, pair in enumerate(loads)])
        count += len(loads)
    copies = []
    for wait, (_, compute, stores) in zip(waits, steps):
        for copy in wait:
            copy.wait()
        compute()
        for pair in stores:
            copies.append(start(*pair, out_sems.at[len(copies)]))
    for copy in copies:
        copy.wait()


def row_kernel(function, turned, count, outs, *refs):
    def cut(n):
        nonlocal refs
        head, refs = refs[:n], refs[n:]
        return head

    ins_hbm, vector, outs_hbm = cut(count), cut(1), cut(outs)
    ins, held, (in_sems, out_sems) = cut(count), cut(outs), refs
    gain = vector[0][...][None, :]
    direct = [ref for ref, t in zip(held, turned) if not t]
    steps = []
    for i in range(ins[0].shape[0] // BLOCK):
        rows = pl.ds(i * BLOCK, BLOCK)
        places = [(slice(None), rows) if t else (rows, slice(None)) for t in turned]

        def compute(i=i, rows=rows, places=places):
            def step(j, carry):
                few = pl.ds(pl.multiple_of(i * BLOCK + j * FEW, FEW), FEW)
                results = function(*(ref[few, :].astype(jnp.float32) for ref in ins), gain)
                for ref, result in zip(direct, results):
                    ref[few, :] = result.astype(jnp.bfloat16)
                return carry

            if direct:
                lax.fori_loop(0, BLOCK // FEW, step, 0, unroll=4)
            for n, t in enumerate(turned):
                if t:
                    source = ins[0] if t == 2 else held[n - 1]
                    held[n][places[n]] = source[rows, :].astype(jnp.float32).T.astype(jnp.bfloat16)

        steps.append((
            [(a.at[rows], b.at[rows]) for a, b in zip(ins_hbm, ins)],
            compute,
            [(a.at[place], b.at[place]) for a, b, place in zip(held, outs_hbm, places)],
        ))
    stream(steps, in_sems, out_sems)


def row_call(function, name, ins, vector, turned):
    rows, width = ins[0].shape
    bf, blocks = jnp.bfloat16, rows // BLOCK
    outs = [jax.ShapeDtypeStruct((width, rows) if t else (rows, width), bf) for t in turned]
    return pl.pallas_call(
        functools.partial(row_kernel, function, turned, len(ins), len(outs)),
        out_shape=tuple(outs),
        in_specs=[HBM] * len(ins) + [VMEM],
        out_specs=[HBM] * len(outs),
        scratch_shapes=[pltpu.VMEM(a.shape, bf) for a in (*ins, *outs)]
        + [pltpu.SemaphoreType.DMA((len(ins) * blocks,)), pltpu.SemaphoreType.DMA((len(outs) * blocks,))],
        compiler_params=pltpu.CompilerParams(vmem_limit_bytes=VMEM_LIMIT),
        cost_estimate=CHEAP,
        name=name,
    )(*ins, vector)


def norm_rows(x, own, got, gain):
    hidden = x + (own + got)
    norm = lax.rsqrt(jnp.mean(hidden * hidden, axis=-1, keepdims=True) + epsilon)
    act = hidden * norm * gain
    return hidden, act


def middle_rows(hidden, own, got, cot, gain):
    return (cot + norm_grad(hidden, own + got, gain),)


def output_rows(hidden, own, got, gain):
    return (hidden + (own + got),)


def input_rows(x, gatt, own, got, gain):
    return (gatt + norm_grad(x, own + got, gain),)


def attention_grads(total, half, kv_half):
    names = (("out", half), ("query", half), ("out", half), ("key", kv_half), ("value", kv_half))
    names += (("query", half), ("key", kv_half), ("value", kv_half))
    found, at = {}, 0
    for name, count in names:
        found.setdefault(name, []).append(total[:, at : at + count])
        at += count
    found = {name: jnp.concatenate(parts, axis=1) for name, parts in found.items()}
    return found["query"], found["key"], found["value"], found["out"].T


def plain(names, chunk, backward):
    v = dict(names)
    layer_input, hidden, bits, blocks, size = (v[n] for n in ("layer_input", "hidden", "bits", "blocks", "size"))
    rows, width = layer_input.shape
    half, kv_half, heads = v["half"], v["kv_half"], v["heads"]
    pieces = []
    for i in range(len(CUTS)):
        units, piece = chunk(i, whole=True)
        pieces.append(piece)
    hidden_units, grad_gate_lin, grad_up_lin = units
    two_own = projection([grad_gate_lin, grad_up_lin], [v["w_gate"], v["w_up"]], NT)
    ffn_own = projection([hidden_units], [v["w_down"]], NN)
    grad_attention, grad_attention_t = row_call(
        middle_rows, "middle", [hidden, two_own, to_other_core(two_own), v["cotangent"]], v["gain_two"], [0, 1]
    )
    (output,) = row_call(output_rows, "output", [hidden, ffn_own, to_other_core(ffn_own)], v["gain_two"], [0])
    back_one = backward(0, gatt=grad_attention)
    pieces.append(gradient_pieces(
        bits, blocks, [grad_attention_t, v["act_one_t"]], [v["mixed"], *back_one], [0, 1, 1],
        [((0, half, 0, 0), (half, heads, 0, 1)), ((0, half, half, 0),), ((0, half, half, 1),)],
    ))
    *back_two, one_own = backward(1, *back_one, gatt=grad_attention)
    pieces.append(gradient_pieces(
        bits, blocks, [v["act_one_t"]], back_two, [0, 0], [((0, half, 0, 0),), ((0, half, 0, 1),)]
    ))
    (grad_input,) = row_call(
        input_rows, "input", [layer_input, grad_attention, one_own, to_other_core(one_own)],
        v["attn_gain"], [0],
    )
    total = scatter_sum(jnp.concatenate([p for piece in pieces for p in joined(piece)], axis=1))
    gates, ups, downs = [], [], []
    for low, high in CUTS:
        count = high - low
        parts = jnp.split(total[:, 3 * low : 3 * high], [count, count * 3 // 2, count * 5 // 2], axis=1)
        for found, part in zip((gates, downs, ups, downs), parts):
            found.append(part)
    grad_gate, grad_up = jnp.concatenate(gates, axis=1), jnp.concatenate(ups, axis=1)
    attention = attention_grads(total[:, 3 * CUTS[-1][1] :], half, kv_half)

    def gain_of(gradients, weights, gain):
        count = width // size
        cut = [lax.dynamic_slice_in_dim(v[w], v["me"] * count, count).astype(jnp.float32) for w in weights]
        return gain_gradient(sum(jnp.sum(g * w, axis=1) for g, w in zip(gradients, cut))[None, :], gain, v["index"])

    return (
        output,
        grad_input,
        gain_of(attention[:3], ("w_query", "w_key", "w_value"), v["attn_gain"]),
        *attention,
        gain_of((grad_gate, grad_up), ("w_gate", "w_up"), v["ffn_gain"]),
        grad_gate,
        grad_up,
        jnp.concatenate(downs, axis=1).T,
    )


def per_device(
    layer_input,
    branch_point,
    attn_gain,
    w_query,
    w_key,
    w_value,
    w_out,
    ffn_gain,
    w_gate,
    w_up,
    w_down,
    cotangent,
):
    rows, width = layer_input.shape
    size = lax.axis_size("dp")
    by_kernel = size == KERNEL_BLOCKS
    blocks = KERNEL_BLOCKS
    me = lax.axis_index("dp")
    index = me.reshape(1).astype(jnp.int32)
    bits = jnp.stack([me & 1, me >> 1 & 1, me >> 2 & 3]).astype(jnp.int32)
    rope = rope_tables()
    act_one_t, queries, keys, values, mixed, log_sums, attn_own = attention_forward(
        branch_point, layer_input, attn_gain, w_query, w_key, w_value, w_out, rope
    )
    attn_got = to_other_core(attn_own)
    kv_half = w_key.shape[1] // 2
    w_key_value = jnp.concatenate(
        [w_key[:, :kv_half], w_value[:, :kv_half], w_key[:, kv_half:], w_value[:, kv_half:]], axis=1
    )
    (cot_t,) = row_call(lambda *_: (), "turn", [cotangent], ffn_gain, [2])
    gain_two = ffn_gain
    *units, sent_a, kept_a, sent_b, kept_b, hidden, act_two, act_two_t = ffn_chunk(
        bits, blocks, (after(gain_two, cot_t, w_key_value), layer_input, attn_own, attn_got), cotangent, cot_t,
        w_gate, w_up, w_down, [], 0, CUTS[0][1],
    )
    first_piece = (sent_a, kept_a, sent_b, kept_b)
    heads, kv = mixed.shape[1], w_key.shape[1]
    half = heads // 2
    def chunk(i, *needed, whole=False):
        nonlocal units
        piece = first_piece
        if i > 0:
            low, high = CUTS[i]
            made = ffn_chunk(
                bits, blocks, (after(act_two, *needed), act_two_t), cotangent, cot_t,
                w_gate, w_up, w_down, units, low, high - low,
            )
            units, piece = made[:3], made[3:]
        return (units, piece) if whole else piece

    def backward(part, *needed, gatt=None):
        return attention_backward(
            part, branch_point, after(grad_attention if gatt is None else gatt, *needed), queries, keys, values, log_sums,
            w_out, w_query, w_key_value, rope, list(needed[:2]) if part else [],
        )

    if not by_kernel:
        return plain(locals(), chunk, backward)
    pieces = [chunk(0)]
    one = [first_stage(pieces[0])]
    pieces.append(chunk(1))
    one.append(first_stage(pieces[1]))
    pieces.append(chunk(2, pieces[1]))
    pieces[2], one[0] = after((pieces[2], one[0]))
    joint = sums(bits, second=one[0])
    two = [second_stage(*joint)]
    pieces.append(chunk(3, joint))
    *units, pieces[3], one[1], two[0] = after((*units, pieces[3], one[1], two[0]))
    joint = sums(bits, second=one[1], third=two[0])
    two.append(second_stage(*joint[0]))
    three = [third_stage(*joint[1])]
    one.append(first_stage(after(pieces[2], units)))
    hidden_units, grad_gate_lin, grad_up_lin = units
    two_own = projection(after([grad_gate_lin, grad_up_lin], joint), [w_gate, w_up], NT)
    two_own, three[0] = after((two_own, three[0]))
    two_got = to_other_core(two_own)
    ffn_own = projection([after(hidden_units, two_own)], [w_down], NN)
    ffn_own, one[2], two[1] = after((ffn_own, one[2], two[1]))
    joint = sums(bits, second=one[2], third=two[1], cost=LONG)
    two.append(second_stage(*joint[0]))
    three.append(third_stage(*joint[1]))
    one.append(first_stage(after(pieces[3], ffn_own)))
    grad_attention, grad_attention_t = row_call(
        middle_rows, "middle", [hidden, two_own, two_got, after(cotangent, joint)], gain_two, [0, 1]
    )
    grad_attention, three[0], three[1] = after((grad_attention, three[0], three[1]))
    joint = sums(bits, fourth=(*three[0], *three[1]))
    four = [fourth_stage(*joint)]
    back_one = backward(0, grad_attention, joint)
    back_one, two[2], one[3], four[0] = after((back_one, two[2], one[3], four[0]))
    joint = sums(bits, second=one[3], third=two[2])
    two.append(second_stage(*joint[0]))
    three.append(third_stage(*joint[1]))
    early = gradient_pieces(
        bits, blocks, [after(grad_attention_t, joint), act_one_t], [mixed, *back_one], [0, 1, 1],
        [((0, half, 0, 0), (half, heads, 0, 1)), ((0, half, half, 0),), ((0, half, half, 1),)],
    )
    early, two[3], three[2] = after((early, two[3], three[2]))
    joint = sums(bits, third=two[3], fourth=three[2])
    three.append(third_stage(*joint[0]))
    four.append(fourth_stage(*joint[1]))
    early_one = first_stage(early)
    ffn_got = to_other_core(after(ffn_own, early))
    *back_two, one_own = backward(1, *back_one, early, joint)
    back_two, one_own, early_one, three[3], four[1], ffn_got = after(
        (back_two, one_own, early_one, three[3], four[1], ffn_got)
    )
    one_got = to_other_core(one_own)
    joint = sums(bits, second=early_one, fourth=three[3])
    early_two = second_stage(*joint[0])
    four.append(fourth_stage(*joint[1]))
    late = gradient_pieces(
        bits, blocks, [after(act_one_t, joint)], back_two, [0, 0], [((0, half, 0, 0),), ((0, half, 0, 1),)]
    )
    late, one_got = after((late, one_got))
    late_one = first_stage(late)
    (output,) = row_call(output_rows, "output", [hidden, after(ffn_own, late), ffn_got], gain_two, [0])
    output, early_two, four[2] = after((output, early_two, four[2]))
    joint = sums(bits, third=early_two)
    early_three = third_stage(*joint)
    (grad_input,) = row_call(
        input_rows, "input", [layer_input, after(grad_attention, joint), one_own, one_got],
        attn_gain, [0],
    )
    grad_input, late_one, early_three = after((grad_input, late_one, early_three))
    joint = sums(bits, second=late_one, fourth=early_three)
    late_two = second_stage(*joint[0])
    early_four = fourth_stage(*joint[1])
    *ffn_grads, ffn_products = ffn_sums(index, [w_gate, w_up], after([p for piece in four for p in piece], joint))
    ffn_grads, late_two = after((ffn_grads, late_two))
    grad_gate, grad_up, grad_down = ffn_grads
    joint = sums(bits, third=late_two)
    late_three = third_stage(*joint)
    grad_ffn_gain = gain_gradient(after(ffn_products, joint), ffn_gain, index)
    late_three, early_four, grad_ffn_gain = after((late_three, early_four, grad_ffn_gain))
    joint = sums(bits, fourth=late_three)
    late_four = fourth_stage(*joint)
    products_sum, attention = attention_sums(index, [w_query, w_key, w_value], *early_four, *late_four, kv_half)
    grad_attn_gain = gain_gradient(products_sum, attn_gain, index)
    return (
        output,
        grad_input,
        grad_attn_gain,
        *attention,
        grad_ffn_gain,
        grad_gate,
        grad_up,
        grad_down.T,
    )


def solution(mesh):
    placed = (
        P("dp", None),
        P("dp", None),
        P(),
        P(None, "tensor"),
        P(None, "tensor"),
        P(None, "tensor"),
        P("tensor", None),
        P(),
        P(None, "tensor"),
        P(None, "tensor"),
        P("tensor", None),
        P("dp", None),
    )
    return jax.shard_map(
        per_device,
        mesh=mesh,
        in_specs=placed,
        out_specs=(
            P("dp", None),
            P("dp", None),
            P("dp"),
            P("dp", "tensor"),
            P("dp", "tensor"),
            P("dp", "tensor"),
            P("tensor", "dp"),
            P("dp"),
            P("dp", "tensor"),
            P("dp", "tensor"),
            P("tensor", "dp"),
        ),
        check_vma=False,
    )
```

```python
import functools

import jax
import jax.numpy as jnp
import numpy as np
from jax import lax
from jax.experimental import pallas as pl
from jax.experimental.pallas import tpu as pltpu
from jax.sharding import PartitionSpec as P

HEAD_DIM = 96
PROMPT = 1024
CONT_LEN = 128
CONT = 2
GROUP_TOK = 1280
BLOCK = 256
BLOCKS = GROUP_TOK // BLOCK
LANES = 128
MIB = 1 << 20
VMEM_LIMIT = 64 * MIB
CHEAP = pl.CostEstimate(flops=10**6, bytes_accessed=10**5, transcendentals=0)
epsilon = 1e-05
rope_base = 100000.0
LOG2E = 1.4426950408889634
SCORE_SCALE = HEAD_DIM ** (-0.5)
NT = (((1,), (1,)), ((), ()))
TN = (((0,), (0,)), ((), ()))

LONG = pl.CostEstimate(flops=10**11, bytes_accessed=10**5, transcendentals=0)


def matmul(left, right, dims=(((1,), (0,)), ((), ()))):
    return lax.dot_general(left, right, dims, preferred_element_type=jnp.float32)


HBM = pl.BlockSpec(memory_space=pl.ANY)
SMEM = pl.BlockSpec(memory_space=pltpu.SMEM)
VMEM = pl.BlockSpec(memory_space=pltpu.VMEM)


def start(source, target, sem):
    copy = pltpu.make_async_copy(source, target, sem)
    copy.start()
    return copy


def rows_of(blocks, width):
    return (blocks // 4, 2, 2, None, width)


def rope_tables():
    half = HEAD_DIM // 2
    frequency = rope_base ** (-np.arange(half, dtype=np.float64) * 2.0 / HEAD_DIM)
    angles = np.arange(PROMPT + CONT_LEN, dtype=np.float64)[:, None] * frequency[None, :]
    pad = np.zeros((angles.shape[0], LANES - HEAD_DIM))
    cosine = np.concatenate([np.cos(angles), np.cos(angles), pad], axis=1)
    sine = np.concatenate([-np.sin(angles), np.sin(angles), pad], axis=1)
    return jnp.asarray(np.stack([cosine, sine]), jnp.float32)


def place_rope(branch_ref, table_ref, rope_ref):
    rope_ref[:, :PROMPT, :] = table_ref[:, :PROMPT, :]
    for c in range(CONT):
        rows = pl.ds(PROMPT + c * CONT_LEN, CONT_LEN)
        for i in range(2):
            rope_ref[i, rows, :] = table_ref[i, pl.ds(branch_ref[0, c], CONT_LEN), :]


def lane_ids(shape):
    return lax.broadcasted_iota(jnp.int32, shape, 1)


def swap_halves(head):
    half = HEAD_DIM // 2
    return jnp.where(
        lane_ids(head.shape) < half, pltpu.roll(head, LANES - half, 1), pltpu.roll(head, half, 1)
    )


def take_head(full, h):
    first = h * HEAD_DIM
    start, shift = first // LANES * LANES, first % LANES
    width = LANES if shift + HEAD_DIM <= LANES else 2 * LANES
    part = full[:, start : start + width]
    return part[:, :LANES] if shift == 0 else pltpu.roll(part, width - shift, 1)[:, :LANES]


def join_heads(heads):
    lanes = lane_ids(heads[0].shape)
    out = []
    for i in range(0, len(heads), 4):
        one, two, three = (pltpu.roll(heads[i + j], LANES - 32 * j, 1) for j in (1, 2, 3))
        out.append(jnp.where(lanes < 96, heads[i], one))
        out.append(jnp.where(lanes < 64, one, two))
        out.append(jnp.where(lanes < 32, two, three))
    return jnp.concatenate(out, axis=1)


def own_mask(shape, query_axis, block):
    query = lax.broadcasted_iota(jnp.int32, shape, query_axis) & (BLOCK - 1)
    key = lax.broadcasted_iota(jnp.int32, shape, 1 - query_axis)
    mask = key <= query
    if block * BLOCK >= PROMPT:
        mask = mask & ((key // CONT_LEN) == (query // CONT_LEN))
    return mask


def reach_mask(shape, query_axis, branch_ref):
    query = lax.broadcasted_iota(jnp.int32, shape, query_axis) & (BLOCK - 1)
    key = lax.broadcasted_iota(jnp.int32, shape, 1 - query_axis) + PROMPT // 2
    return key < jnp.where(query < CONT_LEN, branch_ref[0, 0], branch_ref[0, 1])


def attention_forward_kernel(
    branch_ref, gain_ref, *refs,
):
    ins_hbm, outs_hbm, ins, outs, (o_ref, rope_ref, in_sems, x_sems, out_sems, row_sems) = (
        refs[:6], refs[6:13], refs[13:19], refs[19:26], refs[26:],
    )
    x_ref, wq_ref, wk_ref, wv_ref, wo_ref, table_ref = ins
    act_t_ref, q_ref, k_ref, v_ref, mixed_ref, lse_ref, part_ref = outs
    kv_heads = k_ref.shape[0]
    group = 2 * BLOCK

    def x_in(i):
        rows = pl.ds(pl.multiple_of(i * BLOCK, BLOCK), BLOCK)
        return pltpu.make_async_copy(ins_hbm[0].at[rows], x_ref.at[rows], x_sems.at[i])

    def rows_out(n, which, i):
        rows = pl.ds(pl.multiple_of(i * BLOCK, BLOCK), BLOCK)
        return pltpu.make_async_copy(outs[n].at[rows], outs_hbm[n].at[rows], row_sems.at[which, i])

    x_in(0).start()
    loads = {n: start(ins_hbm[n], ins[n], in_sems.at[n]) for n in (1, 5, 2, 3)}
    for i in range(1, BLOCKS):
        x_in(i).start()
    loads[4] = start(ins_hbm[4], wo_ref, in_sems.at[4])
    for n in (5, 1, 2, 3):
        loads[n].wait()
    place_rope(branch_ref, table_ref, rope_ref)

    def project(i, carry):
        rows = pl.ds(pl.multiple_of(i * BLOCK, BLOCK), BLOCK)
        x_in(i).wait()
        x = x_ref[rows, :].astype(jnp.float32)
        norm = lax.rsqrt(jnp.mean(x * x, axis=-1, keepdims=True) + epsilon)
        act = x * norm * gain_ref[...][None, :]
        act_t_ref[:, rows] = act.T.astype(jnp.bfloat16)
        act = act.astype(jnp.bfloat16)
        cosine, sine = rope_ref[0, rows, :], rope_ref[1, rows, :]
        full = matmul(act, wq_ref[...])
        for h in range(2 * kv_heads):
            head = take_head(full, h)
            rotated = head * cosine + swap_halves(head) * sine
            q_ref[h // 2, i, pl.ds(h % 2 * BLOCK, BLOCK), :] = rotated.astype(jnp.bfloat16)
        full = matmul(act, wk_ref[...])
        for h in range(kv_heads):
            head = take_head(full, h)
            rotated = head * cosine + swap_halves(head) * sine
            k_ref[h, rows, :] = rotated.astype(jnp.bfloat16)
        full = matmul(act, wv_ref[...])
        lanes = lane_ids((BLOCK, LANES))
        for h in range(kv_heads):
            head = jnp.where(lanes < HEAD_DIM, take_head(full, h), 0.0)
            v_ref[h, rows, :] = jnp.where(lanes == HEAD_DIM, 1.0, head).astype(jnp.bfloat16)
        return carry

    lax.fori_loop(0, BLOCKS, project, 0)
    stores = [start(outs[n], outs_hbm[n], out_sems.at[n]) for n in range(4)]
    factor = SCORE_SCALE * LOG2E

    def attend(h, carry):
        for i in range(BLOCKS):
            query = q_ref[h, i]
            before = i * BLOCK
            own = matmul(query, k_ref[h, before : before + BLOCK], NT)
            own = jnp.where(own_mask(own.shape, 0, i), own, -1e30)
            largest = jnp.max(own, axis=-1, keepdims=True)
            spans = []
            if i > 0:
                cuts = [0, before] if before < PROMPT else [0, PROMPT // 2, PROMPT]
                for low, high in zip(cuts[:-1], cuts[1:]):
                    scores = matmul(query, k_ref[h, low:high], NT)
                    if before >= PROMPT and low > 0:
                        scores = jnp.where(reach_mask(scores.shape, 0, branch_ref), scores, -1e30)
                    largest = jnp.maximum(largest, jnp.max(scores, axis=-1, keepdims=True))
                    spans.append((low, high, scores))
            shift = largest * factor
            probs = jnp.exp2(own * factor - shift).astype(jnp.bfloat16)
            total = matmul(probs, v_ref[h, before : before + BLOCK])
            for low, high, scores in spans:
                probs = jnp.exp2(scores * factor - shift).astype(jnp.bfloat16)
                total += matmul(probs, v_ref[h, low:high])
            sums = total[:, HEAD_DIM : HEAD_DIM + 1]
            mixed = total * (1.0 / sums)
            for g in range(2):
                o_ref[2 * h + g, before : before + BLOCK, :] = mixed[g * BLOCK : (g + 1) * BLOCK]
            logs = shift + jnp.log2(sums)
            lse_ref[h, i] = jnp.broadcast_to(logs, (group, LANES)).T[0:1, :]
        return carry

    lax.fori_loop(0, kv_heads, attend, 0)
    stores.append(start(lse_ref, outs_hbm[5], out_sems.at[5]))
    loads[4].wait()

    def finish(i, carry):
        rows = pl.ds(pl.multiple_of(i * BLOCK, BLOCK), BLOCK)
        mixed = join_heads([o_ref[h, rows, :] for h in range(2 * kv_heads)]).astype(jnp.bfloat16)
        mixed_ref[rows, :] = mixed
        part_ref[rows, :] = matmul(mixed, wo_ref[...]).astype(jnp.bfloat16)
        rows_out(4, 0, i).start()
        rows_out(6, 1, i).start()
        return carry

    lax.fori_loop(0, BLOCKS, finish, 0)
    for copy in stores:
        copy.wait()
    for i in range(BLOCKS):
        rows_out(4, 0, i).wait()
        rows_out(6, 1, i).wait()


def attention_forward(branch, x, gain, wq, wk, wv, wo, rope):
    kv_heads = wk.shape[1] // HEAD_DIM
    rows, width = x.shape
    bf = jnp.bfloat16
    ins = (x, wq, wk, wv, wo, rope)
    outs = (
        jax.ShapeDtypeStruct((width, rows), bf),
        jax.ShapeDtypeStruct((kv_heads, BLOCKS, 2 * BLOCK, LANES), bf),
        jax.ShapeDtypeStruct((kv_heads, rows, LANES), bf),
        jax.ShapeDtypeStruct((kv_heads, rows, LANES), bf),
        jax.ShapeDtypeStruct((rows, wq.shape[1]), bf),
        jax.ShapeDtypeStruct((kv_heads, BLOCKS, 1, 2 * BLOCK), jnp.float32),
        jax.ShapeDtypeStruct((rows, width), bf),
    )
    return pl.pallas_call(
        attention_forward_kernel,
        out_shape=outs,
        in_specs=[SMEM, VMEM] + [HBM] * 6,
        out_specs=[HBM] * 7,
        scratch_shapes=[pltpu.VMEM(a.shape, a.dtype) for a in ins + outs]
        + [
            pltpu.VMEM((2 * kv_heads, rows, LANES), jnp.float32),
            pltpu.VMEM((2, rows, LANES), jnp.float32),
            pltpu.SemaphoreType.DMA((6,)),
            pltpu.SemaphoreType.DMA((BLOCKS,)),
            pltpu.SemaphoreType.DMA((6,)),
            pltpu.SemaphoreType.DMA((2, BLOCKS)),
        ],
        compiler_params=pltpu.CompilerParams(vmem_limit_bytes=VMEM_LIMIT),
        cost_estimate=CHEAP,
        name="attention_forward",
    )(branch, gain, *ins)


def attention_backward_kernel(
    part, branch_ref, *refs
):
    def cut(count):
        nonlocal refs
        head, refs = refs[:count], refs[count:]
        return head

    count, made = (11, 3) if part else (7, 2)
    ins_hbm, outs_hbm, ins, outs = cut(count), cut(made), cut(count), cut(made)
    do_ref, dq_ref, dk_ref, dv_ref, rope_ref, in_sems, gatt_sems, row_sems = refs
    gatt_ref, wo_ref, q_ref, k_ref, v_ref, lse_ref, table_ref = ins[:7]
    wq_ref, wkv_ref, *first_ref = ins[7:] if part else (None, None)
    gq_ref, gkv_ref = outs[:2]
    part_ref = outs[2] if part else None
    kv_heads = k_ref.shape[0]
    group = 2 * BLOCK
    factor = SCORE_SCALE * LOG2E

    def gatt_in(i):
        rows = pl.ds(pl.multiple_of(i * BLOCK, BLOCK), BLOCK)
        return pltpu.make_async_copy(ins_hbm[0].at[rows], gatt_ref.at[rows], gatt_sems.at[i])

    def rows_out(n, i):
        rows = pl.ds(pl.multiple_of(i * BLOCK, BLOCK), BLOCK)
        return pltpu.make_async_copy(outs[n].at[rows], outs_hbm[n].at[rows], row_sems.at[n, i])

    loads = []
    for n in range(1, count):
        size = ins[n].shape[0]
        source = ins_hbm[n].at[pl.ds(part * size, size)] if n < 6 else ins_hbm[n]
        loads.append(start(source, ins[n], in_sems.at[n]))
        if n == 1:
            for i in range(BLOCKS):
                gatt_in(i).start()
    loads[0].wait()

    def project(i, carry):
        rows = pl.ds(pl.multiple_of(i * BLOCK, BLOCK), BLOCK)
        gatt_in(i).wait()
        full = matmul(gatt_ref[rows, :], wo_ref[...], NT)
        lanes = lane_ids((BLOCK, LANES))
        for h in range(2 * kv_heads):
            head = jnp.where(lanes < HEAD_DIM, take_head(full, h), 0.0)
            do_ref[h // 2, i, pl.ds(h % 2 * BLOCK, BLOCK), :] = head.astype(jnp.bfloat16)
        return carry

    lax.fori_loop(0, BLOCKS, project, 0)
    for copy in loads[1:6]:
        copy.wait()
    place_rope(branch_ref, table_ref, rope_ref)

    def attend(h, carry):
        for i in reversed(range(BLOCKS)):
            query, grad, logs = q_ref[h, i], do_ref[h, i], lse_ref[h, i]
            before = i * BLOCK
            cuts = [(before, before + BLOCK)]
            if i > 0 and before < PROMPT:
                cuts += [(0, before)]
            elif i > 0:
                cuts += [(0, PROMPT // 2), (PROMPT // 2, PROMPT)]
            spans, weighted = [], 0.0
            for low, high in cuts:
                scores = matmul(k_ref[h, low:high], query, NT)
                probs = jnp.exp2(scores * factor - logs)
                if low == before:
                    probs = jnp.where(own_mask(probs.shape, 1, i), probs, 0.0)
                elif before >= PROMPT and low > 0:
                    probs = jnp.where(reach_mask(probs.shape, 1, branch_ref), probs, 0.0)
                grad_probs = matmul(v_ref[h, low:high], grad, NT)
                weighted += jnp.sum(probs * grad_probs, axis=0, keepdims=True)
                spans.append((low, high, probs, grad_probs))
            grad_query = jnp.zeros((LANES, group), jnp.float32)
            for low, high, probs, grad_probs in spans:
                grad_scores = (probs * (grad_probs - weighted)).astype(jnp.bfloat16)
                grad_query += matmul(k_ref[h, low:high], grad_scores, TN)
                grad_key = matmul(grad_scores, query)
                grad_value = matmul(probs.astype(jnp.bfloat16), grad)
                if before >= PROMPT:
                    dk_ref[h, low:high] = grad_key
                    dv_ref[h, low:high] = grad_value
                else:
                    dk_ref[h, low:high] += grad_key
                    dv_ref[h, low:high] += grad_value
            dq_ref[h, i] = grad_query.T
        return carry

    lax.fori_loop(0, kv_heads, attend, 0)
    for copy in loads[6:]:
        copy.wait()

    def finish(i, carry):
        rows = pl.ds(pl.multiple_of(i * BLOCK, BLOCK), BLOCK)
        cosine, sine = rope_ref[0, rows, :] * SCORE_SCALE, rope_ref[1, rows, :] * SCORE_SCALE
        heads = []
        for h in range(2 * kv_heads):
            head = dq_ref[h // 2, i, pl.ds(h % 2 * BLOCK, BLOCK), :]
            heads.append(head * cosine - swap_halves(head) * sine)
        grad_q = join_heads(heads).astype(jnp.bfloat16)
        heads = []
        for h in range(kv_heads):
            head = dk_ref[h, rows, :]
            heads.append(head * cosine - swap_halves(head) * sine)
        heads += [dv_ref[h, rows, :] for h in range(kv_heads)]
        grad_kv = join_heads(heads).astype(jnp.bfloat16)
        gq_ref[rows, :] = grad_q
        gkv_ref[rows, :] = grad_kv
        if part:
            grad_q = jnp.concatenate([first_ref[0][rows, :], grad_q], axis=1)
            grad_kv = jnp.concatenate([first_ref[1][rows, :], grad_kv], axis=1)
            total = matmul(grad_q, wq_ref[...], NT) + matmul(grad_kv, wkv_ref[...], NT)
            part_ref[rows, :] = total.astype(jnp.bfloat16)
        for n in range(made):
            rows_out(n, i).start()
        return carry

    lax.fori_loop(0, BLOCKS, finish, 0)
    for n in range(made):
        for i in range(BLOCKS):
            rows_out(n, i).wait()


def attention_backward(part, branch, gatt, q, k, v, lse, wo, wq, wkv, rope, first):
    kv_heads = k.shape[0] // 2
    rows, width = gatt.shape
    bf = jnp.bfloat16
    small = jax.ShapeDtypeStruct((rows, wq.shape[1] // 2), bf)
    outs = (small, small) + ((jax.ShapeDtypeStruct((rows, width), bf),) if part else ())
    ins = (gatt, wo, q, k, v, lse, rope) + ((wq, wkv, *first) if part else ())

    def held(n, array):
        halves = (array.shape[0] // 2,) + array.shape[1:]
        return pltpu.VMEM(halves if 0 < n < 6 else array.shape, array.dtype)

    return pl.pallas_call(
        functools.partial(attention_backward_kernel, part),
        out_shape=outs,
        in_specs=[SMEM] + [HBM] * len(ins),
        out_specs=[HBM] * len(outs),
        scratch_shapes=[held(n, a) for n, a in enumerate(ins)]
        + [pltpu.VMEM(o.shape, bf) for o in outs]
        + [
            pltpu.VMEM((kv_heads, BLOCKS, 2 * BLOCK, LANES), bf),
            pltpu.VMEM((kv_heads, BLOCKS, 2 * BLOCK, LANES), jnp.float32),
            pltpu.VMEM((kv_heads, rows, LANES), jnp.float32),
            pltpu.VMEM((kv_heads, rows, LANES), jnp.float32),
            pltpu.VMEM((2, rows, LANES), jnp.float32),
            pltpu.SemaphoreType.DMA((len(ins),)),
            pltpu.SemaphoreType.DMA((BLOCKS,)),
            pltpu.SemaphoreType.DMA((len(outs), BLOCKS)),
        ],
        compiler_params=pltpu.CompilerParams(vmem_limit_bytes=VMEM_LIMIT),
        cost_estimate=CHEAP,
        name="attention_backward",
    )(branch, *ins)


KERNEL_BLOCKS = 16
WIDE = 512
FEW = 16
CUTS = ((0, 512), (512, 1024), (1024, 1536), (1536, 2048))


NN = (((1,), (0,)), ((), ()))


def split_copies(tile, low, high, at, sent, kept, axis, mine, sems, k, begin=True):
    copies = []
    for half, target in ((1 - mine, sent), (mine, kept)):
        part = tile.at[:, :, half] if axis == 0 else tile.at[:, half]
        copy = pltpu.make_async_copy(
            part.at[:, :, :, pl.ds(low, high - low)],
            target.at[:, :, :, pl.ds(at, high - low)],
            sems.at[k + len(copies)],
        )
        if begin:
            copy.start()
        copies.append(copy)
    return copies


def gradient_tile(tile, left, right, arrive=None):
    parts = 1 if arrive is None else 2
    zs, tall = tile.shape[0] // parts, left.shape[0] // parts

    def step(i, carry):
        if arrive is not None:
            arrive(i)
        out = matmul(left[pl.ds(pl.multiple_of(i * tall, tall), tall), :], right[...])
        tile[pl.ds(i * zs, zs)] = out.astype(jnp.bfloat16).reshape((zs,) + tile.shape[1:])
        return carry

    lax.fori_loop(0, parts, step, 0)


def ffn_kernel(first, count, norm, *refs):
    if norm:
        (bits_ref, gain_ref, *sums_hbm, cot_hbm, cot_t_hbm, wg_hbm, wu_hbm, wd_hbm), refs = refs[:10], refs[10:]
    else:
        (bits_ref, act_hbm, cot_hbm, act_t_hbm, cot_t_hbm, wg_hbm, wu_hbm, wd_hbm), refs = refs[:8], refs[11:]
    (hidden_hbm, ggate_hbm, gup_hbm, sent_a, kept_a, sent_b, kept_b), refs = refs[:7], refs[7:]
    if norm:
        (state_hbm, act_hbm, act_t_hbm, state, *held, sum_sems, made_sems), refs = refs[:9], refs[9:]
    act, cot, lefts, wg, wu, wd, lines, tiles, in_sems, row_sems, out_sems = refs
    units = pl.ds(first, count)
    tall = act.shape[0] // 2

    def rows_in(i, which):
        rows = pl.ds(pl.multiple_of(i * tall, tall), tall)
        source, target = ((act_hbm, act), (cot_hbm, cot))[which]
        return pltpu.make_async_copy(source.at[rows], target.at[rows], row_sems.at[which, i])

    def sums_in(which, i):
        rows = pl.ds(pl.multiple_of(i * BLOCK, BLOCK), BLOCK)
        return pltpu.make_async_copy(sums_hbm[which].at[rows], held[which].at[rows], sum_sems.at[which, i])

    if norm:
        for i in range(act.shape[0] // BLOCK):
            for which in range(3):
                sums_in(which, i).start()
    weights = [start(wg_hbm.at[:, units], wg, in_sems.at[0])]
    if not norm:
        rows_in(0, 0).start()
    weights.append(start(wu_hbm.at[:, units], wu, in_sems.at[1]))
    weights.append(start(wd_hbm.at[units], wd, in_sems.at[2]))
    rows_in(0, 1).start()
    if not norm:
        rows_in(1, 0).start()
    rows_in(1, 1).start()
    sources = [start(cot_t_hbm, lefts.at[0], in_sems.at[3])]
    if not norm:
        sources.append(start(act_t_hbm, lefts.at[1], in_sems.at[4]))

    def norm_step(i, carry):
        for which in range(3):
            sums_in(which, i).wait()

        def few_step(j, carry):
            few = pl.ds(pl.multiple_of(i * BLOCK + j * FEW, FEW), FEW)
            total, rows = norm_rows(*(ref[few, :].astype(jnp.float32) for ref in held), gain_ref[...][None, :])
            state[few, :] = total.astype(jnp.bfloat16)
            act[few, :] = rows.astype(jnp.bfloat16)
            return carry

        lax.fori_loop(0, BLOCK // FEW, few_step, 0, unroll=8)
        rows = pl.ds(pl.multiple_of(i * BLOCK, BLOCK), BLOCK)
        lefts[1, :, rows] = act[rows, :].astype(jnp.float32).T.astype(jnp.bfloat16)
        return carry

    made = []
    if norm:
        lax.fori_loop(0, act.shape[0] // BLOCK, norm_step, 0)
        pairs = ((state, state_hbm), (act, act_hbm), (lefts.at[1], act_t_hbm))
        made = [start(*pair, made_sems.at[i]) for i, pair in enumerate(pairs)]
    weights[0].wait()

    def units_step(i, carry):
        rows = pl.ds(pl.multiple_of(i * tall, tall), tall)
        if not norm:
            rows_in(i, 0).wait()
        gate = matmul(act[rows, :], wg[...])

        @pl.when(i == 0)
        def _():
            weights[1].wait()
            weights[2].wait()

        up = matmul(act[rows, :], wu[...])
        rows_in(i, 1).wait()
        grad = matmul(cot[rows, :], wd[...], NT)
        sigmoid = 1.0 / (1.0 + jnp.exp(-gate))
        silu = gate * sigmoid
        lines[0, rows, :] = (silu * up).astype(jnp.bfloat16)
        lines[1, rows, :] = (grad * up * (sigmoid * (1.0 + gate * (1.0 - sigmoid)))).astype(jnp.bfloat16)
        lines[2, rows, :] = (grad * silu).astype(jnp.bfloat16)
        return carry

    lax.fori_loop(0, 2, units_step, 0)
    copies = [
        start(lines.at[0], hidden_hbm.at[:, units], out_sems.at[0]),
        start(lines.at[1], ggate_hbm.at[:, units], out_sems.at[1]),
        start(lines.at[2], gup_hbm.at[:, units], out_sems.at[2]),
    ]
    half = count // 2
    x, y = bits_ref[0], bits_ref[1]
    for copy in sources:
        copy.wait()

    def stores(t, begin):
        if t == 0:
            return split_copies(tiles.at[0], 0, half, count, sent_a, kept_a, 0, x, out_sems, 3, begin) + split_copies(
                tiles.at[0], half, count, count, sent_b, kept_b, 1, y, out_sems, 5, begin
            )
        if t == 1:
            return split_copies(tiles.at[1], 0, count, 0, sent_a, kept_a, 0, x, out_sems, 7, begin)
        return split_copies(tiles.at[2], 0, count, 0, sent_b, kept_b, 1, y, out_sems, 9, begin)

    def tile_step(t, carry):
        gradient_tile(tiles.at[t], lefts.at[jnp.minimum(t, 1)], lines.at[t])
        for one in range(3):

            @pl.when(t == one)
            def _(one=one):
                stores(one, True)

        return carry

    lax.fori_loop(0, 3, tile_step, 0)
    copies += made
    for t in range(3):
        copies += stores(t, False)
    for copy in copies:
        copy.wait()


def ffn_chunk(bits, blocks, act, cot, cot_t, wg, wu, wd, before, first, count):
    norm = not before
    rows, width = cot.shape
    bf = jnp.bfloat16
    piece = jax.ShapeDtypeStruct((blocks // 4, 2, width // blocks, count + count // 2), bf)
    units = jax.ShapeDtypeStruct((rows, wg.shape[1]), bf)
    by_rows = jax.ShapeDtypeStruct((rows, width), bf)
    outs = (units,) * 3 + (piece,) * 4
    ins = (cot, cot_t, wg, wu, wd)
    if norm:
        outs += (by_rows, by_rows, jax.ShapeDtypeStruct((width, rows), bf))
        ins = (*act, *ins)
    else:
        ins = (act[0], cot, act[1], cot_t, wg, wu, wd, *before)
    return pl.pallas_call(
        functools.partial(ffn_kernel, first, count, norm),
        out_shape=outs,
        in_specs=[SMEM] + [VMEM] * norm + [HBM] * (len(ins) - norm),
        out_specs=[HBM] * len(outs),
        scratch_shapes=(
            [pltpu.VMEM((rows, width), bf)] * 4
            + [pltpu.SemaphoreType.DMA((3, rows // BLOCK)), pltpu.SemaphoreType.DMA((3,))]
        ) * norm
        + [
            pltpu.VMEM((rows, width), bf),
            pltpu.VMEM((rows, width), bf),
            pltpu.VMEM((2, width, rows), bf),
            pltpu.VMEM((width, count), bf),
            pltpu.VMEM((width, count), bf),
            pltpu.VMEM((count, width), bf),
            pltpu.VMEM((3, rows, count), bf),
            pltpu.VMEM((3, blocks // 4, 2, 2, width // blocks, count), bf),
            pltpu.SemaphoreType.DMA((5,)),
            pltpu.SemaphoreType.DMA((2, 2)),
            pltpu.SemaphoreType.DMA((11,)),
        ],
        input_output_aliases={8 + i: i for i in range(len(before))},
        compiler_params=pltpu.CompilerParams(vmem_limit_bytes=VMEM_LIMIT),
        cost_estimate=CHEAP,
        name="ffn_chunk",
    )(bits, *ins)


def gradient_kernel(lefts, parts, bits_ref, *refs):
    def cut(count):
        nonlocal refs
        head, refs = refs[:count], refs[count:]
        return head

    left_hbm, right_hbm, pieces = cut(lefts), cut(len(parts)), cut(4)
    left, right, tiles, (in_sems, out_sems) = cut(lefts), cut(len(parts)), cut(len(parts)), refs
    tall = left[0].shape[0] // 2

    def left_in(which, i):
        rows = pl.ds(pl.multiple_of(i * tall, tall), tall)
        return pltpu.make_async_copy(left_hbm[which].at[rows], left[which].at[rows], in_sems.at[2 * which + i])

    right_in, copies, seen = [], [], set()
    for i, (which, _) in enumerate(parts):
        if which not in seen:
            left_in(which, 0).start()
        right_in.append(start(right_hbm[i], right[i], in_sems.at[2 * lefts + i]))
        if which not in seen:
            left_in(which, 1).start()
        seen.add(which)
    for i, (which, places) in enumerate(parts):
        right_in[i].wait()
        arrive = functools.partial(lambda which, i: left_in(which, i).wait(), which) if which in seen else None
        seen.discard(which)
        gradient_tile(tiles[i], left[which], right[i], arrive)
        for low, high, at, first in places:
            sent, kept = pieces[2 * first], pieces[2 * first + 1]
            copies += split_copies(tiles[i], low, high, at, sent, kept, first, bits_ref[first], out_sems, len(copies))
    for copy in copies:
        copy.wait()


def gradient_pieces(bits, blocks, lefts, rights, which, places):
    width, rows = lefts[0].shape
    bf = jnp.bfloat16
    flat = [place for part in places for place in part]
    widths = [sum(high - low for low, high, _, first in flat if first == axis) for axis in (0, 1)]
    pieces = [jax.ShapeDtypeStruct((blocks // 4, 2, width // blocks, w), bf) for w in widths for _ in range(2)]
    return pl.pallas_call(
        functools.partial(gradient_kernel, len(lefts), tuple(zip(which, places))),
        out_shape=tuple(pieces),
        in_specs=[SMEM] + [HBM] * (len(lefts) + len(rights)),
        out_specs=[HBM] * 4,
        scratch_shapes=[pltpu.VMEM(a.shape, bf) for a in (*lefts, *rights)]
        + [pltpu.VMEM((blocks // 4, 2, 2, width // blocks, r.shape[1]), bf) for r in rights]
        + [pltpu.SemaphoreType.DMA((2 * len(lefts) + len(rights),)), pltpu.SemaphoreType.DMA((2 * len(flat),))],
        compiler_params=pltpu.CompilerParams(vmem_limit_bytes=VMEM_LIMIT),
        cost_estimate=CHEAP,
        name="gradient_pieces",
    )(bits, *lefts, *rights)


def projection_kernel(dims, count, *refs):
    left_hbm, right_hbm, out_hbm, refs = refs[:count], refs[count : 2 * count], refs[2 * count], refs[2 * count + 1 :]
    left, right, (out, left_sems, right_sems, out_sems) = refs[:count], refs[count : 2 * count], refs[2 * count :]
    turned = dims is NT
    rows, width = out.shape
    tall = rows // 2

    def columns(ref, n):
        cut = pl.ds(pl.multiple_of(n * WIDE, WIDE), WIDE)
        return ref.at[cut, :] if turned else ref.at[:, cut]

    def right_in(p, n):
        return pltpu.make_async_copy(columns(right_hbm[p], n), columns(right[p], n), right_sems.at[p, n])

    def left_in(p, i):
        cut = pl.ds(pl.multiple_of(i * tall, tall), tall)
        return pltpu.make_async_copy(left_hbm[p].at[cut], left[p].at[cut], left_sems.at[p, i])

    def out_copy(n):
        wide = pl.ds(pl.multiple_of(n * WIDE, WIDE), WIDE)
        return pltpu.make_async_copy(out.at[:, wide], out_hbm.at[:, wide], out_sems.at[n])

    for p in range(count):
        right_in(p, 0).start()
        left_in(p, 0).start()
    for p in range(count):
        left_in(p, 1).start()
    for n in range(1, width // WIDE):
        for p in range(count):
            right_in(p, n).start()

    def step(j, carry):
        n, i = j // 2, j % 2

        @pl.when(i == 0)
        def _():
            for p in range(count):
                right_in(p, n).wait()

        @pl.when(n == 0)
        def _():
            for p in range(count):
                left_in(p, i).wait()

        cut = pl.ds(pl.multiple_of(i * tall, tall), tall)
        total = sum(matmul(left[p][cut, :], columns(right[p], n)[...], dims) for p in range(count))
        out[cut, pl.ds(pl.multiple_of(n * WIDE, WIDE), WIDE)] = total.astype(jnp.bfloat16)

        @pl.when(i == 1)
        def _():
            out_copy(n).start()

        return carry

    lax.fori_loop(0, 2 * width // WIDE, step, 0)
    for n in range(width // WIDE):
        out_copy(n).wait()


def projection(lefts, rights, dims):
    rows = lefts[0].shape[0]
    width = rights[0].shape[0 if dims is NT else 1]
    bf, count = jnp.bfloat16, len(lefts)
    return pl.pallas_call(
        functools.partial(projection_kernel, dims, count),
        out_shape=jax.ShapeDtypeStruct((rows, width), bf),
        in_specs=[HBM] * (2 * count),
        out_specs=HBM,
        scratch_shapes=[pltpu.VMEM(a.shape, bf) for a in (*lefts, *rights)]
        + [
            pltpu.VMEM((rows, width), bf),
            pltpu.SemaphoreType.DMA((count, 2)),
            pltpu.SemaphoreType.DMA((count, width // WIDE)),
            pltpu.SemaphoreType.DMA((width // WIDE,)),
        ],
        compiler_params=pltpu.CompilerParams(vmem_limit_bytes=VMEM_LIMIT),
        cost_estimate=CHEAP,
        name="projection",
    )(*lefts, *rights)


def add_two(one, two):
    return one.astype(jnp.float32) + two.astype(jnp.float32)


def second_steps(bits_ref, ins_hbm, ins, outs_hbm, outs):
    steps = []
    for first in range(0, outs[0].shape[0], 2):
        pair = pl.ds(first, 2)

        def compute(first=first):
            for z in (first, first + 1):
                for i in range(2):
                    kept, got, send, keep, mine = *ins[2 * i : 2 * i + 2], *outs[2 * i : 2 * i + 2], bits_ref[1 - i]
                    send[z] = kept[z, 1 - mine] + got[z, 1 - mine]
                    keep[z] = kept[z, mine] + got[z, mine]

        steps.append((
            [(a.at[pair], b.at[pair]) for a, b in zip(ins_hbm, ins)],
            compute,
            [(a.at[pair], b.at[pair]) for a, b in zip(outs, outs_hbm)],
        ))
    return steps


def third_steps(bits_ref, ins_hbm, ins, outs_hbm, outs):
    low = bits_ref[2] & 1
    steps = []
    for half, out, out_hbm in zip((1 - low, low), outs, outs_hbm):
        for high in range(2):
            block = 2 * high + half

            def compute(block=block, out=out, high=high):
                width = ins[0].shape[-1]
                out[high, :, :width] = ins[0][block] + ins[1][block]
                out[high, :, width:] = ins[2][block] + ins[3][block]

            steps.append((
                [(a.at[block], b.at[block]) for a, b in zip(ins_hbm, ins)], compute, [(out.at[high], out_hbm.at[high])]
            ))
    return steps


def fourth_steps(bits_ref, ins_hbm, ins, outs_hbm, outs):
    high = bits_ref[2] >> 1
    steps = []
    for block, out, out_hbm in zip((1 - high, high), outs, outs_hbm):

        def compute(block=block, out=out):
            for i in range(0, len(ins), 2):
                width = ins[i].shape[-1]
                out[:, i // 2 * width : (i // 2 + 1) * width] = ins[i][block] + ins[i + 1][block]

        steps.append((
            [(a.at[block], b.at[block]) for a, b in zip(ins_hbm, ins)], compute, [(out, out_hbm)]
        ))
    return steps


def sums_kernel(jobs, bits_ref, *refs):
    count, made = sum(j[1] for j in jobs), sum(j[2] for j in jobs)
    ins_hbm, outs_hbm, refs = refs[:count], refs[count : count + made], refs[count + made :]
    ins, outs, (in_sems, out_sems) = refs[:count], refs[count : count + made], refs[count + made :]
    steps = []
    for build, n, m in jobs:
        steps += build(bits_ref, ins_hbm[:n], ins[:n], outs_hbm[:m], outs[:m])
        ins_hbm, ins, outs_hbm, outs = ins_hbm[n:], ins[n:], outs_hbm[m:], outs[m:]
    stream(steps, in_sems, out_sems)


def sums(bits, second=None, third=None, fourth=None, cost=None):
    jobs, ins, outs = [], [], []
    if second is not None:
        made = [a.shape[:1] + a.shape[2:] for a in second]
        jobs.append((second_steps, 4, 4))
        ins, outs = ins + list(second), outs + made
    if third is not None:
        made = [(2, third[0].shape[1], third[0].shape[2] + third[2].shape[2])] * 2
        jobs.append((third_steps, 4, 2))
        ins, outs = ins + list(third), outs + made
    if fourth is not None:
        made = [(fourth[0].shape[1], sum(a.shape[2] for a in fourth[::2]))] * 2
        jobs.append((fourth_steps, len(fourth), 2))
        ins, outs = ins + list(fourth), outs + made
    bf = jnp.bfloat16
    results = pl.pallas_call(
        functools.partial(sums_kernel, tuple(jobs)),
        out_shape=tuple(jax.ShapeDtypeStruct(o, bf) for o in outs),
        in_specs=[SMEM] + [HBM] * len(ins),
        out_specs=[HBM] * len(outs),
        scratch_shapes=[pltpu.VMEM(a.shape, bf) for a in ins]
        + [pltpu.VMEM(o, bf) for o in outs]
        + [pltpu.SemaphoreType.DMA((4 * len(ins),)), pltpu.SemaphoreType.DMA((4 * len(outs),))],
        compiler_params=pltpu.CompilerParams(vmem_limit_bytes=VMEM_LIMIT),
        cost_estimate=cost or CHEAP,
        name="sums",
    )(bits, *ins)
    split = []
    for _, _, m in jobs:
        split.append(results[:m])
        results = results[m:]
    return split[0] if len(split) == 1 else split


def over_dp(array, flip):
    size = lax.axis_size("dp")
    return lax.ppermute(array, "dp", [(i, i ^ flip) for i in range(size)])


def after(arrays, *needed):
    return lax.optimization_barrier((arrays, needed))[0]


def first_stage(pieces):
    sent_a, kept_a, sent_b, kept_b = pieces
    return (kept_a, over_dp(sent_a, 1), kept_b, over_dp(sent_b, 2))


def second_stage(sent_a, kept_a, sent_b, kept_b):
    return (kept_a, over_dp(sent_a, 2), kept_b, over_dp(sent_b, 1))


def third_stage(send, keep):
    return (keep, over_dp(send, 4))


def fourth_stage(send, keep):
    return (keep, over_dp(send, 8))


def attention_sums_kernel(kv_half, index_ref, *refs):
    weights, refs = refs[:3], refs[3:]
    kept_a, got_a, kept_b, got_b, query_ref, key_ref, value_ref, out_ref, gain_ref, *helds, sems = refs
    copies = weight_rows(index_ref, weights, helds, sems)
    half = query_ref.shape[1] // 2
    first, second = add_two(kept_a[...], got_a[...]), add_two(kept_b[...], got_b[...])
    out_ref[:, :half] = first[:, :half]
    out_ref[:, half:] = first[:, 2 * half : 3 * half]
    query_ref[:, :half] = first[:, half : 2 * half]
    query_ref[:, half:] = second[:, :half]
    first, second = first[:, 3 * half :], second[:, half:]
    key_ref[...] = jnp.concatenate([first[:, :kv_half], second[:, :kv_half]], axis=1)
    value_ref[...] = jnp.concatenate([first[:, kv_half:], second[:, kv_half:]], axis=1)
    for copy in copies:
        copy.wait()
    gain_ref[...] = as_row(
        sum(products(ref[...], held[...]) for ref, held in zip((query_ref, key_ref, value_ref), helds))
    )


def attention_sums(index, weights, kept_a, got_a, kept_b, got_b, kv_half):
    rows, heads = kept_b.shape
    shapes = [(rows, heads), (rows, heads // 2), (rows, heads // 2), (rows, heads), (1, LANES)]
    *others, out, gain = pl.pallas_call(
        functools.partial(attention_sums_kernel, kv_half),
        out_shape=tuple(jax.ShapeDtypeStruct(shape, jnp.float32) for shape in shapes),
        in_specs=[SMEM] + [HBM] * 3 + [VMEM] * 4,
        out_specs=[VMEM] * 5,
        scratch_shapes=[pltpu.VMEM((rows, w.shape[1]), w.dtype) for w in weights] + [pltpu.SemaphoreType.DMA((3,))],
        compiler_params=pltpu.CompilerParams(vmem_limit_bytes=VMEM_LIMIT),
        cost_estimate=CHEAP,
        name="attention_sums",
    )(index, *weights, kept_a, got_a, kept_b, got_b)
    return gain, (*others, out.T)


def joined(pieces):
    sent_a, kept_a, sent_b, kept_b = pieces
    first, second = lax.axis_index("dp") & 1, lax.axis_index("dp") >> 1 & 1
    out = []
    for sent, kept, axis, mine in ((sent_a, kept_a, 2, first), (sent_b, kept_b, 1, second)):
        low = jnp.where(mine == 0, kept, sent)
        high = jnp.where(mine == 0, sent, kept)
        out.append(jnp.stack([low, high], axis=axis).reshape(-1, sent.shape[-1]))
    return out


def scatter_sum(grads):
    size = lax.axis_size("dp")
    bits = size.bit_length() - 1
    me = lax.axis_index("dp")
    rows, width = grads.shape
    work = grads.reshape((2,) * bits + (rows // size, width))
    for bit in range(bits):
        axis = bits - 1 - bit
        mine = (me >> bit) & 1
        sent = lax.dynamic_index_in_dim(work, 1 - mine, axis, keepdims=False)
        kept = lax.dynamic_index_in_dim(work, mine, axis, keepdims=False)
        work = kept.astype(jnp.float32) + over_dp(sent, 1 << bit).astype(jnp.float32)
        work = work.astype(grads.dtype)
    return work.astype(jnp.float32)


def weight_rows(index_ref, weights, helds, sems):
    rows = helds[0].shape[0]
    block = pl.ds(pl.multiple_of(index_ref[0] * rows, rows), rows)
    return [start(w.at[block], h, sems.at[i]) for i, (w, h) in enumerate(zip(weights, helds))]


def products(gradient, weight):
    return jnp.sum(gradient * weight.astype(jnp.float32), axis=1, keepdims=True)


def as_row(column):
    column = jnp.concatenate([column, jnp.zeros((LANES - column.shape[0], 1), jnp.float32)], axis=0)
    return jnp.broadcast_to(column, (LANES, LANES)).T[:1]


def ffn_sums_kernel(index_ref, *refs):
    weights, refs = refs[:2], refs[2:]
    ins, (gate_ref, up_ref, down_ref, gain_ref, *helds, sems) = refs[:-7], refs[-7:]
    copies = weight_rows(index_ref, weights, helds, sems)
    chunks = [
        (kept, got, at)
        for kept, got in zip(ins[0::2], ins[1::2])
        for at in range(0, kept.shape[-1], 3 * (CUTS[0][1] - CUTS[0][0]))
    ]
    for copy in copies:
        copy.wait()
    gain = 0.0
    for (low, high), (kept, got, at) in zip(CUTS, chunks):
        count, half = high - low, (high - low) // 2
        total = add_two(kept[:, at : at + 3 * count], got[:, at : at + 3 * count])
        gate, up = total[:, :count], total[:, count + half : 2 * count + half]
        gate_ref[:, low:high] = gate
        down_ref[:, low : low + half] = total[:, count : count + half]
        up_ref[:, low:high] = up
        down_ref[:, low + half : high] = total[:, 2 * count + half :]
        gain += products(gate, helds[0][:, low:high]) + products(up, helds[1][:, low:high])
    gain_ref[...] = as_row(gain)


def ffn_sums(index, weights, pieces):
    rows, units = pieces[0].shape[0], CUTS[-1][1]
    wide = jax.ShapeDtypeStruct((rows, units), jnp.float32)
    return pl.pallas_call(
        ffn_sums_kernel,
        out_shape=(wide,) * 3 + (jax.ShapeDtypeStruct((1, LANES), jnp.float32),),
        in_specs=[SMEM] + [HBM] * 2 + [VMEM] * len(pieces),
        out_specs=[VMEM] * 4,
        scratch_shapes=[pltpu.VMEM((rows, w.shape[1]), w.dtype) for w in weights] + [pltpu.SemaphoreType.DMA((2,))],
        compiler_params=pltpu.CompilerParams(vmem_limit_bytes=VMEM_LIMIT),
        cost_estimate=CHEAP,
        name="ffn_sums",
    )(index, *weights, *pieces)


def gain_gradient(products_sum, gain, index):
    total = products_sum + to_other_core(products_sum)
    rows = gain.shape[0] // lax.axis_size("dp")
    return total[0, :rows] / lax.dynamic_slice_in_dim(gain, index[0] * rows, rows)


def to_other_core(array):
    return lax.ppermute(array, "tensor", [(0, 1), (1, 0)])


def norm_grad(value, grad, gain):
    scale = lax.rsqrt(jnp.mean(value * value, axis=-1, keepdims=True) + epsilon)
    scaled = grad * gain
    back = scale * scaled - value * scale**3 * jnp.mean(scaled * value, axis=-1, keepdims=True)
    return back


def stream(steps, in_sems, out_sems):
    waits, count = [], 0
    for loads, _, _ in steps:
        waits.append([start(*pair, in_sems.at[count + i]) for i, pair in enumerate(loads)])
        count += len(loads)
    copies = []
    for wait, (_, compute, stores) in zip(waits, steps):
        for copy in wait:
            copy.wait()
        compute()
        for pair in stores:
            copies.append(start(*pair, out_sems.at[len(copies)]))
    for copy in copies:
        copy.wait()


def row_kernel(function, turned, count, outs, *refs):
    def cut(n):
        nonlocal refs
        head, refs = refs[:n], refs[n:]
        return head

    ins_hbm, vector, outs_hbm = cut(count), cut(1), cut(outs)
    ins, held, (in_sems, out_sems) = cut(count), cut(outs), refs
    gain = vector[0][...][None, :]
    direct = [ref for ref, t in zip(held, turned) if not t]
    steps = []
    for i in range(ins[0].shape[0] // BLOCK):
        rows = pl.ds(i * BLOCK, BLOCK)
        places = [(slice(None), rows) if t else (rows, slice(None)) for t in turned]

        def compute(i=i, rows=rows, places=places):
            def step(j, carry):
                few = pl.ds(pl.multiple_of(i * BLOCK + j * FEW, FEW), FEW)
                results = function(*(ref[few, :].astype(jnp.float32) for ref in ins), gain)
                for ref, result in zip(direct, results):
                    ref[few, :] = result.astype(jnp.bfloat16)
                return carry

            if direct:
                lax.fori_loop(0, BLOCK // FEW, step, 0, unroll=8)
            for n, t in enumerate(turned):
                if t:
                    source = ins[0] if t == 2 else held[n - 1]
                    held[n][places[n]] = source[rows, :].astype(jnp.float32).T.astype(jnp.bfloat16)

        steps.append((
            [(a.at[rows], b.at[rows]) for a, b in zip(ins_hbm, ins)],
            compute,
            [(a.at[place], b.at[place]) for a, b, place in zip(held, outs_hbm, places)],
        ))
    stream(steps, in_sems, out_sems)


def row_call(function, name, ins, vector, turned):
    rows, width = ins[0].shape
    bf, blocks = jnp.bfloat16, rows // BLOCK
    outs = [jax.ShapeDtypeStruct((width, rows) if t else (rows, width), bf) for t in turned]
    return pl.pallas_call(
        functools.partial(row_kernel, function, turned, len(ins), len(outs)),
        out_shape=tuple(outs),
        in_specs=[HBM] * len(ins) + [VMEM],
        out_specs=[HBM] * len(outs),
        scratch_shapes=[pltpu.VMEM(a.shape, bf) for a in (*ins, *outs)]
        + [pltpu.SemaphoreType.DMA((len(ins) * blocks,)), pltpu.SemaphoreType.DMA((len(outs) * blocks,))],
        compiler_params=pltpu.CompilerParams(vmem_limit_bytes=VMEM_LIMIT),
        cost_estimate=CHEAP,
        name=name,
    )(*ins, vector)


def norm_rows(x, own, got, gain):
    hidden = x + (own + got)
    norm = lax.rsqrt(jnp.mean(hidden * hidden, axis=-1, keepdims=True) + epsilon)
    act = hidden * norm * gain
    return hidden, act


def middle_rows(hidden, own, got, cot, gain):
    return (cot + norm_grad(hidden, own + got, gain),)


def output_rows(hidden, own, got, gain):
    return (hidden + (own + got),)


def input_rows(x, gatt, own, got, gain):
    return (gatt + norm_grad(x, own + got, gain),)


def attention_grads(total, half, kv_half):
    names = (("out", half), ("query", half), ("out", half), ("key", kv_half), ("value", kv_half))
    names += (("query", half), ("key", kv_half), ("value", kv_half))
    found, at = {}, 0
    for name, count in names:
        found.setdefault(name, []).append(total[:, at : at + count])
        at += count
    found = {name: jnp.concatenate(parts, axis=1) for name, parts in found.items()}
    return found["query"], found["key"], found["value"], found["out"].T


def plain(names, chunk, backward):
    v = dict(names)
    layer_input, hidden, bits, blocks, size = (v[n] for n in ("layer_input", "hidden", "bits", "blocks", "size"))
    rows, width = layer_input.shape
    half, kv_half, heads = v["half"], v["kv_half"], v["heads"]
    pieces = []
    for i in range(len(CUTS)):
        units, piece = chunk(i, whole=True)
        pieces.append(piece)
    hidden_units, grad_gate_lin, grad_up_lin = units
    two_own = projection([grad_gate_lin, grad_up_lin], [v["w_gate"], v["w_up"]], NT)
    ffn_own = projection([hidden_units], [v["w_down"]], NN)
    grad_attention, grad_attention_t = row_call(
        middle_rows, "middle", [hidden, two_own, to_other_core(two_own), v["cotangent"]], v["gain_two"], [0, 1]
    )
    (output,) = row_call(output_rows, "output", [hidden, ffn_own, to_other_core(ffn_own)], v["gain_two"], [0])
    back_one = backward(0, gatt=grad_attention)
    pieces.append(gradient_pieces(
        bits, blocks, [grad_attention_t, v["act_one_t"]], [v["mixed"], *back_one], [0, 1, 1],
        [((0, half, 0, 0), (half, heads, 0, 1)), ((0, half, half, 0),), ((0, half, half, 1),)],
    ))
    *back_two, one_own = backward(1, *back_one, gatt=grad_attention)
    pieces.append(gradient_pieces(
        bits, blocks, [v["act_one_t"]], back_two, [0, 0], [((0, half, 0, 0),), ((0, half, 0, 1),)]
    ))
    (grad_input,) = row_call(
        input_rows, "input", [layer_input, grad_attention, one_own, to_other_core(one_own)],
        v["attn_gain"], [0],
    )
    total = scatter_sum(jnp.concatenate([p for piece in pieces for p in joined(piece)], axis=1))
    gates, ups, downs = [], [], []
    for low, high in CUTS:
        count = high - low
        parts = jnp.split(total[:, 3 * low : 3 * high], [count, count * 3 // 2, count * 5 // 2], axis=1)
        for found, part in zip((gates, downs, ups, downs), parts):
            found.append(part)
    grad_gate, grad_up = jnp.concatenate(gates, axis=1), jnp.concatenate(ups, axis=1)
    attention = attention_grads(total[:, 3 * CUTS[-1][1] :], half, kv_half)

    def gain_of(gradients, weights, gain):
        count = width // size
        cut = [lax.dynamic_slice_in_dim(v[w], v["me"] * count, count).astype(jnp.float32) for w in weights]
        return gain_gradient(sum(jnp.sum(g * w, axis=1) for g, w in zip(gradients, cut))[None, :], gain, v["index"])

    return (
        output,
        grad_input,
        gain_of(attention[:3], ("w_query", "w_key", "w_value"), v["attn_gain"]),
        *attention,
        gain_of((grad_gate, grad_up), ("w_gate", "w_up"), v["ffn_gain"]),
        grad_gate,
        grad_up,
        jnp.concatenate(downs, axis=1).T,
    )


def per_device(
    layer_input,
    branch_point,
    attn_gain,
    w_query,
    w_key,
    w_value,
    w_out,
    ffn_gain,
    w_gate,
    w_up,
    w_down,
    cotangent,
):
    rows, width = layer_input.shape
    size = lax.axis_size("dp")
    by_kernel = size == KERNEL_BLOCKS
    blocks = KERNEL_BLOCKS
    me = lax.axis_index("dp")
    index = me.reshape(1).astype(jnp.int32)
    bits = jnp.stack([me & 1, me >> 1 & 1, me >> 2 & 3]).astype(jnp.int32)
    rope = rope_tables()
    act_one_t, queries, keys, values, mixed, log_sums, attn_own = attention_forward(
        branch_point, layer_input, attn_gain, w_query, w_key, w_value, w_out, rope
    )
    attn_got = to_other_core(attn_own)
    kv_half = w_key.shape[1] // 2
    w_key_value = jnp.concatenate(
        [w_key[:, :kv_half], w_value[:, :kv_half], w_key[:, kv_half:], w_value[:, kv_half:]], axis=1
    )
    (cot_t,) = row_call(lambda *_: (), "turn", [cotangent], ffn_gain, [2])
    gain_two = ffn_gain
    *units, sent_a, kept_a, sent_b, kept_b, hidden, act_two, act_two_t = ffn_chunk(
        bits, blocks, (after(gain_two, cot_t, w_key_value), layer_input, attn_own, attn_got), cotangent, cot_t,
        w_gate, w_up, w_down, [], 0, CUTS[0][1],
    )
    first_piece = (sent_a, kept_a, sent_b, kept_b)
    heads, kv = mixed.shape[1], w_key.shape[1]
    half = heads // 2
    def chunk(i, *needed, whole=False):
        nonlocal units
        piece = first_piece
        if i > 0:
            low, high = CUTS[i]
            made = ffn_chunk(
                bits, blocks, (after(act_two, *needed), act_two_t), cotangent, cot_t,
                w_gate, w_up, w_down, units, low, high - low,
            )
            units, piece = made[:3], made[3:]
        return (units, piece) if whole else piece

    def backward(part, *needed, gatt=None):
        return attention_backward(
            part, branch_point, after(grad_attention if gatt is None else gatt, *needed), queries, keys, values, log_sums,
            w_out, w_query, w_key_value, rope, list(needed[:2]) if part else [],
        )

    if not by_kernel:
        return plain(locals(), chunk, backward)
    pieces = [chunk(0)]
    one = [first_stage(pieces[0])]
    pieces.append(chunk(1))
    one.append(first_stage(pieces[1]))
    pieces.append(chunk(2, pieces[1]))
    pieces[2], one[0] = after((pieces[2], one[0]))
    joint = sums(bits, second=one[0])
    two = [second_stage(*joint)]
    pieces.append(chunk(3, joint))
    *units, pieces[3], one[1], two[0] = after((*units, pieces[3], one[1], two[0]))
    joint = sums(bits, second=one[1], third=two[0])
    two.append(second_stage(*joint[0]))
    three = [third_stage(*joint[1])]
    one.append(first_stage(after(pieces[2], units)))
    hidden_units, grad_gate_lin, grad_up_lin = units
    two_own = projection(after([grad_gate_lin, grad_up_lin], joint), [w_gate, w_up], NT)
    two_own, three[0] = after((two_own, three[0]))
    two_got = to_other_core(two_own)
    ffn_own = projection([after(hidden_units, two_own)], [w_down], NN)
    ffn_own, one[2], two[1] = after((ffn_own, one[2], two[1]))
    joint = sums(bits, second=one[2], third=two[1], cost=LONG)
    two.append(second_stage(*joint[0]))
    three.append(third_stage(*joint[1]))
    one.append(first_stage(after(pieces[3], ffn_own)))
    grad_attention, grad_attention_t = row_call(
        middle_rows, "middle", [hidden, two_own, two_got, after(cotangent, joint)], gain_two, [0, 1]
    )
    grad_attention, three[0], three[1] = after((grad_attention, three[0], three[1]))
    joint = sums(bits, fourth=(*three[0], *three[1]))
    four = [fourth_stage(*joint)]
    back_one = backward(0, grad_attention, joint)
    back_one, two[2], one[3], four[0] = after((back_one, two[2], one[3], four[0]))
    joint = sums(bits, second=one[3], third=two[2])
    two.append(second_stage(*joint[0]))
    three.append(third_stage(*joint[1]))
    early = gradient_pieces(
        bits, blocks, [after(grad_attention_t, joint), act_one_t], [mixed, *back_one], [0, 1, 1],
        [((0, half, 0, 0), (half, heads, 0, 1)), ((0, half, half, 0),), ((0, half, half, 1),)],
    )
    early, two[3], three[2] = after((early, two[3], three[2]))
    joint = sums(bits, third=two[3], fourth=three[2])
    three.append(third_stage(*joint[0]))
    four.append(fourth_stage(*joint[1]))
    early_one = first_stage(early)
    ffn_got = to_other_core(after(ffn_own, early))
    *back_two, one_own = backward(1, *back_one, early, joint)
    back_two, one_own, early_one, three[3], four[1], ffn_got = after(
        (back_two, one_own, early_one, three[3], four[1], ffn_got)
    )
    one_got = to_other_core(one_own)
    joint = sums(bits, second=early_one, fourth=three[3])
    early_two = second_stage(*joint[0])
    four.append(fourth_stage(*joint[1]))
    late = gradient_pieces(
        bits, blocks, [after(act_one_t, joint)], back_two, [0, 0], [((0, half, 0, 0),), ((0, half, 0, 1),)]
    )
    late, one_got = after((late, one_got))
    late_one = first_stage(late)
    (output,) = row_call(output_rows, "output", [hidden, after(ffn_own, late), ffn_got], gain_two, [0])
    output, early_two, four[2] = after((output, early_two, four[2]))
    joint = sums(bits, third=early_two)
    early_three = third_stage(*joint)
    (grad_input,) = row_call(
        input_rows, "input", [layer_input, after(grad_attention, joint), one_own, one_got],
        attn_gain, [0],
    )
    grad_input, late_one, early_three = after((grad_input, late_one, early_three))
    joint = sums(bits, second=late_one, fourth=early_three)
    late_two = second_stage(*joint[0])
    early_four = fourth_stage(*joint[1])
    *ffn_grads, ffn_products = ffn_sums(index, [w_gate, w_up], after([p for piece in four for p in piece], joint))
    ffn_grads, late_two = after((ffn_grads, late_two))
    grad_gate, grad_up, grad_down = ffn_grads
    joint = sums(bits, third=late_two)
    late_three = third_stage(*joint)
    grad_ffn_gain = gain_gradient(after(ffn_products, joint), ffn_gain, index)
    late_three, early_four, grad_ffn_gain = after((late_three, early_four, grad_ffn_gain))
    joint = sums(bits, fourth=late_three)
    late_four = fourth_stage(*joint)
    products_sum, attention = attention_sums(index, [w_query, w_key, w_value], *early_four, *late_four, kv_half)
    grad_attn_gain = gain_gradient(products_sum, attn_gain, index)
    return (
        output,
        grad_input,
        grad_attn_gain,
        *attention,
        grad_ffn_gain,
        grad_gate,
        grad_up,
        grad_down.T,
    )


def solution(mesh):
    placed = (
        P("dp", None),
        P("dp", None),
        P(),
        P(None, "tensor"),
        P(None, "tensor"),
        P(None, "tensor"),
        P("tensor", None),
        P(),
        P(None, "tensor"),
        P(None, "tensor"),
        P("tensor", None),
        P("dp", None),
    )
    return jax.shard_map(
        per_device,
        mesh=mesh,
        in_specs=placed,
        out_specs=(
            P("dp", None),
            P("dp", None),
            P("dp"),
            P("dp", "tensor"),
            P("dp", "tensor"),
            P("dp", "tensor"),
            P("tensor", "dp"),
            P("dp"),
            P("dp", "tensor"),
            P("dp", "tensor"),
            P("tensor", "dp"),
        ),
        check_vma=False,
    )
```
